32 devices in a mesh: img: 4 (over y, core), ha: 8 (over z, x).
Axes of the slice: x: 2, y: 2, z: 4, core: 2. Of those that a mesh axis runs over, the one named last changes fastest.
Arguments:
- image: bfloat16 [4, 64, 64, 512], P('img', 'ha'), may hold values from -6 to 6
- mask: int32 [4, 64, 64], P('img'), may hold values from 0 to 1, as said below
- timestep: int32 [4], P('img'), may hold values from 0 to 999
- pooled: float32 [4, 1024], P('img'), may hold values from -6 to 6
- text: bfloat16 [4, 77, 4096], P('img'), may hold values from -6 to 6
- text_mask: int32 [4, 77], P('img'), may hold values from 0 to 1, as said below
- cotangent: bfloat16 [4, 64, 64, 1024], P('img', 'ha'), may hold values from -6 to 6
- conv1_weight: bfloat16 [1024, 4608], P(('img', 'ha')), may hold values from -0.09375 to 0.09375
- conv2_weight: bfloat16 [1024, 9216], P(('img', 'ha')), may hold values from -0.0625 to 0.0625
- skip_weight: bfloat16 [1024, 512], P(('img', 'ha')), may hold values from -0.25 to 0.25
- emb_weight: bfloat16 [2048, 1024], P(('img', 'ha')), may hold values from -0.1875 to 0.1875
- qkv_weight: bfloat16 [3072, 1024], P(('img', 'ha')), may hold values from -0.1875 to 0.1875
- out_weight: bfloat16 [1024, 1024], P(('img', 'ha')), may hold values from -4 to 4
- text_weight: bfloat16 [4096, 2048], P('img', 'ha'), may hold values from -0.09375 to 0.09375
- gn1_gain: bfloat16 [512], P(('img', 'ha')), may hold values from 0.5 to 1.5
- gn1_bias: bfloat16 [512], P(('img', 'ha')), may hold values from -3 to 3
- emb_bias: bfloat16 [2048], P(('img', 'ha')), may hold values from -3 to 3
- gn2_gain: bfloat16 [1024], P(('img', 'ha')), may hold values from 0.5 to 1.5
- gn2_bias: bfloat16 [1024], P(('img', 'ha')), may hold values from -3 to 3
- skip_bias: bfloat16 [1024], P(('img', 'ha')), may hold values from -3 to 3
- gn3_gain: bfloat16 [1024], P(('img', 'ha')), may hold values from 0.5 to 1.5
- gn3_bias: bfloat16 [1024], P(('img', 'ha')), may hold values from -3 to 3
- out_bias: bfloat16 [1024], P(('img', 'ha')), may hold values from -3 to 3
Outputs:
- output: bfloat16 [4, 64, 64, 1024], P('img', 'ha')
- image_grad: float32 [4, 64, 64, 512], P('img', 'ha')
- conv1_grad: float32 [1024, 4608], P(('img', 'ha'))
- conv2_grad: float32 [1024, 9216], P(('img', 'ha'))
- skip_grad: float32 [1024, 512], P(('img', 'ha'))
- emb_grad: float32 [2048, 1024], P(('img', 'ha'))
- qkv_grad: float32 [3072, 1024], P(('img', 'ha'))
- out_grad: float32 [1024, 1024], P(('img', 'ha'))
- text_grad: float32 [4096, 2048], P('img', 'ha')
- gn1_gain_grad: float32 [512], P(('img', 'ha'))
- gn1_bias_grad: float32 [512], P(('img', 'ha'))
- emb_bias_grad: float32 [2048], P(('img', 'ha'))
- gn2_gain_grad: float32 [1024], P(('img', 'ha'))
- gn2_bias_grad: float32 [1024], P(('img', 'ha'))
- skip_bias_grad: float32 [1024], P(('img', 'ha'))
- gn3_gain_grad: float32 [1024], P(('img', 'ha'))
- gn3_bias_grad: float32 [1024], P(('img', 'ha'))
- out_bias_grad: float32 [1024], P(('img', 'ha'))
The draws below stay inside these ranges and needn't reach their ends.
Inputs may be any that keep to these rules, and one draw needn't show every extreme that they name: `mask`: each image's valid pixels are its first hv rows and first wv columns, hv at least 32, wv at least 32. Split the images, from image 0 on, into consecutive groups of 1: each group contains one image with all 64 rows valid. `text_mask`: each image's counted text tokens are its first 1 to 77 tokens; some image counts all of them.
All inputs are finite; a program needn't handle non-finite values.
Results may differ from the reference program's by a relative error of at most 0.02.
Values may be sent and summed in bfloat16 or wider, within the bound.
No kernel may reach another device: no remote copies, remote signals or barrier semaphores. Data moves between devices by JAX's collectives and lax.ppermute only.
A program may use at most 320 MiB of HBM per device.

```python
import math
import jax
import jax.numpy as jnp
from jax import lax

C_IN = 512
C = 1024
HEADS = 16
HEAD_DIM = 64
GROUPS = 32
EMB = 1024
TEXT_DIM = 4096
TEXT_LEN = 77
HEIGHT = 64
WIDTH = 64
IMG_DEV = 1
IMAGES = 4


def draw_mask(key, part):
    key = jax.random.fold_in(key, 11)
    first_key, second_key, third_key = jax.random.split(key, 3)
    valid_rows = jax.random.randint(first_key, (IMAGES,), HEIGHT // 2, HEIGHT + 1)
    valid_cols = jax.random.randint(second_key, (IMAGES,), WIDTH // 2, WIDTH + 1)
    chosen = jax.random.randint(third_key, (IMAGES // IMG_DEV,), 0, IMG_DEV)
    full_image = jnp.arange(IMAGES) % IMG_DEV == jnp.repeat(chosen, IMG_DEV)
    valid_rows = jnp.where(full_image, HEIGHT, valid_rows)
    row_ok = jnp.arange(HEIGHT)[None, :, None] < valid_rows[:, None, None]
    col_ok = jnp.arange(WIDTH)[None, None, :] < valid_cols[:, None, None]
    return (row_ok & col_ok).astype(jnp.int32)


def draw_text_mask(key, part):
    key = jax.random.fold_in(key, 23)
    first_key, second_key = jax.random.split(key, 2)
    lengths = jax.random.randint(first_key, (IMAGES,), 1, TEXT_LEN + 1)
    chosen = jax.random.randint(second_key, (), 0, IMAGES)
    lengths = jnp.where(jnp.arange(IMAGES) == chosen, TEXT_LEN, lengths)
    return (jnp.arange(TEXT_LEN)[None, :] < lengths[:, None]).astype(jnp.int32)


def touch_ends(values, stream_key, smallest, top_value):
    dims = values.shape
    index_at = [jax.random.randint(jax.random.fold_in(stream_key, axis), (), 0, dims[axis]) for axis in range(len(dims))]
    values = values.at[tuple(index_at)].set(smallest)
    longest = dims.index(max(dims))
    index_at[longest] = (index_at[longest] + 1) % dims[longest]
    return values.at[tuple(index_at)].set(top_value)


def shard_levels(own_key, extent, shards, least, largest):
    loudness, own = 1.0, jax.random.fold_in(own_key, 6)
    for axis_at, parts in shards:
        steps = jnp.exp(jax.random.uniform(jax.random.fold_in(own, axis_at), (parts,), jnp.float32, least / len(shards), largest / len(shards)))
        loudness = loudness * jnp.repeat(steps, extent[axis_at] // parts).reshape([-1 if axis == axis_at else 1 for axis in range(len(extent))])
    return loudness


def noise(own_key, extent, scale, most, cuts=(), kind=jnp.bfloat16):
    gain = shard_levels(own_key, extent, cuts, -0.22, 0.18) if cuts else 1.0
    array = jax.random.normal(own_key, extent, jnp.float32) * scale * gain
    return jnp.minimum(jnp.maximum(array, -most), most).astype(kind)


def setup_inputs(seed: int = 0) -> dict:
    splits = jax.random.split(jax.random.key(seed), 24)
    return {
        "image": noise(splits[0], (IMAGES, HEIGHT, WIDTH, C_IN), 1.0, 6.0, ((0, 4), (1, 8))),
        "mask": draw_mask(jax.random.fold_in(splits[23], 71), 0),
        "timestep": touch_ends(jax.random.randint(splits[2], (IMAGES,), 0, 1000), jax.random.fold_in(splits[2], 1), 0, 999).astype(jnp.int32),
        "pooled": noise(splits[3], (IMAGES, EMB), 1.0, 6.0, ((0, 4),), jnp.float32),
        "text": noise(splits[4], (IMAGES, TEXT_LEN, TEXT_DIM), 1.0, 6.0, ((0, 4),)),
        "text_mask": draw_text_mask(jax.random.fold_in(splits[23], 71), 0),
        "cotangent": noise(splits[6], (IMAGES, HEIGHT, WIDTH, C), 1.0, 6.0, ((0, 4), (1, 8))),
        "conv1_weight": noise(splits[7], (C, 9 * C_IN), (9 * C_IN) ** -0.5, 0.09375, ((0, 32),)),
        "conv2_weight": noise(splits[8], (C, 9 * C), (9 * C) ** -0.5, 0.0625, ((0, 32),)),
        "skip_weight": noise(splits[9], (C, C_IN), C_IN ** -0.5, 0.25, ((0, 32),)),
        "emb_weight": noise(splits[10], (2 * C, EMB), EMB ** -0.5, 0.1875, ((0, 32),)),
        "qkv_weight": noise(splits[11], (3 * C, C), C ** -0.5, 0.1875, ((0, 32),)),
        "out_weight": noise(splits[12], (C, C), 2 ** -0.5, 4.0, ((0, 32),)),
        "text_weight": noise(splits[13], (TEXT_DIM, 2 * C), TEXT_DIM ** -0.5, 0.09375, ((0, 4), (1, 8))),
        "gn1_gain": jnp.clip(1.0 + 0.1 * jax.random.normal(splits[14], (C_IN,), jnp.float32), 0.5, 1.5).astype(jnp.bfloat16),
        "gn1_bias": noise(splits[15], (C_IN,), 0.5, 3.0, ((0, 32),)),
        "emb_bias": noise(splits[16], (2 * C,), 0.5, 3.0, ((0, 32),)),
        "gn2_gain": jnp.clip(1.0 + 0.1 * jax.random.normal(splits[17], (C,), jnp.float32), 0.5, 1.5).astype(jnp.bfloat16),
        "gn2_bias": noise(splits[18], (C,), 0.5, 3.0, ((0, 32),)),
        "skip_bias": noise(splits[19], (C,), 0.5, 3.0, ((0, 32),)),
        "gn3_gain": jnp.clip(1.0 + 0.1 * jax.random.normal(splits[20], (C,), jnp.float32), 0.5, 1.5).astype(jnp.bfloat16),
        "gn3_bias": noise(splits[21], (C,), 0.5, 3.0, ((0, 32),)),
        "out_bias": noise(splits[22], (C,), 0.5, 3.0, ((0, 32),)),
    }


@jax.custom_vjp
def low(v):
    return lax.optimization_barrier(v.astype(jnp.bfloat16)).astype(jnp.float32)

@jax.custom_vjp
def low_back(v):
    return v

def low_keep(v):
    return (low(v), None)

def low_pass(kept, grad):
    return (grad,)

def back_keep(v):
    return (v, None)

def back_low(kept, grad):
    return (low(grad),)
low.defvjp(low_keep, low_pass)
low_back.defvjp(back_keep, back_low)
neg_big = -1e+30
eps_norm = 1e-05
top_precision = lax.Precision.HIGHEST

def group_norm(features, validity, gain_vec, bias_vec):
    pixels, channels = features.shape
    per_group = channels // GROUPS
    shaped = features.reshape(pixels, GROUPS, per_group)
    masked = shaped * validity[:, None, None]
    entries = jnp.sum(validity) * per_group
    group_mean = lax.optimization_barrier(jnp.sum(masked, axis=(0, 2))) / entries
    square = lax.optimization_barrier(jnp.sum(masked * shaped, axis=(0, 2))) / entries
    inv_std = lax.rsqrt(square - group_mean * group_mean + eps_norm)
    normed = (shaped - group_mean[None, :, None]) * inv_std[None, :, None]
    return normed.reshape(pixels, channels) * gain_vec + bias_vec

def columns(features):
    padded = jnp.pad(features, ((1, 1), (1, 1), (0, 0)))
    taps = [padded[row_off:row_off + HEIGHT, col_off:col_off + WIDTH] for row_off in range(3) for col_off in range(3)]
    return jnp.concatenate(taps, axis=-1).reshape(HEIGHT * WIDTH, -1)

def convolve(features, weight):
    return jnp.dot(columns(features), weight.T, precision=top_precision)

def attend(queries, keys_all, values_all, key_valid):
    head_keys = keys_all.reshape(-1, HEADS, HEAD_DIM)
    head_values = values_all.reshape(-1, HEADS, HEAD_DIM)
    scale_factor = 1.0 / math.sqrt(HEAD_DIM)

    def one_block(query_rows):
        head_queries = query_rows.reshape(-1, HEADS, HEAD_DIM)
        scores = low_back(jnp.einsum('qhd,khd->hqk', head_queries, head_keys, precision=top_precision) * scale_factor)
        scores = jnp.where(key_valid[None, None, :] > 0, scores, neg_big)
        highest = lax.optimization_barrier(jnp.max(scores, axis=-1, keepdims=True))
        weights = jnp.exp(scores - highest)
        totals = lax.optimization_barrier(jnp.sum(weights, axis=-1))
        mixed = jnp.einsum('hqk,khd->qhd', low(weights), head_values, precision=top_precision)
        mixed = mixed / jnp.transpose(totals)[:, :, None]
        return mixed.reshape(-1, HEADS * HEAD_DIM)
    block_rows = min(512, HEIGHT * WIDTH)
    blocks = queries.reshape(-1, block_rows, HEADS * HEAD_DIM)
    return lax.map(jax.checkpoint(one_block), blocks).reshape(-1, HEADS * HEAD_DIM)

def forward(image_rows, validity, embedding, text_rows, text_valid, params):
    conv1_w, conv2_w, skip_w, emb_w, qkv_w, out_w, text_w, gain_one, bias_one, emb_b, gain_two, bias_two, skip_b, gain_three, bias_three, out_b = params
    first_act = low(jax.nn.silu(group_norm(image_rows, validity, gain_one, bias_one)) * validity[:, None])
    hidden_one = low_back(convolve(first_act.reshape(HEIGHT, WIDTH, C_IN), conv1_w))
    modulation = jnp.dot(embedding, emb_w.T, precision=top_precision) + emb_b
    second_pre = group_norm(hidden_one, validity, gain_two, bias_two) * (1.0 + modulation[:C]) + modulation[C:]
    second_act = low(jax.nn.silu(second_pre) * validity[:, None])
    skipped = jnp.dot(image_rows, skip_w.T, precision=top_precision)
    residual = low_back(convolve(second_act.reshape(HEIGHT, WIDTH, C), conv2_w) + skipped) + skip_b
    normed = low(group_norm(residual, validity, gain_three, bias_three))
    triple = low_back(low(jnp.dot(normed, qkv_w.T, precision=top_precision)))
    text_pairs = low_back(low(jnp.dot(text_rows, text_w, precision=top_precision)))
    keys_all = jnp.concatenate([text_pairs[:, :C], triple[:, C:2 * C]], axis=0)
    values_all = jnp.concatenate([text_pairs[:, C:], triple[:, 2 * C:]], axis=0)
    key_valid = jnp.concatenate([text_valid, validity])
    mixed = low_back(low(attend(triple[:, :C], keys_all, values_all, key_valid)))
    return residual + jnp.dot(mixed, out_w.T, precision=top_precision) + out_b

def reference(image, mask, timestep, pooled, text, text_mask, cotangent, conv1_weight, conv2_weight, skip_weight, emb_weight, qkv_weight, out_weight, text_weight, gn1_gain, gn1_bias, emb_bias, gn2_gain, gn2_bias, skip_bias, gn3_gain, gn3_bias, out_bias):
    params = tuple((item.astype(jnp.float32) for item in (conv1_weight, conv2_weight, skip_weight, emb_weight, qkv_weight, out_weight, text_weight, gn1_gain, gn1_bias, emb_bias, gn2_gain, gn2_bias, skip_bias, gn3_gain, gn3_bias, out_bias)))
    half_width = EMB // 2
    frequency = jnp.exp(-math.log(10000.0) * jnp.arange(half_width, dtype=jnp.float32) / half_width)
    angles = timestep.astype(jnp.float32)[:, None] * frequency[None, :]
    embedding = low(jax.nn.silu(jnp.concatenate([jnp.cos(angles), jnp.sin(angles)], axis=1) + pooled))

    def per_image(running, inputs):
        image_one, valid_one, emb_one, text_one, tvalid_one, cot_one = inputs

        def run(image_rows, weights):
            return forward(image_rows, valid_one, emb_one, text_one, tvalid_one, weights)
        result, pullback = jax.vjp(run, image_one, params)
        image_part, param_grads = pullback(cot_one)
        running = jax.tree.map(lambda left, right: left + right, running, param_grads)
        return (running, (result, image_part))
    zeros_start = jax.tree.map(jnp.zeros_like, params)
    inputs = (image.astype(jnp.float32).reshape(IMAGES, HEIGHT * WIDTH, C_IN), mask.astype(jnp.float32).reshape(IMAGES, HEIGHT * WIDTH), embedding, text.astype(jnp.float32), text_mask.astype(jnp.float32), cotangent.astype(jnp.float32).reshape(IMAGES, HEIGHT * WIDTH, C))
    grads, (results, image_grads) = lax.scan(per_image, zeros_start, inputs)
    return (results.reshape(IMAGES, HEIGHT, WIDTH, C).astype(jnp.bfloat16), image_grads.reshape(IMAGES, HEIGHT, WIDTH, C_IN), grads[0], grads[1], grads[2], grads[3], grads[4], grads[5], grads[6], grads[7], grads[8], grads[9], grads[10], grads[11], grads[12], grads[13], grads[14], grads[15])
```

```python
import functools
import math

import jax
import jax.numpy as jnp
from jax import lax
from jax.experimental import pallas as pl
from jax.experimental.pallas import tpu as pltpu
from jax.sharding import Mesh
from jax.sharding import PartitionSpec as P

C_IN = 512
C = 1024
HEADS = 16
HEAD_DIM = 64
GROUPS = 32
EMB = 1024
HEIGHT = 64
WIDTH = 64


neg_big = -1e30
eps_norm = 1e-05


def extended(cells, sides, width):
    for axis, dim in sides:
        count = lax.axis_size(axis)
        ends = count - 1
        head = lax.slice_in_dim(cells, 0, width, axis=dim)
        tail = lax.slice_in_dim(cells, cells.shape[dim] - width, cells.shape[dim], axis=dim)
        cells = jnp.concatenate(
            [
                lax.ppermute(tail, axis, [(i, (i + 1) % count) for i in range(ends)]),
                cells,
                lax.ppermute(head, axis, [((i + 1) % count, i) for i in range(ends)]),
            ],
            axis=dim,
        )
    return cells


def rounded(values):
    return values.astype(jnp.bfloat16)


def silu_slope(inputs):
    sigmoid = jax.nn.sigmoid(inputs)
    return sigmoid * (1.0 + inputs * (1.0 - sigmoid))


def group_view(features):
    return features.reshape(
        features.shape[0], features.shape[1], GROUPS, features.shape[2] // GROUPS
    )


def group_totals(first_sum, second_sum):
    return lax.psum((first_sum, second_sum), "ha")


def norm_stats(features, validity, counts):
    shaped = group_view(features)
    masked = shaped * validity[:, :, None, None]
    first_sum, second_sum = group_totals(
        jnp.sum(masked, axis=(1, 3)), jnp.sum(masked * shaped, axis=(1, 3))
    )
    entries = counts[:, None] * shaped.shape[3]
    group_mean = first_sum / entries
    inv_std = lax.rsqrt(second_sum / entries - group_mean * group_mean + eps_norm)
    return (group_mean, inv_std)


def normalize(features, group_mean, inv_std):
    shaped = group_view(features)
    normed = (shaped - group_mean[:, None, :, None]) * inv_std[:, None, :, None]
    return normed.reshape(features.shape)


def norm_back(grad_normed, normed, validity, counts, inv_std):
    grad_shaped = group_view(grad_normed)
    norm_shaped = group_view(normed)
    first_sum, second_sum = group_totals(
        jnp.sum(grad_shaped, axis=(1, 3)), jnp.sum(grad_shaped * norm_shaped, axis=(1, 3))
    )
    entries = counts[:, None] * grad_shaped.shape[3]
    correction = (
        first_sum[:, None, :, None] + norm_shaped * second_sum[:, None, :, None]
    ) / entries[:, None, :, None]
    result = (grad_shaped - validity[:, :, None, None] * correction) * inv_std[:, None, :, None]
    return result.reshape(grad_normed.shape)


def conv_columns(features):
    padded = extended(features, (("ha", 1),), 1)
    padded = jnp.pad(padded, ((0, 0), (0, 0), (1, 1), (0, 0)))
    batch_size, row_count, col_count, channels = features.shape
    taps = [
        padded[:, row_off : row_off + row_count, col_off : col_off + col_count]
        for row_off in range(3)
        for col_off in range(3)
    ]
    return jnp.concatenate(taps, axis=-1).reshape(batch_size * row_count * col_count, 9 * channels)


def project(inputs, weight):
    return lax.dot_general(
        inputs, weight, (((1,), (1,)), ((), ())), preferred_element_type=jnp.float32
    )


def weight_grad(grads, inputs):
    return lax.dot_general(
        grads, inputs, (((0,), (0,)), ((), ())), preferred_element_type=jnp.float32
    )


def back_project(grads, weight):
    return jnp.dot(grads, weight, preferred_element_type=jnp.float32)


def flipped(weight, in_channels):
    out_channels = weight.shape[0]
    taps = weight.reshape(out_channels, 3, 3, in_channels)[:, ::-1, ::-1, :]
    return jnp.transpose(taps, (1, 2, 0, 3)).reshape(9 * out_channels, in_channels)


def split_heads(values):
    return values.reshape(values.shape[0], values.shape[1], HEADS, HEAD_DIM)


def score_block(head_queries, head_keys, valid_block):
    raw = jnp.einsum(
        "bqhd,bkhd->bhqk", head_queries, head_keys, preferred_element_type=jnp.float32
    ) * (1.0 / math.sqrt(HEAD_DIM))
    return jnp.where(valid_block[:, None, None, :] > 0, raw, neg_big)


def absorb(running, head_queries, pairs, valid_block):
    highest, totals, accumulated = running
    head_keys = split_heads(pairs[:, :, :C])
    head_values = split_heads(pairs[:, :, C:])
    scores = score_block(head_queries, head_keys, valid_block)
    new_high = jnp.maximum(highest, jnp.max(scores, axis=-1))
    weights = jnp.exp(scores - new_high[..., None])
    decay = jnp.exp(highest - new_high)
    totals = totals * decay + jnp.sum(weights, axis=-1)
    update = jnp.einsum(
        "bhqk,bkhd->bqhd", rounded(weights), head_values, preferred_element_type=jnp.float32
    )
    accumulated = accumulated * jnp.transpose(decay, (0, 2, 1))[..., None] + update
    return (new_high, totals, accumulated)


def back_block(grad_query, head_queries, grad_mixed, log_total, delta, pairs, valid_block):
    head_keys = split_heads(pairs[:, :, :C])
    head_values = split_heads(pairs[:, :, C:])
    scores = score_block(head_queries, head_keys, valid_block)
    probs = jnp.exp(scores - log_total[..., None])
    grad_values = jnp.einsum(
        "bhqk,bqhd->bkhd", rounded(probs), grad_mixed, preferred_element_type=jnp.float32
    )
    grad_probs = jnp.einsum(
        "bqhd,bkhd->bhqk", grad_mixed, head_values, preferred_element_type=jnp.float32
    )
    grad_scores = rounded(probs * (grad_probs - delta[..., None]))
    scale_factor = 1.0 / math.sqrt(HEAD_DIM)
    grad_query = (
        grad_query
        + jnp.einsum("bhqk,bkhd->bqhd", grad_scores, head_keys, preferred_element_type=jnp.float32)
        * scale_factor
    )
    grad_keys = (
        jnp.einsum("bhqk,bqhd->bkhd", grad_scores, head_queries, preferred_element_type=jnp.float32)
        * scale_factor
    )
    batch_size, key_count = (pairs.shape[0], pairs.shape[1])
    grad_pairs = jnp.concatenate(
        [
            grad_keys.reshape(batch_size, key_count, C),
            grad_values.reshape(batch_size, key_count, C),
        ],
        axis=2,
    )
    return (grad_query, grad_pairs)


def over_blocks(block_fn, running, pairs, validity):
    key_count = pairs.shape[1]
    block_len = 512

    def over_advance(block_index, carried):
        offset = block_index * block_len
        return block_fn(
            carried,
            lax.dynamic_slice_in_dim(pairs, offset, block_len, 1),
            lax.dynamic_slice_in_dim(validity, offset, block_len, 1),
        )

    return lax.fori_loop(0, key_count // block_len, over_advance, running)


def shards(
    image,
    mask,
    timestep,
    pooled,
    text,
    text_mask,
    cotangent,
    conv1_weight,
    conv2_weight,
    skip_weight,
    emb_weight,
    qkv_weight,
    out_weight,
    text_weight,
    gn1_gain,
    gn1_bias,
    emb_bias,
    gn2_gain,
    gn2_bias,
    skip_bias,
    gn3_gain,
    gn3_bias,
    out_bias,
):
    batch_size, row_count, col_count = (image.shape[0], image.shape[1], image.shape[2])
    pixel_count = row_count * col_count
    gathered = (
        lax.all_gather(conv1_weight, ("img", "ha"), axis=0, tiled=True),
        lax.all_gather(conv2_weight, ("img", "ha"), axis=0, tiled=True),
        lax.all_gather(skip_weight, ("img", "ha"), axis=0, tiled=True),
        lax.all_gather(emb_weight, ("img", "ha"), axis=0, tiled=True),
        lax.all_gather(qkv_weight, ("img", "ha"), axis=0, tiled=True),
        lax.all_gather(out_weight, ("img", "ha"), axis=0, tiled=True),
        lax.all_gather(gn1_gain, ("img", "ha"), axis=0, tiled=True),
        lax.all_gather(gn1_bias, ("img", "ha"), axis=0, tiled=True),
        lax.all_gather(emb_bias, ("img", "ha"), axis=0, tiled=True),
        lax.all_gather(gn2_gain, ("img", "ha"), axis=0, tiled=True),
        lax.all_gather(gn2_bias, ("img", "ha"), axis=0, tiled=True),
        lax.all_gather(skip_bias, ("img", "ha"), axis=0, tiled=True),
        lax.all_gather(gn3_gain, ("img", "ha"), axis=0, tiled=True),
        lax.all_gather(gn3_bias, ("img", "ha"), axis=0, tiled=True),
        lax.all_gather(out_bias, ("img", "ha"), axis=0, tiled=True),
    )
    conv1_full, conv2_full, skip_full, emb_full, qkv_full, out_full = gathered[:6]
    (
        gain_one,
        bias_one,
        emb_shift,
        gain_two,
        bias_two,
        skip_shift,
        gain_three,
        bias_three,
        out_shift,
    ) = (item.astype(jnp.float32) for item in gathered[6:])
    full_valid = mask.reshape(batch_size, HEIGHT * WIDTH).astype(jnp.float32)
    counts = jnp.sum(full_valid, axis=1)
    local_mask = lax.dynamic_slice_in_dim(mask, lax.axis_index("ha") * row_count, row_count, 1)
    validity = local_mask.reshape(batch_size, pixel_count).astype(jnp.float32)
    half_width = EMB // 2
    frequency = jnp.exp(-math.log(10000.0) * jnp.arange(half_width, dtype=jnp.float32) / half_width)
    angles = timestep.astype(jnp.float32)[:, None] * frequency[None, :]
    embedding = rounded(
        jax.nn.silu(jnp.concatenate([jnp.cos(angles), jnp.sin(angles)], axis=1) + pooled)
    )
    modulation = project(embedding, emb_full) + emb_shift
    scale_rows = 1.0 + modulation[:, None, :C]
    shift_rows = modulation[:, None, C:]
    image_flat = image.reshape(batch_size, pixel_count, C_IN)
    image_wide = image_flat.astype(jnp.float32)

    def front(known):
        fresh = known is None
        first_mean, first_std = norm_stats(image_wide, validity, counts) if fresh else known[0]
        first_normed = normalize(image_wide, first_mean, first_std)
        first_pre = first_normed * gain_one + bias_one
        first_act = rounded(jax.nn.silu(first_pre) * validity[:, :, None])
        first_columns = conv_columns(first_act.reshape(batch_size, row_count, col_count, C_IN))
        hidden_one = project(first_columns, conv1_full).reshape(batch_size, pixel_count, C)
        second_mean, second_std = norm_stats(hidden_one, validity, counts) if fresh else known[1]
        second_normed = normalize(hidden_one, second_mean, second_std)
        second_shifted = second_normed * gain_two + bias_two
        second_pre = second_shifted * scale_rows + shift_rows
        second_act = rounded(jax.nn.silu(second_pre) * validity[:, :, None])
        second_columns = conv_columns(second_act.reshape(batch_size, row_count, col_count, C))
        stats = ((first_mean, first_std), (second_mean, second_std))
        return (
            stats,
            (
                first_normed,
                first_pre,
                first_columns,
                second_normed,
                second_shifted,
                second_pre,
                second_columns,
            ),
        )

    stats, saved = front(None)
    residual = (
        project(saved[6], conv2_full) + project(image_flat.reshape(-1, C_IN), skip_full)
    ).reshape(batch_size, pixel_count, C) + skip_shift
    third_mean, third_std = norm_stats(residual, validity, counts)
    third_normed = normalize(residual, third_mean, third_std)
    attn_input = rounded(third_normed * gain_three + bias_three)
    triple = rounded(project(attn_input.reshape(-1, C), qkv_full)).reshape(
        batch_size, pixel_count, 3 * C
    )
    head_queries = split_heads(triple[:, :, :C])
    local_pairs = triple[:, :, C:]
    text_piece = lax.all_gather(text_weight, "img", axis=0, tiled=True)
    text_slice = rounded(
        jnp.einsum("blt,tc->blc", text, text_piece, preferred_element_type=jnp.float32)
    )
    text_pairs = lax.all_gather(text_slice, "ha", axis=2, tiled=True)
    text_valid = text_mask.astype(jnp.float32)

    def absorb_here(carried, pairs, valid_block):
        return absorb(carried, head_queries, pairs, valid_block)

    running = (
        jnp.full((batch_size, HEADS, pixel_count), neg_big, jnp.float32),
        jnp.zeros((batch_size, HEADS, pixel_count), jnp.float32),
        jnp.zeros((batch_size, pixel_count, HEADS, HEAD_DIM), jnp.float32),
    )
    running = absorb_here(running, text_pairs, text_valid)
    valid_block = full_valid
    running = over_blocks(
        absorb_here, running, lax.all_gather(local_pairs, "ha", axis=1, tiled=True), valid_block
    )
    highest, totals, accumulated = running
    attended = accumulated / jnp.transpose(totals, (0, 2, 1))[..., None]
    log_total = highest + jnp.log(totals)
    mixed_rows = rounded(attended.reshape(-1, C))
    output = residual.reshape(-1, C) + project(mixed_rows, out_full) + out_shift
    output = rounded(output).reshape(batch_size, row_count, col_count, C)
    cot_rows = cotangent.reshape(-1, C)
    out_weight_grad = weight_grad(cot_rows, mixed_rows)
    out_bias_grad = jnp.sum(cot_rows.astype(jnp.float32), axis=0)
    grad_mixed = split_heads(
        rounded(back_project(cot_rows, out_full)).reshape(batch_size, pixel_count, C)
    )
    delta = jnp.transpose(jnp.sum(grad_mixed.astype(jnp.float32) * attended, axis=-1), (0, 2, 1))

    def back_here(grad_query, pairs, valid_block):
        return back_block(
            grad_query, head_queries, grad_mixed, log_total, delta, pairs, valid_block
        )

    grad_query = jnp.zeros((batch_size, pixel_count, HEADS, HEAD_DIM), jnp.float32)
    grad_query, text_term = back_here(grad_query, text_pairs, text_valid)
    pixel_pairs = lax.all_gather(local_pairs, "ha", axis=1, tiled=True)
    key_count = pixel_pairs.shape[1]
    block_len = 512

    def body_advance(block_index, carried):
        query_grad, term_now = carried
        offset = block_index * block_len
        query_grad, grad_pairs = back_here(
            query_grad,
            lax.dynamic_slice_in_dim(pixel_pairs, offset, block_len, 1),
            lax.dynamic_slice_in_dim(full_valid, offset, block_len, 1),
        )
        return (query_grad, lax.dynamic_update_slice_in_dim(term_now, grad_pairs, offset, 1))

    key_term = jnp.zeros((batch_size, key_count, 2 * C), jnp.float32)
    grad_query, key_term = lax.fori_loop(
        0, key_count // block_len, body_advance, (grad_query, key_term)
    )
    pair_grads = rounded(
        lax.psum_scatter(
            key_term.astype(jnp.bfloat16), "ha", scatter_dimension=1, tiled=True
        ).astype(jnp.float32)
    )
    text_grads = rounded(
        lax.psum_scatter(
            text_term.astype(jnp.bfloat16), "ha", scatter_dimension=2, tiled=True
        ).astype(jnp.float32)
    )
    text_weight_grad = lax.psum_scatter(
        jnp.einsum("blt,blc->tc", text, text_grads, preferred_element_type=jnp.float32).astype(
            jnp.bfloat16
        ),
        "img",
        scatter_dimension=0,
        tiled=True,
    ).astype(jnp.float32)
    triple_grads = jnp.concatenate(
        [rounded(grad_query.reshape(batch_size, pixel_count, C)), pair_grads], axis=2
    ).reshape(-1, 3 * C)
    qkv_weight_grad = weight_grad(triple_grads, attn_input.reshape(-1, C))
    grad_third = back_project(triple_grads, qkv_full).reshape(batch_size, pixel_count, C)
    gain_three_grad = jnp.sum(grad_third * third_normed, axis=(0, 1))
    bias_three_grad = jnp.sum(grad_third, axis=(0, 1))
    attn_sums = (
        lax.psum_scatter(qkv_weight_grad, ("img", "ha"), scatter_dimension=0, tiled=True),
        lax.psum_scatter(out_weight_grad, ("img", "ha"), scatter_dimension=0, tiled=True),
        lax.psum_scatter(gain_three_grad, ("img", "ha"), scatter_dimension=0, tiled=True),
        lax.psum_scatter(bias_three_grad, ("img", "ha"), scatter_dimension=0, tiled=True),
        lax.psum_scatter(out_bias_grad, ("img", "ha"), scatter_dimension=0, tiled=True),
    )
    grad_residual = cot_rows.astype(jnp.float32).reshape(batch_size, pixel_count, C) + norm_back(
        grad_third * gain_three, third_normed, validity, counts, third_std
    )
    skip_bias_grad = jnp.sum(grad_residual, axis=(0, 1))
    residual_low = rounded(grad_residual)
    residual_rows = residual_low.reshape(-1, C)
    skip_weight_grad = weight_grad(residual_rows, image_flat.reshape(-1, C_IN))
    image_from_skip = back_project(residual_rows, skip_full)
    unused, kept = front(stats)
    (
        first_normed,
        first_pre,
        first_columns,
        second_normed,
        second_shifted,
        second_pre,
        second_columns,
    ) = kept
    conv2_weight_grad = weight_grad(residual_rows, second_columns)
    grad_second_act = jnp.dot(
        conv_columns(residual_low.reshape(batch_size, row_count, col_count, C)),
        flipped(conv2_full, C),
        preferred_element_type=jnp.float32,
    )
    grad_second_pre = (
        grad_second_act.reshape(batch_size, pixel_count, C)
        * validity[:, :, None]
        * silu_slope(second_pre)
    )
    grad_mods = jnp.concatenate(
        [jnp.sum(grad_second_pre * second_shifted, axis=1), jnp.sum(grad_second_pre, axis=1)],
        axis=1,
    )
    emb_weight_grad = jnp.dot(
        grad_mods.T, embedding.astype(jnp.float32), precision=lax.Precision.HIGHEST
    )
    emb_bias_grad = jnp.sum(grad_mods, axis=0)
    grad_second_shift = grad_second_pre * scale_rows
    gain_two_grad = jnp.sum(grad_second_shift * second_normed, axis=(0, 1))
    bias_two_grad = jnp.sum(grad_second_shift, axis=(0, 1))
    hidden_low = rounded(
        norm_back(grad_second_shift * gain_two, second_normed, validity, counts, stats[1][1])
    )
    conv1_weight_grad = weight_grad(hidden_low.reshape(-1, C), first_columns)
    grad_first_act = jnp.dot(
        conv_columns(hidden_low.reshape(batch_size, row_count, col_count, C)),
        flipped(conv1_full, C_IN),
        preferred_element_type=jnp.float32,
    )
    grad_first_pre = (
        grad_first_act.reshape(batch_size, pixel_count, C_IN)
        * validity[:, :, None]
        * silu_slope(first_pre)
    )
    gain_one_grad = jnp.sum(grad_first_pre * first_normed, axis=(0, 1))
    bias_one_grad = jnp.sum(grad_first_pre, axis=(0, 1))
    image_grad = norm_back(
        grad_first_pre * gain_one, first_normed, validity, counts, stats[0][1]
    ) + image_from_skip.reshape(batch_size, pixel_count, C_IN)
    block_sums = (
        lax.psum_scatter(conv1_weight_grad, ("img", "ha"), scatter_dimension=0, tiled=True),
        lax.psum_scatter(conv2_weight_grad, ("img", "ha"), scatter_dimension=0, tiled=True),
        lax.psum_scatter(skip_weight_grad, ("img", "ha"), scatter_dimension=0, tiled=True),
        lax.psum_scatter(emb_weight_grad, ("img", "ha"), scatter_dimension=0, tiled=True),
        lax.psum_scatter(gain_one_grad, ("img", "ha"), scatter_dimension=0, tiled=True),
        lax.psum_scatter(bias_one_grad, ("img", "ha"), scatter_dimension=0, tiled=True),
        lax.psum_scatter(emb_bias_grad, ("img", "ha"), scatter_dimension=0, tiled=True),
        lax.psum_scatter(gain_two_grad, ("img", "ha"), scatter_dimension=0, tiled=True),
        lax.psum_scatter(bias_two_grad, ("img", "ha"), scatter_dimension=0, tiled=True),
        lax.psum_scatter(skip_bias_grad, ("img", "ha"), scatter_dimension=0, tiled=True),
    )
    return (
        output,
        image_grad.reshape(batch_size, row_count, col_count, C_IN),
        block_sums[0],
        block_sums[1],
        block_sums[2],
        block_sums[3],
        attn_sums[0],
        attn_sums[1],
        text_weight_grad,
        block_sums[4],
        block_sums[5],
        block_sums[6],
        block_sums[7],
        block_sums[8],
        block_sums[9],
        attn_sums[2],
        attn_sums[3],
        attn_sums[4],
    )


EVERY = ("y", "core", "z", "x")
PLANE = ("y", "core", "x")
LANES = 128
TEXT_PAD = 128


def plane_mesh(mesh):
    images, rows = mesh.shape["img"], mesh.shape["ha"]
    if images % 2 or rows % images:
        return None
    across = rows // images
    members = images * across
    if members != C // LANES or HEADS % members or HEIGHT % members:
        return None
    return Mesh(mesh.devices.reshape(images // 2, 2, images, across), EVERY)


def split_spec(spec):
    names = {"img": ("y", "core"), "ha": ("z", "x")}
    entries = []
    for entry in spec:
        parts = (entry,) if isinstance(entry, str) else (entry or ())
        axes = tuple(axis for part in parts for axis in names[part])
        entries.append(axes or None)
    return P(*entries)


def swapped(values):
    planes, across = lax.axis_size("z"), lax.axis_size("x")
    pairs = [
        ((a * planes + z) * across + x, (z * planes + a) * across + x)
        for a in range(planes)
        for z in range(planes)
        for x in range(across)
    ]
    return lax.ppermute(values, EVERY, pairs)


def own_channels(by_device):
    a, x = lax.axis_index(("y", "core")), lax.axis_index("x")
    part = lax.dynamic_index_in_dim(by_device, a, 0, keepdims=False)
    return lax.dynamic_index_in_dim(part, x, 1, keepdims=False)


def to_own_order(values):
    planes, across = lax.axis_size("z"), lax.axis_size("x")
    shaped = values.reshape(values.shape[:-1] + (planes, planes, across, -1))
    return jnp.swapaxes(shaped, -3, -2).reshape(values.shape)


def to_natural_order(values):
    planes, across = lax.axis_size("z"), lax.axis_size("x")
    shaped = values.reshape(values.shape[:-1] + (planes, across, planes, -1))
    return jnp.swapaxes(shaped, -3, -2).reshape(values.shape)


def local_stats(features, validity, count, width):
    channels = features.shape[1]
    masked = features * validity
    sums = jnp.stack([jnp.sum(masked, axis=0), jnp.sum(masked * features, axis=0)])
    grouped = jnp.sum(sums.reshape(2, channels // width, width), axis=2) / (count * width)
    mean = grouped[0]
    inv_std = lax.rsqrt(grouped[1] - mean * mean + eps_norm)
    return (jnp.repeat(mean, width), jnp.repeat(inv_std, width))


def local_back(grad_normed, normed, validity, count, inv_std, width):
    channels = grad_normed.shape[1]
    sums = jnp.stack([jnp.sum(grad_normed, axis=0), jnp.sum(grad_normed * normed, axis=0)])
    grouped = jnp.sum(sums.reshape(2, channels // width, width), axis=2) / (count * width)
    first, second = (jnp.repeat(item, width) for item in grouped)
    return (grad_normed - validity * (first + normed * second)) * inv_std


def shifted(features, row_off, col_off):
    rows, cols = features.shape[0], features.shape[1]
    padded = jnp.pad(features, ((1, 1), (1, 1), (0, 0)))
    return padded[1 + row_off : 1 + row_off + rows, 1 + col_off : 1 + col_off + cols]


def own_conv(features, weight):
    own = weight.shape[1]
    products = project(features, weight.reshape(9 * own, -1)).reshape(HEIGHT, WIDTH, 9 * own)
    total = None
    for tap in range(9):
        term = shifted(products[:, :, tap * own : (tap + 1) * own], tap // 3 - 1, tap % 3 - 1)
        total = term if total is None else total + term
    return total.reshape(HEIGHT * WIDTH, own)


def tap_columns(grads):
    shaped = grads.reshape(HEIGHT, WIDTH, -1)
    taps = [shifted(shaped, 1 - tap // 3, 1 - tap % 3) for tap in range(9)]
    return jnp.concatenate(taps, axis=-1).reshape(HEIGHT * WIDTH, -1)


def attend_kernel(widths, q_ref, k_ref, v_ref, out_ref, log_ref):
    queries = q_ref[0]
    highest, accumulated, offset = None, None, 0
    for width in widths:
        keys = k_ref[0, offset : offset + width]
        scores = lax.dot_general(
            queries, keys, (((1,), (1,)), ((), ())), preferred_element_type=jnp.float32
        )
        top = jnp.max(scores, axis=1, keepdims=True)
        if highest is not None:
            top = jnp.maximum(highest, top)
        weights = jnp.exp(scores - top).astype(jnp.bfloat16)
        update = jnp.dot(
            weights, v_ref[0, offset : offset + width], preferred_element_type=jnp.float32
        )
        accumulated = update if highest is None else accumulated * jnp.exp(highest - top) + update
        highest = top
        offset += width
    total = accumulated[:, HEAD_DIM : HEAD_DIM + 1]
    out_ref[0] = accumulated[:, :HEAD_DIM] / total
    log_ref[0] = highest + jnp.log(total)


def attend(queries, keys, values):
    heads, query_count, lanes = queries.shape
    key_count = keys.shape[1]
    block = min(1024, query_count)
    widths = [1408] * (key_count // 1408)
    if sum(widths) < key_count:
        widths.append(key_count - sum(widths))
    return pl.pallas_call(
        functools.partial(attend_kernel, widths),
        grid=(heads, query_count // block),
        in_specs=[
            pl.BlockSpec((1, block, lanes), lambda head, step: (head, step, 0)),
            pl.BlockSpec((1, key_count, lanes), lambda head, step: (head, 0, 0)),
            pl.BlockSpec((1, key_count, lanes), lambda head, step: (head, 0, 0)),
        ],
        out_specs=[
            pl.BlockSpec((1, block, HEAD_DIM), lambda head, step: (head, step, 0)),
            pl.BlockSpec((1, block, 1), lambda head, step: (head, step, 0)),
        ],
        out_shape=[
            jax.ShapeDtypeStruct((heads, query_count, HEAD_DIM), jnp.float32),
            jax.ShapeDtypeStruct((heads, query_count, 1), jnp.float32),
        ],
        compiler_params=pltpu.CompilerParams(vmem_limit_bytes=56 * 1024 * 1024),
        cost_estimate=pl.CostEstimate(
            flops=4 * heads * query_count * key_count * lanes,
            bytes_accessed=8 * heads * key_count * lanes,
            transcendentals=heads * query_count * key_count,
        ),
        name="attend",
    )(queries, keys, values)


def attend_back_kernel(block, q_ref, do_ref, k_ref, kt_ref, v_ref, dqt_ref, dk_ref, dv_ref):
    step = pl.program_id(1)
    keys, keys_across, values = k_ref[0], kt_ref[0], v_ref[0]
    grad_keys, grad_values = None, None

    @pl.when(step == 0)
    def _():
        dqt_ref[...] = jnp.zeros_like(dqt_ref)

    for start in range(0, q_ref.shape[1], block):
        queries = q_ref[0, start : start + block]
        grads = do_ref[0, start : start + block]
        shifted_scores = lax.dot_general(
            keys, queries, (((1,), (1,)), ((), ())), preferred_element_type=jnp.float32
        )
        grad_probs = lax.dot_general(
            values, grads, (((1,), (1,)), ((), ())), preferred_element_type=jnp.float32
        )
        probs = jnp.exp(shifted_scores)
        grad_scores = (probs * grad_probs).astype(jnp.bfloat16)
        value_term = jnp.dot(
            probs.astype(jnp.bfloat16), grads, preferred_element_type=jnp.float32
        )
        key_term = jnp.dot(grad_scores, queries, preferred_element_type=jnp.float32)
        grad_values = value_term if grad_values is None else grad_values + value_term
        grad_keys = key_term if grad_keys is None else grad_keys + key_term
        dqt_ref[0, :, start : start + block] += jnp.dot(
            keys_across, grad_scores, preferred_element_type=jnp.float32
        )
    dk_ref[0] = grad_keys[:, :HEAD_DIM]
    dv_ref[0] = grad_values[:, :HEAD_DIM]


def attend_back(queries, grads, keys, keys_across, values):
    heads, query_count, lanes = queries.shape
    key_count = keys.shape[1]
    key_block = 1408 if key_count % 1408 == 0 else LANES
    return pl.pallas_call(
        functools.partial(attend_back_kernel, min(512, query_count)),
        grid=(heads, key_count // key_block),
        in_specs=[
            pl.BlockSpec((1, query_count, lanes), lambda head, step: (head, 0, 0)),
            pl.BlockSpec((1, query_count, lanes), lambda head, step: (head, 0, 0)),
            pl.BlockSpec((1, key_block, lanes), lambda head, step: (head, step, 0)),
            pl.BlockSpec((1, HEAD_DIM, key_block), lambda head, step: (head, 0, step)),
            pl.BlockSpec((1, key_block, lanes), lambda head, step: (head, step, 0)),
        ],
        out_specs=[
            pl.BlockSpec((1, HEAD_DIM, query_count), lambda head, step: (head, 0, 0)),
            pl.BlockSpec((1, key_block, HEAD_DIM), lambda head, step: (head, step, 0)),
            pl.BlockSpec((1, key_block, HEAD_DIM), lambda head, step: (head, step, 0)),
        ],
        out_shape=[
            jax.ShapeDtypeStruct((heads, HEAD_DIM, query_count), jnp.float32),
            jax.ShapeDtypeStruct((heads, key_count, HEAD_DIM), jnp.float32),
            jax.ShapeDtypeStruct((heads, key_count, HEAD_DIM), jnp.float32),
        ],
        compiler_params=pltpu.CompilerParams(vmem_limit_bytes=56 * 1024 * 1024),
        cost_estimate=pl.CostEstimate(
            flops=10 * heads * query_count * key_count * lanes,
            bytes_accessed=16 * heads * key_count * lanes,
            transcendentals=heads * query_count * key_count,
        ),
        name="attend_back",
    )(queries, grads, keys, keys_across, values)


def pieces(column):
    parts = []
    for _ in range(3):
        part = lax.reduce_precision(column, 8, 7)
        parts.append(part.astype(jnp.bfloat16))
        column = column - part
    return parts


def with_lanes(*columns):
    joined = jnp.concatenate(columns, axis=-1)
    room = -joined.shape[-1] % LANES
    return jnp.pad(joined, [(0, 0)] * (joined.ndim - 1) + [(0, room)])


def by_head(values):
    return jnp.transpose(values.reshape(values.shape[0], -1, HEAD_DIM), (1, 0, 2))


def from_heads(values):
    return jnp.transpose(values, (1, 0, 2)).reshape(values.shape[1], -1)


def plane_shards(
    image,
    mask,
    timestep,
    pooled,
    text,
    text_mask,
    cotangent,
    conv1_weight,
    conv2_weight,
    skip_weight,
    emb_weight,
    qkv_weight,
    out_weight,
    text_weight,
    gn1_gain,
    gn1_bias,
    emb_bias,
    gn2_gain,
    gn2_bias,
    skip_bias,
    gn3_gain,
    gn3_bias,
    out_bias,
):
    planes, across = lax.axis_size("z"), lax.axis_size("x")
    members = planes * across
    devices = planes * members
    own = C // members
    a_here, z_here, x_here = lax.axis_index(("y", "core")), lax.axis_index("z"), lax.axis_index("x")
    member = a_here * across + x_here
    device = (a_here * planes + z_here) * across + x_here
    pixels = HEIGHT * WIDTH
    wide = 32 * across
    del wide

    vectors = (
        gn1_gain,
        gn1_bias,
        emb_bias,
        gn2_gain,
        gn2_bias,
        skip_bias,
        gn3_gain,
        gn3_bias,
        out_bias,
    )
    share = EMB // members
    pooled_share = lax.dynamic_slice_in_dim(pooled[0], (z_here * across + x_here) * share, share, 0)
    packed = jnp.concatenate(
        [item.astype(jnp.float32) for item in vectors] + [pooled_share, timestep.astype(jnp.float32)]
    )
    small = lax.all_gather(packed, EVERY, axis=0, tiled=False)
    bounds = [0]
    for item in vectors:
        bounds.append(bounds[-1] + item.shape[0])
    small_parts = [small[:, bounds[at] : bounds[at + 1]] for at in range(len(vectors))]
    gain_one, bias_one = (part.reshape(-1) for part in small_parts[:2])
    out_shift = small_parts[8].reshape(-1)

    def own_vector(part):
        return own_channels(part.reshape(planes, planes, across, -1)).reshape(-1)

    gain_two, bias_two, skip_shift, gain_three, bias_three = (
        own_vector(part) for part in small_parts[3:8]
    )
    pooled_all = small[:, bounds[-1] : bounds[-1] + share].reshape(planes, EMB)
    times = small[:, -1].reshape(planes, members)[:, 0]

    image_block = swapped(image[0].reshape(-1, C_IN))
    image_all = lax.all_gather(image_block, PLANE, axis=0, tiled=True)
    plane_mask = swapped(mask[0])
    validity = plane_mask.reshape(pixels, 1).astype(jnp.float32)
    count = jnp.sum(validity)
    text_valid = swapped(text_mask)[0].astype(jnp.float32)

    conv1_own = lax.all_gather(jnp.concatenate([conv1_weight, skip_weight], axis=1), "z", axis=0, tiled=True)
    conv1_own, skip_own = conv1_own[:, : 9 * C_IN], conv1_own[:, 9 * C_IN :]
    conv1_own = jnp.transpose(conv1_own.reshape(own, 9, C_IN), (1, 0, 2))
    conv2_own = lax.all_gather(conv2_weight, "z", axis=0, tiled=True)
    conv2_own = to_own_order(jnp.transpose(conv2_own.reshape(own, 9, C), (1, 0, 2)))
    qkv_all = lax.all_gather(qkv_weight, EVERY, axis=0, tiled=True).reshape(3, members, own, C)
    qkv_own = to_own_order(
        lax.dynamic_index_in_dim(qkv_all, member, 1, keepdims=False).reshape(3 * own, C)
    )

    half_width = EMB // 2
    frequency = jnp.exp(-math.log(10000.0) * jnp.arange(half_width, dtype=jnp.float32) / half_width)
    angles = times[:, None] * frequency[None, :]
    embedding = rounded(
        jax.nn.silu(jnp.concatenate([jnp.cos(angles), jnp.sin(angles)], axis=1) + pooled_all)
    )
    mods_here = project(embedding, emb_weight) + emb_bias.astype(jnp.float32)
    mods_all = lax.all_gather(mods_here, EVERY, axis=0, tiled=False)
    mods_plane = lax.dynamic_index_in_dim(mods_all, z_here, 1, keepdims=False).reshape(2, C)
    scale_own = 1.0 + own_vector(mods_plane[0])
    shift_own = own_vector(mods_plane[1])

    image_wide = image_all.astype(jnp.float32)
    first_mean, first_std = local_stats(image_wide, validity, count, C_IN // GROUPS)
    first_normed = (image_wide - first_mean) * first_std
    first_pre = first_normed * gain_one + bias_one
    first_act = rounded(jax.nn.silu(first_pre) * validity)
    hidden_one = own_conv(first_act, conv1_own)

    per_group = C // GROUPS
    second_mean, second_std = local_stats(hidden_one, validity, count, per_group)
    second_normed = (hidden_one - second_mean) * second_std
    second_shifted = second_normed * gain_two + bias_two
    second_pre = second_shifted * scale_own + shift_own
    second_act = rounded(jax.nn.silu(second_pre) * validity)
    second_all = lax.all_gather(second_act, PLANE, axis=1, tiled=True)
    residual = own_conv(second_all, conv2_own) + project(image_all, skip_own) + skip_shift

    third_mean, third_std = local_stats(residual, validity, count, per_group)
    third_normed = (residual - third_mean) * third_std
    attn_input = rounded(third_normed * gain_three + bias_three)
    attn_all = lax.all_gather(attn_input, PLANE, axis=1, tiled=True)
    triple = rounded(project(attn_all, qkv_own))

    text_piece = lax.all_gather(text_weight, ("y", "core"), axis=0, tiled=True)
    text_slice = rounded(jnp.dot(text[0], text_piece, preferred_element_type=jnp.float32))
    text_len = text_slice.shape[0]
    text_all = lax.all_gather(swapped(text_slice), PLANE, axis=1, tiled=True)
    text_own = lax.dynamic_index_in_dim(
        text_all.reshape(text_len, 2, members, own), member, 2, keepdims=False
    )
    text_own = jnp.pad(text_own, ((0, TEXT_PAD - text_len), (0, 0), (0, 0)))
    keys = by_head(jnp.concatenate([triple[:, own : 2 * own], text_own[:, 0]], axis=0))
    values = by_head(jnp.concatenate([triple[:, 2 * own :], text_own[:, 1]], axis=0))
    queries = by_head(triple[:, :own]) * jnp.bfloat16(1.0 / math.sqrt(HEAD_DIM))
    counted = jnp.concatenate([validity[:, 0], jnp.pad(text_valid, (0, TEXT_PAD - text_len))])
    heads_here, key_count = keys.shape[0], keys.shape[1]
    bias = jnp.where(counted > 0, 0.0, neg_big).astype(jnp.bfloat16)
    bias = jnp.broadcast_to(bias[None, :, None], (heads_here, key_count, 1))
    ones_query = jnp.ones((heads_here, pixels, 1), jnp.bfloat16)
    ones_key = jnp.ones((heads_here, key_count, 1), jnp.bfloat16)
    attended, log_total = attend(
        with_lanes(queries, ones_query), with_lanes(keys, bias), with_lanes(values, ones_key)
    )

    out_all = lax.all_gather(out_weight, EVERY, axis=0, tiled=True)
    mixed_rows = lax.all_to_all(
        rounded(from_heads(attended)), PLANE, split_axis=0, concat_axis=1, tiled=True
    )
    residual_rows = lax.all_to_all(
        rounded(residual), PLANE, split_axis=0, concat_axis=1, tiled=True
    )
    residual_rows = to_natural_order(residual_rows).astype(jnp.float32)
    output = rounded(residual_rows + project(mixed_rows, out_all) + out_shift)
    output = swapped(output).reshape(1, -1, WIDTH, C)

    cot_rows = swapped(cotangent[0].reshape(-1, C))
    out_weight_grad = lax.psum_scatter(
        rounded(weight_grad(cot_rows, mixed_rows)), EVERY, scatter_dimension=0, tiled=True
    ).astype(jnp.float32)
    grad_mixed = lax.all_to_all(
        rounded(back_project(cot_rows, out_all)), PLANE, split_axis=1, concat_axis=0, tiled=True
    )
    cot_own = lax.all_to_all(
        to_own_order(cot_rows), PLANE, split_axis=1, concat_axis=0, tiled=True
    ).astype(jnp.float32)
    out_bias_sum = jnp.sum(cot_own, axis=0)

    grad_heads = by_head(grad_mixed)
    delta = jnp.sum(grad_heads.astype(jnp.float32) * attended, axis=-1, keepdims=True)
    dq, dk, dv = attend_back(
        with_lanes(queries, ones_query, *pieces(log_total)),
        with_lanes(grad_heads, *pieces(delta)),
        with_lanes(keys, bias, *([-ones_key] * 3)),
        jnp.transpose(keys, (0, 2, 1)),
        with_lanes(values, *([-ones_key] * 3)),
    )
    dq = jnp.transpose(dq, (2, 0, 1)).reshape(pixels, own) * (1.0 / math.sqrt(HEAD_DIM))
    pair_grads = rounded(jnp.concatenate([from_heads(dk), from_heads(dv)], axis=1))
    triple_grads = jnp.concatenate([rounded(dq), pair_grads[:pixels]], axis=1)

    text_grads = pair_grads[pixels : pixels + text_len].reshape(text_len, 2, 1, own)
    text_grads = lax.all_gather(text_grads, PLANE, axis=2, tiled=True).reshape(text_len, 2 * C)
    text_grads = swapped(
        lax.dynamic_slice_in_dim(text_grads, member * 2 * own, 2 * own, 1)
    )
    text_weight_grad = lax.psum_scatter(
        rounded(weight_grad(text[0], text_grads)), ("y", "core"), scatter_dimension=0, tiled=True
    ).astype(jnp.float32)

    qkv_grad = to_natural_order(rounded(weight_grad(triple_grads, attn_all)))
    qkv_rows = lax.dynamic_update_index_in_dim(
        jnp.zeros((3, members, own, C), jnp.bfloat16), qkv_grad.reshape(3, own, C), member, 1
    )
    qkv_weight_grad = lax.psum_scatter(
        qkv_rows.reshape(3 * C, C), EVERY, scatter_dimension=0, tiled=True
    ).astype(jnp.float32)
    grad_third = lax.psum_scatter(
        rounded(back_project(triple_grads, qkv_own)), PLANE, scatter_dimension=1, tiled=True
    ).astype(jnp.float32)
    gain_three_grad = jnp.sum(grad_third * third_normed, axis=0)
    bias_three_grad = jnp.sum(grad_third, axis=0)
    grad_residual = cot_own + local_back(
        grad_third * gain_three, third_normed, validity, count, third_std, per_group
    )
    skip_bias_grad = jnp.sum(grad_residual, axis=0)
    residual_low = rounded(grad_residual)
    skip_grad = weight_grad(residual_low, image_all)

    residual_taps = tap_columns(residual_low)
    grad_second_act = lax.psum_scatter(
        rounded(back_project(residual_taps, conv2_own.reshape(9 * own, C))),
        PLANE,
        scatter_dimension=1,
        tiled=True,
    ).astype(jnp.float32)
    conv2_grad = to_natural_order(rounded(weight_grad(residual_taps, second_all)))
    conv2_grad = jnp.transpose(conv2_grad.reshape(9, own, C), (1, 0, 2)).reshape(own, 9 * C)
    conv2_grad = lax.psum_scatter(conv2_grad, "z", scatter_dimension=0, tiled=True).astype(jnp.float32)
    grad_second_pre = grad_second_act * validity * silu_slope(second_pre)
    grad_scale = jnp.sum(grad_second_pre * second_shifted, axis=0)
    grad_shift = jnp.sum(grad_second_pre, axis=0)
    grad_second_shift = grad_second_pre * scale_own
    gain_two_grad = jnp.sum(grad_second_shift * second_normed, axis=0)
    bias_two_grad = jnp.sum(grad_second_shift, axis=0)
    hidden_low = rounded(
        local_back(
            grad_second_shift * gain_two, second_normed, validity, count, second_std, per_group
        )
    )

    hidden_taps = tap_columns(hidden_low)
    grad_first_act = back_project(hidden_taps, conv1_own.reshape(9 * own, C_IN))
    conv1_grad = rounded(weight_grad(hidden_taps, first_act)).reshape(9, own, C_IN)
    conv1_grad = jnp.transpose(conv1_grad, (1, 0, 2)).reshape(own, 9 * C_IN)
    conv1_grad = jnp.concatenate([conv1_grad, rounded(skip_grad)], axis=1)
    conv1_grad = lax.psum_scatter(conv1_grad, "z", scatter_dimension=0, tiled=True).astype(jnp.float32)
    grad_first_pre = grad_first_act * validity * silu_slope(first_pre)
    first_sums = jnp.concatenate(
        [jnp.sum(grad_first_pre * first_normed, axis=0), jnp.sum(grad_first_pre, axis=0)]
    )
    image_part = rounded(
        grad_first_pre * (gain_one * first_std) + back_project(residual_low, skip_own)
    )
    image_part = lax.psum_scatter(image_part, PLANE, scatter_dimension=0, tiled=True)

    own_sums = jnp.stack(
        [
            grad_scale,
            grad_shift,
            gain_two_grad,
            bias_two_grad,
            skip_bias_grad,
            gain_three_grad,
            bias_three_grad,
            out_bias_sum,
        ]
    )
    own_all = lax.all_gather(own_sums, EVERY, axis=0, tiled=False)
    own_all = own_all.reshape(planes, planes, across, 8, planes, own // planes)
    mods_grad = jnp.transpose(own_all[:, :, :, :2], (1, 3, 0, 4, 2, 5)).reshape(planes, 2 * C)
    emb_rows = emb_weight.shape[0]
    mods_grad = lax.dynamic_slice_in_dim(mods_grad, device * emb_rows, emb_rows, 1)
    emb_weight_grad = jnp.dot(
        mods_grad.T, embedding.astype(jnp.float32), precision=lax.Precision.HIGHEST
    )
    emb_bias_grad = jnp.sum(mods_grad, axis=0)
    channel_sums = jnp.sum(own_all, axis=1)
    channel_sums = lax.dynamic_index_in_dim(channel_sums, a_here, 0, keepdims=False)
    channel_sums = lax.dynamic_index_in_dim(channel_sums, x_here, 0, keepdims=False)
    channel_sums = lax.dynamic_index_in_dim(channel_sums, z_here, 1, keepdims=False)

    first_all = lax.all_gather(first_sums, EVERY, axis=0, tiled=False)
    first_all = jnp.sum(first_all.reshape(planes, planes, across, 2, C_IN), axis=(0, 2))
    first_here = lax.dynamic_index_in_dim(first_all, z_here, 0, keepdims=False)
    first_width = C_IN // GROUPS
    grouped = jnp.sum((first_here * gain_one).reshape(2, GROUPS, first_width), axis=2)
    grouped = jnp.repeat(grouped / (count * first_width), first_width, axis=1)
    rows_here = lax.dynamic_slice_in_dim(image_block, 0, image_block.shape[0], 0)
    row_valid = lax.dynamic_slice_in_dim(
        validity, member * rows_here.shape[0], rows_here.shape[0], 0
    )
    rows_normed = (rows_here.astype(jnp.float32) - first_mean) * first_std
    image_grad = image_part.astype(jnp.float32) - row_valid * first_std * (
        grouped[1] + rows_normed * grouped[0]
    )
    image_grad = swapped(rounded(image_grad)).astype(jnp.float32).reshape(1, -1, WIDTH, C_IN)
    first_grads = lax.dynamic_slice_in_dim(
        jnp.sum(first_all, axis=0), device * first_width, first_width, 1
    )
    return (
        output,
        image_grad,
        conv1_grad[:, : 9 * C_IN],
        conv2_grad,
        conv1_grad[:, 9 * C_IN :],
        emb_weight_grad,
        qkv_weight_grad,
        out_weight_grad,
        text_weight_grad,
        first_grads[0],
        first_grads[1],
        emb_bias_grad,
        channel_sums[2],
        channel_sums[3],
        channel_sums[4],
        channel_sums[5],
        channel_sums[6],
        channel_sums[7],
    )


def solution(mesh):
    in_specs = (
        P("img", "ha", None, None),
        P("img", None, None),
        P("img"),
        P("img", None),
        P("img", None, None),
        P("img", None),
        P("img", "ha", None, None),
        P(("img", "ha"), None),
        P(("img", "ha"), None),
        P(("img", "ha"), None),
        P(("img", "ha"), None),
        P(("img", "ha"), None),
        P(("img", "ha"), None),
        P("img", "ha"),
        P(("img", "ha")),
        P(("img", "ha")),
        P(("img", "ha")),
        P(("img", "ha")),
        P(("img", "ha")),
        P(("img", "ha")),
        P(("img", "ha")),
        P(("img", "ha")),
        P(("img", "ha")),
    )
    out_specs = (
        P("img", "ha", None, None),
        P("img", "ha", None, None),
        P(("img", "ha"), None),
        P(("img", "ha"), None),
        P(("img", "ha"), None),
        P(("img", "ha"), None),
        P(("img", "ha"), None),
        P(("img", "ha"), None),
        P("img", "ha"),
        P(("img", "ha")),
        P(("img", "ha")),
        P(("img", "ha")),
        P(("img", "ha")),
        P(("img", "ha")),
        P(("img", "ha")),
        P(("img", "ha")),
        P(("img", "ha")),
        P(("img", "ha")),
    )
    split_mesh = plane_mesh(mesh)
    if split_mesh is None:
        return jax.shard_map(
            shards, mesh=mesh, in_specs=in_specs, out_specs=out_specs, check_vma=False
        )
    in_specs, out_specs = (tuple(split_spec(item) for item in specs) for specs in (in_specs, out_specs))
    return jax.shard_map(
        plane_shards, mesh=split_mesh, in_specs=in_specs, out_specs=out_specs, check_vma=False
    )
```

```python
import functools
import math

import jax
import jax.numpy as jnp
from jax import lax
from jax.experimental import pallas as pl
from jax.experimental.pallas import tpu as pltpu
from jax.sharding import Mesh
from jax.sharding import PartitionSpec as P

C_IN = 512
C = 1024
HEADS = 16
HEAD_DIM = 64
GROUPS = 32
EMB = 1024
HEIGHT = 64
WIDTH = 64


neg_big = -1e30
eps_norm = 1e-05


def extended(cells, sides, width):
    for axis, dim in sides:
        count = lax.axis_size(axis)
        ends = count - 1
        head = lax.slice_in_dim(cells, 0, width, axis=dim)
        tail = lax.slice_in_dim(cells, cells.shape[dim] - width, cells.shape[dim], axis=dim)
        cells = jnp.concatenate(
            [
                lax.ppermute(tail, axis, [(i, (i + 1) % count) for i in range(ends)]),
                cells,
                lax.ppermute(head, axis, [((i + 1) % count, i) for i in range(ends)]),
            ],
            axis=dim,
        )
    return cells


def rounded(values):
    return values.astype(jnp.bfloat16)


def silu_slope(inputs):
    sigmoid = jax.nn.sigmoid(inputs)
    return sigmoid * (1.0 + inputs * (1.0 - sigmoid))


def group_view(features):
    return features.reshape(
        features.shape[0], features.shape[1], GROUPS, features.shape[2] // GROUPS
    )


def group_totals(first_sum, second_sum):
    return lax.psum((first_sum, second_sum), "ha")


def norm_stats(features, validity, counts):
    shaped = group_view(features)
    masked = shaped * validity[:, :, None, None]
    first_sum, second_sum = group_totals(
        jnp.sum(masked, axis=(1, 3)), jnp.sum(masked * shaped, axis=(1, 3))
    )
    entries = counts[:, None] * shaped.shape[3]
    group_mean = first_sum / entries
    inv_std = lax.rsqrt(second_sum / entries - group_mean * group_mean + eps_norm)
    return (group_mean, inv_std)


def normalize(features, group_mean, inv_std):
    shaped = group_view(features)
    normed = (shaped - group_mean[:, None, :, None]) * inv_std[:, None, :, None]
    return normed.reshape(features.shape)


def norm_back(grad_normed, normed, validity, counts, inv_std):
    grad_shaped = group_view(grad_normed)
    norm_shaped = group_view(normed)
    first_sum, second_sum = group_totals(
        jnp.sum(grad_shaped, axis=(1, 3)), jnp.sum(grad_shaped * norm_shaped, axis=(1, 3))
    )
    entries = counts[:, None] * grad_shaped.shape[3]
    correction = (
        first_sum[:, None, :, None] + norm_shaped * second_sum[:, None, :, None]
    ) / entries[:, None, :, None]
    result = (grad_shaped - validity[:, :, None, None] * correction) * inv_std[:, None, :, None]
    return result.reshape(grad_normed.shape)


def conv_columns(features):
    padded = extended(features, (("ha", 1),), 1)
    padded = jnp.pad(padded, ((0, 0), (0, 0), (1, 1), (0, 0)))
    batch_size, row_count, col_count, channels = features.shape
    taps = [
        padded[:, row_off : row_off + row_count, col_off : col_off + col_count]
        for row_off in range(3)
        for col_off in range(3)
    ]
    return jnp.concatenate(taps, axis=-1).reshape(batch_size * row_count * col_count, 9 * channels)


def project(inputs, weight):
    return lax.dot_general(
        inputs, weight, (((1,), (1,)), ((), ())), preferred_element_type=jnp.float32
    )


def weight_grad(grads, inputs):
    return lax.dot_general(
        grads, inputs, (((0,), (0,)), ((), ())), preferred_element_type=jnp.float32
    )


def back_project(grads, weight):
    return jnp.dot(grads, weight, preferred_element_type=jnp.float32)


def flipped(weight, in_channels):
    out_channels = weight.shape[0]
    taps = weight.reshape(out_channels, 3, 3, in_channels)[:, ::-1, ::-1, :]
    return jnp.transpose(taps, (1, 2, 0, 3)).reshape(9 * out_channels, in_channels)


def split_heads(values):
    return values.reshape(values.shape[0], values.shape[1], HEADS, HEAD_DIM)


def score_block(head_queries, head_keys, valid_block):
    raw = jnp.einsum(
        "bqhd,bkhd->bhqk", head_queries, head_keys, preferred_element_type=jnp.float32
    ) * (1.0 / math.sqrt(HEAD_DIM))
    return jnp.where(valid_block[:, None, None, :] > 0, raw, neg_big)


def absorb(running, head_queries, pairs, valid_block):
    highest, totals, accumulated = running
    head_keys = split_heads(pairs[:, :, :C])
    head_values = split_heads(pairs[:, :, C:])
    scores = score_block(head_queries, head_keys, valid_block)
    new_high = jnp.maximum(highest, jnp.max(scores, axis=-1))
    weights = jnp.exp(scores - new_high[..., None])
    decay = jnp.exp(highest - new_high)
    totals = totals * decay + jnp.sum(weights, axis=-1)
    update = jnp.einsum(
        "bhqk,bkhd->bqhd", rounded(weights), head_values, preferred_element_type=jnp.float32
    )
    accumulated = accumulated * jnp.transpose(decay, (0, 2, 1))[..., None] + update
    return (new_high, totals, accumulated)


def back_block(grad_query, head_queries, grad_mixed, log_total, delta, pairs, valid_block):
    head_keys = split_heads(pairs[:, :, :C])
    head_values = split_heads(pairs[:, :, C:])
    scores = score_block(head_queries, head_keys, valid_block)
    probs = jnp.exp(scores - log_total[..., None])
    grad_values = jnp.einsum(
        "bhqk,bqhd->bkhd", rounded(probs), grad_mixed, preferred_element_type=jnp.float32
    )
    grad_probs = jnp.einsum(
        "bqhd,bkhd->bhqk", grad_mixed, head_values, preferred_element_type=jnp.float32
    )
    grad_scores = rounded(probs * (grad_probs - delta[..., None]))
    scale_factor = 1.0 / math.sqrt(HEAD_DIM)
    grad_query = (
        grad_query
        + jnp.einsum("bhqk,bkhd->bqhd", grad_scores, head_keys, preferred_element_type=jnp.float32)
        * scale_factor
    )
    grad_keys = (
        jnp.einsum("bhqk,bqhd->bkhd", grad_scores, head_queries, preferred_element_type=jnp.float32)
        * scale_factor
    )
    batch_size, key_count = (pairs.shape[0], pairs.shape[1])
    grad_pairs = jnp.concatenate(
        [
            grad_keys.reshape(batch_size, key_count, C),
            grad_values.reshape(batch_size, key_count, C),
        ],
        axis=2,
    )
    return (grad_query, grad_pairs)


def over_blocks(block_fn, running, pairs, validity):
    key_count = pairs.shape[1]
    block_len = 512

    def over_advance(block_index, carried):
        offset = block_index * block_len
        return block_fn(
            carried,
            lax.dynamic_slice_in_dim(pairs, offset, block_len, 1),
            lax.dynamic_slice_in_dim(validity, offset, block_len, 1),
        )

    return lax.fori_loop(0, key_count // block_len, over_advance, running)


def shards(
    image,
    mask,
    timestep,
    pooled,
    text,
    text_mask,
    cotangent,
    conv1_weight,
    conv2_weight,
    skip_weight,
    emb_weight,
    qkv_weight,
    out_weight,
    text_weight,
    gn1_gain,
    gn1_bias,
    emb_bias,
    gn2_gain,
    gn2_bias,
    skip_bias,
    gn3_gain,
    gn3_bias,
    out_bias,
):
    batch_size, row_count, col_count = (image.shape[0], image.shape[1], image.shape[2])
    pixel_count = row_count * col_count
    gathered = (
        lax.all_gather(conv1_weight, ("img", "ha"), axis=0, tiled=True),
        lax.all_gather(conv2_weight, ("img", "ha"), axis=0, tiled=True),
        lax.all_gather(skip_weight, ("img", "ha"), axis=0, tiled=True),
        lax.all_gather(emb_weight, ("img", "ha"), axis=0, tiled=True),
        lax.all_gather(qkv_weight, ("img", "ha"), axis=0, tiled=True),
        lax.all_gather(out_weight, ("img", "ha"), axis=0, tiled=True),
        lax.all_gather(gn1_gain, ("img", "ha"), axis=0, tiled=True),
        lax.all_gather(gn1_bias, ("img", "ha"), axis=0, tiled=True),
        lax.all_gather(emb_bias, ("img", "ha"), axis=0, tiled=True),
        lax.all_gather(gn2_gain, ("img", "ha"), axis=0, tiled=True),
        lax.all_gather(gn2_bias, ("img", "ha"), axis=0, tiled=True),
        lax.all_gather(skip_bias, ("img", "ha"), axis=0, tiled=True),
        lax.all_gather(gn3_gain, ("img", "ha"), axis=0, tiled=True),
        lax.all_gather(gn3_bias, ("img", "ha"), axis=0, tiled=True),
        lax.all_gather(out_bias, ("img", "ha"), axis=0, tiled=True),
    )
    conv1_full, conv2_full, skip_full, emb_full, qkv_full, out_full = gathered[:6]
    (
        gain_one,
        bias_one,
        emb_shift,
        gain_two,
        bias_two,
        skip_shift,
        gain_three,
        bias_three,
        out_shift,
    ) = (item.astype(jnp.float32) for item in gathered[6:])
    full_valid = mask.reshape(batch_size, HEIGHT * WIDTH).astype(jnp.float32)
    counts = jnp.sum(full_valid, axis=1)
    local_mask = lax.dynamic_slice_in_dim(mask, lax.axis_index("ha") * row_count, row_count, 1)
    validity = local_mask.reshape(batch_size, pixel_count).astype(jnp.float32)
    half_width = EMB // 2
    frequency = jnp.exp(-math.log(10000.0) * jnp.arange(half_width, dtype=jnp.float32) / half_width)
    angles = timestep.astype(jnp.float32)[:, None] * frequency[None, :]
    embedding = rounded(
        jax.nn.silu(jnp.concatenate([jnp.cos(angles), jnp.sin(angles)], axis=1) + pooled)
    )
    modulation = project(embedding, emb_full) + emb_shift
    scale_rows = 1.0 + modulation[:, None, :C]
    shift_rows = modulation[:, None, C:]
    image_flat = image.reshape(batch_size, pixel_count, C_IN)
    image_wide = image_flat.astype(jnp.float32)

    def front(known):
        fresh = known is None
        first_mean, first_std = norm_stats(image_wide, validity, counts) if fresh else known[0]
        first_normed = normalize(image_wide, first_mean, first_std)
        first_pre = first_normed * gain_one + bias_one
        first_act = rounded(jax.nn.silu(first_pre) * validity[:, :, None])
        first_columns = conv_columns(first_act.reshape(batch_size, row_count, col_count, C_IN))
        hidden_one = project(first_columns, conv1_full).reshape(batch_size, pixel_count, C)
        second_mean, second_std = norm_stats(hidden_one, validity, counts) if fresh else known[1]
        second_normed = normalize(hidden_one, second_mean, second_std)
        second_shifted = second_normed * gain_two + bias_two
        second_pre = second_shifted * scale_rows + shift_rows
        second_act = rounded(jax.nn.silu(second_pre) * validity[:, :, None])
        second_columns = conv_columns(second_act.reshape(batch_size, row_count, col_count, C))
        stats = ((first_mean, first_std), (second_mean, second_std))
        return (
            stats,
            (
                first_normed,
                first_pre,
                first_columns,
                second_normed,
                second_shifted,
                second_pre,
                second_columns,
            ),
        )

    stats, saved = front(None)
    residual = (
        project(saved[6], conv2_full) + project(image_flat.reshape(-1, C_IN), skip_full)
    ).reshape(batch_size, pixel_count, C) + skip_shift
    third_mean, third_std = norm_stats(residual, validity, counts)
    third_normed = normalize(residual, third_mean, third_std)
    attn_input = rounded(third_normed * gain_three + bias_three)
    triple = rounded(project(attn_input.reshape(-1, C), qkv_full)).reshape(
        batch_size, pixel_count, 3 * C
    )
    head_queries = split_heads(triple[:, :, :C])
    local_pairs = triple[:, :, C:]
    text_piece = lax.all_gather(text_weight, "img", axis=0, tiled=True)
    text_slice = rounded(
        jnp.einsum("blt,tc->blc", text, text_piece, preferred_element_type=jnp.float32)
    )
    text_pairs = lax.all_gather(text_slice, "ha", axis=2, tiled=True)
    text_valid = text_mask.astype(jnp.float32)

    def absorb_here(carried, pairs, valid_block):
        return absorb(carried, head_queries, pairs, valid_block)

    running = (
        jnp.full((batch_size, HEADS, pixel_count), neg_big, jnp.float32),
        jnp.zeros((batch_size, HEADS, pixel_count), jnp.float32),
        jnp.zeros((batch_size, pixel_count, HEADS, HEAD_DIM), jnp.float32),
    )
    running = absorb_here(running, text_pairs, text_valid)
    valid_block = full_valid
    running = over_blocks(
        absorb_here, running, lax.all_gather(local_pairs, "ha", axis=1, tiled=True), valid_block
    )
    highest, totals, accumulated = running
    attended = accumulated / jnp.transpose(totals, (0, 2, 1))[..., None]
    log_total = highest + jnp.log(totals)
    mixed_rows = rounded(attended.reshape(-1, C))
    output = residual.reshape(-1, C) + project(mixed_rows, out_full) + out_shift
    output = rounded(output).reshape(batch_size, row_count, col_count, C)
    cot_rows = cotangent.reshape(-1, C)
    out_weight_grad = weight_grad(cot_rows, mixed_rows)
    out_bias_grad = jnp.sum(cot_rows.astype(jnp.float32), axis=0)
    grad_mixed = split_heads(
        rounded(back_project(cot_rows, out_full)).reshape(batch_size, pixel_count, C)
    )
    delta = jnp.transpose(jnp.sum(grad_mixed.astype(jnp.float32) * attended, axis=-1), (0, 2, 1))

    def back_here(grad_query, pairs, valid_block):
        return back_block(
            grad_query, head_queries, grad_mixed, log_total, delta, pairs, valid_block
        )

    grad_query = jnp.zeros((batch_size, pixel_count, HEADS, HEAD_DIM), jnp.float32)
    grad_query, text_term = back_here(grad_query, text_pairs, text_valid)
    pixel_pairs = lax.all_gather(local_pairs, "ha", axis=1, tiled=True)
    key_count = pixel_pairs.shape[1]
    block_len = 512

    def body_advance(block_index, carried):
        query_grad, term_now = carried
        offset = block_index * block_len
        query_grad, grad_pairs = back_here(
            query_grad,
            lax.dynamic_slice_in_dim(pixel_pairs, offset, block_len, 1),
            lax.dynamic_slice_in_dim(full_valid, offset, block_len, 1),
        )
        return (query_grad, lax.dynamic_update_slice_in_dim(term_now, grad_pairs, offset, 1))

    key_term = jnp.zeros((batch_size, key_count, 2 * C), jnp.float32)
    grad_query, key_term = lax.fori_loop(
        0, key_count // block_len, body_advance, (grad_query, key_term)
    )
    pair_grads = rounded(
        lax.psum_scatter(
            key_term.astype(jnp.bfloat16), "ha", scatter_dimension=1, tiled=True
        ).astype(jnp.float32)
    )
    text_grads = rounded(
        lax.psum_scatter(
            text_term.astype(jnp.bfloat16), "ha", scatter_dimension=2, tiled=True
        ).astype(jnp.float32)
    )
    text_weight_grad = lax.psum_scatter(
        jnp.einsum("blt,blc->tc", text, text_grads, preferred_element_type=jnp.float32).astype(
            jnp.bfloat16
        ),
        "img",
        scatter_dimension=0,
        tiled=True,
    ).astype(jnp.float32)
    triple_grads = jnp.concatenate(
        [rounded(grad_query.reshape(batch_size, pixel_count, C)), pair_grads], axis=2
    ).reshape(-1, 3 * C)
    qkv_weight_grad = weight_grad(triple_grads, attn_input.reshape(-1, C))
    grad_third = back_project(triple_grads, qkv_full).reshape(batch_size, pixel_count, C)
    gain_three_grad = jnp.sum(grad_third * third_normed, axis=(0, 1))
    bias_three_grad = jnp.sum(grad_third, axis=(0, 1))
    attn_sums = (
        lax.psum_scatter(qkv_weight_grad, ("img", "ha"), scatter_dimension=0, tiled=True),
        lax.psum_scatter(out_weight_grad, ("img", "ha"), scatter_dimension=0, tiled=True),
        lax.psum_scatter(gain_three_grad, ("img", "ha"), scatter_dimension=0, tiled=True),
        lax.psum_scatter(bias_three_grad, ("img", "ha"), scatter_dimension=0, tiled=True),
        lax.psum_scatter(out_bias_grad, ("img", "ha"), scatter_dimension=0, tiled=True),
    )
    grad_residual = cot_rows.astype(jnp.float32).reshape(batch_size, pixel_count, C) + norm_back(
        grad_third * gain_three, third_normed, validity, counts, third_std
    )
    skip_bias_grad = jnp.sum(grad_residual, axis=(0, 1))
    residual_low = rounded(grad_residual)
    residual_rows = residual_low.reshape(-1, C)
    skip_weight_grad = weight_grad(residual_rows, image_flat.reshape(-1, C_IN))
    image_from_skip = back_project(residual_rows, skip_full)
    unused, kept = front(stats)
    (
        first_normed,
        first_pre,
        first_columns,
        second_normed,
        second_shifted,
        second_pre,
        second_columns,
    ) = kept
    conv2_weight_grad = weight_grad(residual_rows, second_columns)
    grad_second_act = jnp.dot(
        conv_columns(residual_low.reshape(batch_size, row_count, col_count, C)),
        flipped(conv2_full, C),
        preferred_element_type=jnp.float32,
    )
    grad_second_pre = (
        grad_second_act.reshape(batch_size, pixel_count, C)
        * validity[:, :, None]
        * silu_slope(second_pre)
    )
    grad_mods = jnp.concatenate(
        [jnp.sum(grad_second_pre * second_shifted, axis=1), jnp.sum(grad_second_pre, axis=1)],
        axis=1,
    )
    emb_weight_grad = jnp.dot(
        grad_mods.T, embedding.astype(jnp.float32), precision=lax.Precision.HIGHEST
    )
    emb_bias_grad = jnp.sum(grad_mods, axis=0)
    grad_second_shift = grad_second_pre * scale_rows
    gain_two_grad = jnp.sum(grad_second_shift * second_normed, axis=(0, 1))
    bias_two_grad = jnp.sum(grad_second_shift, axis=(0, 1))
    hidden_low = rounded(
        norm_back(grad_second_shift * gain_two, second_normed, validity, counts, stats[1][1])
    )
    conv1_weight_grad = weight_grad(hidden_low.reshape(-1, C), first_columns)
    grad_first_act = jnp.dot(
        conv_columns(hidden_low.reshape(batch_size, row_count, col_count, C)),
        flipped(conv1_full, C_IN),
        preferred_element_type=jnp.float32,
    )
    grad_first_pre = (
        grad_first_act.reshape(batch_size, pixel_count, C_IN)
        * validity[:, :, None]
        * silu_slope(first_pre)
    )
    gain_one_grad = jnp.sum(grad_first_pre * first_normed, axis=(0, 1))
    bias_one_grad = jnp.sum(grad_first_pre, axis=(0, 1))
    image_grad = norm_back(
        grad_first_pre * gain_one, first_normed, validity, counts, stats[0][1]
    ) + image_from_skip.reshape(batch_size, pixel_count, C_IN)
    block_sums = (
        lax.psum_scatter(conv1_weight_grad, ("img", "ha"), scatter_dimension=0, tiled=True),
        lax.psum_scatter(conv2_weight_grad, ("img", "ha"), scatter_dimension=0, tiled=True),
        lax.psum_scatter(skip_weight_grad, ("img", "ha"), scatter_dimension=0, tiled=True),
        lax.psum_scatter(emb_weight_grad, ("img", "ha"), scatter_dimension=0, tiled=True),
        lax.psum_scatter(gain_one_grad, ("img", "ha"), scatter_dimension=0, tiled=True),
        lax.psum_scatter(bias_one_grad, ("img", "ha"), scatter_dimension=0, tiled=True),
        lax.psum_scatter(emb_bias_grad, ("img", "ha"), scatter_dimension=0, tiled=True),
        lax.psum_scatter(gain_two_grad, ("img", "ha"), scatter_dimension=0, tiled=True),
        lax.psum_scatter(bias_two_grad, ("img", "ha"), scatter_dimension=0, tiled=True),
        lax.psum_scatter(skip_bias_grad, ("img", "ha"), scatter_dimension=0, tiled=True),
    )
    return (
        output,
        image_grad.reshape(batch_size, row_count, col_count, C_IN),
        block_sums[0],
        block_sums[1],
        block_sums[2],
        block_sums[3],
        attn_sums[0],
        attn_sums[1],
        text_weight_grad,
        block_sums[4],
        block_sums[5],
        block_sums[6],
        block_sums[7],
        block_sums[8],
        block_sums[9],
        attn_sums[2],
        attn_sums[3],
        attn_sums[4],
    )


EVERY = ("y", "core", "z", "x")
PLANE = ("core", "y", "x")
PLANE_SORTED = ("y", "core", "x")
PLANES = 4
ACROSS = 2
MEMBERS = 8
OWN = C // MEMBERS
LANES = 128
TEXT_PAD = 128
CHUNK = 512
STEPS = HEIGHT * WIDTH // CHUNK
PIXELS = HEIGHT * WIDTH
TAPS = 9 * OWN
VMEM_BYTES = 56 * 1024 * 1024
SWITCH = ((0, 1), (1, 0))
NT = (((1,), (1,)), ((), ()))
TN = (((0,), (0,)), ((), ()))


def plane_mesh(mesh):
    images, rows = mesh.shape["img"], mesh.shape["ha"]
    if images != PLANES or rows != PLANES * ACROSS:
        return None
    return Mesh(mesh.devices.reshape(PLANES // 2, 2, PLANES, ACROSS), EVERY)


def split_spec(spec):
    names = {"img": ("y", "core"), "ha": ("z", "x")}
    entries = []
    for entry in spec:
        parts = (entry,) if isinstance(entry, str) else (entry or ())
        axes = tuple(axis for part in parts for axis in names[part])
        entries.append(axes or None)
    return P(*entries)


def flat_device(y, core, z, x):
    return ((y * 2 + core) * PLANES + z) * ACROSS + x


def every_place():
    return [(y, c, z, x) for y in range(2) for c in range(2) for z in range(PLANES) for x in range(ACROSS)]


def swapped(values):
    pairs = [
        (flat_device(y, c, z, x), flat_device(z % 2, z // 2, 2 * c + y, x)) for y, c, z, x in every_place()
    ]
    return lax.ppermute(values, EVERY, pairs)


def crossing(first):
    pairs = []
    for place in range(MEMBERS):
        along_x = (place // 2 % 2 == 0) == (first == "x")
        pairs.append((place, place ^ (1 if along_x else 4)))
    return pairs


def by_core(first, second):
    return jnp.where(lax.axis_index("core") == 0, first, second)


def pick_kernel(core_ref, first_ref, second_ref, out_ref):
    out_ref[...] = jnp.where(core_ref[0] == 0, first_ref[...], second_ref[...])


def pick(first, second, after):
    rows, columns = first.shape
    steps = 4 if rows % 64 == 0 else 1
    block = (rows // steps, columns)
    return call(
        pick_kernel,
        "pick",
        (steps,),
        [(lax.axis_index("core").reshape(1), None, None)]
        + [(item, block, row_chunk) for item in (first, second)],
        [(first.shape, first.dtype, block, row_chunk)],
        read=3 * rows * columns * 2,
        after=after,
    )[0]


def plane_gather(piece, after=()):
    from_x = lax.ppermute(piece, "x", SWITCH)
    from_y = lax.ppermute(piece, "y", SWITCH)
    from_core = lax.ppermute(piece, "core", SWITCH)
    from_xy = lax.ppermute(pick(from_x, from_y, after), PLANE_SORTED, crossing("y"))
    near = [piece, from_x, from_y, from_xy]
    far = [from_core] + [lax.ppermute(item, "core", SWITCH) for item in near[1:]]
    return near + far


def plane_sum(terms):
    near = []
    for distance in (3, 1, 2, 0):
        arrived = lax.ppermute(terms[distance ^ 4], "core", SWITCH)
        near.append(
            rounded(terms[distance].astype(jnp.float32) + arrived.astype(jnp.float32))
        )
    for_xy, for_x, for_y, mine = near
    passing = lax.ppermute(for_xy, PLANE_SORTED, crossing("x"))
    first = lax.ppermute(by_core(for_x, for_y), PLANE_SORTED, crossing("x"))
    second = rounded(by_core(for_y, for_x).astype(jnp.float32) + passing.astype(jnp.float32))
    arrived = lax.ppermute(second, PLANE_SORTED, crossing("y"))
    return (mine, first, arrived), second


def small_gather(values):
    def both(item, axis):
        other = lax.ppermute(item, axis, SWITCH)
        low = lax.axis_index(axis) == 0
        return jnp.stack([jnp.where(low, item, other), jnp.where(low, other, item)])

    values = both(values, "x")
    z = lax.axis_index("z")
    turned = [values] + [
        lax.ppermute(values, "z", [(at, (at + turn) % PLANES) for at in range(PLANES)])
        for turn in range(1, PLANES)
    ]
    values = jnp.stack(
        [
            sum(jnp.where((z - at) % PLANES == turn, turned[turn], 0.0) for turn in range(PLANES))
            for at in range(PLANES)
        ]
    )
    values = both(both(values, "core"), "y")
    return values.reshape((PLANES,) + values.shape[2:])


def own_channels(by_device):
    a, x = lax.axis_index(("y", "core")), lax.axis_index("x")
    part = lax.dynamic_index_in_dim(by_device, a, 0, keepdims=False)
    return lax.dynamic_index_in_dim(part, x, 1, keepdims=False)


def to_own_order(values):
    lead = values.shape[:-1]
    shaped = values.reshape(lead + (2, 2, PLANES, ACROSS, -1))
    at = len(lead)
    order = tuple(range(at)) + (at + 1, at, at + 3, at + 2, at + 4)
    return jnp.transpose(shaped, order).reshape(lead + (MEMBERS, OWN))


def to_natural_order(values):
    lead = values.shape[:-2]
    shaped = values.reshape(lead + (2, 2, ACROSS, PLANES, -1))
    at = len(lead)
    order = tuple(range(at)) + (at + 1, at, at + 3, at + 2, at + 4)
    return jnp.transpose(shaped, order).reshape(lead + (C,))


def unit_rounds():
    places = every_place()
    count = len(places)
    wants = {}
    for y, c, z, x in places:
        here, member = flat_device(y, c, z, x), 4 * c + 2 * y + x
        for kind in range(3):
            unit = 32 * kind + 4 * member + z
            wants.setdefault(unit // 3, []).append((here, kind, unit % 3))
    free = {home: list(items) for home, items in wants.items()}
    rounds = []
    for _ in range(3):
        taken = {}

        def place(home, seen, taken=taken):
            for item in free[home]:
                if item[0] in seen:
                    continue
                seen.add(item[0])
                if item[0] not in taken or place(taken[item[0]][0], seen):
                    taken[item[0]] = (home, item)
                    return True
            return False

        for home in range(count):
            place(home, set())
        kinds, slots, pairs = [0] * count, [0] * count, []
        for worker, (home, item) in sorted(taken.items()):
            kinds[worker], slots[home] = item[1], item[2]
            pairs.append((home, worker))
            free[home].remove(item)
        rounds.append((kinds, slots, pairs))
    return rounds


def move_units(units, outward):
    device = lax.axis_index(EVERY)
    total = None
    for kinds, slots, pairs in unit_rounds():
        kind, slot = jnp.array(kinds)[device], jnp.array(slots)[device]
        source, target = (slot, kind) if outward else (kind, slot)
        sent = lax.dynamic_index_in_dim(units, source, 0, keepdims=False)
        if not outward:
            pairs = [(worker, home) for home, worker in pairs]
        arrived = lax.ppermute(sent, EVERY, pairs)
        mask = (jnp.arange(3) == target).reshape((3,) + (1,) * (units.ndim - 1))
        part = jnp.where(mask, arrived[None], jnp.zeros_like(arrived)[None])
        total = part if total is None else total + part
    return total


def call(kernel, name, grid, operands, outputs, scratch=(), flops=0, read=0, after=()):
    def body(*refs):
        kernel(*refs[len(after) :])

    def spec(shape, index):
        if shape is None:
            return pl.BlockSpec(memory_space=pltpu.SMEM)
        if index is None:
            return pl.BlockSpec(shape, lambda *_: (0,) * len(shape))
        return pl.BlockSpec(shape, index)

    return pl.pallas_call(
        body,
        grid=grid,
        in_specs=[pl.BlockSpec(memory_space=pl.ANY)] * len(after)
        + [spec(shape, index) for _, shape, index in operands],
        out_specs=[spec(shape, index) for _, _, shape, index in outputs],
        out_shape=[jax.ShapeDtypeStruct(full, dtype) for full, dtype, _, _ in outputs],
        scratch_shapes=list(scratch),
        compiler_params=pltpu.CompilerParams(vmem_limit_bytes=VMEM_BYTES),
        cost_estimate=pl.CostEstimate(flops=flops, bytes_accessed=read, transcendentals=0),
        name=name,
    )(*after, *[array for array, _, _ in operands])


def whole(array):
    return (array, array.shape, None)


def row_chunk(step):
    return (step, 0)


def group_matrix(channels, width):
    row = lax.broadcasted_iota(jnp.int32, (channels, channels), 0) // width
    column = lax.broadcasted_iota(jnp.int32, (channels, channels), 1) // width
    return (row == column).astype(jnp.float32)


def group_sums(first, second, width):
    channels = first.shape[1]
    rows = jnp.concatenate([first, second, jnp.zeros((6, channels), jnp.float32)], axis=0)
    sums = jnp.dot(
        rows,
        group_matrix(channels, width),
        precision=lax.Precision.HIGHEST,
        preferred_element_type=jnp.float32,
    )
    return sums[0:1], sums[1:2]


def column_sums(values):
    return jnp.sum(values, axis=0, keepdims=True)


def sigmoid(values):
    return 1.0 / (1.0 + jnp.exp(-values))


def chunk_rows(step):
    return pl.ds(pl.multiple_of(step * CHUNK, CHUNK), CHUNK)


def padded_rows(step, row):
    start = step * CHUNK + (1 + row) * WIDTH
    return pl.ds(pl.multiple_of(start, WIDTH), CHUNK)


def sideways(values, by):
    place = lax.broadcasted_iota(jnp.int32, values.shape, 0) % WIDTH
    rolled = pltpu.roll(values, by % values.shape[0], 0)
    return jnp.where(place == (0 if by == 1 else WIDTH - 1), 0.0, rolled)


def add_taps(sums_ref, products, step):
    for tap in range(9):
        dy, dx = tap // 3, tap % 3
        rows = padded_rows(step, 1 - dy)
        sums_ref[dx, rows, :] += products[:, tap * OWN : (tap + 1) * OWN]


def tap_total(sums_ref, step):
    rows = padded_rows(step, 0)
    return (
        sums_ref[1, rows, :]
        + sideways(sums_ref[0, rows, :], 1)
        + sideways(sums_ref[2, rows, :], -1)
    )


def write_sideways(taps_ref, values_fn):
    for dx in range(3):
        taps_ref[dx, 0:WIDTH, :] = jnp.zeros((WIDTH, OWN), jnp.bfloat16)
        taps_ref[dx, PIXELS + WIDTH :, :] = jnp.zeros((WIDTH, OWN), jnp.bfloat16)

    def advance(step, carried):
        values = values_fn(step)
        rows = padded_rows(step, 0)
        taps_ref[0, rows, :] = sideways(values, -1).astype(jnp.bfloat16)
        taps_ref[1, rows, :] = values.astype(jnp.bfloat16)
        taps_ref[2, rows, :] = sideways(values, 1).astype(jnp.bfloat16)
        return carried

    lax.fori_loop(0, STEPS, advance, 0)


def tap_chunk(taps_ref, step):
    return jnp.concatenate(
        [taps_ref[tap % 3, padded_rows(step, 1 - tap // 3), :] for tap in range(9)], axis=1
    )


def first_kernel(
    member_ref,
    *refs,
):
    blocks, refs = refs[:MEMBERS], refs[MEMBERS:]
    image_ref = refs[4]
    for distance in range(MEMBERS):
        image_ref[chunk_rows(member_ref[0] ^ distance), :] = blocks[distance][:CHUNK]
    first_rows(image_ref, *refs[:4], *refs[5:])


def first_rows(
    image_ref,
    valid_ref,
    raw_ref,
    full_ref,
    own_ref,
    act_ref,
    normed_ref,
    next_ref,
    weight_ref,
    first_ref,
    second_ref,
    sums_ref,
):
    for tap in range(9):
        weight_ref[tap * OWN : (tap + 1) * OWN, :] = raw_ref[:, tap * C_IN : (tap + 1) * C_IN]
    zero = jnp.zeros((1, C_IN), jnp.float32)

    def gather_sums(step, carried):
        values = image_ref[chunk_rows(step), :].astype(jnp.float32)
        valid = valid_ref[chunk_rows(step), :].astype(jnp.float32)
        masked = values * jnp.concatenate([valid] * (C_IN // LANES), axis=1)
        return (carried[0] + column_sums(masked), carried[1] + column_sums(masked * values))

    sums = lax.fori_loop(0, STEPS, gather_sums, (zero, zero))
    mean, square = (item * full_ref[2:3] for item in group_sums(*sums, C_IN // GROUPS))
    inv_std = lax.rsqrt(square - mean * mean + eps_norm)
    factor = inv_std * full_ref[0:1]
    offset = full_ref[1:2] - mean * factor
    first_ref[...] = jnp.concatenate(
        [mean, inv_std, factor, offset, jnp.zeros((4, C_IN), jnp.float32)], axis=0
    )
    sums_ref[...] = jnp.zeros_like(sums_ref)

    def multiply(step, carried):
        values = image_ref[chunk_rows(step), :].astype(jnp.float32) * factor + offset
        valid = valid_ref[chunk_rows(step), :].astype(jnp.float32)
        valid = jnp.concatenate([valid] * (C_IN // LANES), axis=1)
        act = (values * sigmoid(values) * valid).astype(jnp.bfloat16)
        act_ref[chunk_rows(step), :] = act
        add_taps(
            sums_ref,
            lax.dot_general(act, weight_ref[...], NT, preferred_element_type=jnp.float32),
            step,
        )
        return carried

    lax.fori_loop(0, STEPS, multiply, 0)
    zero = jnp.zeros((1, OWN), jnp.float32)

    def gather_total(step, carried):
        values = tap_total(sums_ref, step)
        masked = values * valid_ref[chunk_rows(step), :].astype(jnp.float32)
        normed_ref[chunk_rows(step), :] = values
        return (carried[0] + column_sums(masked), carried[1] + column_sums(masked * values))

    sums = lax.fori_loop(0, STEPS, gather_total, (zero, zero))
    mean, square = (item * own_ref[8:9] for item in group_sums(*sums, C // GROUPS))
    inv_std = lax.rsqrt(square - mean * mean + eps_norm)
    second_ref[...] = jnp.concatenate(
        [mean, inv_std, jnp.zeros((6, OWN), jnp.float32)], axis=0
    )

    def activate(step, carried):
        normed = (normed_ref[chunk_rows(step), :] - mean) * inv_std
        normed_ref[chunk_rows(step), :] = normed
        values = (normed * own_ref[0:1] + own_ref[1:2]) * own_ref[2:3] + own_ref[3:4]
        valid = valid_ref[chunk_rows(step), :].astype(jnp.float32)
        next_ref[chunk_rows(step), :] = (values * sigmoid(values) * valid).astype(jnp.bfloat16)
        return carried

    lax.fori_loop(0, STEPS, activate, 0)


def first_layer(member, blocks, valid, raw, full, own, after):
    return call(
        first_kernel,
        "first_layer",
        (),
        [(member, None, None)]
        + [whole(item) for item in blocks]
        + [whole(valid), whole(raw), whole(full), whole(own)],
        [
            ((PIXELS, C_IN), jnp.bfloat16, (PIXELS, C_IN), None),
            ((PIXELS, C_IN), jnp.bfloat16, (PIXELS, C_IN), None),
            ((PIXELS, OWN), jnp.float32, (PIXELS, OWN), None),
            ((PIXELS, OWN), jnp.bfloat16, (PIXELS, OWN), None),
            ((TAPS, C_IN), jnp.bfloat16, (TAPS, C_IN), None),
            ((8, C_IN), jnp.float32, (8, C_IN), None),
            ((8, OWN), jnp.float32, (8, OWN), None),
        ],
        [pltpu.VMEM((3, PIXELS + 2 * WIDTH, OWN), jnp.float32)],
        flops=2 * PIXELS * TAPS * C_IN,
        read=PIXELS * C_IN * 4,
        after=after,
    )


def near_weights(member_ref, weight_ref, near_ref):
    for distance in range(MEMBERS):
        near_ref[:, distance * OWN : (distance + 1) * OWN] = weight_ref[member_ref[0] ^ distance]


def second_kernel(
    member_ref,
    *refs,
):
    pieces_in, refs = refs[:MEMBERS], refs[MEMBERS:]
    image_ref, valid_ref, weight_ref, skip_ref, own_ref = refs[:5]
    normed_ref, next_ref, low_ref, third_ref, sums_ref, near_ref = refs[5:]
    step = pl.program_id(0)

    @pl.when(step == 0)
    def _():
        sums_ref[...] = jnp.zeros_like(sums_ref)
        near_weights(member_ref, weight_ref, near_ref)

    joined = jnp.concatenate([item[...] for item in pieces_in], axis=1)
    add_taps(
        sums_ref,
        lax.dot_general(joined, near_ref[...], NT, preferred_element_type=jnp.float32),
        step,
    )
    sums_ref[1, padded_rows(step, 0), :] += lax.dot_general(
        image_ref[...], skip_ref[...], NT, preferred_element_type=jnp.float32
    )

    @pl.when(step == STEPS - 1)
    def _():
        zero = jnp.zeros((1, OWN), jnp.float32)

        def gather_total(step, carried):
            values = tap_total(sums_ref, step) + own_ref[6:7]
            masked = values * valid_ref[chunk_rows(step), :].astype(jnp.float32)
            normed_ref[chunk_rows(step), :] = values
            low_ref[chunk_rows(step), :] = values.astype(jnp.bfloat16)
            return (carried[0] + column_sums(masked), carried[1] + column_sums(masked * values))

        sums = lax.fori_loop(0, STEPS, gather_total, (zero, zero))
        mean, square = (item * own_ref[8:9] for item in group_sums(*sums, C // GROUPS))
        inv_std = lax.rsqrt(square - mean * mean + eps_norm)
        third_ref[...] = jnp.concatenate(
            [mean, inv_std, jnp.zeros((6, OWN), jnp.float32)], axis=0
        )

        def normalize_rows(step, carried):
            normed = (normed_ref[chunk_rows(step), :] - mean) * inv_std
            normed_ref[chunk_rows(step), :] = normed
            next_ref[chunk_rows(step), :] = (normed * own_ref[4:5] + own_ref[5:6]).astype(
                jnp.bfloat16
            )
            return carried

        lax.fori_loop(0, STEPS, normalize_rows, 0)


def skip_block(raw):
    return (raw, (OWN, C_IN), lambda step: (0, 9))


def second_layer(member, pieces_in, image_all, valid, weight, raw, own):
    return call(
        second_kernel,
        "second_layer",
        (STEPS,),
        [(member, None, None)]
        + [(item, (CHUNK, OWN), row_chunk) for item in pieces_in]
        + [(image_all, (CHUNK, C_IN), row_chunk)]
        + [whole(valid), whole(weight), skip_block(raw), whole(own)],
        [
            ((PIXELS, OWN), jnp.float32, (PIXELS, OWN), None),
            ((PIXELS, OWN), jnp.bfloat16, (PIXELS, OWN), None),
            ((PIXELS, OWN), jnp.bfloat16, (PIXELS, OWN), None),
            ((8, OWN), jnp.float32, (8, OWN), None),
        ],
        [
            pltpu.VMEM((3, PIXELS + 2 * WIDTH, OWN), jnp.float32),
            pltpu.VMEM((TAPS, C), jnp.bfloat16),
        ],
        flops=2 * PIXELS * TAPS * C,
        read=PIXELS * C * 4,
    )


def head_columns(values, head):
    return values if head == 0 else pltpu.roll(values, HEAD_DIM, 1)


def beside(values, *columns):
    lane = lax.broadcasted_iota(jnp.int32, values.shape, 1)
    out = jnp.where(lane < HEAD_DIM, values, 0.0)
    for at, column in enumerate(columns):
        out = jnp.where(lane == HEAD_DIM + at, column, out)
    return out


def qkv_kernel(member_ref, *refs):
    pieces_in, refs = refs[:MEMBERS], refs[MEMBERS:]
    valid_ref, weight_ref, cot_ref, q_ref, k_ref, v_ref, rows_ref, near_ref = refs
    rows_ref[...] = cot_ref[...]

    @pl.when(pl.program_id(0) == 0)
    def _():
        near_weights(member_ref, weight_ref, near_ref)

    joined = jnp.concatenate([item[...] for item in pieces_in], axis=1)
    triple = lax.dot_general(joined, near_ref[...], NT, preferred_element_type=jnp.float32)
    queries, keys, values = (triple[:, at * OWN : (at + 1) * OWN] for at in range(3))
    bias = jnp.where(valid_ref[...].astype(jnp.float32) > 0, 0.0, neg_big)
    for head in range(2):
        q_ref[head] = beside(head_columns(queries, head) * (1.0 / math.sqrt(HEAD_DIM)), 1.0).astype(
            jnp.bfloat16
        )
        k_ref[head] = beside(head_columns(keys, head), bias, -1.0, -1.0, -1.0).astype(jnp.bfloat16)
        v_ref[head] = beside(head_columns(values, head), 1.0, -1.0, -1.0, -1.0).astype(jnp.bfloat16)


def project_qkv(member, pieces_in, valid, weight, cots):
    cot_spec = ((1, CHUNK, 2 * OWN), lambda step: (step, 0, 0))
    out = ((2, PIXELS, LANES), jnp.bfloat16, (2, CHUNK, LANES), lambda step: (0, step, 0))
    return call(
        qkv_kernel,
        "project_qkv",
        (STEPS,),
        [(member, None, None)]
        + [(item, (CHUNK, OWN), row_chunk) for item in pieces_in]
        + [(valid, (CHUNK, OWN), row_chunk), whole(weight)]
        + [(cots, *cot_spec)],
        [out] * 3 + [(cots.shape, jnp.bfloat16, *cot_spec)],
        [pltpu.VMEM((3 * OWN, C), jnp.bfloat16)],
        flops=2 * PIXELS * 3 * OWN * C,
        read=PIXELS * C * 4,
    )


def split_float(column):
    parts = []
    for _ in range(3):
        part = column.astype(jnp.bfloat16).astype(jnp.float32)
        parts.append(part)
        column = column - part
    return parts


def attend_kernel(
    q_ref, low_ref, k_ref, v_ref, tk_ref, tv_ref, attn_ref, mixed_ref, back_ref
):
    width = 1024
    attended = []
    for head in range(2):
        queries = q_ref[head]
        parts = [(tk_ref[head], tv_ref[head])] + [
            (k_ref[head, at : at + width], v_ref[head, at : at + width])
            for at in range(0, PIXELS, width)
        ]
        highest, accumulated = None, None
        for keys, values in parts:
            scores = lax.dot_general(queries, keys, NT, preferred_element_type=jnp.float32)
            top = jnp.max(scores, axis=1, keepdims=True)
            if highest is not None:
                top = jnp.maximum(highest, top)
            weights = jnp.exp(scores - top).astype(jnp.bfloat16)
            update = jnp.dot(weights, values, preferred_element_type=jnp.float32)
            accumulated = (
                update if highest is None else accumulated * jnp.exp(highest - top) + update
            )
            highest = top
        total = accumulated[:, HEAD_DIM : HEAD_DIM + 1]
        attended.append(accumulated / total)
        logs = split_float(highest + jnp.log(total))
        back_ref[head] = beside(queries.astype(jnp.float32), 1.0, *logs).astype(jnp.bfloat16)
    lane = lax.broadcasted_iota(jnp.int32, attended[0].shape, 1)
    both = jnp.where(lane < HEAD_DIM, attended[0], pltpu.roll(attended[1], HEAD_DIM, 1))
    attn_ref[...] = both
    mixed_ref[:, :OWN] = both.astype(jnp.bfloat16)
    mixed_ref[:, OWN:] = low_ref[...]


def attend(queries, low, keys, values, text_keys, text_values):
    block = 1024
    return call(
        attend_kernel,
        "attend",
        (PIXELS // block,),
        [(queries, (2, block, LANES), lambda step: (0, step, 0)), (low, (block, OWN), row_chunk)]
        + [whole(keys), whole(values), whole(text_keys), whole(text_values)],
        [
            ((PIXELS, OWN), jnp.float32, (block, OWN), row_chunk),
            ((PIXELS, 2 * OWN), jnp.bfloat16, (block, 2 * OWN), row_chunk),
            ((2, PIXELS, LANES), jnp.bfloat16, (2, block, LANES), lambda step: (0, step, 0)),
        ],
        flops=8 * PIXELS * (PIXELS + TEXT_PAD) * LANES,
        read=PIXELS * LANES * 12,
    )


def attend_back_kernel(
    q_ref,
    do_ref,
    attn_ref,
    k_ref,
    v_ref,
    tk_ref,
    tv_ref,
    dq_ref,
    dk_ref,
    dv_ref,
    dtk_ref,
    dtv_ref,
    grads_ref,
    dqt_ref,
):
    step = pl.program_id(0)
    block = 512

    @pl.when(step == 0)
    def _():
        dqt_ref[...] = jnp.zeros_like(dqt_ref)

        def prepare(at, carried):
            grads = do_ref[chunk_rows(at), :].astype(jnp.float32)
            terms = grads * attn_ref[chunk_rows(at), :]
            lane = lax.broadcasted_iota(jnp.int32, terms.shape, 1)
            for head in range(2):
                inside = (lane < HEAD_DIM) == (head == 0)
                delta = jnp.sum(jnp.where(inside, terms, 0.0), axis=1, keepdims=True)
                grads_ref[head, chunk_rows(at), :] = beside(
                    head_columns(grads, head), 0.0, *split_float(delta)
                ).astype(jnp.bfloat16)
            return carried

        lax.fori_loop(0, STEPS, prepare, 0)

    def absorb_keys(head, keys, values):
        keys_across = jnp.transpose(keys.astype(jnp.float32))[:HEAD_DIM].astype(jnp.bfloat16)
        grad_keys, grad_values = None, None
        for start in range(0, PIXELS, block):
            queries = q_ref[head, start : start + block]
            grads = grads_ref[head, start : start + block]
            scores = lax.dot_general(keys, queries, NT, preferred_element_type=jnp.float32)
            grad_probs = lax.dot_general(values, grads, NT, preferred_element_type=jnp.float32)
            probs = jnp.exp(scores)
            grad_scores = (probs * grad_probs).astype(jnp.bfloat16)
            value_term = jnp.dot(
                probs.astype(jnp.bfloat16), grads, preferred_element_type=jnp.float32
            )
            key_term = jnp.dot(grad_scores, queries, preferred_element_type=jnp.float32)
            grad_values = value_term if grad_values is None else grad_values + value_term
            grad_keys = key_term if grad_keys is None else grad_keys + key_term
            rows = slice(head * HEAD_DIM, (head + 1) * HEAD_DIM)
            dqt_ref[rows, start : start + block] += jnp.dot(
                keys_across, grad_scores, preferred_element_type=jnp.float32
            )
        return grad_keys, grad_values

    def both_heads(key_source, value_source):
        (dk0, dv0), (dk1, dv1) = (
            absorb_keys(head, key_source[head], value_source[head]) for head in range(2)
        )
        lane = lax.broadcasted_iota(jnp.int32, dk0.shape, 1)
        return (
            jnp.where(lane < HEAD_DIM, low, pltpu.roll(high, HEAD_DIM, 1)).astype(jnp.bfloat16)
            for low, high in ((dk0, dk1), (dv0, dv1))
        )

    dk_ref[...], dv_ref[...] = both_heads(k_ref, v_ref)

    @pl.when(step == pl.num_programs(0) - 1)
    def _():
        dtk_ref[...], dtv_ref[...] = both_heads(tk_ref, tv_ref)
        for start in range(0, PIXELS, block):
            dq_ref[start : start + block, :] = (
                jnp.transpose(dqt_ref[:, start : start + block]) * (1.0 / math.sqrt(HEAD_DIM))
            ).astype(jnp.bfloat16)


def attend_back(queries, grads, attended, keys, values, text_keys, text_values):
    block = 1024
    rows = (PIXELS, OWN)
    text_rows = (TEXT_PAD, OWN)
    return call(
        attend_back_kernel,
        "attend_back",
        (PIXELS // block,),
        [whole(queries), whole(grads), whole(attended)]
        + [(item, (2, block, LANES), lambda step: (0, step, 0)) for item in (keys, values)]
        + [whole(text_keys), whole(text_values)],
        [
            (rows, jnp.bfloat16, rows, None),
            (rows, jnp.bfloat16, (block, OWN), row_chunk),
            (rows, jnp.bfloat16, (block, OWN), row_chunk),
            (text_rows, jnp.bfloat16, text_rows, None),
            (text_rows, jnp.bfloat16, text_rows, None),
        ],
        [
            pltpu.VMEM((2, PIXELS, LANES), jnp.bfloat16),
            pltpu.VMEM((OWN, PIXELS), jnp.float32),
        ],
        flops=20 * PIXELS * (PIXELS + TEXT_PAD) * LANES,
        read=PIXELS * LANES * 20,
    )


def triple_blocks(grads):
    return [(item, (CHUNK, OWN), row_chunk) for item in grads]


def join_triple(refs):
    return jnp.concatenate([item[...] for item in refs], axis=1)


def qkv_back_kernel(member_ref, *refs):
    triple, weight_ref, outs, near_ref = refs[:3], refs[3], refs[4 : 4 + MEMBERS], refs[4 + MEMBERS]

    @pl.when(pl.program_id(0) == 0)
    def _():
        near_weights(member_ref, weight_ref, near_ref)

    terms = jnp.dot(join_triple(triple), near_ref[...], preferred_element_type=jnp.float32)
    for distance in range(MEMBERS):
        outs[distance][...] = terms[:, distance * OWN : (distance + 1) * OWN].astype(jnp.bfloat16)


def qkv_back(member, grads, weight, after):
    return call(
        qkv_back_kernel,
        "qkv_back",
        (STEPS,),
        [(member, None, None)] + triple_blocks(grads) + [whole(weight)],
        [((PIXELS, OWN), jnp.bfloat16, (CHUNK, OWN), row_chunk)] * MEMBERS,
        [pltpu.VMEM((3 * OWN, C), jnp.bfloat16)],
        flops=2 * PIXELS * 3 * OWN * C,
        read=PIXELS * C * 4,
        after=after,
    )


def norm_back_rows(step_fn, own_ref, inv_std, rows_ref):
    zero = jnp.zeros((1, OWN), jnp.float32)

    def gather_sums(step, carried):
        grads, normed, _ = step_fn(step)
        return (carried[0] + column_sums(grads), carried[1] + column_sums(grads * normed))

    sums = lax.fori_loop(0, STEPS, gather_sums, (zero, zero))
    first, second = (item * own_ref[8:9] for item in group_sums(*sums, C // GROUPS))

    def advance(step, carried):
        grads, normed, valid = step_fn(step)
        rows_ref[chunk_rows(step), :] = (grads - valid * (first + normed * second)) * inv_std
        return carried

    lax.fori_loop(0, STEPS, advance, 0)


def third_back_kernel(
    member_ref,
    mine_ref,
    first_ref,
    second_ref,
    normed_ref,
    cot_ref,
    valid_ref,
    third_ref,
    own_ref,
    weight_ref,
    *refs,
):
    outs, refs = refs[:MEMBERS], refs[MEMBERS:]
    low_ref, taps_ref, totals_ref, near_ref, rows_ref, grads_ref = refs
    step = pl.program_id(0)

    @pl.when(step == 0)
    def _():
        near_weights(member_ref, weight_ref, near_ref)
        zero = jnp.zeros((1, OWN), jnp.float32)

        def gather(at, carried):
            rows = chunk_rows(at)
            grads = (
                mine_ref[rows, :].astype(jnp.float32)
                + first_ref[rows, :].astype(jnp.float32)
                + second_ref[rows, :].astype(jnp.float32)
            )
            cots = cot_ref[at].astype(jnp.float32)
            grads_ref[rows, :] = grads * own_ref[4:5]
            return (
                carried[0] + column_sums(grads * normed_ref[rows, :]),
                carried[1] + column_sums(grads),
                carried[2] + column_sums(cots),
            )

        gain_sum, bias_sum, cot_sum = lax.fori_loop(0, STEPS, gather, (zero, zero, zero))

        def terms(at):
            rows = chunk_rows(at)
            return (
                grads_ref[rows, :],
                normed_ref[rows, :],
                valid_ref[rows, :].astype(jnp.float32),
            )

        norm_back_rows(terms, own_ref, third_ref[1:2], rows_ref)

        def finish(at, carried):
            rows = chunk_rows(at)
            total = rows_ref[rows, :] + cot_ref[at].astype(jnp.float32)
            rows_ref[rows, :] = total
            low_ref[rows, :] = total.astype(jnp.bfloat16)
            return carried + column_sums(total)

        skip_sum = lax.fori_loop(0, STEPS, finish, zero)
        totals_ref[...] = jnp.concatenate(
            [gain_sum, bias_sum, skip_sum, cot_sum, jnp.zeros((4, OWN), jnp.float32)], axis=0
        )
        write_sideways(taps_ref, lambda at: rows_ref[chunk_rows(at), :])

    terms = jnp.dot(tap_chunk(taps_ref, step), near_ref[...], preferred_element_type=jnp.float32)
    for distance in range(MEMBERS):
        outs[distance][...] = terms[:, distance * OWN : (distance + 1) * OWN].astype(jnp.bfloat16)


def third_back(member, sums, normed, cots, valid, third, own, weight):
    rows = (PIXELS, OWN)
    taps = (3, PIXELS + 2 * WIDTH, OWN)
    return call(
        third_back_kernel,
        "third_back",
        (STEPS,),
        [(member, None, None)]
        + [whole(item) for item in sums]
        + [whole(normed), whole(cots), whole(valid), whole(third), whole(own), whole(weight)],
        [(rows, jnp.bfloat16, (CHUNK, OWN), row_chunk)] * MEMBERS
        + [
            (rows, jnp.bfloat16, rows, None),
            (taps, jnp.bfloat16, taps, None),
            ((8, OWN), jnp.float32, (8, OWN), None),
        ],
        [
            pltpu.VMEM((TAPS, C), jnp.bfloat16),
            pltpu.VMEM(rows, jnp.float32),
            pltpu.VMEM(rows, jnp.float32),
        ],
        flops=2 * PIXELS * TAPS * C,
        read=PIXELS * C * 4,
    )


def second_back_kernel(
    member_ref,
    mine_ref,
    first_ref,
    second_ref,
    normed_ref,
    low_ref,
    valid_ref,
    stats_ref,
    own_ref,
    weight_ref,
    skip_ref,
    image_ref,
    full_ref,
    out_ref,
    taps_ref,
    totals_ref,
    firsts_ref,
    rows_ref,
    grads_ref,
):
    step = pl.program_id(0)

    @pl.when(step == 0)
    def _():
        zero = jnp.zeros((1, OWN), jnp.float32)

        def gather(at, carried):
            rows = chunk_rows(at)
            normed = normed_ref[rows, :]
            shifted_rows = normed * own_ref[0:1] + own_ref[1:2]
            values = shifted_rows * own_ref[2:3] + own_ref[3:4]
            gate = sigmoid(values)
            slope = gate * (1.0 + values * (1.0 - gate))
            grads = (
                mine_ref[rows, :].astype(jnp.float32)
                + first_ref[rows, :].astype(jnp.float32)
                + second_ref[rows, :].astype(jnp.float32)
            )
            grads = grads * valid_ref[rows, :].astype(jnp.float32) * slope
            inner = grads * own_ref[2:3]
            grads_ref[rows, :] = inner * own_ref[0:1]
            return (
                carried[0] + column_sums(grads * shifted_rows),
                carried[1] + column_sums(grads),
                carried[2] + column_sums(inner * normed),
                carried[3] + column_sums(inner),
            )

        totals = lax.fori_loop(0, STEPS, gather, (zero,) * 4)
        totals_ref[...] = jnp.concatenate(
            list(totals) + [jnp.zeros((4, OWN), jnp.float32)], axis=0
        )

        def terms(at):
            rows = chunk_rows(at)
            return (
                grads_ref[rows, :],
                normed_ref[rows, :],
                valid_ref[rows, :].astype(jnp.float32),
            )

        norm_back_rows(terms, own_ref, stats_ref[1:2], rows_ref)
        write_sideways(taps_ref, lambda at: rows_ref[chunk_rows(at), :])
        firsts_ref[...] = jnp.zeros_like(firsts_ref)

    at = member_ref[0] ^ step
    rows = chunk_rows(at)
    grads = jnp.dot(tap_chunk(taps_ref, at), weight_ref[...], preferred_element_type=jnp.float32)
    image = image_ref[rows, :].astype(jnp.float32)
    values = image * full_ref[2:3] + full_ref[3:4]
    gate = sigmoid(values)
    slope = gate * (1.0 + values * (1.0 - gate))
    valid = valid_ref[rows, :].astype(jnp.float32)
    grads = grads * jnp.concatenate([valid] * (C_IN // LANES), axis=1) * slope
    normed = (image - full_ref[0:1]) * full_ref[1:2]
    firsts_ref[0:1] += column_sums(grads * normed)
    firsts_ref[1:2] += column_sums(grads)
    skipped = jnp.dot(low_ref[rows, :], skip_ref[...], preferred_element_type=jnp.float32)
    out_ref[0] = (grads * full_ref[2:3] + skipped).astype(jnp.bfloat16)


def second_back(member, sums, normed, low, valid, stats, own, weight, raw, image_all, full, after):
    rows = (PIXELS, OWN)
    taps = (3, PIXELS + 2 * WIDTH, OWN)
    return call(
        second_back_kernel,
        "second_back",
        (STEPS,),
        [(member, None, None)]
        + [whole(item) for item in sums]
        + [whole(normed), whole(low), whole(valid), whole(stats), whole(own)]
        + [whole(weight), skip_block(raw), whole(image_all), whole(full)],
        [
            (
                (MEMBERS, CHUNK, C_IN),
                jnp.bfloat16,
                (1, CHUNK, C_IN),
                lambda step: (step, 0, 0),
            ),
            (taps, jnp.bfloat16, taps, None),
            ((8, OWN), jnp.float32, (8, OWN), None),
            ((8, C_IN), jnp.float32, (8, C_IN), None),
        ],
        [pltpu.VMEM(rows, jnp.float32), pltpu.VMEM(rows, jnp.float32)],
        flops=2 * PIXELS * TAPS * C_IN,
        read=PIXELS * C_IN * 4,
        after=after,
    )


def tap_grad_kernel(count, member_ref, taps_ref, *refs):
    inputs, refs = refs[:count], refs[count:]
    if count == 1:
        low_ref, image_ref, out_ref, sums_ref, skip_ref = refs
    else:
        out_ref, sums_ref = refs
    step = pl.program_id(0)

    @pl.when(step == 0)
    def _():
        sums_ref[...] = jnp.zeros_like(sums_ref)
        if count == 1:
            skip_ref[...] = jnp.zeros_like(skip_ref)

    if count == 1:
        skip_ref[...] += lax.dot_general(
            low_ref[...], image_ref[...], TN, preferred_element_type=jnp.float32
        )

    joined = jnp.concatenate([item[...] for item in inputs], axis=1)
    sums_ref[...] += lax.dot_general(
        tap_chunk(taps_ref, step), joined, TN, preferred_element_type=jnp.float32
    )

    @pl.when(step == STEPS - 1)
    def _():
        share = OWN // PLANES
        if count == 1:
            for z in range(PLANES):
                out_ref[z, 0, 9] = skip_ref[z * share : (z + 1) * share, :].astype(jnp.bfloat16)
        for tap in range(9):
            for z in range(PLANES):
                rows = slice(tap * OWN + z * share, tap * OWN + (z + 1) * share)
                if count == 1:
                    out_ref[z, 0, tap] = sums_ref[rows, :].astype(jnp.bfloat16)
                else:
                    for distance in range(count):
                        columns = slice(distance * OWN, (distance + 1) * OWN)
                        out_ref[z, member_ref[0] ^ distance, tap] = sums_ref[rows, columns].astype(
                            jnp.bfloat16
                        )


def tap_grad(member, taps, inputs, skip=(), after=()):
    count, width = len(inputs), inputs[0].shape[1]
    shape = (PLANES, count, 10 if skip else 9, OWN // PLANES, width)
    return call(
        functools.partial(tap_grad_kernel, count),
        "tap_grad",
        (STEPS,),
        [(member, None, None), whole(taps)]
        + [(item, (CHUNK, item.shape[1]), row_chunk) for item in inputs + list(skip)],
        [(shape, jnp.bfloat16, shape, None)],
        [pltpu.VMEM((TAPS, count * width), jnp.float32)]
        + [pltpu.VMEM((OWN, C_IN), jnp.float32)] * (1 if skip else 0),
        flops=2 * PIXELS * TAPS * count * width,
        read=PIXELS * count * width * 2,
        after=after,
    )[0]


def qkv_grad_kernel(member_ref, *refs):
    triple, inputs, (out_ref, sums_ref) = refs[:3], refs[3 : 3 + MEMBERS], refs[3 + MEMBERS :]
    step = pl.program_id(0)

    @pl.when(step == 0)
    def _():
        sums_ref[...] = jnp.zeros_like(sums_ref)

    joined = jnp.concatenate([item[...] for item in inputs], axis=1)
    sums_ref[...] += lax.dot_general(join_triple(triple), joined, TN, preferred_element_type=jnp.float32)

    @pl.when(step == STEPS - 1)
    def _():
        share = OWN // PLANES
        for kind in range(3):
            for z in range(PLANES):
                rows = slice(kind * OWN + z * share, kind * OWN + (z + 1) * share)
                for distance in range(MEMBERS):
                    columns = slice(distance * OWN, (distance + 1) * OWN)
                    out_ref[z, kind, member_ref[0] ^ distance] = sums_ref[rows, columns].astype(
                        jnp.bfloat16
                    )


def qkv_grad(member, grads, inputs, after):
    shape = (PLANES, 3, MEMBERS, OWN // PLANES, OWN)
    return call(
        qkv_grad_kernel,
        "qkv_grad",
        (STEPS,),
        [(member, None, None)]
        + triple_blocks(grads)
        + [(item, (CHUNK, OWN), row_chunk) for item in inputs],
        [(shape, jnp.bfloat16, shape, None)],
        [pltpu.VMEM((3 * OWN, C), jnp.float32)],
        flops=2 * PIXELS * 3 * OWN * C,
        read=PIXELS * C * 2,
        after=after,
    )[0]


def widen_kernel(value_ref, out_ref):
    out_ref[...] = value_ref[...].astype(jnp.float32)


def widened(values, after):
    return call(
        widen_kernel,
        "widen",
        (),
        [whole(values)],
        [(values.shape, jnp.float32, values.shape, None)],
        after=after,
    )[0]


def along_z(blocks):
    z = lax.axis_index("z")
    arrived = [lax.dynamic_index_in_dim(blocks, z, 0, keepdims=False)]
    for turn in range(1, PLANES):
        sent = lax.dynamic_index_in_dim(blocks, (z + turn) % PLANES, 0, keepdims=False)
        pairs = [(at, (at + turn) % PLANES) for at in range(PLANES)]
        arrived.append(lax.ppermute(sent, "z", pairs))
    return arrived


def turns_z(piece):
    return [piece] + [
        lax.ppermute(piece, "z", [(at, (at + turn) % PLANES) for at in range(PLANES)])
        for turn in range(1, PLANES)
    ]


def gather_z(piece):
    z = lax.axis_index("z")
    turned = turns_z(piece)
    zero = jnp.zeros_like(piece)
    return jnp.stack(
        [
            sum(jnp.where((z - at) % PLANES == turn, turned[turn], zero) for turn in range(PLANES))
            for at in range(PLANES)
        ]
    )


def order_matrix(dtype):
    shape = (ACROSS * OWN, ACROSS * OWN)
    source = lax.broadcasted_iota(jnp.int32, shape, 0)
    target = lax.broadcasted_iota(jnp.int32, shape, 1)
    x, z, place = source // OWN, source % OWN // 32, source % 32
    return (target == (z * ACROSS + x) * 32 + place).astype(jnp.float32).astype(dtype)


def own_columns(values, order, y, core):
    start = (2 * y + core) * ACROSS * OWN
    block = values[:, start : start + ACROSS * OWN]
    return lax.dot_general(block, order, NT, preferred_element_type=jnp.float32).astype(jnp.bfloat16)


def square(count):
    return [(core, y) for core in range(2) for y in range(count)]


def conv2_kernel(raw_ref, out_ref):
    order = order_matrix(jnp.bfloat16)
    for tap in range(9):
        rows = slice(tap * OWN, (tap + 1) * OWN)
        values = raw_ref[:, tap * C : (tap + 1) * C]
        for core, y in square(2):
            columns = own_columns(values, order, y, core)
            for x in range(ACROSS):
                out_ref[4 * core + 2 * y + x, rows, :] = columns[:, x * OWN : (x + 1) * OWN]


def conv2_blocks(raw):
    shape = (MEMBERS, TAPS, OWN)
    return call(
        conv2_kernel, "conv2_blocks", (), [whole(raw)], [(shape, jnp.bfloat16, shape, None)]
    )[0]


def qkv_blocks_kernel(z_ref, *refs):
    units, out_ref = refs[:PLANES], refs[PLANES]
    order = order_matrix(jnp.bfloat16)
    for turn in range(PLANES):
        place = lax.rem(z_ref[0] - turn + PLANES, PLANES) * 32
        for kind in range(3):
            rows = pl.ds(pl.multiple_of(kind * OWN + place, 32), 32)
            values = units[turn][kind]
            for core, y in square(2):
                columns = own_columns(values, order, y, core)
                for x in range(ACROSS):
                    out_ref[4 * core + 2 * y + x, rows, :] = columns[:, x * OWN : (x + 1) * OWN]


def qkv_blocks(units):
    shape = (MEMBERS, 3 * OWN, OWN)
    return call(
        qkv_blocks_kernel,
        "qkv_blocks",
        (),
        [(lax.axis_index("z").reshape(1), None, None)] + [whole(item) for item in units],
        [(shape, jnp.bfloat16, shape, None)],
    )[0]


def cot_kernel(cot_ref, weight_ref, out_ref):
    cots = cot_ref[...]
    order = order_matrix(jnp.bfloat16)
    mixed = jnp.dot(cots, weight_ref[...], preferred_element_type=jnp.float32).astype(jnp.bfloat16)
    for core, y in square(2):
        columns = own_columns(cots, order, y, core)
        for x in range(ACROSS):
            out_ref[4 * core + 2 * y + x, :, :OWN] = columns[:, x * OWN : (x + 1) * OWN]
    for member in range(MEMBERS):
        out_ref[member, :, OWN:] = mixed[:, member * OWN : (member + 1) * OWN]


def cot_blocks(cots, weight):
    shape = (MEMBERS, CHUNK, 2 * OWN)
    return call(
        cot_kernel,
        "cot_blocks",
        (),
        [whole(cots), whole(weight)],
        [(shape, jnp.bfloat16, shape, None)],
        flops=2 * CHUNK * C * C,
    )[0]


def output_kernel(moved_ref, weight_ref, cot_ref, shift_ref, out_ref, grad_ref):
    mixed = jnp.concatenate([moved_ref[member, :, :OWN] for member in range(MEMBERS)], axis=1)
    product = lax.dot_general(mixed, weight_ref[...], NT, preferred_element_type=jnp.float32)
    order = order_matrix(jnp.bfloat16)
    for core, y in square(2):
        member = 4 * core + 2 * y
        residual = jnp.concatenate(
            [moved_ref[member, :, OWN:], moved_ref[member + 1, :, OWN:]], axis=1
        )
        residual = jnp.dot(residual, order, preferred_element_type=jnp.float32)
        start = (2 * y + core) * ACROSS * OWN
        columns = slice(start, start + ACROSS * OWN)
        out_ref[:, columns] = (residual + product[:, columns] + shift_ref[:, columns]).astype(
            jnp.bfloat16
        )
    grads = lax.dot_general(cot_ref[...], mixed, TN, preferred_element_type=jnp.float32)
    for core, y in square(2):
        for z in range(PLANES):
            for x in range(ACROSS):
                start = ((2 * y + core) * PLANES + z) * ACROSS * 32 + x * 32
                grad_ref[4 * core + 2 * y + x, z * 32 : (z + 1) * 32, :] = grads[
                    start : start + 32
                ].astype(jnp.bfloat16)


def output_rows(moved, weight, cots, shift, after):
    shapes = ((CHUNK, C), (MEMBERS, OWN, C))
    return call(
        output_kernel,
        "output_rows",
        (),
        [whole(moved), whole(weight), whole(cots), whole(shift)],
        [(shape, jnp.bfloat16, shape, None) for shape in shapes],
        flops=4 * CHUNK * C * C,
        after=after,
    )


def natural_kernel(first_ref, second_ref, third_ref, fourth_ref, out_ref):
    taps, rows = first_ref.shape[1], first_ref.shape[2]
    width = ACROSS * OWN
    order = order_matrix(jnp.float32)

    def total(at):
        parts = [item[at].astype(jnp.float32) for item in (first_ref, second_ref, third_ref, fourth_ref)]
        return ((parts[0] + parts[1]) + (parts[2] + parts[3])).reshape(taps * rows, OWN)

    for core in range(2):
        for y in range(2):
            at = 4 * core + 2 * y
            joined = jnp.concatenate([total(at), total(at + 1)], axis=1)
            ordered = jnp.dot(
                joined, order, precision=lax.Precision.HIGHEST, preferred_element_type=jnp.float32
            )
            for tap in range(taps):
                columns = slice(tap * C + (2 * y + core) * width, tap * C + (2 * y + core + 1) * width)
                out_ref[:, columns] = ordered[tap * rows : (tap + 1) * rows]


def natural_sum(parts, after):
    taps, rows = parts[0].shape[1:3]
    shape = (rows, taps * C)
    return call(
        natural_kernel,
        "natural_sum",
        (),
        [whole(item) for item in parts],
        [(shape, jnp.float32, shape, None)],
        after=after,
    )[0]


def plain_kernel(first_ref, second_ref, third_ref, fourth_ref, out_ref, skip_ref):
    taps, width = first_ref.shape[0] - 1, first_ref.shape[2]
    for tap in range(taps + 1):
        parts = [item[tap].astype(jnp.float32) for item in (first_ref, second_ref, third_ref, fourth_ref)]
        total = (parts[0] + parts[1]) + (parts[2] + parts[3])
        if tap < taps:
            out_ref[:, tap * width : (tap + 1) * width] = total
        else:
            skip_ref[...] = total


def plain_sum(parts):
    taps, rows, width = parts[0].shape
    shapes = ((rows, (taps - 1) * width), (rows, width))
    return call(
        plain_kernel,
        "plain_sum",
        (),
        [whole(item) for item in parts],
        [(shape, jnp.float32, shape, None) for shape in shapes],
    )


def text_pairs(back):
    rounds = ([], [])
    for y, c, z, x in every_place():
        piece, plane = 2 * z + x, 2 * c + y
        for half in range(2):
            member = 2 * (piece % 4) + half
            target = flat_device(member // 2 % 2, member // 4, plane, member % 2)
            pair = (flat_device(y, c, z, x), target)
            rounds[half ^ (piece // 4)].append(pair[::-1] if back else pair)
    return rounds


def text_to_heads(text_slice):
    late = (2 * lax.axis_index("z") + lax.axis_index("x")) // 4
    halves = (text_slice[:, :OWN], text_slice[:, OWN:])
    first, second = (
        lax.ppermute(jnp.where(late == at, halves[0], halves[1]), EVERY, text_pairs(False)[at])
        for at in range(2)
    )
    even = lax.axis_index("x") == 0
    return jnp.where(even, first, second), jnp.where(even, second, first)


def text_from_heads(text_keys, text_values):
    even = lax.axis_index("x") == 0
    first = jnp.where(even, text_keys, text_values)
    second = jnp.where(even, text_values, text_keys)
    first, second = (
        lax.ppermute(item, EVERY, text_pairs(True)[at]) for at, item in enumerate((first, second))
    )
    late = (2 * lax.axis_index("z") + lax.axis_index("x")) // 4 == 1
    return jnp.concatenate(
        [jnp.where(late, second, first), jnp.where(late, first, second)], axis=1
    )


def text_lanes(values, *columns):
    padded = jnp.pad(values, ((0, TEXT_PAD - values.shape[0]), (0, 0)))
    heads = jnp.transpose(padded.reshape(TEXT_PAD, 2, HEAD_DIM), (1, 0, 2))
    extra = [
        jnp.broadcast_to(jnp.asarray(column, jnp.bfloat16).reshape(1, -1, 1), (2, TEXT_PAD, 1))
        for column in columns
    ]
    joined = jnp.concatenate([heads] + extra, axis=2)
    return jnp.pad(joined, ((0, 0), (0, 0), (0, LANES - joined.shape[2])))


def plane_shards(
    image,
    mask,
    timestep,
    pooled,
    text,
    text_mask,
    cotangent,
    conv1_weight,
    conv2_weight,
    skip_weight,
    emb_weight,
    qkv_weight,
    out_weight,
    text_weight,
    gn1_gain,
    gn1_bias,
    emb_bias,
    gn2_gain,
    gn2_bias,
    skip_bias,
    gn3_gain,
    gn3_bias,
    out_bias,
):
    z_here, x_here = lax.axis_index("z"), lax.axis_index("x")
    a_here = lax.axis_index(("y", "core"))
    member = lax.axis_index(PLANE)
    member_word = member.reshape(1).astype(jnp.int32)
    device = lax.axis_index(EVERY)

    extents = jnp.stack([timestep[0], jnp.sum(mask[0, :, 0]), jnp.sum(mask[0, 0]), jnp.sum(text_mask)])
    exact = jnp.concatenate([pooled[0], extents.astype(jnp.float32)])

    def both(values, axis):
        other = lax.ppermute(values, axis, SWITCH)
        low = lax.axis_index(axis) == 0
        return jnp.stack([jnp.where(low, values, other), jnp.where(low, other, values)])

    exact = both(both(exact, "y"), "core").reshape(PLANES, -1)
    extents = exact[:, EMB:]
    valid_rows, valid_columns, text_count = extents[z_here, 1:]
    count = valid_rows * valid_columns
    pixel = lax.broadcasted_iota(jnp.int32, (PIXELS, OWN), 0).astype(jnp.float32)
    pixel_row = jnp.floor(pixel / WIDTH)
    valid = (pixel_row < valid_rows) & (pixel - pixel_row * WIDTH < valid_columns)
    valid = valid.astype(jnp.bfloat16)
    half_width = EMB // 2
    frequency = jnp.exp(-math.log(10000.0) * jnp.arange(half_width, dtype=jnp.float32) / half_width)
    angles = extents[:, :1] * frequency[None, :]
    embedding = rounded(
        jax.nn.silu(jnp.concatenate([jnp.cos(angles), jnp.sin(angles)], axis=1) + exact[:, :EMB])
    )
    rest = project(embedding, emb_weight) + emb_bias.astype(jnp.float32)

    parts = []
    for _ in range(3):
        part = lax.reduce_precision(rest, 8, 7)
        parts.append(rounded(part).reshape(-1))
        rest = rest - part
    vectors = (
        gn1_gain,
        gn1_bias,
        gn2_gain,
        gn2_bias,
        skip_bias,
        gn3_gain,
        gn3_bias,
        out_bias,
    )
    packed = jnp.concatenate(list(vectors) + parts)
    filled = -packed.shape[0] % (4 * C_IN) + packed.shape[0]
    packed = gather_z(jnp.pad(packed, (0, filled - packed.shape[0])))
    image_block = swapped(image[0].reshape(CHUNK, C_IN))
    image_blocks = plane_gather(
        jnp.concatenate([image_block, packed.reshape(-1, C_IN)], axis=0)
    )
    small = jnp.stack([block[CHUNK:].reshape(PLANES, filled) for block in image_blocks])
    distances = jnp.arange(MEMBERS)[:, None] ^ member
    chosen = distances == jnp.arange(MEMBERS)[None, :]
    small = jnp.sum(
        jnp.where(chosen[:, :, None, None], small[None].astype(jnp.float32), 0.0), axis=1
    )
    small = jnp.transpose(small.reshape(2, 2, ACROSS, PLANES, filled), (1, 0, 3, 2, 4))
    small = small.reshape(PLANES, PLANES, ACROSS, filled)
    bounds = [0]
    for item in vectors:
        bounds.append(bounds[-1] + item.shape[0])
    small_parts = [small[..., bounds[at] : bounds[at + 1]] for at in range(len(vectors))]
    gain_one, bias_one = (part.reshape(-1) for part in small_parts[:2])
    out_shift = small_parts[7].reshape(1, C)
    own_parts = [own_channels(part).reshape(-1) for part in small_parts[2:7]]
    gain_two, bias_two, skip_shift, gain_three, bias_three = own_parts
    emb_rows = emb_weight.shape[0]
    mods = small[..., bounds[-1] : bounds[-1] + 3 * PLANES * emb_rows]
    mods = mods.reshape(PLANES * MEMBERS, 3, PLANES, emb_rows)
    mods = lax.dynamic_index_in_dim(mods, z_here, 2, keepdims=False)
    mods = ((mods[:, 0] + mods[:, 1]) + mods[:, 2]).reshape(2, PLANES, PLANES, ACROSS, -1)
    scale_own = 1.0 + own_channels(mods[0]).reshape(-1)
    shift_own = own_channels(mods[1]).reshape(-1)

    rows_here = conv1_weight.shape[0]
    conv1_raw = lax.all_gather(
        jnp.concatenate([conv1_weight, skip_weight], axis=1), "z", axis=0, tiled=True
    )
    conv2_own = conv2_blocks(lax.all_gather(conv2_weight, "z", axis=0, tiled=True))
    qkv_units = move_units(qkv_weight.reshape(3, rows_here, C), True)
    qkv_own = qkv_blocks(turns_z(qkv_units))

    per_group, first_width = C // GROUPS, C_IN // GROUPS
    own = jnp.stack(
        [gain_two, bias_two, scale_own, shift_own, gain_three, bias_three, skip_shift, skip_shift]
        + [jnp.broadcast_to(1.0 / (count * per_group), (OWN,))]
        + [jnp.zeros((OWN,), jnp.float32)] * 7
    )
    full = jnp.stack(
        [gain_one, bias_one, jnp.broadcast_to(1.0 / (count * first_width), (C_IN,))]
        + [jnp.zeros((C_IN,), jnp.float32)] * 5
    )

    image_all, first_act, second_normed, second_act, conv1_own, first_stats, second_stats = first_layer(
        member_word, image_blocks, valid, conv1_raw, full, own, (qkv_units,)
    )
    second_pieces = plane_gather(second_act, (conv2_own,))
    third_normed, attn_input, residual_low, third_stats = second_layer(
        member_word, second_pieces, image_all, valid, conv2_own, conv1_raw, own
    )

    from_y = lax.ppermute(text_weight, "y", SWITCH)
    text_pieces = (text_weight, lax.ppermute(text_weight, "core", SWITCH), from_y)
    text_pieces += (lax.ppermute(from_y, "core", SWITCH),)
    text_len = text.shape[1]
    text_blocks = text[0].reshape(text_len, PLANES, -1)
    text_slice = rounded(
        sum(
            jnp.dot(
                lax.dynamic_index_in_dim(text_blocks, a_here ^ distance, 1, keepdims=False),
                piece,
                preferred_element_type=jnp.float32,
            )
            for distance, piece in enumerate(text_pieces)
        )
    )
    text_keys, text_values = text_to_heads(text_slice)
    text_bias = jnp.where(jnp.arange(TEXT_PAD) < text_count, 0.0, neg_big)
    minus = -jnp.ones((TEXT_PAD,), jnp.float32)
    text_keys = text_lanes(text_keys, text_bias, minus, minus, minus)
    text_values = text_lanes(text_values, -minus, minus, minus, minus)

    attn_pieces = plane_gather(attn_input, (qkv_own, text_keys, text_values))

    def exchange(blocks):
        return lax.all_to_all(blocks, PLANE, split_axis=0, concat_axis=0, tiled=True)

    out_all = lax.all_gather(out_weight, EVERY, axis=0, tiled=True)
    cot_rows = swapped(cotangent[0].reshape(CHUNK, C))
    queries, keys, values, cot_passed = project_qkv(
        member_word, attn_pieces, valid, qkv_own, cot_blocks(cot_rows, out_all)
    )
    cot_moved = exchange(cot_passed)
    cot_own, grad_mixed = cot_moved[:, :, :OWN], cot_moved[:, :, OWN:].reshape(PIXELS, OWN)

    attended, mixed, back_queries = attend(
        queries, residual_low, keys, values, text_keys, text_values
    )

    moved = exchange(mixed.reshape(MEMBERS, CHUNK, 2 * OWN))

    triple_grads = attend_back(
        back_queries, grad_mixed, attended, keys, values, text_keys, text_values
    )
    triple_grads, (text_dk, text_dv) = triple_grads[:3], triple_grads[3:]

    grad_third, third_token = plane_sum(qkv_back(member_word, triple_grads, qkv_own, (moved,)))
    qkv_sums = lax.psum_scatter(
        qkv_grad(member_word, triple_grads, attn_pieces, ()), "z", scatter_dimension=0, tiled=True
    )[0]

    output, out_grad = output_rows(moved, out_all, cot_rows, out_shift, (third_token,))
    output = swapped(output).reshape(1, -1, WIDTH, C)
    out_grad = lax.psum_scatter(out_grad, PLANE, scatter_dimension=0, tiled=True)[0]
    out_grad = lax.psum_scatter(out_grad, "z", scatter_dimension=0, tiled=True)

    qkv_sums = to_natural_order(jnp.swapaxes(qkv_sums, 1, 2))
    qkv_weight_grad = move_units(qkv_sums, False).reshape(-1, C).astype(jnp.float32)

    text_grads = text_from_heads(text_dk[:text_len], text_dv[:text_len])
    text_weight_grad = lax.psum_scatter(
        rounded(weight_grad(text[0], text_grads)), ("y", "core"), scatter_dimension=0, tiled=True
    )

    third = third_back(
        member_word, grad_third, third_normed, cot_own, valid, third_stats, own, conv2_own
    )
    second_terms, (dres, residual_taps, third_sums) = third[:MEMBERS], third[MEMBERS:]
    grad_second, second_token = plane_sum(second_terms)
    conv2_parts = along_z(tap_grad(member_word, residual_taps, second_pieces))

    image_terms, hidden_taps, second_sums, first_sums = second_back(
        member_word,
        grad_second,
        second_normed,
        dres,
        valid,
        second_stats,
        own,
        conv1_own,
        conv1_raw,
        image_all,
        first_stats,
        (qkv_weight_grad,),
    )
    image_part, image_token = plane_sum([image_terms[distance] for distance in range(MEMBERS)])
    image_part = sum(item.astype(jnp.float32) for item in image_part)
    conv1_parts = tap_grad(member_word, hidden_taps, [first_act], (dres, image_all))[:, 0]
    conv1_grad, skip_grad = plain_sum(along_z(conv1_parts))
    conv2_grad = natural_sum(conv2_parts, (image_token,))

    out_weight_grad = widened(out_grad, (image_token,))
    text_weight_grad = widened(text_weight_grad, (image_token,))

    own_all = small_gather(jnp.concatenate([second_sums[:4], third_sums[:4]], axis=0))
    own_all = own_all.reshape(PLANES, PLANES, ACROSS, 8, PLANES, OWN // PLANES)
    mods_grad = jnp.transpose(own_all[:, :, :, :2], (1, 3, 0, 4, 2, 5)).reshape(PLANES, 2 * C)
    mods_grad = lax.dynamic_slice_in_dim(mods_grad, device * emb_rows, emb_rows, 1)
    emb_weight_grad = jnp.dot(
        mods_grad.T, embedding.astype(jnp.float32), precision=lax.Precision.HIGHEST
    )
    emb_bias_grad = jnp.sum(mods_grad, axis=0)
    channel_sums = jnp.sum(own_all, axis=1)
    channel_sums = lax.dynamic_index_in_dim(channel_sums, a_here, 0, keepdims=False)
    channel_sums = lax.dynamic_index_in_dim(channel_sums, x_here, 0, keepdims=False)
    channel_sums = lax.dynamic_index_in_dim(channel_sums, z_here, 1, keepdims=False)

    first_here = first_sums[:2]
    for axis in PLANE:
        first_here = first_here + lax.ppermute(first_here, axis, SWITCH)
    grouped = jnp.sum((first_here * gain_one).reshape(2, GROUPS, first_width), axis=2)
    grouped = jnp.repeat(grouped / (count * first_width), first_width, axis=1)
    row_valid = lax.dynamic_slice_in_dim(valid[:, :1], member * CHUNK, CHUNK, 0)
    rows_normed = (image_block.astype(jnp.float32) - first_stats[0]) * first_stats[1]
    image_grad = image_part - row_valid.astype(jnp.float32) * first_stats[1] * (
        grouped[1] + rows_normed * grouped[0]
    )
    image_grad = swapped(rounded(image_grad)).astype(jnp.float32).reshape(1, -1, WIDTH, C_IN)
    first_grads = lax.dynamic_slice_in_dim(
        sum(turns_z(first_here)), device * first_width, first_width, 1
    )
    return (
        output,
        image_grad,
        conv1_grad,
        conv2_grad,
        skip_grad,
        emb_weight_grad,
        qkv_weight_grad,
        out_weight_grad,
        text_weight_grad,
        first_grads[0],
        first_grads[1],
        emb_bias_grad,
        channel_sums[2],
        channel_sums[3],
        channel_sums[6],
        channel_sums[4],
        channel_sums[5],
        channel_sums[7],
    )


def solution(mesh):
    in_specs = (
        P("img", "ha", None, None),
        P("img", None, None),
        P("img"),
        P("img", None),
        P("img", None, None),
        P("img", None),
        P("img", "ha", None, None),
        P(("img", "ha"), None),
        P(("img", "ha"), None),
        P(("img", "ha"), None),
        P(("img", "ha"), None),
        P(("img", "ha"), None),
        P(("img", "ha"), None),
        P("img", "ha"),
        P(("img", "ha")),
        P(("img", "ha")),
        P(("img", "ha")),
        P(("img", "ha")),
        P(("img", "ha")),
        P(("img", "ha")),
        P(("img", "ha")),
        P(("img", "ha")),
        P(("img", "ha")),
    )
    out_specs = (
        P("img", "ha", None, None),
        P("img", "ha", None, None),
        P(("img", "ha"), None),
        P(("img", "ha"), None),
        P(("img", "ha"), None),
        P(("img", "ha"), None),
        P(("img", "ha"), None),
        P(("img", "ha"), None),
        P("img", "ha"),
        P(("img", "ha")),
        P(("img", "ha")),
        P(("img", "ha")),
        P(("img", "ha")),
        P(("img", "ha")),
        P(("img", "ha")),
        P(("img", "ha")),
        P(("img", "ha")),
        P(("img", "ha")),
    )
    split_mesh = plane_mesh(mesh)
    if split_mesh is None:
        return jax.shard_map(
            shards, mesh=mesh, in_specs=in_specs, out_specs=out_specs, check_vma=False
        )
    in_specs, out_specs = (tuple(split_spec(item) for item in specs) for specs in (in_specs, out_specs))
    return jax.shard_map(
        plane_shards, mesh=split_mesh, in_specs=in_specs, out_specs=out_specs, check_vma=False
    )
```

```python
import functools
import math

import jax
import jax.numpy as jnp
from jax import lax
from jax.experimental import pallas as pl
from jax.experimental.pallas import tpu as pltpu
from jax.sharding import Mesh
from jax.sharding import PartitionSpec as P

C_IN = 512
C = 1024
HEADS = 16
HEAD_DIM = 64
GROUPS = 32
EMB = 1024
HEIGHT = 64
WIDTH = 64


neg_big = -1e30
eps_norm = 1e-05


def extended(cells, sides, width):
    for axis, dim in sides:
        count = lax.axis_size(axis)
        ends = count - 1
        head = lax.slice_in_dim(cells, 0, width, axis=dim)
        tail = lax.slice_in_dim(cells, cells.shape[dim] - width, cells.shape[dim], axis=dim)
        cells = jnp.concatenate(
            [
                lax.ppermute(tail, axis, [(i, (i + 1) % count) for i in range(ends)]),
                cells,
                lax.ppermute(head, axis, [((i + 1) % count, i) for i in range(ends)]),
            ],
            axis=dim,
        )
    return cells


def rounded(values):
    return values.astype(jnp.bfloat16)


def silu_slope(inputs):
    sigmoid = jax.nn.sigmoid(inputs)
    return sigmoid * (1.0 + inputs * (1.0 - sigmoid))


def group_view(features):
    return features.reshape(
        features.shape[0], features.shape[1], GROUPS, features.shape[2] // GROUPS
    )


def group_totals(first_sum, second_sum):
    return lax.psum((first_sum, second_sum), "ha")


def norm_stats(features, validity, counts):
    shaped = group_view(features)
    masked = shaped * validity[:, :, None, None]
    first_sum, second_sum = group_totals(
        jnp.sum(masked, axis=(1, 3)), jnp.sum(masked * shaped, axis=(1, 3))
    )
    entries = counts[:, None] * shaped.shape[3]
    group_mean = first_sum / entries
    inv_std = lax.rsqrt(second_sum / entries - group_mean * group_mean + eps_norm)
    return (group_mean, inv_std)


def normalize(features, group_mean, inv_std):
    shaped = group_view(features)
    normed = (shaped - group_mean[:, None, :, None]) * inv_std[:, None, :, None]
    return normed.reshape(features.shape)


def norm_back(grad_normed, normed, validity, counts, inv_std):
    grad_shaped = group_view(grad_normed)
    norm_shaped = group_view(normed)
    first_sum, second_sum = group_totals(
        jnp.sum(grad_shaped, axis=(1, 3)), jnp.sum(grad_shaped * norm_shaped, axis=(1, 3))
    )
    entries = counts[:, None] * grad_shaped.shape[3]
    correction = (
        first_sum[:, None, :, None] + norm_shaped * second_sum[:, None, :, None]
    ) / entries[:, None, :, None]
    result = (grad_shaped - validity[:, :, None, None] * correction) * inv_std[:, None, :, None]
    return result.reshape(grad_normed.shape)


def conv_columns(features):
    padded = extended(features, (("ha", 1),), 1)
    padded = jnp.pad(padded, ((0, 0), (0, 0), (1, 1), (0, 0)))
    batch_size, row_count, col_count, channels = features.shape
    taps = [
        padded[:, row_off : row_off + row_count, col_off : col_off + col_count]
        for row_off in range(3)
        for col_off in range(3)
    ]
    return jnp.concatenate(taps, axis=-1).reshape(batch_size * row_count * col_count, 9 * channels)


def project(inputs, weight):
    return lax.dot_general(
        inputs, weight, (((1,), (1,)), ((), ())), preferred_element_type=jnp.float32
    )


def weight_grad(grads, inputs):
    return lax.dot_general(
        grads, inputs, (((0,), (0,)), ((), ())), preferred_element_type=jnp.float32
    )


def back_project(grads, weight):
    return jnp.dot(grads, weight, preferred_element_type=jnp.float32)


def flipped(weight, in_channels):
    out_channels = weight.shape[0]
    taps = weight.reshape(out_channels, 3, 3, in_channels)[:, ::-1, ::-1, :]
    return jnp.transpose(taps, (1, 2, 0, 3)).reshape(9 * out_channels, in_channels)


def split_heads(values):
    return values.reshape(values.shape[0], values.shape[1], HEADS, HEAD_DIM)


def score_block(head_queries, head_keys, valid_block):
    raw = jnp.einsum(
        "bqhd,bkhd->bhqk", head_queries, head_keys, preferred_element_type=jnp.float32
    ) * (1.0 / math.sqrt(HEAD_DIM))
    return jnp.where(valid_block[:, None, None, :] > 0, raw, neg_big)


def absorb(running, head_queries, pairs, valid_block):
    highest, totals, accumulated = running
    head_keys = split_heads(pairs[:, :, :C])
    head_values = split_heads(pairs[:, :, C:])
    scores = score_block(head_queries, head_keys, valid_block)
    new_high = jnp.maximum(highest, jnp.max(scores, axis=-1))
    weights = jnp.exp(scores - new_high[..., None])
    decay = jnp.exp(highest - new_high)
    totals = totals * decay + jnp.sum(weights, axis=-1)
    update = jnp.einsum(
        "bhqk,bkhd->bqhd", rounded(weights), head_values, preferred_element_type=jnp.float32
    )
    accumulated = accumulated * jnp.transpose(decay, (0, 2, 1))[..., None] + update
    return (new_high, totals, accumulated)


def back_block(grad_query, head_queries, grad_mixed, log_total, delta, pairs, valid_block):
    head_keys = split_heads(pairs[:, :, :C])
    head_values = split_heads(pairs[:, :, C:])
    scores = score_block(head_queries, head_keys, valid_block)
    probs = jnp.exp(scores - log_total[..., None])
    grad_values = jnp.einsum(
        "bhqk,bqhd->bkhd", rounded(probs), grad_mixed, preferred_element_type=jnp.float32
    )
    grad_probs = jnp.einsum(
        "bqhd,bkhd->bhqk", grad_mixed, head_values, preferred_element_type=jnp.float32
    )
    grad_scores = rounded(probs * (grad_probs - delta[..., None]))
    scale_factor = 1.0 / math.sqrt(HEAD_DIM)
    grad_query = (
        grad_query
        + jnp.einsum("bhqk,bkhd->bqhd", grad_scores, head_keys, preferred_element_type=jnp.float32)
        * scale_factor
    )
    grad_keys = (
        jnp.einsum("bhqk,bqhd->bkhd", grad_scores, head_queries, preferred_element_type=jnp.float32)
        * scale_factor
    )
    batch_size, key_count = (pairs.shape[0], pairs.shape[1])
    grad_pairs = jnp.concatenate(
        [
            grad_keys.reshape(batch_size, key_count, C),
            grad_values.reshape(batch_size, key_count, C),
        ],
        axis=2,
    )
    return (grad_query, grad_pairs)


def over_blocks(block_fn, running, pairs, validity):
    key_count = pairs.shape[1]
    block_len = 512

    def over_advance(block_index, carried):
        offset = block_index * block_len
        return block_fn(
            carried,
            lax.dynamic_slice_in_dim(pairs, offset, block_len, 1),
            lax.dynamic_slice_in_dim(validity, offset, block_len, 1),
        )

    return lax.fori_loop(0, key_count // block_len, over_advance, running)


def shards(
    image,
    mask,
    timestep,
    pooled,
    text,
    text_mask,
    cotangent,
    conv1_weight,
    conv2_weight,
    skip_weight,
    emb_weight,
    qkv_weight,
    out_weight,
    text_weight,
    gn1_gain,
    gn1_bias,
    emb_bias,
    gn2_gain,
    gn2_bias,
    skip_bias,
    gn3_gain,
    gn3_bias,
    out_bias,
):
    batch_size, row_count, col_count = (image.shape[0], image.shape[1], image.shape[2])
    pixel_count = row_count * col_count
    gathered = (
        lax.all_gather(conv1_weight, ("img", "ha"), axis=0, tiled=True),
        lax.all_gather(conv2_weight, ("img", "ha"), axis=0, tiled=True),
        lax.all_gather(skip_weight, ("img", "ha"), axis=0, tiled=True),
        lax.all_gather(emb_weight, ("img", "ha"), axis=0, tiled=True),
        lax.all_gather(qkv_weight, ("img", "ha"), axis=0, tiled=True),
        lax.all_gather(out_weight, ("img", "ha"), axis=0, tiled=True),
        lax.all_gather(gn1_gain, ("img", "ha"), axis=0, tiled=True),
        lax.all_gather(gn1_bias, ("img", "ha"), axis=0, tiled=True),
        lax.all_gather(emb_bias, ("img", "ha"), axis=0, tiled=True),
        lax.all_gather(gn2_gain, ("img", "ha"), axis=0, tiled=True),
        lax.all_gather(gn2_bias, ("img", "ha"), axis=0, tiled=True),
        lax.all_gather(skip_bias, ("img", "ha"), axis=0, tiled=True),
        lax.all_gather(gn3_gain, ("img", "ha"), axis=0, tiled=True),
        lax.all_gather(gn3_bias, ("img", "ha"), axis=0, tiled=True),
        lax.all_gather(out_bias, ("img", "ha"), axis=0, tiled=True),
    )
    conv1_full, conv2_full, skip_full, emb_full, qkv_full, out_full = gathered[:6]
    (
        gain_one,
        bias_one,
        emb_shift,
        gain_two,
        bias_two,
        skip_shift,
        gain_three,
        bias_three,
        out_shift,
    ) = (item.astype(jnp.float32) for item in gathered[6:])
    full_valid = mask.reshape(batch_size, HEIGHT * WIDTH).astype(jnp.float32)
    counts = jnp.sum(full_valid, axis=1)
    local_mask = lax.dynamic_slice_in_dim(mask, lax.axis_index("ha") * row_count, row_count, 1)
    validity = local_mask.reshape(batch_size, pixel_count).astype(jnp.float32)
    half_width = EMB // 2
    frequency = jnp.exp(-math.log(10000.0) * jnp.arange(half_width, dtype=jnp.float32) / half_width)
    angles = timestep.astype(jnp.float32)[:, None] * frequency[None, :]
    embedding = rounded(
        jax.nn.silu(jnp.concatenate([jnp.cos(angles), jnp.sin(angles)], axis=1) + pooled)
    )
    modulation = project(embedding, emb_full) + emb_shift
    scale_rows = 1.0 + modulation[:, None, :C]
    shift_rows = modulation[:, None, C:]
    image_flat = image.reshape(batch_size, pixel_count, C_IN)
    image_wide = image_flat.astype(jnp.float32)

    def front(known):
        fresh = known is None
        first_mean, first_std = norm_stats(image_wide, validity, counts) if fresh else known[0]
        first_normed = normalize(image_wide, first_mean, first_std)
        first_pre = first_normed * gain_one + bias_one
        first_act = rounded(jax.nn.silu(first_pre) * validity[:, :, None])
        first_columns = conv_columns(first_act.reshape(batch_size, row_count, col_count, C_IN))
        hidden_one = project(first_columns, conv1_full).reshape(batch_size, pixel_count, C)
        second_mean, second_std = norm_stats(hidden_one, validity, counts) if fresh else known[1]
        second_normed = normalize(hidden_one, second_mean, second_std)
        second_shifted = second_normed * gain_two + bias_two
        second_pre = second_shifted * scale_rows + shift_rows
        second_act = rounded(jax.nn.silu(second_pre) * validity[:, :, None])
        second_columns = conv_columns(second_act.reshape(batch_size, row_count, col_count, C))
        stats = ((first_mean, first_std), (second_mean, second_std))
        return (
            stats,
            (
                first_normed,
                first_pre,
                first_columns,
                second_normed,
                second_shifted,
                second_pre,
                second_columns,
            ),
        )

    stats, saved = front(None)
    residual = (
        project(saved[6], conv2_full) + project(image_flat.reshape(-1, C_IN), skip_full)
    ).reshape(batch_size, pixel_count, C) + skip_shift
    third_mean, third_std = norm_stats(residual, validity, counts)
    third_normed = normalize(residual, third_mean, third_std)
    attn_input = rounded(third_normed * gain_three + bias_three)
    triple = rounded(project(attn_input.reshape(-1, C), qkv_full)).reshape(
        batch_size, pixel_count, 3 * C
    )
    head_queries = split_heads(triple[:, :, :C])
    local_pairs = triple[:, :, C:]
    text_piece = lax.all_gather(text_weight, "img", axis=0, tiled=True)
    text_slice = rounded(
        jnp.einsum("blt,tc->blc", text, text_piece, preferred_element_type=jnp.float32)
    )
    text_pairs = lax.all_gather(text_slice, "ha", axis=2, tiled=True)
    text_valid = text_mask.astype(jnp.float32)

    def absorb_here(carried, pairs, valid_block):
        return absorb(carried, head_queries, pairs, valid_block)

    running = (
        jnp.full((batch_size, HEADS, pixel_count), neg_big, jnp.float32),
        jnp.zeros((batch_size, HEADS, pixel_count), jnp.float32),
        jnp.zeros((batch_size, pixel_count, HEADS, HEAD_DIM), jnp.float32),
    )
    running = absorb_here(running, text_pairs, text_valid)
    valid_block = full_valid
    running = over_blocks(
        absorb_here, running, lax.all_gather(local_pairs, "ha", axis=1, tiled=True), valid_block
    )
    highest, totals, accumulated = running
    attended = accumulated / jnp.transpose(totals, (0, 2, 1))[..., None]
    log_total = highest + jnp.log(totals)
    mixed_rows = rounded(attended.reshape(-1, C))
    output = residual.reshape(-1, C) + project(mixed_rows, out_full) + out_shift
    output = rounded(output).reshape(batch_size, row_count, col_count, C)
    cot_rows = cotangent.reshape(-1, C)
    out_weight_grad = weight_grad(cot_rows, mixed_rows)
    out_bias_grad = jnp.sum(cot_rows.astype(jnp.float32), axis=0)
    grad_mixed = split_heads(
        rounded(back_project(cot_rows, out_full)).reshape(batch_size, pixel_count, C)
    )
    delta = jnp.transpose(jnp.sum(grad_mixed.astype(jnp.float32) * attended, axis=-1), (0, 2, 1))

    def back_here(grad_query, pairs, valid_block):
        return back_block(
            grad_query, head_queries, grad_mixed, log_total, delta, pairs, valid_block
        )

    grad_query = jnp.zeros((batch_size, pixel_count, HEADS, HEAD_DIM), jnp.float32)
    grad_query, text_term = back_here(grad_query, text_pairs, text_valid)
    pixel_pairs = lax.all_gather(local_pairs, "ha", axis=1, tiled=True)
    key_count = pixel_pairs.shape[1]
    block_len = 512

    def body_advance(block_index, carried):
        query_grad, term_now = carried
        offset = block_index * block_len
        query_grad, grad_pairs = back_here(
            query_grad,
            lax.dynamic_slice_in_dim(pixel_pairs, offset, block_len, 1),
            lax.dynamic_slice_in_dim(full_valid, offset, block_len, 1),
        )
        return (query_grad, lax.dynamic_update_slice_in_dim(term_now, grad_pairs, offset, 1))

    key_term = jnp.zeros((batch_size, key_count, 2 * C), jnp.float32)
    grad_query, key_term = lax.fori_loop(
        0, key_count // block_len, body_advance, (grad_query, key_term)
    )
    pair_grads = rounded(
        lax.psum_scatter(
            key_term.astype(jnp.bfloat16), "ha", scatter_dimension=1, tiled=True
        ).astype(jnp.float32)
    )
    text_grads = rounded(
        lax.psum_scatter(
            text_term.astype(jnp.bfloat16), "ha", scatter_dimension=2, tiled=True
        ).astype(jnp.float32)
    )
    text_weight_grad = lax.psum_scatter(
        jnp.einsum("blt,blc->tc", text, text_grads, preferred_element_type=jnp.float32).astype(
            jnp.bfloat16
        ),
        "img",
        scatter_dimension=0,
        tiled=True,
    ).astype(jnp.float32)
    triple_grads = jnp.concatenate(
        [rounded(grad_query.reshape(batch_size, pixel_count, C)), pair_grads], axis=2
    ).reshape(-1, 3 * C)
    qkv_weight_grad = weight_grad(triple_grads, attn_input.reshape(-1, C))
    grad_third = back_project(triple_grads, qkv_full).reshape(batch_size, pixel_count, C)
    gain_three_grad = jnp.sum(grad_third * third_normed, axis=(0, 1))
    bias_three_grad = jnp.sum(grad_third, axis=(0, 1))
    attn_sums = (
        lax.psum_scatter(qkv_weight_grad, ("img", "ha"), scatter_dimension=0, tiled=True),
        lax.psum_scatter(out_weight_grad, ("img", "ha"), scatter_dimension=0, tiled=True),
        lax.psum_scatter(gain_three_grad, ("img", "ha"), scatter_dimension=0, tiled=True),
        lax.psum_scatter(bias_three_grad, ("img", "ha"), scatter_dimension=0, tiled=True),
        lax.psum_scatter(out_bias_grad, ("img", "ha"), scatter_dimension=0, tiled=True),
    )
    grad_residual = cot_rows.astype(jnp.float32).reshape(batch_size, pixel_count, C) + norm_back(
        grad_third * gain_three, third_normed, validity, counts, third_std
    )
    skip_bias_grad = jnp.sum(grad_residual, axis=(0, 1))
    residual_low = rounded(grad_residual)
    residual_rows = residual_low.reshape(-1, C)
    skip_weight_grad = weight_grad(residual_rows, image_flat.reshape(-1, C_IN))
    image_from_skip = back_project(residual_rows, skip_full)
    unused, kept = front(stats)
    (
        first_normed,
        first_pre,
        first_columns,
        second_normed,
        second_shifted,
        second_pre,
        second_columns,
    ) = kept
    conv2_weight_grad = weight_grad(residual_rows, second_columns)
    grad_second_act = jnp.dot(
        conv_columns(residual_low.reshape(batch_size, row_count, col_count, C)),
        flipped(conv2_full, C),
        preferred_element_type=jnp.float32,
    )
    grad_second_pre = (
        grad_second_act.reshape(batch_size, pixel_count, C)
        * validity[:, :, None]
        * silu_slope(second_pre)
    )
    grad_mods = jnp.concatenate(
        [jnp.sum(grad_second_pre * second_shifted, axis=1), jnp.sum(grad_second_pre, axis=1)],
        axis=1,
    )
    emb_weight_grad = jnp.dot(
        grad_mods.T, embedding.astype(jnp.float32), precision=lax.Precision.HIGHEST
    )
    emb_bias_grad = jnp.sum(grad_mods, axis=0)
    grad_second_shift = grad_second_pre * scale_rows
    gain_two_grad = jnp.sum(grad_second_shift * second_normed, axis=(0, 1))
    bias_two_grad = jnp.sum(grad_second_shift, axis=(0, 1))
    hidden_low = rounded(
        norm_back(grad_second_shift * gain_two, second_normed, validity, counts, stats[1][1])
    )
    conv1_weight_grad = weight_grad(hidden_low.reshape(-1, C), first_columns)
    grad_first_act = jnp.dot(
        conv_columns(hidden_low.reshape(batch_size, row_count, col_count, C)),
        flipped(conv1_full, C_IN),
        preferred_element_type=jnp.float32,
    )
    grad_first_pre = (
        grad_first_act.reshape(batch_size, pixel_count, C_IN)
        * validity[:, :, None]
        * silu_slope(first_pre)
    )
    gain_one_grad = jnp.sum(grad_first_pre * first_normed, axis=(0, 1))
    bias_one_grad = jnp.sum(grad_first_pre, axis=(0, 1))
    image_grad = norm_back(
        grad_first_pre * gain_one, first_normed, validity, counts, stats[0][1]
    ) + image_from_skip.reshape(batch_size, pixel_count, C_IN)
    block_sums = (
        lax.psum_scatter(conv1_weight_grad, ("img", "ha"), scatter_dimension=0, tiled=True),
        lax.psum_scatter(conv2_weight_grad, ("img", "ha"), scatter_dimension=0, tiled=True),
        lax.psum_scatter(skip_weight_grad, ("img", "ha"), scatter_dimension=0, tiled=True),
        lax.psum_scatter(emb_weight_grad, ("img", "ha"), scatter_dimension=0, tiled=True),
        lax.psum_scatter(gain_one_grad, ("img", "ha"), scatter_dimension=0, tiled=True),
        lax.psum_scatter(bias_one_grad, ("img", "ha"), scatter_dimension=0, tiled=True),
        lax.psum_scatter(emb_bias_grad, ("img", "ha"), scatter_dimension=0, tiled=True),
        lax.psum_scatter(gain_two_grad, ("img", "ha"), scatter_dimension=0, tiled=True),
        lax.psum_scatter(bias_two_grad, ("img", "ha"), scatter_dimension=0, tiled=True),
        lax.psum_scatter(skip_bias_grad, ("img", "ha"), scatter_dimension=0, tiled=True),
    )
    return (
        output,
        image_grad.reshape(batch_size, row_count, col_count, C_IN),
        block_sums[0],
        block_sums[1],
        block_sums[2],
        block_sums[3],
        attn_sums[0],
        attn_sums[1],
        text_weight_grad,
        block_sums[4],
        block_sums[5],
        block_sums[6],
        block_sums[7],
        block_sums[8],
        block_sums[9],
        attn_sums[2],
        attn_sums[3],
        attn_sums[4],
    )


EVERY = ("y", "core", "z", "x")
PLANE = ("core", "y", "x")
PLANE_SORTED = ("y", "core", "x")
PLANES = 4
ACROSS = 2
MEMBERS = 8
OWN = C // MEMBERS
LANES = 128
TEXT_PAD = 128
SLOTS = 4
ATTEND_ROWS = 1024
ATTEND_KEYS = 1024
BACK_ROWS = 512
BACK_KEYS = 1024
CHUNK = 512
STEPS = HEIGHT * WIDTH // CHUNK
PIXELS = HEIGHT * WIDTH
TAPS = 9 * OWN
VMEM_BYTES = 56 * 1024 * 1024
SWITCH = ((0, 1), (1, 0))
NT = (((1,), (1,)), ((), ()))
TN = (((0,), (0,)), ((), ()))


def plane_mesh(mesh):
    images, rows = mesh.shape["img"], mesh.shape["ha"]
    if images != PLANES or rows != PLANES * ACROSS:
        return None
    return Mesh(mesh.devices.reshape(PLANES // 2, 2, PLANES, ACROSS), EVERY)


def split_spec(spec):
    names = {"img": ("y", "core"), "ha": ("z", "x")}
    entries = []
    for entry in spec:
        parts = (entry,) if isinstance(entry, str) else (entry or ())
        axes = tuple(axis for part in parts for axis in names[part])
        entries.append(axes or None)
    return P(*entries)


def flat_device(y, core, z, x):
    return ((y * 2 + core) * PLANES + z) * ACROSS + x


def every_place():
    return [(y, c, z, x) for y in range(2) for c in range(2) for z in range(PLANES) for x in range(ACROSS)]


def swapped(values):
    pairs = [
        (flat_device(y, c, z, x), flat_device(z % 2, z // 2, 2 * c + y, x)) for y, c, z, x in every_place()
    ]
    return lax.ppermute(values, EVERY, pairs)


def crossing(first):
    pairs = []
    for place in range(MEMBERS):
        along_x = (place // 2 % 2 == 0) == (first == "x")
        pairs.append((place, place ^ (1 if along_x else 4)))
    return pairs


def by_core(first, second):
    return jnp.where(lax.axis_index("core") == 0, first, second)


def pick_kernel(core_ref, first_ref, second_ref, out_ref):
    out_ref[...] = jnp.where(core_ref[0] == 0, first_ref[...], second_ref[...])


def pick(first, second, after):
    rows, columns = first.shape
    steps = 4 if rows % 64 == 0 else 1
    block = (rows // steps, columns)
    return call(
        pick_kernel,
        "pick",
        (steps,),
        [(lax.axis_index("core").reshape(1), None, None)]
        + [(item, block, row_chunk) for item in (first, second)],
        [(first.shape, first.dtype, block, row_chunk)],
        read=3 * rows * columns * 2,
        after=after,
    )[0]


def plane_gather(piece, after=()):
    from_x = lax.ppermute(piece, "x", SWITCH)
    from_y = lax.ppermute(piece, "y", SWITCH)
    from_core = lax.ppermute(piece, "core", SWITCH)
    from_xy = lax.ppermute(pick(from_x, from_y, after), PLANE_SORTED, crossing("y"))
    near = [piece, from_x, from_y, from_xy]
    far = [from_core] + [lax.ppermute(item, "core", SWITCH) for item in near[1:]]
    return near + far


def added(first, second):
    return rounded(first.astype(jnp.float32) + second.astype(jnp.float32))


def plane_sum(terms, between=None):
    arrived = [lax.ppermute(terms[distance ^ 4], "core", SWITCH) for distance in (3, 1, 2, 0)]
    for_xy = added(terms[3], arrived[0])
    passing = lax.ppermute(for_xy, PLANE_SORTED, crossing("x"))
    for_x, for_y = added(terms[1], arrived[1]), added(terms[2], arrived[2])
    early = by_core(for_x, for_y)
    first = lax.ppermute(early, PLANE_SORTED, crossing("x"))
    second = added(by_core(for_y, for_x), passing)
    if between is not None:
        second = passed(second, between((early, for_xy)))
    mine = added(terms[0], arrived[3])
    return (mine, first, lax.ppermute(second, PLANE_SORTED, crossing("y"))), (early, second)


def small_gather(values):
    def both(item, axis):
        other = lax.ppermute(item, axis, SWITCH)
        low = lax.axis_index(axis) == 0
        return jnp.stack([jnp.where(low, item, other), jnp.where(low, other, item)])

    values = both(values, "x")
    z = lax.axis_index("z")
    turned = [values] + [
        lax.ppermute(values, "z", [(at, (at + turn) % PLANES) for at in range(PLANES)])
        for turn in range(1, PLANES)
    ]
    values = jnp.stack(
        [
            sum(jnp.where((z - at) % PLANES == turn, turned[turn], 0.0) for turn in range(PLANES))
            for at in range(PLANES)
        ]
    )
    values = both(both(values, "core"), "y")
    return values.reshape((PLANES,) + values.shape[2:])


def own_channels(by_device):
    a, x = lax.axis_index(("y", "core")), lax.axis_index("x")
    part = lax.dynamic_index_in_dim(by_device, a, 0, keepdims=False)
    return lax.dynamic_index_in_dim(part, x, 1, keepdims=False)


def to_own_order(values):
    lead = values.shape[:-1]
    shaped = values.reshape(lead + (2, 2, PLANES, ACROSS, -1))
    at = len(lead)
    order = tuple(range(at)) + (at + 1, at, at + 3, at + 2, at + 4)
    return jnp.transpose(shaped, order).reshape(lead + (MEMBERS, OWN))


def to_natural_order(values):
    lead = values.shape[:-2]
    shaped = values.reshape(lead + (2, 2, ACROSS, PLANES, -1))
    at = len(lead)
    order = tuple(range(at)) + (at + 1, at, at + 3, at + 2, at + 4)
    return jnp.transpose(shaped, order).reshape(lead + (C,))


def unit_tables():
    where, rows, back = {}, {}, {}
    for z in range(PLANES):
        for member in range(MEMBERS):
            home = flat_device(member // 2 % 2, member // 4, z, member % 2)
            for place in range(3):
                unit = 3 * home + place
                worker = unit % 32 // 4
                entry = where.setdefault((z, worker), [])
                back[home, place] = worker * SLOTS + len(entry)
                entry.append(3 * member + place)
                rows.setdefault((z, worker), []).append(unit // 32 * OWN + unit % 4 * 32)
    pad = {key: entry + entry[:1] * (SLOTS - len(entry)) for key, entry in where.items()}
    places = [[pad[z, t] for t in range(MEMBERS)] for z in range(PLANES)]
    pad = {key: entry + entry[:1] * (SLOTS - len(entry)) for key, entry in rows.items()}
    targets = [[pad[z, t] for t in range(MEMBERS)] for z in range(PLANES)]
    count = PLANES * MEMBERS
    return places, targets, [[back[home, place] for place in range(3)] for home in range(count)]


def call(kernel, name, grid, operands, outputs, scratch=(), flops=0, read=0, after=()):
    def body(*refs):
        kernel(*refs[len(after) :])

    def spec(shape, index):
        if shape is None:
            return pl.BlockSpec(memory_space=pltpu.SMEM)
        if index is None:
            return pl.BlockSpec(shape, lambda *_: (0,) * len(shape))
        return pl.BlockSpec(shape, index)

    return pl.pallas_call(
        body,
        grid=grid,
        in_specs=[pl.BlockSpec(memory_space=pl.ANY)] * len(after)
        + [spec(shape, index) for _, shape, index in operands],
        out_specs=[spec(shape, index) for _, _, shape, index in outputs],
        out_shape=[jax.ShapeDtypeStruct(full, dtype) for full, dtype, _, _ in outputs],
        scratch_shapes=list(scratch),
        compiler_params=pltpu.CompilerParams(vmem_limit_bytes=VMEM_BYTES),
        cost_estimate=pl.CostEstimate(flops=flops, bytes_accessed=read, transcendentals=0),
        name=name,
    )(*after, *[array for array, _, _ in operands])


def whole(array):
    return (array, array.shape, None)


def row_chunk(step):
    return (step, 0)


def group_matrix(channels, width):
    row = lax.broadcasted_iota(jnp.int32, (channels, channels), 0) // width
    column = lax.broadcasted_iota(jnp.int32, (channels, channels), 1) // width
    return (row == column).astype(jnp.float32)


def group_sums(first, second, width):
    channels = first.shape[1]
    rows = jnp.concatenate([first, second, jnp.zeros((6, channels), jnp.float32)], axis=0)
    sums = jnp.dot(
        rows,
        group_matrix(channels, width),
        precision=lax.Precision.HIGHEST,
        preferred_element_type=jnp.float32,
    )
    return sums[0:1], sums[1:2]


def column_sums(values):
    return jnp.sum(values, axis=0, keepdims=True)


def sigmoid(values):
    return 1.0 / (1.0 + jnp.exp(-values))


def chunk_rows(step):
    if isinstance(step, int):
        return slice(step * CHUNK, (step + 1) * CHUNK)
    return pl.ds(pl.multiple_of(step * CHUNK, CHUNK), CHUNK)


def padded_rows(step, row):
    start = step * CHUNK + (1 + row) * WIDTH
    if isinstance(step, int):
        return slice(start, start + CHUNK)
    return pl.ds(pl.multiple_of(start, WIDTH), CHUNK)


def sideways(values, by):
    place = lax.broadcasted_iota(jnp.int32, values.shape, 0) % WIDTH
    rolled = pltpu.roll(values, by % values.shape[0], 0)
    return jnp.where(place == (0 if by == 1 else WIDTH - 1), 0.0, rolled)


SUMS = (3, PIXELS + 2 * WIDTH + CHUNK, OWN)


def add_taps(sums_ref, products_ref, step):
    for tap in range(9):
        dy, dx = tap // 3, tap % 3
        rows = padded_rows(step + 1, 1 - dy)
        sums_ref[dx, rows, :] += products_ref[:, tap * OWN : (tap + 1) * OWN]


def tap_total(sums_ref, step):
    rows = padded_rows(step + 1, 0)
    return (
        sums_ref[1, rows, :]
        + sideways(sums_ref[0, rows, :], 1)
        + sideways(sums_ref[2, rows, :], -1)
    )


def write_sideways(taps_ref, values_fn):
    for dx in range(3):
        taps_ref[dx, 0:WIDTH, :] = jnp.zeros((WIDTH, OWN), jnp.bfloat16)
        taps_ref[dx, PIXELS + WIDTH :, :] = jnp.zeros((WIDTH, OWN), jnp.bfloat16)

    def advance(step, carried):
        values = values_fn(step)
        rows = padded_rows(step, 0)
        taps_ref[0, rows, :] = sideways(values, -1).astype(jnp.bfloat16)
        taps_ref[1, rows, :] = values.astype(jnp.bfloat16)
        taps_ref[2, rows, :] = sideways(values, 1).astype(jnp.bfloat16)
        return carried

    lax.fori_loop(0, STEPS, advance, 0)


def tap_chunk(taps_ref, step):
    return jnp.concatenate(
        [taps_ref[tap % 3, padded_rows(step, 1 - tap // 3), :] for tap in range(9)], axis=1
    )


def first_kernel(
    member_ref,
    *refs,
):
    blocks, refs = refs[:MEMBERS], refs[MEMBERS:]
    image_ref = refs[4]
    for distance in range(MEMBERS):
        image_ref[chunk_rows(member_ref[0] ^ distance), :] = blocks[distance][:CHUNK]
    first_rows(image_ref, *refs[:4], *refs[5:])


def first_rows(
    image_ref,
    valid_ref,
    raw_ref,
    full_ref,
    own_ref,
    act_ref,
    normed_ref,
    next_ref,
    weight_ref,
    first_ref,
    second_ref,
    sums_ref,
    *products_ref,
):
    for tap in range(9):
        weight_ref[tap * OWN : (tap + 1) * OWN, :] = raw_ref[:, tap * C_IN : (tap + 1) * C_IN]
    zero = jnp.zeros((1, C_IN), jnp.float32)

    def gather_sums(step, carried):
        values = image_ref[chunk_rows(step), :].astype(jnp.float32)
        valid = valid_ref[chunk_rows(step), :].astype(jnp.float32)
        masked = values * jnp.concatenate([valid] * (C_IN // LANES), axis=1)
        return (carried[0] + column_sums(masked), carried[1] + column_sums(masked * values))

    sums = lax.fori_loop(0, STEPS, gather_sums, (zero, zero))
    mean, square = (item * full_ref[2:3] for item in group_sums(*sums, C_IN // GROUPS))
    inv_std = lax.rsqrt(square - mean * mean + eps_norm)
    factor = inv_std * full_ref[0:1]
    offset = full_ref[1:2] - mean * factor
    first_ref[...] = jnp.concatenate(
        [mean, inv_std, factor, offset, jnp.zeros((4, C_IN), jnp.float32)], axis=0
    )
    sums_ref[...] = jnp.zeros_like(sums_ref)

    sums = [jnp.zeros((1, OWN), jnp.float32)] * 2
    for step in range(STEPS + 3):
        if 1 <= step <= STEPS:
            products_ref[step % 2][...] = lax.dot_general(
                act_ref[chunk_rows(step - 1), :],
                weight_ref[...],
                NT,
                preferred_element_type=jnp.float32,
            )
        if 2 <= step <= STEPS + 1:
            add_taps(sums_ref, products_ref[(step - 1) % 2], step - 2)
        if step < STEPS:
            rows = chunk_rows(step)
            values = image_ref[rows, :].astype(jnp.float32) * factor + offset
            valid = valid_ref[rows, :].astype(jnp.float32)
            valid = jnp.concatenate([valid] * (C_IN // LANES), axis=1)
            act_ref[rows, :] = (values * sigmoid(values) * valid).astype(jnp.bfloat16)
        if step >= 3:
            rows = chunk_rows(step - 3)
            values = tap_total(sums_ref, step - 3)
            masked = values * valid_ref[rows, :].astype(jnp.float32)
            normed_ref[rows, :] = values
            sums = [sums[0] + column_sums(masked), sums[1] + column_sums(masked * values)]

    mean, square = (item * own_ref[8:9] for item in group_sums(*sums, C // GROUPS))
    inv_std = lax.rsqrt(square - mean * mean + eps_norm)
    second_ref[...] = jnp.concatenate(
        [mean, inv_std, jnp.zeros((6, OWN), jnp.float32)], axis=0
    )

    def activate(step, carried):
        normed = (normed_ref[chunk_rows(step), :] - mean) * inv_std
        normed_ref[chunk_rows(step), :] = normed
        values = (normed * own_ref[0:1] + own_ref[1:2]) * own_ref[2:3] + own_ref[3:4]
        valid = valid_ref[chunk_rows(step), :].astype(jnp.float32)
        next_ref[chunk_rows(step), :] = (values * sigmoid(values) * valid).astype(jnp.bfloat16)
        return carried

    lax.fori_loop(0, STEPS, activate, 0)


def first_layer(member, blocks, valid, raw, full, own, after):
    return call(
        first_kernel,
        "first_layer",
        (),
        [(member, None, None)]
        + [whole(item) for item in blocks]
        + [whole(valid), whole(raw), whole(full), whole(own)],
        [
            ((PIXELS, C_IN), jnp.bfloat16, (PIXELS, C_IN), None),
            ((PIXELS, C_IN), jnp.bfloat16, (PIXELS, C_IN), None),
            ((PIXELS, OWN), jnp.float32, (PIXELS, OWN), None),
            ((PIXELS, OWN), jnp.bfloat16, (PIXELS, OWN), None),
            ((TAPS, C_IN), jnp.bfloat16, (TAPS, C_IN), None),
            ((8, C_IN), jnp.float32, (8, C_IN), None),
            ((8, OWN), jnp.float32, (8, OWN), None),
        ],
        [pltpu.VMEM(SUMS, jnp.float32)] + [pltpu.VMEM((CHUNK, TAPS), jnp.float32)] * 2,
        flops=2 * PIXELS * TAPS * C_IN,
        read=PIXELS * C_IN * 4,
        after=after,
    )


def near_weights(member_ref, weight_ref, near_ref):
    for distance in range(MEMBERS):
        near_ref[:, distance * OWN : (distance + 1) * OWN] = weight_ref[member_ref[0] ^ distance]


def second_kernel(
    member_ref,
    *refs,
):
    pieces_in, refs = refs[:MEMBERS], refs[MEMBERS:]
    image_ref, valid_ref, weight_ref, skip_ref, own_ref = refs[:5]
    normed_ref, next_ref, low_ref, third_ref, sums_ref, near_ref, stats_ref, *products_ref = refs[5:]
    step = pl.program_id(0)

    @pl.when(step == 0)
    def _():
        sums_ref[...] = jnp.zeros_like(sums_ref)
        stats_ref[...] = jnp.zeros_like(stats_ref)
        products_ref[1][...] = jnp.zeros_like(products_ref[1])
        near_weights(member_ref, weight_ref, near_ref)

    def settle(at, counted):
        rows = chunk_rows(at)
        values = tap_total(sums_ref, at) + own_ref[6:7]
        masked = values * valid_ref[rows, :].astype(jnp.float32)
        normed_ref[rows, :] = values
        low_ref[rows, :] = values.astype(jnp.bfloat16)
        stats_ref[0:1] += jnp.where(counted, column_sums(masked), 0.0)
        stats_ref[1:2] += jnp.where(counted, column_sums(masked * values), 0.0)

    def stage(now_ref, before_ref):
        joined = jnp.concatenate([item[...] for item in pieces_in], axis=1)
        now_ref[...] = lax.dot_general(
            joined, near_ref[...], NT, preferred_element_type=jnp.float32
        )
        add_taps(sums_ref, before_ref, step - 1)
        sums_ref[1, padded_rows(step + 1, 0), :] += lax.dot_general(
            image_ref[...], skip_ref[...], NT, preferred_element_type=jnp.float32
        )
        settle(jnp.maximum(step - 2, 0), step >= 2)

    for parity in range(2):
        @pl.when(lax.rem(step, 2) == parity)
        def _(parity=parity):
            stage(products_ref[parity], products_ref[1 - parity])

    @pl.when(step == STEPS - 1)
    def _():
        add_taps(sums_ref, products_ref[(STEPS - 1) % 2], STEPS - 1)
        settle(STEPS - 2, True)
        settle(STEPS - 1, True)
        sums = (stats_ref[0:1], stats_ref[1:2])
        mean, square = (item * own_ref[8:9] for item in group_sums(*sums, C // GROUPS))
        inv_std = lax.rsqrt(square - mean * mean + eps_norm)
        third_ref[...] = jnp.concatenate(
            [mean, inv_std, jnp.zeros((6, OWN), jnp.float32)], axis=0
        )

        def normalize_rows(step, carried):
            normed = (normed_ref[chunk_rows(step), :] - mean) * inv_std
            normed_ref[chunk_rows(step), :] = normed
            next_ref[chunk_rows(step), :] = (normed * own_ref[4:5] + own_ref[5:6]).astype(
                jnp.bfloat16
            )
            return carried

        lax.fori_loop(0, STEPS, normalize_rows, 0)


def skip_block(raw):
    return (raw, (OWN, C_IN), lambda step: (0, 9))


def second_layer(member, pieces_in, image_all, valid, weight, raw, own, after):
    return call(
        second_kernel,
        "second_layer",
        (STEPS,),
        [(member, None, None)]
        + [(item, (CHUNK, OWN), row_chunk) for item in pieces_in]
        + [(image_all, (CHUNK, C_IN), row_chunk)]
        + [whole(valid), whole(weight), skip_block(raw), whole(own)],
        [
            ((PIXELS, OWN), jnp.float32, (PIXELS, OWN), None),
            ((PIXELS, OWN), jnp.bfloat16, (PIXELS, OWN), None),
            ((PIXELS, OWN), jnp.bfloat16, (PIXELS, OWN), None),
            ((8, OWN), jnp.float32, (8, OWN), None),
        ],
        [
            pltpu.VMEM(SUMS, jnp.float32),
            pltpu.VMEM((TAPS, C), jnp.bfloat16),
            pltpu.VMEM((8, OWN), jnp.float32),
            pltpu.VMEM((CHUNK, TAPS), jnp.float32),
            pltpu.VMEM((CHUNK, TAPS), jnp.float32),
        ],
        flops=2 * PIXELS * TAPS * C,
        read=PIXELS * C * 4,
        after=after,
    )


def head_columns(values, head):
    return values if head == 0 else pltpu.roll(values, HEAD_DIM, 1)


def beside(values, *columns):
    lane = lax.broadcasted_iota(jnp.int32, values.shape, 1)
    out = jnp.where(lane < HEAD_DIM, values, 0.0)
    for at, column in enumerate(columns):
        out = jnp.where(lane == HEAD_DIM + at, column, out)
    return out


def qkv_kernel(member_ref, *refs):
    pieces_in, refs = refs[:MEMBERS], refs[MEMBERS:]
    valid_ref, weight_ref, cot_ref, q_ref, k_ref, v_ref, rows_ref, near_ref = refs
    rows_ref[...] = cot_ref[...]

    @pl.when(pl.program_id(0) == 0)
    def _():
        near_weights(member_ref, weight_ref, near_ref)

    joined = jnp.concatenate([item[...] for item in pieces_in], axis=1)
    triple = lax.dot_general(joined, near_ref[...], NT, preferred_element_type=jnp.float32)
    queries, keys, values = (triple[:, at * OWN : (at + 1) * OWN] for at in range(3))
    bias = jnp.where(valid_ref[...].astype(jnp.float32) > 0, 0.0, neg_big)
    for head in range(2):
        q_ref[head] = beside(head_columns(queries, head) * (1.0 / math.sqrt(HEAD_DIM)), 1.0).astype(
            jnp.bfloat16
        )
        k_ref[head] = beside(head_columns(keys, head), bias, -1.0, -1.0, -1.0).astype(jnp.bfloat16)
        v_ref[head] = beside(head_columns(values, head), 1.0, -1.0, -1.0, -1.0).astype(jnp.bfloat16)


def project_qkv(member, pieces_in, valid, weight, cots):
    cot_spec = ((1, CHUNK, 2 * OWN), lambda step: (step, 0, 0))
    out = ((2, PIXELS, LANES), jnp.bfloat16, (2, CHUNK, LANES), lambda step: (0, step, 0))
    return call(
        qkv_kernel,
        "project_qkv",
        (STEPS,),
        [(member, None, None)]
        + [(item, (CHUNK, OWN), row_chunk) for item in pieces_in]
        + [(valid, (CHUNK, OWN), row_chunk), whole(weight)]
        + [(cots, *cot_spec)],
        [out] * 3 + [(cots.shape, jnp.bfloat16, *cot_spec)],
        [pltpu.VMEM((3 * OWN, C), jnp.bfloat16)],
        flops=2 * PIXELS * 3 * OWN * C,
        read=PIXELS * C * 4,
    )


def split_float(column):
    parts = []
    for _ in range(3):
        part = column.astype(jnp.bfloat16).astype(jnp.float32)
        parts.append(part)
        column = column - part
    return parts


def attend_kernel(
    q_ref, low_ref, k_ref, v_ref, tk_ref, tv_ref, attn_ref, mixed_ref, back_ref
):
    width = ATTEND_KEYS
    attended = []
    for head in range(2):
        queries = q_ref[head]
        parts = [(tk_ref[head], tv_ref[head])] + [
            (k_ref[head, at : at + width], v_ref[head, at : at + width])
            for at in range(0, PIXELS, width)
        ]
        highest, accumulated = None, None
        for keys, values in parts:
            scores = lax.dot_general(queries, keys, NT, preferred_element_type=jnp.float32)
            top = jnp.max(scores, axis=1, keepdims=True)
            if highest is not None:
                top = jnp.maximum(highest, top)
            weights = jnp.exp(scores - top).astype(jnp.bfloat16)
            update = jnp.dot(weights, values, preferred_element_type=jnp.float32)
            accumulated = (
                update if highest is None else accumulated * jnp.exp(highest - top) + update
            )
            highest = top
        total = accumulated[:, HEAD_DIM : HEAD_DIM + 1]
        attended.append(accumulated / total)
        logs = split_float(highest + jnp.log(total))
        back_ref[head] = beside(queries.astype(jnp.float32), 1.0, *logs).astype(jnp.bfloat16)
    lane = lax.broadcasted_iota(jnp.int32, attended[0].shape, 1)
    both = jnp.where(lane < HEAD_DIM, attended[0], pltpu.roll(attended[1], HEAD_DIM, 1))
    attn_ref[...] = both
    mixed_ref[:, :OWN] = both.astype(jnp.bfloat16)
    mixed_ref[:, OWN:] = low_ref[...]


def attend(queries, low, keys, values, text_keys, text_values):
    block = ATTEND_ROWS
    return call(
        attend_kernel,
        "attend",
        (PIXELS // block,),
        [(queries, (2, block, LANES), lambda step: (0, step, 0)), (low, (block, OWN), row_chunk)]
        + [whole(keys), whole(values), whole(text_keys), whole(text_values)],
        [
            ((PIXELS, OWN), jnp.float32, (block, OWN), row_chunk),
            ((PIXELS, 2 * OWN), jnp.bfloat16, (block, 2 * OWN), row_chunk),
            ((2, PIXELS, LANES), jnp.bfloat16, (2, block, LANES), lambda step: (0, step, 0)),
        ],
        flops=8 * PIXELS * (PIXELS + TEXT_PAD) * LANES,
        read=PIXELS * LANES * 12,
    )


def attend_back_kernel(
    q_ref,
    do_ref,
    attn_ref,
    k_ref,
    v_ref,
    tk_ref,
    tv_ref,
    dq_ref,
    dk_ref,
    dv_ref,
    dtk_ref,
    dtv_ref,
    grads_ref,
    dqt_ref,
):
    step = pl.program_id(0)
    block = BACK_ROWS

    @pl.when(step == 0)
    def _():
        dqt_ref[...] = jnp.zeros_like(dqt_ref)

        def prepare(at, carried):
            grads = do_ref[chunk_rows(at), :].astype(jnp.float32)
            terms = grads * attn_ref[chunk_rows(at), :]
            lane = lax.broadcasted_iota(jnp.int32, terms.shape, 1)
            for head in range(2):
                inside = (lane < HEAD_DIM) == (head == 0)
                delta = jnp.sum(jnp.where(inside, terms, 0.0), axis=1, keepdims=True)
                grads_ref[head, chunk_rows(at), :] = beside(
                    head_columns(grads, head), 0.0, *split_float(delta)
                ).astype(jnp.bfloat16)
            return carried

        lax.fori_loop(0, STEPS, prepare, 0)

    def absorb_keys(head, keys, values):
        keys_across = jnp.transpose(keys.astype(jnp.float32))[:HEAD_DIM].astype(jnp.bfloat16)
        grad_keys, grad_values = None, None
        for start in range(0, PIXELS, block):
            queries = q_ref[head, start : start + block]
            grads = grads_ref[head, start : start + block]
            scores = lax.dot_general(keys, queries, NT, preferred_element_type=jnp.float32)
            grad_probs = lax.dot_general(values, grads, NT, preferred_element_type=jnp.float32)
            probs = jnp.exp(scores)
            grad_scores = (probs * grad_probs).astype(jnp.bfloat16)
            value_term = jnp.dot(
                probs.astype(jnp.bfloat16), grads, preferred_element_type=jnp.float32
            )
            key_term = jnp.dot(grad_scores, queries, preferred_element_type=jnp.float32)
            grad_values = value_term if grad_values is None else grad_values + value_term
            grad_keys = key_term if grad_keys is None else grad_keys + key_term
            rows = slice(head * HEAD_DIM, (head + 1) * HEAD_DIM)
            dqt_ref[rows, start : start + block] += jnp.dot(
                keys_across, grad_scores, preferred_element_type=jnp.float32
            )
        return grad_keys, grad_values

    def both_heads(key_source, value_source):
        (dk0, dv0), (dk1, dv1) = (
            absorb_keys(head, key_source[head], value_source[head]) for head in range(2)
        )
        lane = lax.broadcasted_iota(jnp.int32, dk0.shape, 1)
        return (
            jnp.where(lane < HEAD_DIM, low, pltpu.roll(high, HEAD_DIM, 1)).astype(jnp.bfloat16)
            for low, high in ((dk0, dk1), (dv0, dv1))
        )

    dk_ref[...], dv_ref[...] = both_heads(k_ref, v_ref)

    @pl.when(step == pl.num_programs(0) - 1)
    def _():
        dtk_ref[...], dtv_ref[...] = both_heads(tk_ref, tv_ref)
        for start in range(0, PIXELS, block):
            dq_ref[start : start + block, :] = (
                jnp.transpose(dqt_ref[:, start : start + block]) * (1.0 / math.sqrt(HEAD_DIM))
            ).astype(jnp.bfloat16)


def attend_back(queries, grads, attended, keys, values, text_keys, text_values):
    block = BACK_KEYS
    rows = (PIXELS, OWN)
    text_rows = (TEXT_PAD, OWN)
    return call(
        attend_back_kernel,
        "attend_back",
        (PIXELS // block,),
        [whole(queries), whole(grads), whole(attended)]
        + [(item, (2, block, LANES), lambda step: (0, step, 0)) for item in (keys, values)]
        + [whole(text_keys), whole(text_values)],
        [
            (rows, jnp.bfloat16, rows, None),
            (rows, jnp.bfloat16, (block, OWN), row_chunk),
            (rows, jnp.bfloat16, (block, OWN), row_chunk),
            (text_rows, jnp.bfloat16, text_rows, None),
            (text_rows, jnp.bfloat16, text_rows, None),
        ],
        [
            pltpu.VMEM((2, PIXELS, LANES), jnp.bfloat16),
            pltpu.VMEM((OWN, PIXELS), jnp.float32),
        ],
        flops=20 * PIXELS * (PIXELS + TEXT_PAD) * LANES,
        read=PIXELS * LANES * 20,
    )


def triple_blocks(grads):
    return [(item, (CHUNK, OWN), row_chunk) for item in grads]


def join_triple(refs):
    return jnp.concatenate([item[...] for item in refs], axis=1)


def qkv_back_kernel(member_ref, *refs):
    triple, weight_ref, outs, near_ref = refs[:3], refs[3], refs[4 : 4 + MEMBERS], refs[4 + MEMBERS]

    @pl.when(pl.program_id(0) == 0)
    def _():
        near_weights(member_ref, weight_ref, near_ref)

    terms = jnp.dot(join_triple(triple), near_ref[...], preferred_element_type=jnp.float32)
    for distance in range(MEMBERS):
        outs[distance][...] = terms[:, distance * OWN : (distance + 1) * OWN].astype(jnp.bfloat16)


def qkv_back(member, grads, weight, after):
    return call(
        qkv_back_kernel,
        "qkv_back",
        (STEPS,),
        [(member, None, None)] + triple_blocks(grads) + [whole(weight)],
        [((PIXELS, OWN), jnp.bfloat16, (CHUNK, OWN), row_chunk)] * MEMBERS,
        [pltpu.VMEM((3 * OWN, C), jnp.bfloat16)],
        flops=2 * PIXELS * 3 * OWN * C,
        read=PIXELS * C * 4,
        after=after,
    )


def norm_back_terms(gain_sum, bias_sum, own_ref, gain):
    first, second = group_sums(gain * bias_sum, gain * gain_sum, C // GROUPS)
    return first * own_ref[8:9], second * own_ref[8:9]


def third_back_kernel(
    member_ref,
    mine_ref,
    first_ref,
    second_ref,
    normed_ref,
    cot_ref,
    valid_ref,
    third_ref,
    own_ref,
    weight_ref,
    *refs,
):
    outs, refs = refs[:MEMBERS], refs[MEMBERS:]
    low_ref, taps_ref, totals_ref, near_ref, grads_ref = refs
    step = pl.program_id(0)

    @pl.when(step == 0)
    def _():
        near_weights(member_ref, weight_ref, near_ref)
        zero = jnp.zeros((1, OWN), jnp.float32)

        def gather(at, carried):
            rows = chunk_rows(at)
            grads = (
                mine_ref[rows, :].astype(jnp.float32)
                + first_ref[rows, :].astype(jnp.float32)
                + second_ref[rows, :].astype(jnp.float32)
            )
            cots = cot_ref[at].astype(jnp.float32)
            grads_ref[rows, :] = grads * own_ref[4:5]
            return (
                carried[0] + column_sums(grads * normed_ref[rows, :]),
                carried[1] + column_sums(grads),
                carried[2] + column_sums(cots),
            )

        gain_sum, bias_sum, cot_sum = lax.fori_loop(0, STEPS, gather, (zero, zero, zero))

        first, second = norm_back_terms(gain_sum, bias_sum, own_ref, own_ref[4:5])
        totals_ref[...] = jnp.concatenate(
            [gain_sum, bias_sum, zero, cot_sum, jnp.zeros((4, OWN), jnp.float32)], axis=0
        )

        def finish(at):
            rows = chunk_rows(at)
            valid = valid_ref[rows, :].astype(jnp.float32)
            total = grads_ref[rows, :] - valid * (first + normed_ref[rows, :] * second)
            total = total * third_ref[1:2] + cot_ref[at].astype(jnp.float32)
            low_ref[rows, :] = total.astype(jnp.bfloat16)
            totals_ref[2:3] += column_sums(total)
            return total

        write_sideways(taps_ref, finish)

    terms = jnp.dot(tap_chunk(taps_ref, step), near_ref[...], preferred_element_type=jnp.float32)
    for distance in range(MEMBERS):
        outs[distance][...] = terms[:, distance * OWN : (distance + 1) * OWN].astype(jnp.bfloat16)


def third_back(member, sums, normed, cots, valid, third, own, weight, after):
    rows = (PIXELS, OWN)
    taps = (3, PIXELS + 2 * WIDTH, OWN)
    return call(
        third_back_kernel,
        "third_back",
        (STEPS,),
        [(member, None, None)]
        + [whole(item) for item in sums]
        + [whole(normed), whole(cots), whole(valid), whole(third), whole(own), whole(weight)],
        [(rows, jnp.bfloat16, (CHUNK, OWN), row_chunk)] * MEMBERS
        + [
            (rows, jnp.bfloat16, rows, None),
            (taps, jnp.bfloat16, taps, None),
            ((8, OWN), jnp.float32, (8, OWN), None),
        ],
        [
            pltpu.VMEM((TAPS, C), jnp.bfloat16),
            pltpu.VMEM(rows, jnp.float32),
        ],
        flops=2 * PIXELS * TAPS * C,
        read=PIXELS * C * 4,
        after=after,
    )


def second_back_kernel(
    member_ref,
    mine_ref,
    first_ref,
    second_ref,
    normed_ref,
    low_ref,
    valid_ref,
    stats_ref,
    own_ref,
    weight_ref,
    skip_ref,
    image_ref,
    full_ref,
    out_ref,
    taps_ref,
    totals_ref,
    firsts_ref,
    grads_ref,
):
    step = pl.program_id(0)

    @pl.when(step == 0)
    def _():
        zero = jnp.zeros((1, OWN), jnp.float32)

        def gather(at, carried):
            rows = chunk_rows(at)
            normed = normed_ref[rows, :]
            shifted_rows = normed * own_ref[0:1] + own_ref[1:2]
            values = shifted_rows * own_ref[2:3] + own_ref[3:4]
            gate = sigmoid(values)
            slope = gate * (1.0 + values * (1.0 - gate))
            grads = (
                mine_ref[rows, :].astype(jnp.float32)
                + first_ref[rows, :].astype(jnp.float32)
                + second_ref[rows, :].astype(jnp.float32)
            )
            grads = grads * valid_ref[rows, :].astype(jnp.float32) * slope
            inner = grads * own_ref[2:3]
            grads_ref[rows, :] = inner * own_ref[0:1]
            return (
                carried[0] + column_sums(grads * shifted_rows),
                carried[1] + column_sums(grads),
                carried[2] + column_sums(inner * normed),
                carried[3] + column_sums(inner),
            )

        totals = lax.fori_loop(0, STEPS, gather, (zero,) * 4)
        totals_ref[...] = jnp.concatenate(
            list(totals) + [jnp.zeros((4, OWN), jnp.float32)], axis=0
        )

        first, second = norm_back_terms(totals[2], totals[3], own_ref, own_ref[0:1])

        def finish(at):
            rows = chunk_rows(at)
            valid = valid_ref[rows, :].astype(jnp.float32)
            total = grads_ref[rows, :] - valid * (first + normed_ref[rows, :] * second)
            return total * stats_ref[1:2]

        write_sideways(taps_ref, finish)
        firsts_ref[...] = jnp.zeros_like(firsts_ref)

    at = member_ref[0] ^ step
    rows = chunk_rows(at)
    grads = jnp.dot(tap_chunk(taps_ref, at), weight_ref[...], preferred_element_type=jnp.float32)
    image = image_ref[rows, :].astype(jnp.float32)
    values = image * full_ref[2:3] + full_ref[3:4]
    gate = sigmoid(values)
    slope = gate * (1.0 + values * (1.0 - gate))
    valid = valid_ref[rows, :].astype(jnp.float32)
    grads = grads * jnp.concatenate([valid] * (C_IN // LANES), axis=1) * slope
    normed = (image - full_ref[0:1]) * full_ref[1:2]
    firsts_ref[0:1] += column_sums(grads * normed)
    firsts_ref[1:2] += column_sums(grads)
    skipped = jnp.dot(low_ref[rows, :], skip_ref[...], preferred_element_type=jnp.float32)
    out_ref[0] = (grads * full_ref[2:3] + skipped).astype(jnp.bfloat16)


def second_back(member, sums, normed, low, valid, stats, own, weight, raw, image_all, full, after):
    rows = (PIXELS, OWN)
    taps = (3, PIXELS + 2 * WIDTH, OWN)
    return call(
        second_back_kernel,
        "second_back",
        (STEPS,),
        [(member, None, None)]
        + [whole(item) for item in sums]
        + [whole(normed), whole(low), whole(valid), whole(stats), whole(own)]
        + [whole(weight), skip_block(raw), whole(image_all), whole(full)],
        [
            (
                (MEMBERS, CHUNK, C_IN),
                jnp.bfloat16,
                (1, CHUNK, C_IN),
                lambda step: (step, 0, 0),
            ),
            (taps, jnp.bfloat16, taps, None),
            ((8, OWN), jnp.float32, (8, OWN), None),
            ((8, C_IN), jnp.float32, (8, C_IN), None),
        ],
        [pltpu.VMEM(rows, jnp.float32)],
        flops=0,
        read=0,
        after=after,
    )


def tap_grad_kernel(count, member_ref, taps_ref, *refs):
    inputs, refs = refs[:count], refs[count:]
    if count == 1:
        low_ref, image_ref, out_ref, sums_ref, skip_ref = refs
    else:
        out_ref, sums_ref = refs
    step = pl.program_id(0)

    @pl.when(step == 0)
    def _():
        sums_ref[...] = jnp.zeros_like(sums_ref)
        if count == 1:
            skip_ref[...] = jnp.zeros_like(skip_ref)

    if count == 1:
        skip_ref[...] += lax.dot_general(
            low_ref[...], image_ref[...], TN, preferred_element_type=jnp.float32
        )

    joined = jnp.concatenate([item[...] for item in inputs], axis=1)
    sums_ref[...] += lax.dot_general(
        tap_chunk(taps_ref, step), joined, TN, preferred_element_type=jnp.float32
    )

    @pl.when(step == STEPS - 1)
    def _():
        share = OWN // PLANES
        if count == 1:
            for z in range(PLANES):
                out_ref[z, 0, 9] = skip_ref[z * share : (z + 1) * share, :].astype(jnp.bfloat16)
        for tap in range(9):
            for z in range(PLANES):
                rows = slice(tap * OWN + z * share, tap * OWN + (z + 1) * share)
                if count == 1:
                    out_ref[z, 0, tap] = sums_ref[rows, :].astype(jnp.bfloat16)
                else:
                    for distance in range(count):
                        columns = slice(distance * OWN, (distance + 1) * OWN)
                        out_ref[z, member_ref[0] ^ distance, tap] = sums_ref[rows, columns].astype(
                            jnp.bfloat16
                        )


def tap_grad(member, taps, inputs, skip=(), after=()):
    count, width = len(inputs), inputs[0].shape[1]
    shape = (PLANES, count, 10 if skip else 9, OWN // PLANES, width)
    return call(
        functools.partial(tap_grad_kernel, count),
        "tap_grad",
        (STEPS,),
        [(member, None, None), whole(taps)]
        + [(item, (CHUNK, item.shape[1]), row_chunk) for item in inputs + list(skip)],
        [(shape, jnp.bfloat16, shape, None)],
        [pltpu.VMEM((TAPS, count * width), jnp.float32)]
        + [pltpu.VMEM((OWN, C_IN), jnp.float32)] * (1 if skip else 0),
        flops=0,
        after=after,
    )[0]


def qkv_grad_kernel(member_ref, targets_ref, *refs):
    triple, inputs, (out_ref, sums_ref) = refs[:3], refs[3 : 3 + MEMBERS], refs[3 + MEMBERS :]
    step = pl.program_id(0)

    @pl.when(step == 0)
    def _():
        sums_ref[...] = jnp.zeros_like(sums_ref)

    joined = jnp.concatenate([item[...] for item in inputs], axis=1)
    sums_ref[...] += lax.dot_general(join_triple(triple), joined, TN, preferred_element_type=jnp.float32)

    @pl.when(step == STEPS - 1)
    def _():
        for z in range(PLANES):
            for slot in range(SLOTS):
                rows = pl.ds(pl.multiple_of(targets_ref[z * SLOTS + slot], 32), 32)
                for distance in range(MEMBERS):
                    columns = slice(distance * OWN, (distance + 1) * OWN)
                    out_ref[z, slot, member_ref[0] ^ distance] = sums_ref[rows, columns].astype(
                        jnp.bfloat16
                    )


def qkv_grad(member, targets, grads, inputs, after):
    shape = (PLANES, SLOTS, MEMBERS, OWN // PLANES, OWN)
    return call(
        qkv_grad_kernel,
        "qkv_grad",
        (STEPS,),
        [(member, None, None), (targets, None, None)]
        + triple_blocks(grads)
        + [(item, (CHUNK, OWN), row_chunk) for item in inputs],
        [(shape, jnp.bfloat16, shape, None)],
        [pltpu.VMEM((3 * OWN, C), jnp.float32)],
        flops=0,
        after=after,
    )[0]


def pass_kernel(value_ref, out_ref):
    out_ref[...] = value_ref[...]


def passed(values, after):
    spec = (values.shape, values.dtype, values.shape, None)
    return call(pass_kernel, "passed", (), [whole(values)], [spec], after=after)[0]


def widen_kernel(value_ref, out_ref):
    out_ref[...] = value_ref[...].astype(jnp.float32)


def widened(values, after):
    return call(
        widen_kernel,
        "widen",
        (),
        [whole(values)],
        [(values.shape, jnp.float32, values.shape, None)],
        after=after,
    )[0]


def along_z(blocks):
    z = lax.axis_index("z")
    arrived = [lax.dynamic_index_in_dim(blocks, z, 0, keepdims=False)]
    for turn in range(1, PLANES):
        sent = lax.dynamic_index_in_dim(blocks, (z + turn) % PLANES, 0, keepdims=False)
        pairs = [(at, (at + turn) % PLANES) for at in range(PLANES)]
        arrived.append(lax.ppermute(sent, "z", pairs))
    return arrived


def turns_z(piece):
    return [piece] + [
        lax.ppermute(piece, "z", [(at, (at + turn) % PLANES) for at in range(PLANES)])
        for turn in range(1, PLANES)
    ]


def gather_z(piece):
    z = lax.axis_index("z")
    turned = turns_z(piece)
    zero = jnp.zeros_like(piece)
    return jnp.stack(
        [
            sum(jnp.where((z - at) % PLANES == turn, turned[turn], zero) for turn in range(PLANES))
            for at in range(PLANES)
        ]
    )


def order_matrix(dtype):
    shape = (ACROSS * OWN, ACROSS * OWN)
    source = lax.broadcasted_iota(jnp.int32, shape, 0)
    target = lax.broadcasted_iota(jnp.int32, shape, 1)
    x, z, place = source // OWN, source % OWN // 32, source % 32
    return (target == (z * ACROSS + x) * 32 + place).astype(jnp.float32).astype(dtype)


def own_columns(values, order, y, core):
    start = (2 * y + core) * ACROSS * OWN
    block = values[:, start : start + ACROSS * OWN]
    return lax.dot_general(block, order, NT, preferred_element_type=jnp.float32).astype(jnp.bfloat16)


def square(count):
    return [(core, y) for core in range(2) for y in range(count)]


def conv2_kernel(raw_ref, out_ref):
    order = order_matrix(jnp.bfloat16)
    for tap in range(9):
        rows = slice(tap * OWN, (tap + 1) * OWN)
        values = raw_ref[:, tap * C : (tap + 1) * C]
        for core, y in square(2):
            columns = own_columns(values, order, y, core)
            for x in range(ACROSS):
                out_ref[4 * core + 2 * y + x, rows, :] = columns[:, x * OWN : (x + 1) * OWN]


def conv2_blocks(raw, after):
    shape = (MEMBERS, TAPS, OWN)
    return call(
        conv2_kernel,
        "conv2_blocks",
        (),
        [whole(raw)],
        [(shape, jnp.bfloat16, shape, None)],
        after=after,
    )[0]


def choose_kernel(places_ref, units_ref, out_ref):
    for slot in range(SLOTS):
        out_ref[slot] = units_ref[places_ref[slot]]


def choose_units(places, units):
    shape = (SLOTS,) + units.shape[1:]
    return call(
        choose_kernel,
        "choose_units",
        (),
        [(places, None, None), whole(units)],
        [(shape, units.dtype, shape, None)],
    )[0]


def qkv_blocks_kernel(targets_ref, units_ref, out_ref):
    order = order_matrix(jnp.bfloat16)
    for z in range(PLANES):
        for slot in range(SLOTS):
            rows = pl.ds(pl.multiple_of(targets_ref[z * SLOTS + slot], 32), 32)
            values = units_ref[z, slot]
            for core, y in square(2):
                columns = own_columns(values, order, y, core)
                for x in range(ACROSS):
                    out_ref[4 * core + 2 * y + x, rows, :] = columns[:, x * OWN : (x + 1) * OWN]


def qkv_blocks(targets, units, after):
    shape = (MEMBERS, 3 * OWN, OWN)
    return call(
        qkv_blocks_kernel,
        "qkv_blocks",
        (),
        [(targets, None, None), whole(units)],
        [(shape, jnp.bfloat16, shape, None)],
        after=after,
    )[0]


def qkv_finish_kernel(source_ref, units_ref, out_ref):
    order = order_matrix(jnp.bfloat16)
    for place in range(3):
        unit = units_ref[source_ref[place]]
        for core, y in square(2):
            member = 4 * core + 2 * y
            joined = jnp.concatenate([unit[member], unit[member + 1]], axis=1)
            start = (2 * y + core) * ACROSS * OWN
            out_ref[place * 32 : (place + 1) * 32, start : start + ACROSS * OWN] = jnp.dot(
                joined, order, preferred_element_type=jnp.float32
            )


def qkv_finish(source, units, after):
    shape = (3 * 32, C)
    return call(
        qkv_finish_kernel,
        "qkv_finish",
        (),
        [(source, None, None), whole(units)],
        [(shape, jnp.float32, shape, None)],
        after=after,
    )[0]


def cot_kernel(cot_ref, weight_ref, out_ref):
    cots = cot_ref[...]
    order = order_matrix(jnp.bfloat16)
    mixed = jnp.dot(cots, weight_ref[...], preferred_element_type=jnp.float32).astype(jnp.bfloat16)
    for core, y in square(2):
        columns = own_columns(cots, order, y, core)
        for x in range(ACROSS):
            out_ref[4 * core + 2 * y + x, :, :OWN] = columns[:, x * OWN : (x + 1) * OWN]
    for member in range(MEMBERS):
        out_ref[member, :, OWN:] = mixed[:, member * OWN : (member + 1) * OWN]


def cot_blocks(cots, weight):
    shape = (MEMBERS, CHUNK, 2 * OWN)
    return call(
        cot_kernel,
        "cot_blocks",
        (),
        [whole(cots), whole(weight)],
        [(shape, jnp.bfloat16, shape, None)],
        flops=2 * CHUNK * C * C,
    )[0]


def output_kernel(moved_ref, weight_ref, cot_ref, shift_ref, out_ref, grad_ref):
    mixed = jnp.concatenate([moved_ref[member, :, :OWN] for member in range(MEMBERS)], axis=1)
    product = lax.dot_general(mixed, weight_ref[...], NT, preferred_element_type=jnp.float32)
    order = order_matrix(jnp.bfloat16)
    for core, y in square(2):
        member = 4 * core + 2 * y
        residual = jnp.concatenate(
            [moved_ref[member, :, OWN:], moved_ref[member + 1, :, OWN:]], axis=1
        )
        residual = jnp.dot(residual, order, preferred_element_type=jnp.float32)
        start = (2 * y + core) * ACROSS * OWN
        columns = slice(start, start + ACROSS * OWN)
        out_ref[:, columns] = (residual + product[:, columns] + shift_ref[:, columns]).astype(
            jnp.bfloat16
        )
    grads = lax.dot_general(cot_ref[...], mixed, TN, preferred_element_type=jnp.float32)
    for core, y in square(2):
        for z in range(PLANES):
            for x in range(ACROSS):
                start = ((2 * y + core) * PLANES + z) * ACROSS * 32 + x * 32
                grad_ref[4 * core + 2 * y + x, z * 32 : (z + 1) * 32, :] = grads[
                    start : start + 32
                ].astype(jnp.bfloat16)


def output_rows(moved, weight, cots, shift, after):
    shapes = ((CHUNK, C), (MEMBERS, OWN, C))
    return call(
        output_kernel,
        "output_rows",
        (),
        [whole(moved), whole(weight), whole(cots), whole(shift)],
        [(shape, jnp.bfloat16, shape, None) for shape in shapes],
        flops=0,
        after=after,
    )


def natural_kernel(first_ref, second_ref, third_ref, fourth_ref, out_ref):
    taps, rows = first_ref.shape[1], first_ref.shape[2]
    width = ACROSS * OWN
    order = order_matrix(jnp.float32)

    def total(at):
        parts = [item[at].astype(jnp.float32) for item in (first_ref, second_ref, third_ref, fourth_ref)]
        return ((parts[0] + parts[1]) + (parts[2] + parts[3])).reshape(taps * rows, OWN)

    for core in range(2):
        for y in range(2):
            at = 4 * core + 2 * y
            joined = jnp.concatenate([total(at), total(at + 1)], axis=1)
            ordered = jnp.dot(
                joined, order, precision=lax.Precision.HIGHEST, preferred_element_type=jnp.float32
            )
            for tap in range(taps):
                columns = slice(tap * C + (2 * y + core) * width, tap * C + (2 * y + core + 1) * width)
                out_ref[:, columns] = ordered[tap * rows : (tap + 1) * rows]


def natural_sum(parts, after):
    taps, rows = parts[0].shape[1:3]
    shape = (rows, taps * C)
    return call(
        natural_kernel,
        "natural_sum",
        (),
        [whole(item) for item in parts],
        [(shape, jnp.float32, shape, None)],
        after=after,
    )[0]


def plain_kernel(value_ref, out_ref, skip_ref):
    taps, width = value_ref.shape[0] - 1, value_ref.shape[2]
    for tap in range(taps):
        out_ref[:, tap * width : (tap + 1) * width] = value_ref[tap].astype(jnp.float32)
    skip_ref[...] = value_ref[taps].astype(jnp.float32)


def plain_sum(values, after):
    taps, rows, width = values.shape
    shapes = ((rows, (taps - 1) * width), (rows, width))
    return call(
        plain_kernel,
        "plain_sum",
        (),
        [whole(values)],
        [(shape, jnp.float32, shape, None) for shape in shapes],
        after=after,
    )


def text_pairs(back):
    rounds = ([], [])
    for y, c, z, x in every_place():
        piece, plane = 2 * z + x, 2 * c + y
        for half in range(2):
            member = 2 * (piece % 4) + half
            target = flat_device(member // 2 % 2, member // 4, plane, member % 2)
            pair = (flat_device(y, c, z, x), target)
            rounds[half ^ (piece // 4)].append(pair[::-1] if back else pair)
    return rounds


def text_to_heads(text_slice):
    late = (2 * lax.axis_index("z") + lax.axis_index("x")) // 4
    halves = (text_slice[:, :OWN], text_slice[:, OWN:])
    first, second = (
        lax.ppermute(jnp.where(late == at, halves[0], halves[1]), EVERY, text_pairs(False)[at])
        for at in range(2)
    )
    even = lax.axis_index("x") == 0
    return jnp.where(even, first, second), jnp.where(even, second, first)


def text_from_heads(text_keys, text_values):
    even = lax.axis_index("x") == 0
    first = jnp.where(even, text_keys, text_values)
    second = jnp.where(even, text_values, text_keys)
    first, second = (
        lax.ppermute(item, EVERY, text_pairs(True)[at]) for at, item in enumerate((first, second))
    )
    late = (2 * lax.axis_index("z") + lax.axis_index("x")) // 4 == 1
    return jnp.concatenate(
        [jnp.where(late, second, first), jnp.where(late, first, second)], axis=1
    )


def text_lanes(values, *columns):
    padded = jnp.pad(values, ((0, TEXT_PAD - values.shape[0]), (0, 0)))
    heads = jnp.transpose(padded.reshape(TEXT_PAD, 2, HEAD_DIM), (1, 0, 2))
    extra = [
        jnp.broadcast_to(jnp.asarray(column, jnp.bfloat16).reshape(1, -1, 1), (2, TEXT_PAD, 1))
        for column in columns
    ]
    joined = jnp.concatenate([heads] + extra, axis=2)
    return jnp.pad(joined, ((0, 0), (0, 0), (0, LANES - joined.shape[2])))


def plane_shards(
    image,
    mask,
    timestep,
    pooled,
    text,
    text_mask,
    cotangent,
    conv1_weight,
    conv2_weight,
    skip_weight,
    emb_weight,
    qkv_weight,
    out_weight,
    text_weight,
    gn1_gain,
    gn1_bias,
    emb_bias,
    gn2_gain,
    gn2_bias,
    skip_bias,
    gn3_gain,
    gn3_bias,
    out_bias,
):
    z_here, x_here = lax.axis_index("z"), lax.axis_index("x")
    a_here = lax.axis_index(("y", "core"))
    member = lax.axis_index(PLANE)
    member_word = member.reshape(1).astype(jnp.int32)
    device = lax.axis_index(EVERY)

    extents = jnp.stack([timestep[0], jnp.sum(mask[0, :, 0]), jnp.sum(mask[0, 0]), jnp.sum(text_mask)])
    exact = jnp.concatenate([pooled[0], extents.astype(jnp.float32)])

    def both(values, axis):
        other = lax.ppermute(values, axis, SWITCH)
        low = lax.axis_index(axis) == 0
        return jnp.stack([jnp.where(low, values, other), jnp.where(low, other, values)])

    image_halves = [
        swapped(half) for half in jnp.split(image[0].reshape(CHUNK, C_IN), 2, axis=0)
    ]
    exact = passed(both(exact, "y"), (image_halves[0],))
    exact = both(exact, "core").reshape(PLANES, -1)
    extents = exact[:, EMB:]
    valid_rows, valid_columns, text_count = extents[z_here, 1:]
    count = valid_rows * valid_columns
    pixel = lax.broadcasted_iota(jnp.int32, (PIXELS, OWN), 0).astype(jnp.float32)
    pixel_row = jnp.floor(pixel / WIDTH)
    valid = (pixel_row < valid_rows) & (pixel - pixel_row * WIDTH < valid_columns)
    valid = valid.astype(jnp.bfloat16)
    half_width = EMB // 2
    frequency = jnp.exp(-math.log(10000.0) * jnp.arange(half_width, dtype=jnp.float32) / half_width)
    angles = extents[:, :1] * frequency[None, :]
    embedding = rounded(
        jax.nn.silu(jnp.concatenate([jnp.cos(angles), jnp.sin(angles)], axis=1) + exact[:, :EMB])
    )
    rest = project(embedding, emb_weight) + emb_bias.astype(jnp.float32)

    rows_here = conv1_weight.shape[0]
    places, targets, sources = (jnp.array(table, jnp.int32) for table in unit_tables())
    places = lax.dynamic_slice(places, (z_here, member, 0), (1, 1, SLOTS)).reshape(-1)
    targets = lax.dynamic_slice_in_dim(targets, member, 1, 1).reshape(-1)
    sources = lax.dynamic_index_in_dim(sources, device, 0, keepdims=False)

    from_y = lax.ppermute(text_weight, "y", SWITCH)
    text_pieces = (text_weight, lax.ppermute(text_weight, "core", SWITCH), from_y)
    text_pieces += (lax.ppermute(from_y, "core", SWITCH),)
    text_len = text.shape[1]
    text_blocks = text[0].reshape(text_len, PLANES, -1)
    text_slice = rounded(
        sum(
            jnp.dot(
                lax.dynamic_index_in_dim(text_blocks, a_here ^ distance, 1, keepdims=False),
                piece,
                preferred_element_type=jnp.float32,
            )
            for distance, piece in enumerate(text_pieces)
        )
    )
    text_keys, text_values = text_to_heads(text_slice)
    text_bias = jnp.where(jnp.arange(TEXT_PAD) < text_count, 0.0, neg_big)
    minus = -jnp.ones((TEXT_PAD,), jnp.float32)
    text_keys = text_lanes(text_keys, text_bias, minus, minus, minus)
    text_values = text_lanes(text_values, -minus, minus, minus, minus)

    parts = []
    for _ in range(3):
        part = lax.reduce_precision(rest, 8, 7)
        parts.append(rounded(part).reshape(-1))
        rest = rest - part
    vectors = (
        gn1_gain,
        gn1_bias,
        gn2_gain,
        gn2_bias,
        skip_bias,
        gn3_gain,
        gn3_bias,
        out_bias,
    )
    packed = jnp.concatenate(list(vectors) + parts)
    image_block = jnp.concatenate(image_halves, axis=0)
    filled = -packed.shape[0] % (4 * C_IN) + packed.shape[0]
    packed = jnp.pad(packed, (0, filled - packed.shape[0])).reshape(-1, LANES)
    packed = gather_z(passed(packed, (image_halves[1],)))
    image_blocks = plane_gather(
        jnp.concatenate(image_halves + [packed.reshape(-1, C_IN)], axis=0),
        (text_keys, text_values),
    )
    small = jnp.stack([block[CHUNK:].reshape(PLANES, filled) for block in image_blocks])
    distances = jnp.arange(MEMBERS)[:, None] ^ member
    chosen = distances == jnp.arange(MEMBERS)[None, :]
    small = jnp.sum(
        jnp.where(chosen[:, :, None, None], small[None].astype(jnp.float32), 0.0), axis=1
    )
    small = jnp.transpose(small.reshape(2, 2, ACROSS, PLANES, filled), (1, 0, 3, 2, 4))
    small = small.reshape(PLANES, PLANES, ACROSS, filled)
    bounds = [0]
    for item in vectors:
        bounds.append(bounds[-1] + item.shape[0])
    small_parts = [small[..., bounds[at] : bounds[at + 1]] for at in range(len(vectors))]
    gain_one, bias_one = (part.reshape(-1) for part in small_parts[:2])
    out_shift = small_parts[7].reshape(1, C)
    own_parts = [own_channels(part).reshape(-1) for part in small_parts[2:7]]
    gain_two, bias_two, skip_shift, gain_three, bias_three = own_parts
    emb_rows = emb_weight.shape[0]
    mods = small[..., bounds[-1] : bounds[-1] + 3 * PLANES * emb_rows]
    mods = mods.reshape(PLANES * MEMBERS, 3, PLANES, emb_rows)
    mods = lax.dynamic_index_in_dim(mods, z_here, 2, keepdims=False)
    mods = ((mods[:, 0] + mods[:, 1]) + mods[:, 2]).reshape(2, PLANES, PLANES, ACROSS, -1)
    scale_own = 1.0 + own_channels(mods[0]).reshape(-1)
    shift_own = own_channels(mods[1]).reshape(-1)

    conv1_raw = jnp.concatenate([conv1_weight, skip_weight], axis=1)
    conv1_raw = lax.all_gather(passed(conv1_raw, (image_halves[1],)), "z", axis=0, tiled=True)
    cot_rows = swapped(cotangent[0].reshape(CHUNK, C))
    conv2_own = conv2_blocks(
        lax.all_gather(conv2_weight, "z", axis=0, tiled=True), (cot_rows,)
    )
    qkv_units = lax.all_gather(qkv_weight.reshape(3, rows_here, C), PLANE, axis=0, tiled=True)
    qkv_chosen = choose_units(places, qkv_units)
    qkv_units = lax.all_gather(qkv_chosen, "z", axis=0, tiled=False)
    qkv_own = qkv_blocks(targets, qkv_units, ())

    per_group, first_width = C // GROUPS, C_IN // GROUPS
    own = jnp.stack(
        [gain_two, bias_two, scale_own, shift_own, gain_three, bias_three, skip_shift, skip_shift]
        + [jnp.broadcast_to(1.0 / (count * per_group), (OWN,))]
        + [jnp.zeros((OWN,), jnp.float32)] * 7
    )
    full = jnp.stack(
        [gain_one, bias_one, jnp.broadcast_to(1.0 / (count * first_width), (C_IN,))]
        + [jnp.zeros((C_IN,), jnp.float32)] * 5
    )

    def exchange(blocks):
        return lax.all_to_all(blocks, PLANE, split_axis=0, concat_axis=0, tiled=True)

    out_all = lax.all_gather(out_weight, EVERY, axis=0, tiled=True)
    cot_ready = cot_blocks(cot_rows, out_all)

    image_all, first_act, second_normed, second_act, conv1_own, first_stats, second_stats = first_layer(
        member_word, image_blocks, valid, conv1_raw, full, own, ()
    )
    second_pieces = plane_gather(second_act, (conv2_own, qkv_chosen))
    third_normed, attn_input, residual_low, third_stats = second_layer(
        member_word, second_pieces, image_all, valid, conv2_own, conv1_raw, own, ()
    )

    attn_pieces = plane_gather(attn_input, (qkv_own,))

    queries, keys, values, cot_passed = project_qkv(
        member_word, attn_pieces, valid, qkv_own, cot_ready
    )
    cot_moved = exchange(cot_passed)
    cot_own, grad_mixed = cot_moved[:, :, :OWN], cot_moved[:, :, OWN:].reshape(PIXELS, OWN)

    attended, mixed, back_queries = attend(
        queries, residual_low, keys, values, text_keys, text_values
    )

    moved = exchange(mixed.reshape(MEMBERS, CHUNK, 2 * OWN))

    triple_grads = attend_back(
        back_queries, grad_mixed, attended, keys, values, text_keys, text_values
    )
    triple_grads, (text_dk, text_dv) = triple_grads[:3], triple_grads[3:]

    third_terms = qkv_back(member_word, triple_grads, qkv_own, (moved,))
    grad_third, third_tokens = plane_sum(third_terms)
    qkv_terms = qkv_grad(member_word, targets, triple_grads, attn_pieces, third_tokens[1:])
    qkv_sums = lax.psum_scatter(qkv_terms, "z", scatter_dimension=0, tiled=True)[0]

    output, out_grad = output_rows(moved, out_all, cot_rows, out_shift, third_tokens[1:])
    out_terms = out_grad
    out_grad = lax.psum_scatter(out_grad, PLANE, scatter_dimension=0, tiled=True)[0]

    text_grads = text_from_heads(text_dk[:text_len], text_dv[:text_len])
    text_terms = rounded(weight_grad(text[0], text_grads))
    text_weight_grad = lax.psum_scatter(
        text_terms, ("y", "core"), scatter_dimension=0, tiled=True
    )

    third = third_back(
        member_word,
        grad_third,
        third_normed,
        cot_own,
        valid,
        third_stats,
        own,
        conv2_own,
        (qkv_terms, out_terms, text_terms),
    )
    second_terms, (dres, residual_taps, third_sums) = third[:MEMBERS], third[MEMBERS:]
    conv2_terms = []

    def second_filler(early):
        conv2_terms.append(tap_grad(member_word, residual_taps, second_pieces, (), early))
        return conv2_terms

    grad_second, second_tokens = plane_sum(second_terms, second_filler)
    (conv2_terms,) = conv2_terms
    conv2_parts = along_z(conv2_terms)

    qkv_sums = lax.all_gather(passed(qkv_sums, (conv2_terms,)), PLANE, axis=0, tiled=True)
    out_grad = passed(out_grad, (conv2_terms,))
    out_grad = lax.psum_scatter(out_grad, "z", scatter_dimension=0, tiled=True)

    output = swapped(passed(output, (conv2_terms,)))

    image_terms, hidden_taps, second_sums, first_sums = second_back(
        member_word,
        grad_second,
        second_normed,
        dres,
        valid,
        second_stats,
        own,
        conv1_own,
        conv1_raw,
        image_all,
        first_stats,
        tuple(conv2_parts[1:2]),
    )
    conv1_parts = []

    def image_filler(early):
        conv1_parts.append(
            tap_grad(member_word, hidden_taps, [first_act], (dres, image_all), early + (output,))
        )
        return conv1_parts

    image_part, image_tokens = plane_sum(
        [image_terms[distance] for distance in range(MEMBERS)], image_filler
    )
    image_part = sum(item.astype(jnp.float32) for item in image_part)
    conv1_sums = lax.psum_scatter(conv1_parts[0], "z", scatter_dimension=0, tiled=True)[0, 0]
    conv1_grad, skip_grad = plain_sum(conv1_sums, image_tokens[1:])
    conv2_grad = natural_sum(conv2_parts, image_tokens[1:])

    out_weight_grad = widened(out_grad, image_tokens[1:])
    text_weight_grad = widened(text_weight_grad, image_tokens[1:])

    own_all = small_gather(jnp.concatenate([second_sums[:4], third_sums[:4]], axis=0))
    own_all = own_all.reshape(PLANES, PLANES, ACROSS, 8, PLANES, OWN // PLANES)
    mods_grad = jnp.transpose(own_all[:, :, :, :2], (1, 3, 0, 4, 2, 5)).reshape(PLANES, 2 * C)
    mods_grad = lax.dynamic_slice_in_dim(mods_grad, device * emb_rows, emb_rows, 1)
    emb_weight_grad = jnp.dot(
        mods_grad.T, embedding.astype(jnp.float32), precision=lax.Precision.HIGHEST
    )
    emb_bias_grad = jnp.sum(mods_grad, axis=0)
    channel_sums = jnp.sum(own_all, axis=1)
    channel_sums = lax.dynamic_index_in_dim(channel_sums, a_here, 0, keepdims=False)
    channel_sums = lax.dynamic_index_in_dim(channel_sums, x_here, 0, keepdims=False)
    channel_sums = lax.dynamic_index_in_dim(channel_sums, z_here, 1, keepdims=False)

    first_here = first_sums[:2]
    for axis in PLANE:
        first_here = first_here + lax.ppermute(first_here, axis, SWITCH)
    grouped = jnp.sum((first_here * gain_one).reshape(2, GROUPS, first_width), axis=2)
    grouped = jnp.repeat(grouped / (count * first_width), first_width, axis=1)
    row_valid = lax.dynamic_slice_in_dim(valid[:, :1], member * CHUNK, CHUNK, 0)
    rows_normed = (image_block.astype(jnp.float32) - first_stats[0]) * first_stats[1]
    image_grad = image_part - row_valid.astype(jnp.float32) * first_stats[1] * (
        grouped[1] + rows_normed * grouped[0]
    )
    image_grad = rounded(image_grad)
    qkv_weight_grad = qkv_finish(sources, qkv_sums, (image_grad,))
    image_grad = swapped(image_grad).astype(jnp.float32).reshape(1, -1, WIDTH, C_IN)
    first_grads = lax.dynamic_slice_in_dim(
        sum(turns_z(first_here)), device * first_width, first_width, 1
    )
    return (
        output.reshape(1, -1, WIDTH, C),
        image_grad,
        conv1_grad,
        conv2_grad,
        skip_grad,
        emb_weight_grad,
        qkv_weight_grad,
        out_weight_grad,
        text_weight_grad,
        first_grads[0],
        first_grads[1],
        emb_bias_grad,
        channel_sums[2],
        channel_sums[3],
        channel_sums[6],
        channel_sums[4],
        channel_sums[5],
        channel_sums[7],
    )


def solution(mesh):
    in_specs = (
        P("img", "ha", None, None),
        P("img", None, None),
        P("img"),
        P("img", None),
        P("img", None, None),
        P("img", None),
        P("img", "ha", None, None),
        P(("img", "ha"), None),
        P(("img", "ha"), None),
        P(("img", "ha"), None),
        P(("img", "ha"), None),
        P(("img", "ha"), None),
        P(("img", "ha"), None),
        P("img", "ha"),
        P(("img", "ha")),
        P(("img", "ha")),
        P(("img", "ha")),
        P(("img", "ha")),
        P(("img", "ha")),
        P(("img", "ha")),
        P(("img", "ha")),
        P(("img", "ha")),
        P(("img", "ha")),
    )
    out_specs = (
        P("img", "ha", None, None),
        P("img", "ha", None, None),
        P(("img", "ha"), None),
        P(("img", "ha"), None),
        P(("img", "ha"), None),
        P(("img", "ha"), None),
        P(("img", "ha"), None),
        P(("img", "ha"), None),
        P("img", "ha"),
        P(("img", "ha")),
        P(("img", "ha")),
        P(("img", "ha")),
        P(("img", "ha")),
        P(("img", "ha")),
        P(("img", "ha")),
        P(("img", "ha")),
        P(("img", "ha")),
        P(("img", "ha")),
    )
    split_mesh = plane_mesh(mesh)
    if split_mesh is None:
        return jax.shard_map(
            shards, mesh=mesh, in_specs=in_specs, out_specs=out_specs, check_vma=False
        )
    in_specs, out_specs = (tuple(split_spec(item) for item in specs) for specs in (in_specs, out_specs))
    return jax.shard_map(
        plane_shards, mesh=split_mesh, in_specs=in_specs, out_specs=out_specs, check_vma=False
    )
```

```python
import functools
import math

import jax
import jax.numpy as jnp
from jax import lax
from jax.experimental import pallas as pl
from jax.experimental.pallas import tpu as pltpu
from jax.sharding import Mesh
from jax.sharding import PartitionSpec as P

C_IN = 512
C = 1024
HEADS = 16
HEAD_DIM = 64
GROUPS = 32
EMB = 1024
HEIGHT = 64
WIDTH = 64


neg_big = -1e30
eps_norm = 1e-05


def extended(cells, sides, width):
    for axis, dim in sides:
        count = lax.axis_size(axis)
        ends = count - 1
        head = lax.slice_in_dim(cells, 0, width, axis=dim)
        tail = lax.slice_in_dim(cells, cells.shape[dim] - width, cells.shape[dim], axis=dim)
        cells = jnp.concatenate(
            [
                lax.ppermute(tail, axis, [(i, (i + 1) % count) for i in range(ends)]),
                cells,
                lax.ppermute(head, axis, [((i + 1) % count, i) for i in range(ends)]),
            ],
            axis=dim,
        )
    return cells


def rounded(values):
    return values.astype(jnp.bfloat16)


def silu_slope(inputs):
    sigmoid = jax.nn.sigmoid(inputs)
    return sigmoid * (1.0 + inputs * (1.0 - sigmoid))


def group_view(features):
    return features.reshape(
        features.shape[0], features.shape[1], GROUPS, features.shape[2] // GROUPS
    )


def group_totals(first_sum, second_sum):
    return lax.psum((first_sum, second_sum), "ha")


def norm_stats(features, validity, counts):
    shaped = group_view(features)
    masked = shaped * validity[:, :, None, None]
    first_sum, second_sum = group_totals(
        jnp.sum(masked, axis=(1, 3)), jnp.sum(masked * shaped, axis=(1, 3))
    )
    entries = counts[:, None] * shaped.shape[3]
    group_mean = first_sum / entries
    inv_std = lax.rsqrt(second_sum / entries - group_mean * group_mean + eps_norm)
    return (group_mean, inv_std)


def normalize(features, group_mean, inv_std):
    shaped = group_view(features)
    normed = (shaped - group_mean[:, None, :, None]) * inv_std[:, None, :, None]
    return normed.reshape(features.shape)


def norm_back(grad_normed, normed, validity, counts, inv_std):
    grad_shaped = group_view(grad_normed)
    norm_shaped = group_view(normed)
    first_sum, second_sum = group_totals(
        jnp.sum(grad_shaped, axis=(1, 3)), jnp.sum(grad_shaped * norm_shaped, axis=(1, 3))
    )
    entries = counts[:, None] * grad_shaped.shape[3]
    correction = (
        first_sum[:, None, :, None] + norm_shaped * second_sum[:, None, :, None]
    ) / entries[:, None, :, None]
    result = (grad_shaped - validity[:, :, None, None] * correction) * inv_std[:, None, :, None]
    return result.reshape(grad_normed.shape)


def conv_columns(features):
    padded = extended(features, (("ha", 1),), 1)
    padded = jnp.pad(padded, ((0, 0), (0, 0), (1, 1), (0, 0)))
    batch_size, row_count, col_count, channels = features.shape
    taps = [
        padded[:, row_off : row_off + row_count, col_off : col_off + col_count]
        for row_off in range(3)
        for col_off in range(3)
    ]
    return jnp.concatenate(taps, axis=-1).reshape(batch_size * row_count * col_count, 9 * channels)


def project(inputs, weight):
    return lax.dot_general(
        inputs, weight, (((1,), (1,)), ((), ())), preferred_element_type=jnp.float32
    )


def weight_grad(grads, inputs):
    return lax.dot_general(
        grads, inputs, (((0,), (0,)), ((), ())), preferred_element_type=jnp.float32
    )


def back_project(grads, weight):
    return jnp.dot(grads, weight, preferred_element_type=jnp.float32)


def flipped(weight, in_channels):
    out_channels = weight.shape[0]
    taps = weight.reshape(out_channels, 3, 3, in_channels)[:, ::-1, ::-1, :]
    return jnp.transpose(taps, (1, 2, 0, 3)).reshape(9 * out_channels, in_channels)


def split_heads(values):
    return values.reshape(values.shape[0], values.shape[1], HEADS, HEAD_DIM)


def score_block(head_queries, head_keys, valid_block):
    raw = jnp.einsum(
        "bqhd,bkhd->bhqk", head_queries, head_keys, preferred_element_type=jnp.float32
    ) * (1.0 / math.sqrt(HEAD_DIM))
    return jnp.where(valid_block[:, None, None, :] > 0, raw, neg_big)


def absorb(running, head_queries, pairs, valid_block):
    highest, totals, accumulated = running
    head_keys = split_heads(pairs[:, :, :C])
    head_values = split_heads(pairs[:, :, C:])
    scores = score_block(head_queries, head_keys, valid_block)
    new_high = jnp.maximum(highest, jnp.max(scores, axis=-1))
    weights = jnp.exp(scores - new_high[..., None])
    decay = jnp.exp(highest - new_high)
    totals = totals * decay + jnp.sum(weights, axis=-1)
    update = jnp.einsum(
        "bhqk,bkhd->bqhd", rounded(weights), head_values, preferred_element_type=jnp.float32
    )
    accumulated = accumulated * jnp.transpose(decay, (0, 2, 1))[..., None] + update
    return (new_high, totals, accumulated)


def back_block(grad_query, head_queries, grad_mixed, log_total, delta, pairs, valid_block):
    head_keys = split_heads(pairs[:, :, :C])
    head_values = split_heads(pairs[:, :, C:])
    scores = score_block(head_queries, head_keys, valid_block)
    probs = jnp.exp(scores - log_total[..., None])
    grad_values = jnp.einsum(
        "bhqk,bqhd->bkhd", rounded(probs), grad_mixed, preferred_element_type=jnp.float32
    )
    grad_probs = jnp.einsum(
        "bqhd,bkhd->bhqk", grad_mixed, head_values, preferred_element_type=jnp.float32
    )
    grad_scores = rounded(probs * (grad_probs - delta[..., None]))
    scale_factor = 1.0 / math.sqrt(HEAD_DIM)
    grad_query = (
        grad_query
        + jnp.einsum("bhqk,bkhd->bqhd", grad_scores, head_keys, preferred_element_type=jnp.float32)
        * scale_factor
    )
    grad_keys = (
        jnp.einsum("bhqk,bqhd->bkhd", grad_scores, head_queries, preferred_element_type=jnp.float32)
        * scale_factor
    )
    batch_size, key_count = (pairs.shape[0], pairs.shape[1])
    grad_pairs = jnp.concatenate(
        [
            grad_keys.reshape(batch_size, key_count, C),
            grad_values.reshape(batch_size, key_count, C),
        ],
        axis=2,
    )
    return (grad_query, grad_pairs)


def over_blocks(block_fn, running, pairs, validity):
    key_count = pairs.shape[1]
    block_len = 512

    def over_advance(block_index, carried):
        offset = block_index * block_len
        return block_fn(
            carried,
            lax.dynamic_slice_in_dim(pairs, offset, block_len, 1),
            lax.dynamic_slice_in_dim(validity, offset, block_len, 1),
        )

    return lax.fori_loop(0, key_count // block_len, over_advance, running)


def shards(
    image,
    mask,
    timestep,
    pooled,
    text,
    text_mask,
    cotangent,
    conv1_weight,
    conv2_weight,
    skip_weight,
    emb_weight,
    qkv_weight,
    out_weight,
    text_weight,
    gn1_gain,
    gn1_bias,
    emb_bias,
    gn2_gain,
    gn2_bias,
    skip_bias,
    gn3_gain,
    gn3_bias,
    out_bias,
):
    batch_size, row_count, col_count = (image.shape[0], image.shape[1], image.shape[2])
    pixel_count = row_count * col_count
    gathered = (
        lax.all_gather(conv1_weight, ("img", "ha"), axis=0, tiled=True),
        lax.all_gather(conv2_weight, ("img", "ha"), axis=0, tiled=True),
        lax.all_gather(skip_weight, ("img", "ha"), axis=0, tiled=True),
        lax.all_gather(emb_weight, ("img", "ha"), axis=0, tiled=True),
        lax.all_gather(qkv_weight, ("img", "ha"), axis=0, tiled=True),
        lax.all_gather(out_weight, ("img", "ha"), axis=0, tiled=True),
        lax.all_gather(gn1_gain, ("img", "ha"), axis=0, tiled=True),
        lax.all_gather(gn1_bias, ("img", "ha"), axis=0, tiled=True),
        lax.all_gather(emb_bias, ("img", "ha"), axis=0, tiled=True),
        lax.all_gather(gn2_gain, ("img", "ha"), axis=0, tiled=True),
        lax.all_gather(gn2_bias, ("img", "ha"), axis=0, tiled=True),
        lax.all_gather(skip_bias, ("img", "ha"), axis=0, tiled=True),
        lax.all_gather(gn3_gain, ("img", "ha"), axis=0, tiled=True),
        lax.all_gather(gn3_bias, ("img", "ha"), axis=0, tiled=True),
        lax.all_gather(out_bias, ("img", "ha"), axis=0, tiled=True),
    )
    conv1_full, conv2_full, skip_full, emb_full, qkv_full, out_full = gathered[:6]
    (
        gain_one,
        bias_one,
        emb_shift,
        gain_two,
        bias_two,
        skip_shift,
        gain_three,
        bias_three,
        out_shift,
    ) = (item.astype(jnp.float32) for item in gathered[6:])
    full_valid = mask.reshape(batch_size, HEIGHT * WIDTH).astype(jnp.float32)
    counts = jnp.sum(full_valid, axis=1)
    local_mask = lax.dynamic_slice_in_dim(mask, lax.axis_index("ha") * row_count, row_count, 1)
    validity = local_mask.reshape(batch_size, pixel_count).astype(jnp.float32)
    half_width = EMB // 2
    frequency = jnp.exp(-math.log(10000.0) * jnp.arange(half_width, dtype=jnp.float32) / half_width)
    angles = timestep.astype(jnp.float32)[:, None] * frequency[None, :]
    embedding = rounded(
        jax.nn.silu(jnp.concatenate([jnp.cos(angles), jnp.sin(angles)], axis=1) + pooled)
    )
    modulation = project(embedding, emb_full) + emb_shift
    scale_rows = 1.0 + modulation[:, None, :C]
    shift_rows = modulation[:, None, C:]
    image_flat = image.reshape(batch_size, pixel_count, C_IN)
    image_wide = image_flat.astype(jnp.float32)

    def front(known):
        fresh = known is None
        first_mean, first_std = norm_stats(image_wide, validity, counts) if fresh else known[0]
        first_normed = normalize(image_wide, first_mean, first_std)
        first_pre = first_normed * gain_one + bias_one
        first_act = rounded(jax.nn.silu(first_pre) * validity[:, :, None])
        first_columns = conv_columns(first_act.reshape(batch_size, row_count, col_count, C_IN))
        hidden_one = project(first_columns, conv1_full).reshape(batch_size, pixel_count, C)
        second_mean, second_std = norm_stats(hidden_one, validity, counts) if fresh else known[1]
        second_normed = normalize(hidden_one, second_mean, second_std)
        second_shifted = second_normed * gain_two + bias_two
        second_pre = second_shifted * scale_rows + shift_rows
        second_act = rounded(jax.nn.silu(second_pre) * validity[:, :, None])
        second_columns = conv_columns(second_act.reshape(batch_size, row_count, col_count, C))
        stats = ((first_mean, first_std), (second_mean, second_std))
        return (
            stats,
            (
                first_normed,
                first_pre,
                first_columns,
                second_normed,
                second_shifted,
                second_pre,
                second_columns,
            ),
        )

    stats, saved = front(None)
    residual = (
        project(saved[6], conv2_full) + project(image_flat.reshape(-1, C_IN), skip_full)
    ).reshape(batch_size, pixel_count, C) + skip_shift
    third_mean, third_std = norm_stats(residual, validity, counts)
    third_normed = normalize(residual, third_mean, third_std)
    attn_input = rounded(third_normed * gain_three + bias_three)
    triple = rounded(project(attn_input.reshape(-1, C), qkv_full)).reshape(
        batch_size, pixel_count, 3 * C
    )
    head_queries = split_heads(triple[:, :, :C])
    local_pairs = triple[:, :, C:]
    text_piece = lax.all_gather(text_weight, "img", axis=0, tiled=True)
    text_slice = rounded(
        jnp.einsum("blt,tc->blc", text, text_piece, preferred_element_type=jnp.float32)
    )
    text_pairs = lax.all_gather(text_slice, "ha", axis=2, tiled=True)
    text_valid = text_mask.astype(jnp.float32)

    def absorb_here(carried, pairs, valid_block):
        return absorb(carried, head_queries, pairs, valid_block)

    running = (
        jnp.full((batch_size, HEADS, pixel_count), neg_big, jnp.float32),
        jnp.zeros((batch_size, HEADS, pixel_count), jnp.float32),
        jnp.zeros((batch_size, pixel_count, HEADS, HEAD_DIM), jnp.float32),
    )
    running = absorb_here(running, text_pairs, text_valid)
    valid_block = full_valid
    running = over_blocks(
        absorb_here, running, lax.all_gather(local_pairs, "ha", axis=1, tiled=True), valid_block
    )
    highest, totals, accumulated = running
    attended = accumulated / jnp.transpose(totals, (0, 2, 1))[..., None]
    log_total = highest + jnp.log(totals)
    mixed_rows = rounded(attended.reshape(-1, C))
    output = residual.reshape(-1, C) + project(mixed_rows, out_full) + out_shift
    output = rounded(output).reshape(batch_size, row_count, col_count, C)
    cot_rows = cotangent.reshape(-1, C)
    out_weight_grad = weight_grad(cot_rows, mixed_rows)
    out_bias_grad = jnp.sum(cot_rows.astype(jnp.float32), axis=0)
    grad_mixed = split_heads(
        rounded(back_project(cot_rows, out_full)).reshape(batch_size, pixel_count, C)
    )
    delta = jnp.transpose(jnp.sum(grad_mixed.astype(jnp.float32) * attended, axis=-1), (0, 2, 1))

    def back_here(grad_query, pairs, valid_block):
        return back_block(
            grad_query, head_queries, grad_mixed, log_total, delta, pairs, valid_block
        )

    grad_query = jnp.zeros((batch_size, pixel_count, HEADS, HEAD_DIM), jnp.float32)
    grad_query, text_term = back_here(grad_query, text_pairs, text_valid)
    pixel_pairs = lax.all_gather(local_pairs, "ha", axis=1, tiled=True)
    key_count = pixel_pairs.shape[1]
    block_len = 512

    def body_advance(block_index, carried):
        query_grad, term_now = carried
        offset = block_index * block_len
        query_grad, grad_pairs = back_here(
            query_grad,
            lax.dynamic_slice_in_dim(pixel_pairs, offset, block_len, 1),
            lax.dynamic_slice_in_dim(full_valid, offset, block_len, 1),
        )
        return (query_grad, lax.dynamic_update_slice_in_dim(term_now, grad_pairs, offset, 1))

    key_term = jnp.zeros((batch_size, key_count, 2 * C), jnp.float32)
    grad_query, key_term = lax.fori_loop(
        0, key_count // block_len, body_advance, (grad_query, key_term)
    )
    pair_grads = rounded(
        lax.psum_scatter(
            key_term.astype(jnp.bfloat16), "ha", scatter_dimension=1, tiled=True
        ).astype(jnp.float32)
    )
    text_grads = rounded(
        lax.psum_scatter(
            text_term.astype(jnp.bfloat16), "ha", scatter_dimension=2, tiled=True
        ).astype(jnp.float32)
    )
    text_weight_grad = lax.psum_scatter(
        jnp.einsum("blt,blc->tc", text, text_grads, preferred_element_type=jnp.float32).astype(
            jnp.bfloat16
        ),
        "img",
        scatter_dimension=0,
        tiled=True,
    ).astype(jnp.float32)
    triple_grads = jnp.concatenate(
        [rounded(grad_query.reshape(batch_size, pixel_count, C)), pair_grads], axis=2
    ).reshape(-1, 3 * C)
    qkv_weight_grad = weight_grad(triple_grads, attn_input.reshape(-1, C))
    grad_third = back_project(triple_grads, qkv_full).reshape(batch_size, pixel_count, C)
    gain_three_grad = jnp.sum(grad_third * third_normed, axis=(0, 1))
    bias_three_grad = jnp.sum(grad_third, axis=(0, 1))
    attn_sums = (
        lax.psum_scatter(qkv_weight_grad, ("img", "ha"), scatter_dimension=0, tiled=True),
        lax.psum_scatter(out_weight_grad, ("img", "ha"), scatter_dimension=0, tiled=True),
        lax.psum_scatter(gain_three_grad, ("img", "ha"), scatter_dimension=0, tiled=True),
        lax.psum_scatter(bias_three_grad, ("img", "ha"), scatter_dimension=0, tiled=True),
        lax.psum_scatter(out_bias_grad, ("img", "ha"), scatter_dimension=0, tiled=True),
    )
    grad_residual = cot_rows.astype(jnp.float32).reshape(batch_size, pixel_count, C) + norm_back(
        grad_third * gain_three, third_normed, validity, counts, third_std
    )
    skip_bias_grad = jnp.sum(grad_residual, axis=(0, 1))
    residual_low = rounded(grad_residual)
    residual_rows = residual_low.reshape(-1, C)
    skip_weight_grad = weight_grad(residual_rows, image_flat.reshape(-1, C_IN))
    image_from_skip = back_project(residual_rows, skip_full)
    unused, kept = front(stats)
    (
        first_normed,
        first_pre,
        first_columns,
        second_normed,
        second_shifted,
        second_pre,
        second_columns,
    ) = kept
    conv2_weight_grad = weight_grad(residual_rows, second_columns)
    grad_second_act = jnp.dot(
        conv_columns(residual_low.reshape(batch_size, row_count, col_count, C)),
        flipped(conv2_full, C),
        preferred_element_type=jnp.float32,
    )
    grad_second_pre = (
        grad_second_act.reshape(batch_size, pixel_count, C)
        * validity[:, :, None]
        * silu_slope(second_pre)
    )
    grad_mods = jnp.concatenate(
        [jnp.sum(grad_second_pre * second_shifted, axis=1), jnp.sum(grad_second_pre, axis=1)],
        axis=1,
    )
    emb_weight_grad = jnp.dot(
        grad_mods.T, embedding.astype(jnp.float32), precision=lax.Precision.HIGHEST
    )
    emb_bias_grad = jnp.sum(grad_mods, axis=0)
    grad_second_shift = grad_second_pre * scale_rows
    gain_two_grad = jnp.sum(grad_second_shift * second_normed, axis=(0, 1))
    bias_two_grad = jnp.sum(grad_second_shift, axis=(0, 1))
    hidden_low = rounded(
        norm_back(grad_second_shift * gain_two, second_normed, validity, counts, stats[1][1])
    )
    conv1_weight_grad = weight_grad(hidden_low.reshape(-1, C), first_columns)
    grad_first_act = jnp.dot(
        conv_columns(hidden_low.reshape(batch_size, row_count, col_count, C)),
        flipped(conv1_full, C_IN),
        preferred_element_type=jnp.float32,
    )
    grad_first_pre = (
        grad_first_act.reshape(batch_size, pixel_count, C_IN)
        * validity[:, :, None]
        * silu_slope(first_pre)
    )
    gain_one_grad = jnp.sum(grad_first_pre * first_normed, axis=(0, 1))
    bias_one_grad = jnp.sum(grad_first_pre, axis=(0, 1))
    image_grad = norm_back(
        grad_first_pre * gain_one, first_normed, validity, counts, stats[0][1]
    ) + image_from_skip.reshape(batch_size, pixel_count, C_IN)
    block_sums = (
        lax.psum_scatter(conv1_weight_grad, ("img", "ha"), scatter_dimension=0, tiled=True),
        lax.psum_scatter(conv2_weight_grad, ("img", "ha"), scatter_dimension=0, tiled=True),
        lax.psum_scatter(skip_weight_grad, ("img", "ha"), scatter_dimension=0, tiled=True),
        lax.psum_scatter(emb_weight_grad, ("img", "ha"), scatter_dimension=0, tiled=True),
        lax.psum_scatter(gain_one_grad, ("img", "ha"), scatter_dimension=0, tiled=True),
        lax.psum_scatter(bias_one_grad, ("img", "ha"), scatter_dimension=0, tiled=True),
        lax.psum_scatter(emb_bias_grad, ("img", "ha"), scatter_dimension=0, tiled=True),
        lax.psum_scatter(gain_two_grad, ("img", "ha"), scatter_dimension=0, tiled=True),
        lax.psum_scatter(bias_two_grad, ("img", "ha"), scatter_dimension=0, tiled=True),
        lax.psum_scatter(skip_bias_grad, ("img", "ha"), scatter_dimension=0, tiled=True),
    )
    return (
        output,
        image_grad.reshape(batch_size, row_count, col_count, C_IN),
        block_sums[0],
        block_sums[1],
        block_sums[2],
        block_sums[3],
        attn_sums[0],
        attn_sums[1],
        text_weight_grad,
        block_sums[4],
        block_sums[5],
        block_sums[6],
        block_sums[7],
        block_sums[8],
        block_sums[9],
        attn_sums[2],
        attn_sums[3],
        attn_sums[4],
    )


EVERY = ("y", "core", "z", "x")
PLANE = ("core", "y", "x")
PLANE_SORTED = ("y", "core", "x")
PLANES = 4
ACROSS = 2
MEMBERS = 8
OWN = C // MEMBERS
LANES = 128
TEXT_PAD = 128
SLOTS = 4
ATTEND_ROWS = 1024
ATTEND_KEYS = 1024
BACK_ROWS = 512
BACK_KEYS = 1024
CHUNK = 512
STEPS = HEIGHT * WIDTH // CHUNK
PIXELS = HEIGHT * WIDTH
TAPS = 9 * OWN
VMEM_BYTES = 56 * 1024 * 1024
SWITCH = ((0, 1), (1, 0))
NT = (((1,), (1,)), ((), ()))
TN = (((0,), (0,)), ((), ()))


def plane_mesh(mesh):
    images, rows = mesh.shape["img"], mesh.shape["ha"]
    if images != PLANES or rows != PLANES * ACROSS:
        return None
    return Mesh(mesh.devices.reshape(PLANES // 2, 2, PLANES, ACROSS), EVERY)


def split_spec(spec):
    names = {"img": ("y", "core"), "ha": ("z", "x")}
    entries = []
    for entry in spec:
        parts = (entry,) if isinstance(entry, str) else (entry or ())
        axes = tuple(axis for part in parts for axis in names[part])
        entries.append(axes or None)
    return P(*entries)


def flat_device(y, core, z, x):
    return ((y * 2 + core) * PLANES + z) * ACROSS + x


def every_place():
    return [(y, c, z, x) for y in range(2) for c in range(2) for z in range(PLANES) for x in range(ACROSS)]


def swapped(values):
    pairs = [
        (flat_device(y, c, z, x), flat_device(z % 2, z // 2, 2 * c + y, x)) for y, c, z, x in every_place()
    ]
    return lax.ppermute(values, EVERY, pairs)


def crossing(first):
    pairs = []
    for place in range(MEMBERS):
        along_x = (place // 2 % 2 == 0) == (first == "x")
        pairs.append((place, place ^ (1 if along_x else 4)))
    return pairs


def by_core(first, second):
    return jnp.where(lax.axis_index("core") == 0, first, second)


def pick_kernel(core_ref, first_ref, second_ref, out_ref):
    out_ref[...] = jnp.where(core_ref[0] == 0, first_ref[...], second_ref[...])


def pick(first, second, after):
    rows, columns = first.shape
    steps = 4 if rows % 64 == 0 else 1
    block = (rows // steps, columns)
    return call(
        pick_kernel,
        "pick",
        (steps,),
        [(lax.axis_index("core").reshape(1), None, None)]
        + [(item, block, row_chunk) for item in (first, second)],
        [(first.shape, first.dtype, block, row_chunk)],
        read=3 * rows * columns * 2,
        after=after,
    )[0]


def plane_gather(piece, after=()):
    from_x = lax.ppermute(piece, "x", SWITCH)
    from_y = lax.ppermute(piece, "y", SWITCH)
    from_core = lax.ppermute(piece, "core", SWITCH)
    from_xy = lax.ppermute(pick(from_x, from_y, after), PLANE_SORTED, crossing("y"))
    near = [piece, from_x, from_y, from_xy]
    far = [from_core] + [lax.ppermute(item, "core", SWITCH) for item in near[1:]]
    return near + far


def added(first, second):
    return rounded(first.astype(jnp.float32) + second.astype(jnp.float32))


def plane_sum(terms, between=None):
    arrived = [lax.ppermute(terms[distance ^ 4], "core", SWITCH) for distance in (3, 1, 2, 0)]
    for_xy = added(terms[3], arrived[0])
    passing = lax.ppermute(for_xy, PLANE_SORTED, crossing("x"))
    for_x, for_y = added(terms[1], arrived[1]), added(terms[2], arrived[2])
    early = by_core(for_x, for_y)
    first = lax.ppermute(early, PLANE_SORTED, crossing("x"))
    second = added(by_core(for_y, for_x), passing)
    if between is not None:
        second = passed(second, between((early, for_xy)))
    mine = added(terms[0], arrived[3])
    return (mine, first, lax.ppermute(second, PLANE_SORTED, crossing("y"))), (early, second)


def small_gather(values):
    def both(item, axis):
        other = lax.ppermute(item, axis, SWITCH)
        low = lax.axis_index(axis) == 0
        return jnp.stack([jnp.where(low, item, other), jnp.where(low, other, item)])

    values = both(values, "x")
    z = lax.axis_index("z")
    turned = [values] + [
        lax.ppermute(values, "z", [(at, (at + turn) % PLANES) for at in range(PLANES)])
        for turn in range(1, PLANES)
    ]
    values = jnp.stack(
        [
            sum(jnp.where((z - at) % PLANES == turn, turned[turn], 0.0) for turn in range(PLANES))
            for at in range(PLANES)
        ]
    )
    values = both(both(values, "core"), "y")
    return values.reshape((PLANES,) + values.shape[2:])


def own_channels(by_device):
    a, x = lax.axis_index(("y", "core")), lax.axis_index("x")
    part = lax.dynamic_index_in_dim(by_device, a, 0, keepdims=False)
    return lax.dynamic_index_in_dim(part, x, 1, keepdims=False)


def to_own_order(values):
    lead = values.shape[:-1]
    shaped = values.reshape(lead + (2, 2, PLANES, ACROSS, -1))
    at = len(lead)
    order = tuple(range(at)) + (at + 1, at, at + 3, at + 2, at + 4)
    return jnp.transpose(shaped, order).reshape(lead + (MEMBERS, OWN))


def to_natural_order(values):
    lead = values.shape[:-2]
    shaped = values.reshape(lead + (2, 2, ACROSS, PLANES, -1))
    at = len(lead)
    order = tuple(range(at)) + (at + 1, at, at + 3, at + 2, at + 4)
    return jnp.transpose(shaped, order).reshape(lead + (C,))


def unit_tables():
    where, rows, back = {}, {}, {}
    for z in range(PLANES):
        for member in range(MEMBERS):
            home = flat_device(member // 2 % 2, member // 4, z, member % 2)
            for place in range(3):
                unit = 3 * home + place
                worker = unit % 32 // 4
                entry = where.setdefault((z, worker), [])
                back[home, place] = worker * SLOTS + len(entry)
                entry.append(3 * member + place)
                rows.setdefault((z, worker), []).append(unit // 32 * OWN + unit % 4 * 32)
    pad = {key: entry + entry[:1] * (SLOTS - len(entry)) for key, entry in where.items()}
    places = [[pad[z, t] for t in range(MEMBERS)] for z in range(PLANES)]
    pad = {key: entry + entry[:1] * (SLOTS - len(entry)) for key, entry in rows.items()}
    targets = [[pad[z, t] for t in range(MEMBERS)] for z in range(PLANES)]
    count = PLANES * MEMBERS
    return places, targets, [[back[home, place] for place in range(3)] for home in range(count)]


def call(kernel, name, grid, operands, outputs, scratch=(), flops=0, read=0, after=()):
    def body(*refs):
        kernel(*refs[len(after) :])

    def spec(shape, index):
        if shape is None:
            return pl.BlockSpec(memory_space=pltpu.SMEM)
        if index is None:
            return pl.BlockSpec(shape, lambda *_: (0,) * len(shape))
        return pl.BlockSpec(shape, index)

    return pl.pallas_call(
        body,
        grid=grid,
        in_specs=[pl.BlockSpec(memory_space=pl.ANY)] * len(after)
        + [spec(shape, index) for _, shape, index in operands],
        out_specs=[spec(shape, index) for _, _, shape, index in outputs],
        out_shape=[jax.ShapeDtypeStruct(full, dtype) for full, dtype, _, _ in outputs],
        scratch_shapes=list(scratch),
        compiler_params=pltpu.CompilerParams(vmem_limit_bytes=VMEM_BYTES),
        cost_estimate=pl.CostEstimate(flops=flops, bytes_accessed=read, transcendentals=0),
        name=name,
    )(*after, *[array for array, _, _ in operands])


def whole(array):
    return (array, array.shape, None)


def row_chunk(step):
    return (step, 0)


def group_matrix(channels, width):
    row = lax.broadcasted_iota(jnp.int32, (channels, channels), 0) // width
    column = lax.broadcasted_iota(jnp.int32, (channels, channels), 1) // width
    return (row == column).astype(jnp.float32)


def group_sums(first, second, width):
    channels = first.shape[1]
    rows = jnp.concatenate([first, second, jnp.zeros((6, channels), jnp.float32)], axis=0)
    sums = jnp.dot(
        rows,
        group_matrix(channels, width),
        precision=lax.Precision.HIGHEST,
        preferred_element_type=jnp.float32,
    )
    return sums[0:1], sums[1:2]


def column_sums(values):
    return jnp.sum(values, axis=0, keepdims=True)


def sigmoid(values):
    return 1.0 / (1.0 + jnp.exp(-values))


def chunk_rows(step):
    if isinstance(step, int):
        return slice(step * CHUNK, (step + 1) * CHUNK)
    return pl.ds(pl.multiple_of(step * CHUNK, CHUNK), CHUNK)


def padded_rows(step, row):
    start = step * CHUNK + (1 + row) * WIDTH
    if isinstance(step, int):
        return slice(start, start + CHUNK)
    return pl.ds(pl.multiple_of(start, WIDTH), CHUNK)


def sideways(values, by):
    place = lax.broadcasted_iota(jnp.int32, values.shape, 0) % WIDTH
    rolled = pltpu.roll(values, by % values.shape[0], 0)
    return jnp.where(place == (0 if by == 1 else WIDTH - 1), 0.0, rolled)


SUMS = (3, PIXELS + 2 * WIDTH + CHUNK, OWN)


def add_taps(sums_ref, products_ref, step):
    for tap in range(9):
        dy, dx = tap // 3, tap % 3
        rows = padded_rows(step + 1, 1 - dy)
        sums_ref[dx, rows, :] += products_ref[:, tap * OWN : (tap + 1) * OWN]


def tap_total(sums_ref, step):
    rows = padded_rows(step + 1, 0)
    return (
        sums_ref[1, rows, :]
        + sideways(sums_ref[0, rows, :], 1)
        + sideways(sums_ref[2, rows, :], -1)
    )


def write_sideways(taps_ref, values_fn):
    for dx in range(3):
        taps_ref[dx, 0:WIDTH, :] = jnp.zeros((WIDTH, OWN), jnp.bfloat16)
        taps_ref[dx, PIXELS + WIDTH :, :] = jnp.zeros((WIDTH, OWN), jnp.bfloat16)

    def advance(step, carried):
        values = values_fn(step)
        rows = padded_rows(step, 0)
        taps_ref[0, rows, :] = sideways(values, -1).astype(jnp.bfloat16)
        taps_ref[1, rows, :] = values.astype(jnp.bfloat16)
        taps_ref[2, rows, :] = sideways(values, 1).astype(jnp.bfloat16)
        return carried

    lax.fori_loop(0, STEPS, advance, 0)


def tap_chunk(taps_ref, step):
    return jnp.concatenate(
        [taps_ref[tap % 3, padded_rows(step, 1 - tap // 3), :] for tap in range(9)], axis=1
    )


def first_kernel(
    member_ref,
    *refs,
):
    blocks, refs = refs[:MEMBERS], refs[MEMBERS:]
    image_ref = refs[4]
    for distance in range(MEMBERS):
        image_ref[chunk_rows(member_ref[0] ^ distance), :] = blocks[distance][:CHUNK]
    first_rows(image_ref, *refs[:4], *refs[5:])


def first_rows(
    image_ref,
    valid_ref,
    raw_ref,
    full_ref,
    own_ref,
    act_ref,
    normed_ref,
    next_ref,
    weight_ref,
    first_ref,
    second_ref,
    sums_ref,
    *products_ref,
):
    for tap in range(9):
        weight_ref[tap * OWN : (tap + 1) * OWN, :] = raw_ref[:, tap * C_IN : (tap + 1) * C_IN]
    zero = jnp.zeros((1, C_IN), jnp.float32)

    def gather_sums(step, carried):
        values = image_ref[chunk_rows(step), :].astype(jnp.float32)
        valid = valid_ref[chunk_rows(step), :].astype(jnp.float32)
        masked = values * jnp.concatenate([valid] * (C_IN // LANES), axis=1)
        return (carried[0] + column_sums(masked), carried[1] + column_sums(masked * values))

    sums = lax.fori_loop(0, STEPS, gather_sums, (zero, zero))
    mean, square = (item * full_ref[2:3] for item in group_sums(*sums, C_IN // GROUPS))
    inv_std = lax.rsqrt(square - mean * mean + eps_norm)
    factor = inv_std * full_ref[0:1]
    offset = full_ref[1:2] - mean * factor
    first_ref[...] = jnp.concatenate(
        [mean, inv_std, factor, offset, jnp.zeros((4, C_IN), jnp.float32)], axis=0
    )
    sums_ref[...] = jnp.zeros_like(sums_ref)

    sums = [jnp.zeros((1, OWN), jnp.float32)] * 2
    for step in range(STEPS + 3):
        if 1 <= step <= STEPS:
            products_ref[step % 2][...] = lax.dot_general(
                act_ref[chunk_rows(step - 1), :],
                weight_ref[...],
                NT,
                preferred_element_type=jnp.float32,
            )
        if 2 <= step <= STEPS + 1:
            add_taps(sums_ref, products_ref[(step - 1) % 2], step - 2)
        if step < STEPS:
            rows = chunk_rows(step)
            values = image_ref[rows, :].astype(jnp.float32) * factor + offset
            valid = valid_ref[rows, :].astype(jnp.float32)
            valid = jnp.concatenate([valid] * (C_IN // LANES), axis=1)
            act_ref[rows, :] = (values * sigmoid(values) * valid).astype(jnp.bfloat16)
        if step >= 3:
            rows = chunk_rows(step - 3)
            values = tap_total(sums_ref, step - 3)
            masked = values * valid_ref[rows, :].astype(jnp.float32)
            normed_ref[rows, :] = values
            sums = [sums[0] + column_sums(masked), sums[1] + column_sums(masked * values)]

    mean, square = (item * own_ref[8:9] for item in group_sums(*sums, C // GROUPS))
    inv_std = lax.rsqrt(square - mean * mean + eps_norm)
    second_ref[...] = jnp.concatenate(
        [mean, inv_std, jnp.zeros((6, OWN), jnp.float32)], axis=0
    )

    def activate(step, carried):
        normed = (normed_ref[chunk_rows(step), :] - mean) * inv_std
        normed_ref[chunk_rows(step), :] = normed
        values = (normed * own_ref[0:1] + own_ref[1:2]) * own_ref[2:3] + own_ref[3:4]
        valid = valid_ref[chunk_rows(step), :].astype(jnp.float32)
        next_ref[chunk_rows(step), :] = (values * sigmoid(values) * valid).astype(jnp.bfloat16)
        return carried

    lax.fori_loop(0, STEPS, activate, 0)


def first_layer(member, blocks, valid, raw, full, own, after):
    return call(
        first_kernel,
        "first_layer",
        (),
        [(member, None, None)]
        + [whole(item) for item in blocks]
        + [whole(valid), whole(raw), whole(full), whole(own)],
        [
            ((PIXELS, C_IN), jnp.bfloat16, (PIXELS, C_IN), None),
            ((PIXELS, C_IN), jnp.bfloat16, (PIXELS, C_IN), None),
            ((PIXELS, OWN), jnp.float32, (PIXELS, OWN), None),
            ((PIXELS, OWN), jnp.bfloat16, (PIXELS, OWN), None),
            ((TAPS, C_IN), jnp.bfloat16, (TAPS, C_IN), None),
            ((8, C_IN), jnp.float32, (8, C_IN), None),
            ((8, OWN), jnp.float32, (8, OWN), None),
        ],
        [pltpu.VMEM(SUMS, jnp.float32)] + [pltpu.VMEM((CHUNK, TAPS), jnp.float32)] * 2,
        flops=2 * PIXELS * TAPS * C_IN,
        read=PIXELS * C_IN * 4,
        after=after,
    )


def near_weights(member_ref, weight_ref, near_ref):
    for distance in range(MEMBERS):
        near_ref[:, distance * OWN : (distance + 1) * OWN] = weight_ref[member_ref[0] ^ distance]


def second_kernel(
    member_ref,
    *refs,
):
    pieces_in, refs = refs[:MEMBERS], refs[MEMBERS:]
    image_ref, valid_ref, weight_ref, skip_ref, own_ref = refs[:5]
    normed_ref, next_ref, low_ref, third_ref, sums_ref, near_ref, stats_ref, *products_ref = refs[5:]
    step = pl.program_id(0)

    @pl.when(step == 0)
    def _():
        sums_ref[...] = jnp.zeros_like(sums_ref)
        stats_ref[...] = jnp.zeros_like(stats_ref)
        products_ref[1][...] = jnp.zeros_like(products_ref[1])
        near_weights(member_ref, weight_ref, near_ref)

    def settle(at, counted):
        rows = chunk_rows(at)
        values = tap_total(sums_ref, at) + own_ref[6:7]
        masked = values * valid_ref[rows, :].astype(jnp.float32)
        normed_ref[rows, :] = values
        low_ref[rows, :] = values.astype(jnp.bfloat16)
        stats_ref[0:1] += jnp.where(counted, column_sums(masked), 0.0)
        stats_ref[1:2] += jnp.where(counted, column_sums(masked * values), 0.0)

    def stage(now_ref, before_ref):
        joined = jnp.concatenate([item[...] for item in pieces_in], axis=1)
        now_ref[...] = lax.dot_general(
            joined, near_ref[...], NT, preferred_element_type=jnp.float32
        )
        add_taps(sums_ref, before_ref, step - 1)
        sums_ref[1, padded_rows(step + 1, 0), :] += lax.dot_general(
            image_ref[...], skip_ref[...], NT, preferred_element_type=jnp.float32
        )
        settle(jnp.maximum(step - 2, 0), step >= 2)

    for parity in range(2):
        @pl.when(lax.rem(step, 2) == parity)
        def _(parity=parity):
            stage(products_ref[parity], products_ref[1 - parity])

    @pl.when(step == STEPS - 1)
    def _():
        add_taps(sums_ref, products_ref[(STEPS - 1) % 2], STEPS - 1)
        settle(STEPS - 2, True)
        settle(STEPS - 1, True)
        sums = (stats_ref[0:1], stats_ref[1:2])
        mean, square = (item * own_ref[8:9] for item in group_sums(*sums, C // GROUPS))
        inv_std = lax.rsqrt(square - mean * mean + eps_norm)
        third_ref[...] = jnp.concatenate(
            [mean, inv_std, jnp.zeros((6, OWN), jnp.float32)], axis=0
        )

        def normalize_rows(step, carried):
            normed = (normed_ref[chunk_rows(step), :] - mean) * inv_std
            normed_ref[chunk_rows(step), :] = normed
            next_ref[chunk_rows(step), :] = (normed * own_ref[4:5] + own_ref[5:6]).astype(
                jnp.bfloat16
            )
            return carried

        lax.fori_loop(0, STEPS, normalize_rows, 0)


def skip_block(raw):
    return (raw, (OWN, C_IN), lambda step: (0, 9))


def second_layer(member, pieces_in, image_all, valid, weight, raw, own, after):
    return call(
        second_kernel,
        "second_layer",
        (STEPS,),
        [(member, None, None)]
        + [(item, (CHUNK, OWN), row_chunk) for item in pieces_in]
        + [(image_all, (CHUNK, C_IN), row_chunk)]
        + [whole(valid), whole(weight), skip_block(raw), whole(own)],
        [
            ((PIXELS, OWN), jnp.float32, (PIXELS, OWN), None),
            ((PIXELS, OWN), jnp.bfloat16, (PIXELS, OWN), None),
            ((PIXELS, OWN), jnp.bfloat16, (PIXELS, OWN), None),
            ((8, OWN), jnp.float32, (8, OWN), None),
        ],
        [
            pltpu.VMEM(SUMS, jnp.float32),
            pltpu.VMEM((TAPS, C), jnp.bfloat16),
            pltpu.VMEM((8, OWN), jnp.float32),
            pltpu.VMEM((CHUNK, TAPS), jnp.float32),
            pltpu.VMEM((CHUNK, TAPS), jnp.float32),
        ],
        flops=2 * PIXELS * TAPS * C,
        read=PIXELS * C * 4,
        after=after,
    )


def head_columns(values, head):
    return values if head == 0 else pltpu.roll(values, HEAD_DIM, 1)


def beside(values, *columns):
    lane = lax.broadcasted_iota(jnp.int32, values.shape, 1)
    out = jnp.where(lane < HEAD_DIM, values, 0.0)
    for at, column in enumerate(columns):
        out = jnp.where(lane == HEAD_DIM + at, column, out)
    return out


def qkv_kernel(member_ref, *refs):
    pieces_in, refs = refs[:MEMBERS], refs[MEMBERS:]
    valid_ref, weight_ref, cot_ref, q_ref, k_ref, v_ref, rows_ref, near_ref = refs
    rows_ref[...] = cot_ref[...]

    @pl.when(pl.program_id(0) == 0)
    def _():
        near_weights(member_ref, weight_ref, near_ref)

    joined = jnp.concatenate([item[...] for item in pieces_in], axis=1)
    triple = lax.dot_general(joined, near_ref[...], NT, preferred_element_type=jnp.float32)
    queries, keys, values = (triple[:, at * OWN : (at + 1) * OWN] for at in range(3))
    bias = jnp.where(valid_ref[...].astype(jnp.float32) > 0, 0.0, neg_big)
    for head in range(2):
        q_ref[head] = beside(head_columns(queries, head) * (1.0 / math.sqrt(HEAD_DIM)), 1.0).astype(
            jnp.bfloat16
        )
        k_ref[head] = beside(head_columns(keys, head), bias, -1.0, -1.0, -1.0).astype(jnp.bfloat16)
        v_ref[head] = beside(head_columns(values, head), 1.0, -1.0, -1.0, -1.0).astype(jnp.bfloat16)


def project_qkv(member, pieces_in, valid, weight, cots):
    cot_spec = ((1, CHUNK, 2 * OWN), lambda step: (step, 0, 0))
    out = ((2, PIXELS, LANES), jnp.bfloat16, (2, CHUNK, LANES), lambda step: (0, step, 0))
    return call(
        qkv_kernel,
        "project_qkv",
        (STEPS,),
        [(member, None, None)]
        + [(item, (CHUNK, OWN), row_chunk) for item in pieces_in]
        + [(valid, (CHUNK, OWN), row_chunk), whole(weight)]
        + [(cots, *cot_spec)],
        [out] * 3 + [(cots.shape, jnp.bfloat16, *cot_spec)],
        [pltpu.VMEM((3 * OWN, C), jnp.bfloat16)],
        flops=2 * PIXELS * 3 * OWN * C,
        read=PIXELS * C * 4,
    )


def split_float(column):
    parts = []
    for _ in range(3):
        part = column.astype(jnp.bfloat16).astype(jnp.float32)
        parts.append(part)
        column = column - part
    return parts


def attend_kernel(
    q_ref, low_ref, k_ref, v_ref, tk_ref, tv_ref, attn_ref, mixed_ref, back_ref
):
    width = ATTEND_KEYS
    attended = []
    for head in range(2):
        queries = q_ref[head]
        parts = [(tk_ref[head], tv_ref[head])] + [
            (k_ref[head, at : at + width], v_ref[head, at : at + width])
            for at in range(0, PIXELS, width)
        ]
        highest, accumulated = None, None
        for keys, values in parts:
            scores = lax.dot_general(queries, keys, NT, preferred_element_type=jnp.float32)
            top = jnp.max(scores, axis=1, keepdims=True)
            if highest is not None:
                top = jnp.maximum(highest, top)
            weights = jnp.exp(scores - top).astype(jnp.bfloat16)
            update = jnp.dot(weights, values, preferred_element_type=jnp.float32)
            accumulated = (
                update if highest is None else accumulated * jnp.exp(highest - top) + update
            )
            highest = top
        total = accumulated[:, HEAD_DIM : HEAD_DIM + 1]
        attended.append(accumulated / total)
        logs = split_float(highest + jnp.log(total))
        back_ref[head] = beside(queries.astype(jnp.float32), 1.0, *logs).astype(jnp.bfloat16)
    lane = lax.broadcasted_iota(jnp.int32, attended[0].shape, 1)
    both = jnp.where(lane < HEAD_DIM, attended[0], pltpu.roll(attended[1], HEAD_DIM, 1))
    attn_ref[...] = both
    mixed_ref[:, :OWN] = both.astype(jnp.bfloat16)
    mixed_ref[:, OWN:] = low_ref[...]


def attend(queries, low, keys, values, text_keys, text_values):
    block = ATTEND_ROWS
    return call(
        attend_kernel,
        "attend",
        (PIXELS // block,),
        [(queries, (2, block, LANES), lambda step: (0, step, 0)), (low, (block, OWN), row_chunk)]
        + [whole(keys), whole(values), whole(text_keys), whole(text_values)],
        [
            ((PIXELS, OWN), jnp.float32, (block, OWN), row_chunk),
            ((PIXELS, 2 * OWN), jnp.bfloat16, (block, 2 * OWN), row_chunk),
            ((2, PIXELS, LANES), jnp.bfloat16, (2, block, LANES), lambda step: (0, step, 0)),
        ],
        flops=8 * PIXELS * (PIXELS + TEXT_PAD) * LANES,
        read=PIXELS * LANES * 12,
    )


def attend_back_kernel(
    q_ref,
    do_ref,
    attn_ref,
    k_ref,
    v_ref,
    tk_ref,
    tv_ref,
    dq_ref,
    dk_ref,
    dv_ref,
    dtk_ref,
    dtv_ref,
    grads_ref,
    dqt_ref,
):
    step = pl.program_id(0)
    block = BACK_ROWS

    @pl.when(step == 0)
    def _():
        dqt_ref[...] = jnp.zeros_like(dqt_ref)

        def prepare(at, carried):
            grads = do_ref[chunk_rows(at), :].astype(jnp.float32)
            terms = grads * attn_ref[chunk_rows(at), :]
            lane = lax.broadcasted_iota(jnp.int32, terms.shape, 1)
            for head in range(2):
                inside = (lane < HEAD_DIM) == (head == 0)
                delta = jnp.sum(jnp.where(inside, terms, 0.0), axis=1, keepdims=True)
                grads_ref[head, chunk_rows(at), :] = beside(
                    head_columns(grads, head), 0.0, *split_float(delta)
                ).astype(jnp.bfloat16)
            return carried

        lax.fori_loop(0, STEPS, prepare, 0)

    def absorb_keys(head, keys, values):
        keys_across = jnp.transpose(keys.astype(jnp.float32))[:HEAD_DIM].astype(jnp.bfloat16)
        grad_keys, grad_values = None, None
        for start in range(0, PIXELS, block):
            queries = q_ref[head, start : start + block]
            grads = grads_ref[head, start : start + block]
            scores = lax.dot_general(keys, queries, NT, preferred_element_type=jnp.float32)
            grad_probs = lax.dot_general(values, grads, NT, preferred_element_type=jnp.float32)
            probs = jnp.exp(scores)
            grad_scores = (probs * grad_probs).astype(jnp.bfloat16)
            value_term = jnp.dot(
                probs.astype(jnp.bfloat16), grads, preferred_element_type=jnp.float32
            )
            key_term = jnp.dot(grad_scores, queries, preferred_element_type=jnp.float32)
            grad_values = value_term if grad_values is None else grad_values + value_term
            grad_keys = key_term if grad_keys is None else grad_keys + key_term
            rows = slice(head * HEAD_DIM, (head + 1) * HEAD_DIM)
            dqt_ref[rows, start : start + block] += jnp.dot(
                keys_across, grad_scores, preferred_element_type=jnp.float32
            )
        return grad_keys, grad_values

    def both_heads(key_source, value_source):
        (dk0, dv0), (dk1, dv1) = (
            absorb_keys(head, key_source[head], value_source[head]) for head in range(2)
        )
        lane = lax.broadcasted_iota(jnp.int32, dk0.shape, 1)
        return (
            jnp.where(lane < HEAD_DIM, low, pltpu.roll(high, HEAD_DIM, 1)).astype(jnp.bfloat16)
            for low, high in ((dk0, dk1), (dv0, dv1))
        )

    dk_ref[...], dv_ref[...] = both_heads(k_ref, v_ref)

    @pl.when(step == pl.num_programs(0) - 1)
    def _():
        dtk_ref[...], dtv_ref[...] = both_heads(tk_ref, tv_ref)
        for start in range(0, PIXELS, block):
            dq_ref[start : start + block, :] = (
                jnp.transpose(dqt_ref[:, start : start + block]) * (1.0 / math.sqrt(HEAD_DIM))
            ).astype(jnp.bfloat16)


def attend_back(queries, grads, attended, keys, values, text_keys, text_values):
    block = BACK_KEYS
    rows = (PIXELS, OWN)
    text_rows = (TEXT_PAD, OWN)
    return call(
        attend_back_kernel,
        "attend_back",
        (PIXELS // block,),
        [whole(queries), whole(grads), whole(attended)]
        + [(item, (2, block, LANES), lambda step: (0, step, 0)) for item in (keys, values)]
        + [whole(text_keys), whole(text_values)],
        [
            (rows, jnp.bfloat16, rows, None),
            (rows, jnp.bfloat16, (block, OWN), row_chunk),
            (rows, jnp.bfloat16, (block, OWN), row_chunk),
            (text_rows, jnp.bfloat16, text_rows, None),
            (text_rows, jnp.bfloat16, text_rows, None),
        ],
        [
            pltpu.VMEM((2, PIXELS, LANES), jnp.bfloat16),
            pltpu.VMEM((OWN, PIXELS), jnp.float32),
        ],
        flops=20 * PIXELS * (PIXELS + TEXT_PAD) * LANES,
        read=PIXELS * LANES * 20,
    )


def triple_blocks(grads):
    return [(item, (CHUNK, OWN), row_chunk) for item in grads]


def join_triple(refs):
    return jnp.concatenate([item[...] for item in refs], axis=1)


def qkv_back_kernel(member_ref, *refs):
    triple, weight_ref, outs, near_ref = refs[:3], refs[3], refs[4 : 4 + MEMBERS], refs[4 + MEMBERS]

    @pl.when(pl.program_id(0) == 0)
    def _():
        near_weights(member_ref, weight_ref, near_ref)

    terms = jnp.dot(join_triple(triple), near_ref[...], preferred_element_type=jnp.float32)
    for distance in range(MEMBERS):
        outs[distance][...] = terms[:, distance * OWN : (distance + 1) * OWN].astype(jnp.bfloat16)


def qkv_back(member, grads, weight, after):
    return call(
        qkv_back_kernel,
        "qkv_back",
        (STEPS,),
        [(member, None, None)] + triple_blocks(grads) + [whole(weight)],
        [((PIXELS, OWN), jnp.bfloat16, (CHUNK, OWN), row_chunk)] * MEMBERS,
        [pltpu.VMEM((3 * OWN, C), jnp.bfloat16)],
        flops=2 * PIXELS * 3 * OWN * C,
        read=PIXELS * C * 4,
        after=after,
    )


def norm_back_terms(gain_sum, bias_sum, own_ref, gain):
    first, second = group_sums(gain * bias_sum, gain * gain_sum, C // GROUPS)
    return first * own_ref[8:9], second * own_ref[8:9]


def third_back_kernel(
    member_ref,
    mine_ref,
    first_ref,
    second_ref,
    normed_ref,
    cot_ref,
    valid_ref,
    third_ref,
    own_ref,
    weight_ref,
    *refs,
):
    outs, refs = refs[:MEMBERS], refs[MEMBERS:]
    low_ref, taps_ref, totals_ref, near_ref, grads_ref = refs
    step = pl.program_id(0)

    @pl.when(step == 0)
    def _():
        near_weights(member_ref, weight_ref, near_ref)
        zero = jnp.zeros((1, OWN), jnp.float32)

        def gather(at, carried):
            rows = chunk_rows(at)
            grads = (
                mine_ref[rows, :].astype(jnp.float32)
                + first_ref[rows, :].astype(jnp.float32)
                + second_ref[rows, :].astype(jnp.float32)
            )
            cots = cot_ref[at].astype(jnp.float32)
            grads_ref[rows, :] = grads * own_ref[4:5]
            return (
                carried[0] + column_sums(grads * normed_ref[rows, :]),
                carried[1] + column_sums(grads),
                carried[2] + column_sums(cots),
            )

        gain_sum, bias_sum, cot_sum = lax.fori_loop(0, STEPS, gather, (zero, zero, zero))

        first, second = norm_back_terms(gain_sum, bias_sum, own_ref, own_ref[4:5])
        totals_ref[...] = jnp.concatenate(
            [gain_sum, bias_sum, zero, cot_sum, jnp.zeros((4, OWN), jnp.float32)], axis=0
        )

        def finish(at):
            rows = chunk_rows(at)
            valid = valid_ref[rows, :].astype(jnp.float32)
            total = grads_ref[rows, :] - valid * (first + normed_ref[rows, :] * second)
            total = total * third_ref[1:2] + cot_ref[at].astype(jnp.float32)
            low_ref[rows, :] = total.astype(jnp.bfloat16)
            totals_ref[2:3] += column_sums(total)
            return total

        write_sideways(taps_ref, finish)

    terms = jnp.dot(tap_chunk(taps_ref, step), near_ref[...], preferred_element_type=jnp.float32)
    for distance in range(MEMBERS):
        outs[distance][...] = terms[:, distance * OWN : (distance + 1) * OWN].astype(jnp.bfloat16)


def third_back(member, sums, normed, cots, valid, third, own, weight, after):
    rows = (PIXELS, OWN)
    taps = (3, PIXELS + 2 * WIDTH, OWN)
    return call(
        third_back_kernel,
        "third_back",
        (STEPS,),
        [(member, None, None)]
        + [whole(item) for item in sums]
        + [whole(normed), whole(cots), whole(valid), whole(third), whole(own), whole(weight)],
        [(rows, jnp.bfloat16, (CHUNK, OWN), row_chunk)] * MEMBERS
        + [
            (rows, jnp.bfloat16, rows, None),
            (taps, jnp.bfloat16, taps, None),
            ((8, OWN), jnp.float32, (8, OWN), None),
        ],
        [
            pltpu.VMEM((TAPS, C), jnp.bfloat16),
            pltpu.VMEM(rows, jnp.float32),
        ],
        flops=2 * PIXELS * TAPS * C,
        read=PIXELS * C * 4,
        after=after,
    )


def second_back_kernel(
    member_ref,
    mine_ref,
    first_ref,
    second_ref,
    normed_ref,
    low_ref,
    valid_ref,
    stats_ref,
    own_ref,
    weight_ref,
    skip_ref,
    image_ref,
    full_ref,
    out_ref,
    taps_ref,
    totals_ref,
    firsts_ref,
    grads_ref,
):
    step = pl.program_id(0)

    @pl.when(step == 0)
    def _():
        zero = jnp.zeros((1, OWN), jnp.float32)

        def gather(at, carried):
            rows = chunk_rows(at)
            normed = normed_ref[rows, :]
            shifted_rows = normed * own_ref[0:1] + own_ref[1:2]
            values = shifted_rows * own_ref[2:3] + own_ref[3:4]
            gate = sigmoid(values)
            slope = gate * (1.0 + values * (1.0 - gate))
            grads = (
                mine_ref[rows, :].astype(jnp.float32)
                + first_ref[rows, :].astype(jnp.float32)
                + second_ref[rows, :].astype(jnp.float32)
            )
            grads = grads * valid_ref[rows, :].astype(jnp.float32) * slope
            inner = grads * own_ref[2:3]
            grads_ref[rows, :] = inner * own_ref[0:1]
            return (
                carried[0] + column_sums(grads * shifted_rows),
                carried[1] + column_sums(grads),
                carried[2] + column_sums(inner * normed),
                carried[3] + column_sums(inner),
            )

        totals = lax.fori_loop(0, STEPS, gather, (zero,) * 4)
        totals_ref[...] = jnp.concatenate(
            list(totals) + [jnp.zeros((4, OWN), jnp.float32)], axis=0
        )

        first, second = norm_back_terms(totals[2], totals[3], own_ref, own_ref[0:1])

        def finish(at):
            rows = chunk_rows(at)
            valid = valid_ref[rows, :].astype(jnp.float32)
            total = grads_ref[rows, :] - valid * (first + normed_ref[rows, :] * second)
            return total * stats_ref[1:2]

        write_sideways(taps_ref, finish)
        firsts_ref[...] = jnp.zeros_like(firsts_ref)

    at = member_ref[0] ^ step
    rows = chunk_rows(at)
    grads = jnp.dot(tap_chunk(taps_ref, at), weight_ref[...], preferred_element_type=jnp.float32)
    image = image_ref[rows, :].astype(jnp.float32)
    values = image * full_ref[2:3] + full_ref[3:4]
    gate = sigmoid(values)
    slope = gate * (1.0 + values * (1.0 - gate))
    valid = valid_ref[rows, :].astype(jnp.float32)
    grads = grads * jnp.concatenate([valid] * (C_IN // LANES), axis=1) * slope
    normed = (image - full_ref[0:1]) * full_ref[1:2]
    firsts_ref[0:1] += column_sums(grads * normed)
    firsts_ref[1:2] += column_sums(grads)
    skipped = jnp.dot(low_ref[rows, :], skip_ref[...], preferred_element_type=jnp.float32)
    out_ref[0] = (grads * full_ref[2:3] + skipped).astype(jnp.bfloat16)


def second_back(member, sums, normed, low, valid, stats, own, weight, raw, image_all, full, after):
    rows = (PIXELS, OWN)
    taps = (3, PIXELS + 2 * WIDTH, OWN)
    return call(
        second_back_kernel,
        "second_back",
        (STEPS,),
        [(member, None, None)]
        + [whole(item) for item in sums]
        + [whole(normed), whole(low), whole(valid), whole(stats), whole(own)]
        + [whole(weight), skip_block(raw), whole(image_all), whole(full)],
        [
            (
                (MEMBERS, CHUNK, C_IN),
                jnp.bfloat16,
                (1, CHUNK, C_IN),
                lambda step: (step, 0, 0),
            ),
            (taps, jnp.bfloat16, taps, None),
            ((8, OWN), jnp.float32, (8, OWN), None),
            ((8, C_IN), jnp.float32, (8, C_IN), None),
        ],
        [pltpu.VMEM(rows, jnp.float32)],
        flops=0,
        read=0,
        after=after,
    )


def tap_grad_kernel(count, member_ref, taps_ref, *refs):
    inputs, refs = refs[:count], refs[count:]
    if count == 1:
        low_ref, image_ref, out_ref, sums_ref, skip_ref = refs
    else:
        out_ref, sums_ref = refs
    step = pl.program_id(0)

    @pl.when(step == 0)
    def _():
        sums_ref[...] = jnp.zeros_like(sums_ref)
        if count == 1:
            skip_ref[...] = jnp.zeros_like(skip_ref)

    if count == 1:
        skip_ref[...] += lax.dot_general(
            low_ref[...], image_ref[...], TN, preferred_element_type=jnp.float32
        )

    joined = jnp.concatenate([item[...] for item in inputs], axis=1)
    sums_ref[...] += lax.dot_general(
        tap_chunk(taps_ref, step), joined, TN, preferred_element_type=jnp.float32
    )

    @pl.when(step == STEPS - 1)
    def _():
        share = OWN // PLANES
        if count == 1:
            for z in range(PLANES):
                out_ref[z, 0, 9] = skip_ref[z * share : (z + 1) * share, :].astype(jnp.bfloat16)
        for tap in range(9):
            for z in range(PLANES):
                rows = slice(tap * OWN + z * share, tap * OWN + (z + 1) * share)
                if count == 1:
                    out_ref[z, 0, tap] = sums_ref[rows, :].astype(jnp.bfloat16)
                else:
                    for distance in range(count):
                        columns = slice(distance * OWN, (distance + 1) * OWN)
                        out_ref[z, member_ref[0] ^ distance, tap] = sums_ref[rows, columns].astype(
                            jnp.bfloat16
                        )


def tap_grad(member, taps, inputs, skip=(), after=()):
    count, width = len(inputs), inputs[0].shape[1]
    shape = (PLANES, count, 10 if skip else 9, OWN // PLANES, width)
    return call(
        functools.partial(tap_grad_kernel, count),
        "tap_grad",
        (STEPS,),
        [(member, None, None), whole(taps)]
        + [(item, (CHUNK, item.shape[1]), row_chunk) for item in inputs + list(skip)],
        [(shape, jnp.bfloat16, shape, None)],
        [pltpu.VMEM((TAPS, count * width), jnp.float32)]
        + [pltpu.VMEM((OWN, C_IN), jnp.float32)] * (1 if skip else 0),
        flops=0,
        after=after,
    )[0]


def qkv_grad_kernel(member_ref, targets_ref, *refs):
    triple, inputs, (out_ref, sums_ref) = refs[:3], refs[3 : 3 + MEMBERS], refs[3 + MEMBERS :]
    step = pl.program_id(0)

    @pl.when(step == 0)
    def _():
        sums_ref[...] = jnp.zeros_like(sums_ref)

    joined = jnp.concatenate([item[...] for item in inputs], axis=1)
    sums_ref[...] += lax.dot_general(join_triple(triple), joined, TN, preferred_element_type=jnp.float32)

    @pl.when(step == STEPS - 1)
    def _():
        for z in range(PLANES):
            for slot in range(SLOTS):
                rows = pl.ds(pl.multiple_of(targets_ref[z * SLOTS + slot], 32), 32)
                for distance in range(MEMBERS):
                    columns = slice(distance * OWN, (distance + 1) * OWN)
                    out_ref[z, slot, member_ref[0] ^ distance] = sums_ref[rows, columns].astype(
                        jnp.bfloat16
                    )


def qkv_grad(member, targets, grads, inputs, after):
    shape = (PLANES, SLOTS, MEMBERS, OWN // PLANES, OWN)
    return call(
        qkv_grad_kernel,
        "qkv_grad",
        (STEPS,),
        [(member, None, None), (targets, None, None)]
        + triple_blocks(grads)
        + [(item, (CHUNK, OWN), row_chunk) for item in inputs],
        [(shape, jnp.bfloat16, shape, None)],
        [pltpu.VMEM((3 * OWN, C), jnp.float32)],
        flops=0,
        after=after,
    )[0]


def pass_kernel(value_ref, out_ref):
    out_ref[...] = value_ref[...]


def passed(values, after):
    spec = (values.shape, values.dtype, values.shape, None)
    return call(pass_kernel, "passed", (), [whole(values)], [spec], after=after)[0]


def widen_kernel(value_ref, out_ref):
    out_ref[...] = value_ref[...].astype(jnp.float32)


def widened(values, after):
    return call(
        widen_kernel,
        "widen",
        (),
        [whole(values)],
        [(values.shape, jnp.float32, values.shape, None)],
        after=after,
    )[0]


def along_z(blocks):
    z = lax.axis_index("z")

    def block(distance):
        return lax.dynamic_index_in_dim(blocks, z ^ distance, 0, keepdims=False)

    def moved(values, distance):
        return lax.ppermute(values, "z", [(at, at ^ distance) for at in range(PLANES)])

    near, far = moved(block(1), 1), moved(block(3), 1)
    far = rounded(block(2).astype(jnp.float32) + far.astype(jnp.float32))
    return (block(0), near, moved(far, 2)), far


def turns_z(piece):
    return [piece] + [
        lax.ppermute(piece, "z", [(at, (at + turn) % PLANES) for at in range(PLANES)])
        for turn in range(1, PLANES)
    ]


def gather_z(piece):
    z = lax.axis_index("z")
    turned = turns_z(piece)
    zero = jnp.zeros_like(piece)
    return jnp.stack(
        [
            sum(jnp.where((z - at) % PLANES == turn, turned[turn], zero) for turn in range(PLANES))
            for at in range(PLANES)
        ]
    )


def order_matrix(dtype):
    shape = (ACROSS * OWN, ACROSS * OWN)
    source = lax.broadcasted_iota(jnp.int32, shape, 0)
    target = lax.broadcasted_iota(jnp.int32, shape, 1)
    x, z, place = source // OWN, source % OWN // 32, source % 32
    return (target == (z * ACROSS + x) * 32 + place).astype(jnp.float32).astype(dtype)


def own_columns(values, order, y, core):
    start = (2 * y + core) * ACROSS * OWN
    block = values[:, start : start + ACROSS * OWN]
    return lax.dot_general(block, order, NT, preferred_element_type=jnp.float32).astype(jnp.bfloat16)


def square(count):
    return [(core, y) for core in range(2) for y in range(count)]


def conv2_kernel(raw_ref, out_ref):
    order = order_matrix(jnp.bfloat16)
    for tap in range(9):
        rows = slice(tap * OWN, (tap + 1) * OWN)
        values = raw_ref[:, tap * C : (tap + 1) * C]
        for core, y in square(2):
            columns = own_columns(values, order, y, core)
            for x in range(ACROSS):
                out_ref[4 * core + 2 * y + x, rows, :] = columns[:, x * OWN : (x + 1) * OWN]


def conv2_blocks(raw, after):
    shape = (MEMBERS, TAPS, OWN)
    return call(
        conv2_kernel,
        "conv2_blocks",
        (),
        [whole(raw)],
        [(shape, jnp.bfloat16, shape, None)],
        after=after,
    )[0]


def choose_kernel(places_ref, units_ref, out_ref):
    for slot in range(SLOTS):
        out_ref[slot] = units_ref[places_ref[slot]]


def choose_units(places, units):
    shape = (SLOTS,) + units.shape[1:]
    return call(
        choose_kernel,
        "choose_units",
        (),
        [(places, None, None), whole(units)],
        [(shape, units.dtype, shape, None)],
    )[0]


def qkv_blocks_kernel(targets_ref, units_ref, out_ref):
    order = order_matrix(jnp.bfloat16)
    for z in range(PLANES):
        for slot in range(SLOTS):
            rows = pl.ds(pl.multiple_of(targets_ref[z * SLOTS + slot], 32), 32)
            values = units_ref[z, slot]
            for core, y in square(2):
                columns = own_columns(values, order, y, core)
                for x in range(ACROSS):
                    out_ref[4 * core + 2 * y + x, rows, :] = columns[:, x * OWN : (x + 1) * OWN]


def qkv_blocks(targets, units, after):
    shape = (MEMBERS, 3 * OWN, OWN)
    return call(
        qkv_blocks_kernel,
        "qkv_blocks",
        (),
        [(targets, None, None), whole(units)],
        [(shape, jnp.bfloat16, shape, None)],
        after=after,
    )[0]


def qkv_finish_kernel(source_ref, units_ref, out_ref):
    order = order_matrix(jnp.bfloat16)
    for place in range(3):
        unit = units_ref[source_ref[place]]
        for core, y in square(2):
            member = 4 * core + 2 * y
            joined = jnp.concatenate([unit[member], unit[member + 1]], axis=1)
            start = (2 * y + core) * ACROSS * OWN
            out_ref[place * 32 : (place + 1) * 32, start : start + ACROSS * OWN] = jnp.dot(
                joined, order, preferred_element_type=jnp.float32
            )


def qkv_finish(source, units, after):
    shape = (3 * 32, C)
    return call(
        qkv_finish_kernel,
        "qkv_finish",
        (),
        [(source, None, None), whole(units)],
        [(shape, jnp.float32, shape, None)],
        after=after,
    )[0]


def cot_kernel(cot_ref, weight_ref, out_ref):
    cots = cot_ref[...]
    order = order_matrix(jnp.bfloat16)
    mixed = jnp.dot(cots, weight_ref[...], preferred_element_type=jnp.float32).astype(jnp.bfloat16)
    for core, y in square(2):
        columns = own_columns(cots, order, y, core)
        for x in range(ACROSS):
            out_ref[4 * core + 2 * y + x, :, :OWN] = columns[:, x * OWN : (x + 1) * OWN]
    for member in range(MEMBERS):
        out_ref[member, :, OWN:] = mixed[:, member * OWN : (member + 1) * OWN]


def cot_blocks(cots, weight):
    shape = (MEMBERS, CHUNK, 2 * OWN)
    return call(
        cot_kernel,
        "cot_blocks",
        (),
        [whole(cots), whole(weight)],
        [(shape, jnp.bfloat16, shape, None)],
        flops=2 * CHUNK * C * C,
    )[0]


def output_kernel(moved_ref, weight_ref, cot_ref, shift_ref, out_ref, grad_ref):
    mixed = jnp.concatenate([moved_ref[member, :, :OWN] for member in range(MEMBERS)], axis=1)
    product = lax.dot_general(mixed, weight_ref[...], NT, preferred_element_type=jnp.float32)
    order = order_matrix(jnp.bfloat16)
    for core, y in square(2):
        member = 4 * core + 2 * y
        residual = jnp.concatenate(
            [moved_ref[member, :, OWN:], moved_ref[member + 1, :, OWN:]], axis=1
        )
        residual = jnp.dot(residual, order, preferred_element_type=jnp.float32)
        start = (2 * y + core) * ACROSS * OWN
        columns = slice(start, start + ACROSS * OWN)
        out_ref[:, columns] = (residual + product[:, columns] + shift_ref[:, columns]).astype(
            jnp.bfloat16
        )
    grads = lax.dot_general(cot_ref[...], mixed, TN, preferred_element_type=jnp.float32)
    for core, y in square(2):
        for z in range(PLANES):
            for x in range(ACROSS):
                start = ((2 * y + core) * PLANES + z) * ACROSS * 32 + x * 32
                grad_ref[4 * core + 2 * y + x, z * 32 : (z + 1) * 32, :] = grads[
                    start : start + 32
                ].astype(jnp.bfloat16)


def output_rows(moved, weight, cots, shift, after):
    shapes = ((CHUNK, C), (MEMBERS, OWN, C))
    return call(
        output_kernel,
        "output_rows",
        (),
        [whole(moved), whole(weight), whole(cots), whole(shift)],
        [(shape, jnp.bfloat16, shape, None) for shape in shapes],
        flops=0,
        after=after,
    )


def natural_kernel(first_ref, second_ref, third_ref, out_ref):
    taps, rows = first_ref.shape[1], first_ref.shape[2]
    width = ACROSS * OWN
    order = order_matrix(jnp.float32)

    def total(at):
        parts = [item[at].astype(jnp.float32) for item in (first_ref, second_ref, third_ref)]
        return ((parts[0] + parts[1]) + parts[2]).reshape(taps * rows, OWN)

    for core in range(2):
        for y in range(2):
            at = 4 * core + 2 * y
            joined = jnp.concatenate([total(at), total(at + 1)], axis=1)
            ordered = jnp.dot(
                joined, order, precision=lax.Precision.HIGHEST, preferred_element_type=jnp.float32
            )
            for tap in range(taps):
                columns = slice(tap * C + (2 * y + core) * width, tap * C + (2 * y + core + 1) * width)
                out_ref[:, columns] = ordered[tap * rows : (tap + 1) * rows]


def natural_sum(parts, after):
    taps, rows = parts[0].shape[1:3]
    shape = (rows, taps * C)
    return call(
        natural_kernel,
        "natural_sum",
        (),
        [whole(item) for item in parts],
        [(shape, jnp.float32, shape, None)],
        after=after,
    )[0]


def plain_kernel(value_ref, out_ref, skip_ref):
    taps, width = value_ref.shape[0] - 1, value_ref.shape[2]
    for tap in range(taps):
        out_ref[:, tap * width : (tap + 1) * width] = value_ref[tap].astype(jnp.float32)
    skip_ref[...] = value_ref[taps].astype(jnp.float32)


def plain_sum(values, after):
    taps, rows, width = values.shape
    shapes = ((rows, (taps - 1) * width), (rows, width))
    return call(
        plain_kernel,
        "plain_sum",
        (),
        [whole(values)],
        [(shape, jnp.float32, shape, None) for shape in shapes],
        after=after,
    )


def text_pairs(back):
    rounds = ([], [])
    for y, c, z, x in every_place():
        piece, plane = 2 * z + x, 2 * c + y
        for half in range(2):
            member = 2 * (piece % 4) + half
            target = flat_device(member // 2 % 2, member // 4, plane, member % 2)
            pair = (flat_device(y, c, z, x), target)
            rounds[half ^ (piece // 4)].append(pair[::-1] if back else pair)
    return rounds


def text_to_heads(text_slice):
    late = (2 * lax.axis_index("z") + lax.axis_index("x")) // 4
    halves = (text_slice[:, :OWN], text_slice[:, OWN:])
    first, second = (
        lax.ppermute(jnp.where(late == at, halves[0], halves[1]), EVERY, text_pairs(False)[at])
        for at in range(2)
    )
    even = lax.axis_index("x") == 0
    return jnp.where(even, first, second), jnp.where(even, second, first)


def text_from_heads(text_keys, text_values):
    even = lax.axis_index("x") == 0
    first = jnp.where(even, text_keys, text_values)
    second = jnp.where(even, text_values, text_keys)
    first, second = (
        lax.ppermute(item, EVERY, text_pairs(True)[at]) for at, item in enumerate((first, second))
    )
    late = (2 * lax.axis_index("z") + lax.axis_index("x")) // 4 == 1
    return jnp.concatenate(
        [jnp.where(late, second, first), jnp.where(late, first, second)], axis=1
    )


def text_lanes(values, *columns):
    padded = jnp.pad(values, ((0, TEXT_PAD - values.shape[0]), (0, 0)))
    heads = jnp.transpose(padded.reshape(TEXT_PAD, 2, HEAD_DIM), (1, 0, 2))
    extra = [
        jnp.broadcast_to(jnp.asarray(column, jnp.bfloat16).reshape(1, -1, 1), (2, TEXT_PAD, 1))
        for column in columns
    ]
    joined = jnp.concatenate([heads] + extra, axis=2)
    return jnp.pad(joined, ((0, 0), (0, 0), (0, LANES - joined.shape[2])))


def plane_shards(
    image,
    mask,
    timestep,
    pooled,
    text,
    text_mask,
    cotangent,
    conv1_weight,
    conv2_weight,
    skip_weight,
    emb_weight,
    qkv_weight,
    out_weight,
    text_weight,
    gn1_gain,
    gn1_bias,
    emb_bias,
    gn2_gain,
    gn2_bias,
    skip_bias,
    gn3_gain,
    gn3_bias,
    out_bias,
):
    z_here, x_here = lax.axis_index("z"), lax.axis_index("x")
    a_here = lax.axis_index(("y", "core"))
    member = lax.axis_index(PLANE)
    member_word = member.reshape(1).astype(jnp.int32)
    device = lax.axis_index(EVERY)

    extents = jnp.stack([timestep[0], jnp.sum(mask[0, :, 0]), jnp.sum(mask[0, 0]), jnp.sum(text_mask)])
    exact = jnp.concatenate([pooled[0], extents.astype(jnp.float32)])

    def both(values, axis):
        other = lax.ppermute(values, axis, SWITCH)
        low = lax.axis_index(axis) == 0
        return jnp.stack([jnp.where(low, values, other), jnp.where(low, other, values)])

    image_halves = [
        swapped(half) for half in jnp.split(image[0].reshape(CHUNK, C_IN), 2, axis=0)
    ]
    exact = passed(both(exact, "y"), (image_halves[0],))
    exact = both(exact, "core").reshape(PLANES, -1)
    extents = exact[:, EMB:]
    valid_rows, valid_columns, text_count = extents[z_here, 1:]
    count = valid_rows * valid_columns
    pixel = lax.broadcasted_iota(jnp.int32, (PIXELS, OWN), 0).astype(jnp.float32)
    pixel_row = jnp.floor(pixel / WIDTH)
    valid = (pixel_row < valid_rows) & (pixel - pixel_row * WIDTH < valid_columns)
    valid = valid.astype(jnp.bfloat16)
    half_width = EMB // 2
    frequency = jnp.exp(-math.log(10000.0) * jnp.arange(half_width, dtype=jnp.float32) / half_width)
    angles = extents[:, :1] * frequency[None, :]
    embedding = rounded(
        jax.nn.silu(jnp.concatenate([jnp.cos(angles), jnp.sin(angles)], axis=1) + exact[:, :EMB])
    )
    rest = project(embedding, emb_weight) + emb_bias.astype(jnp.float32)

    rows_here = conv1_weight.shape[0]
    places, targets, sources = (jnp.array(table, jnp.int32) for table in unit_tables())
    places = lax.dynamic_slice(places, (z_here, member, 0), (1, 1, SLOTS)).reshape(-1)
    targets = lax.dynamic_slice_in_dim(targets, member, 1, 1).reshape(-1)
    sources = lax.dynamic_index_in_dim(sources, device, 0, keepdims=False)

    from_y = lax.ppermute(text_weight, "y", SWITCH)
    text_pieces = (text_weight, lax.ppermute(text_weight, "core", SWITCH), from_y)
    text_pieces += (lax.ppermute(from_y, "core", SWITCH),)
    text_len = text.shape[1]
    text_blocks = text[0].reshape(text_len, PLANES, -1)
    text_slice = rounded(
        sum(
            jnp.dot(
                lax.dynamic_index_in_dim(text_blocks, a_here ^ distance, 1, keepdims=False),
                piece,
                preferred_element_type=jnp.float32,
            )
            for distance, piece in enumerate(text_pieces)
        )
    )
    text_keys, text_values = text_to_heads(text_slice)
    text_bias = jnp.where(jnp.arange(TEXT_PAD) < text_count, 0.0, neg_big)
    minus = -jnp.ones((TEXT_PAD,), jnp.float32)
    text_keys = text_lanes(text_keys, text_bias, minus, minus, minus)
    text_values = text_lanes(text_values, -minus, minus, minus, minus)

    parts = []
    for _ in range(3):
        part = lax.reduce_precision(rest, 8, 7)
        parts.append(rounded(part).reshape(-1))
        rest = rest - part
    vectors = (
        gn1_gain,
        gn1_bias,
        gn2_gain,
        gn2_bias,
        skip_bias,
        gn3_gain,
        gn3_bias,
        out_bias,
    )
    packed = jnp.concatenate(list(vectors) + parts)
    image_block = jnp.concatenate(image_halves, axis=0)
    filled = -packed.shape[0] % (4 * C_IN) + packed.shape[0]
    packed = jnp.pad(packed, (0, filled - packed.shape[0])).reshape(-1, LANES)
    packed = gather_z(passed(packed, (image_halves[1],)))
    image_blocks = plane_gather(
        jnp.concatenate(image_halves + [packed.reshape(-1, C_IN)], axis=0),
        (text_keys, text_values),
    )
    small = jnp.stack([block[CHUNK:].reshape(PLANES, filled) for block in image_blocks])
    distances = jnp.arange(MEMBERS)[:, None] ^ member
    chosen = distances == jnp.arange(MEMBERS)[None, :]
    small = jnp.sum(
        jnp.where(chosen[:, :, None, None], small[None].astype(jnp.float32), 0.0), axis=1
    )
    small = jnp.transpose(small.reshape(2, 2, ACROSS, PLANES, filled), (1, 0, 3, 2, 4))
    small = small.reshape(PLANES, PLANES, ACROSS, filled)
    bounds = [0]
    for item in vectors:
        bounds.append(bounds[-1] + item.shape[0])
    small_parts = [small[..., bounds[at] : bounds[at + 1]] for at in range(len(vectors))]
    gain_one, bias_one = (part.reshape(-1) for part in small_parts[:2])
    out_shift = small_parts[7].reshape(1, C)
    own_parts = [own_channels(part).reshape(-1) for part in small_parts[2:7]]
    gain_two, bias_two, skip_shift, gain_three, bias_three = own_parts
    emb_rows = emb_weight.shape[0]
    mods = small[..., bounds[-1] : bounds[-1] + 3 * PLANES * emb_rows]
    mods = mods.reshape(PLANES * MEMBERS, 3, PLANES, emb_rows)
    mods = lax.dynamic_index_in_dim(mods, z_here, 2, keepdims=False)
    mods = ((mods[:, 0] + mods[:, 1]) + mods[:, 2]).reshape(2, PLANES, PLANES, ACROSS, -1)
    scale_own = 1.0 + own_channels(mods[0]).reshape(-1)
    shift_own = own_channels(mods[1]).reshape(-1)

    conv1_raw = jnp.concatenate([conv1_weight, skip_weight], axis=1)
    conv1_raw = lax.all_gather(passed(conv1_raw, (image_halves[1],)), "z", axis=0, tiled=True)
    cot_rows = swapped(cotangent[0].reshape(CHUNK, C))
    conv2_own = conv2_blocks(
        lax.all_gather(conv2_weight, "z", axis=0, tiled=True), (cot_rows,)
    )
    qkv_units = lax.all_gather(qkv_weight.reshape(3, rows_here, C), PLANE, axis=0, tiled=True)
    qkv_chosen = choose_units(places, qkv_units)
    qkv_units = lax.all_gather(qkv_chosen, "z", axis=0, tiled=False)
    qkv_own = qkv_blocks(targets, qkv_units, ())

    per_group, first_width = C // GROUPS, C_IN // GROUPS
    own = jnp.stack(
        [gain_two, bias_two, scale_own, shift_own, gain_three, bias_three, skip_shift, skip_shift]
        + [jnp.broadcast_to(1.0 / (count * per_group), (OWN,))]
        + [jnp.zeros((OWN,), jnp.float32)] * 7
    )
    full = jnp.stack(
        [gain_one, bias_one, jnp.broadcast_to(1.0 / (count * first_width), (C_IN,))]
        + [jnp.zeros((C_IN,), jnp.float32)] * 5
    )

    def exchange(blocks):
        return lax.all_to_all(blocks, PLANE, split_axis=0, concat_axis=0, tiled=True)

    out_all = lax.all_gather(out_weight, EVERY, axis=0, tiled=True)
    cot_ready = cot_blocks(cot_rows, out_all)

    image_all, first_act, second_normed, second_act, conv1_own, first_stats, second_stats = first_layer(
        member_word, image_blocks, valid, conv1_raw, full, own, ()
    )
    second_pieces = plane_gather(second_act, (conv2_own, qkv_chosen))
    third_normed, attn_input, residual_low, third_stats = second_layer(
        member_word, second_pieces, image_all, valid, conv2_own, conv1_raw, own, ()
    )

    attn_pieces = plane_gather(attn_input, (qkv_own,))

    queries, keys, values, cot_passed = project_qkv(
        member_word, attn_pieces, valid, qkv_own, cot_ready
    )
    cot_moved = exchange(cot_passed)
    cot_own, grad_mixed = cot_moved[:, :, :OWN], cot_moved[:, :, OWN:].reshape(PIXELS, OWN)

    attended, mixed, back_queries = attend(
        queries, residual_low, keys, values, text_keys, text_values
    )

    moved = exchange(mixed.reshape(MEMBERS, CHUNK, 2 * OWN))

    triple_grads = attend_back(
        back_queries, grad_mixed, attended, keys, values, text_keys, text_values
    )
    triple_grads, (text_dk, text_dv) = triple_grads[:3], triple_grads[3:]

    third_terms = qkv_back(member_word, triple_grads, qkv_own, (moved,))
    grad_third, third_tokens = plane_sum(third_terms)
    qkv_terms = qkv_grad(member_word, targets, triple_grads, attn_pieces, third_tokens[1:])
    qkv_sums = lax.psum_scatter(qkv_terms, "z", scatter_dimension=0, tiled=True)[0]

    output, out_grad = output_rows(moved, out_all, cot_rows, out_shift, third_tokens[1:])
    out_terms = out_grad
    out_grad = lax.psum_scatter(out_grad, PLANE, scatter_dimension=0, tiled=True)[0]

    text_grads = text_from_heads(text_dk[:text_len], text_dv[:text_len])
    text_terms = rounded(weight_grad(text[0], text_grads))
    text_weight_grad = lax.psum_scatter(
        text_terms, ("y", "core"), scatter_dimension=0, tiled=True
    )

    third = third_back(
        member_word,
        grad_third,
        third_normed,
        cot_own,
        valid,
        third_stats,
        own,
        conv2_own,
        (qkv_terms, out_terms, text_terms),
    )
    second_terms, (dres, residual_taps, third_sums) = third[:MEMBERS], third[MEMBERS:]
    conv2_terms = []

    def second_filler(early):
        conv2_terms.append(tap_grad(member_word, residual_taps, second_pieces, (), early))
        return conv2_terms

    grad_second, second_tokens = plane_sum(second_terms, second_filler)
    (conv2_terms,) = conv2_terms
    conv2_parts, conv2_sent = along_z(conv2_terms)

    qkv_sums = passed(qkv_sums, second_tokens[1:])
    out_grad = passed(out_grad, second_tokens[1:])
    out_grad = lax.psum_scatter(out_grad, "z", scatter_dimension=0, tiled=True)

    output = swapped(passed(output, second_tokens[1:]))

    image_terms, hidden_taps, second_sums, first_sums = second_back(
        member_word,
        grad_second,
        second_normed,
        dres,
        valid,
        second_stats,
        own,
        conv1_own,
        conv1_raw,
        image_all,
        first_stats,
        (conv2_sent,),
    )
    image_part, image_tokens = plane_sum([image_terms[distance] for distance in range(MEMBERS)])
    conv1_parts = tap_grad(
        member_word, hidden_taps, [first_act], (dres, image_all), (output, qkv_sums, conv2_parts[2])
    )
    image_part = sum(item.astype(jnp.float32) for item in image_part)
    qkv_sums = lax.all_gather(qkv_sums, PLANE, axis=0, tiled=True)
    conv1_sums = lax.psum_scatter(conv1_parts, "z", scatter_dimension=0, tiled=True)[0, 0]
    conv1_grad, skip_grad = plain_sum(conv1_sums, image_tokens[1:])
    conv2_grad = natural_sum(conv2_parts, image_tokens[1:])

    out_weight_grad = widened(out_grad, image_tokens[1:])
    text_weight_grad = widened(text_weight_grad, image_tokens[1:])

    own_all = small_gather(jnp.concatenate([second_sums[:4], third_sums[:4]], axis=0))
    own_all = own_all.reshape(PLANES, PLANES, ACROSS, 8, PLANES, OWN // PLANES)
    mods_grad = jnp.transpose(own_all[:, :, :, :2], (1, 3, 0, 4, 2, 5)).reshape(PLANES, 2 * C)
    mods_grad = lax.dynamic_slice_in_dim(mods_grad, device * emb_rows, emb_rows, 1)
    emb_weight_grad = jnp.dot(
        mods_grad.T, embedding.astype(jnp.float32), precision=lax.Precision.HIGHEST
    )
    emb_bias_grad = jnp.sum(mods_grad, axis=0)
    channel_sums = jnp.sum(own_all, axis=1)
    channel_sums = lax.dynamic_index_in_dim(channel_sums, a_here, 0, keepdims=False)
    channel_sums = lax.dynamic_index_in_dim(channel_sums, x_here, 0, keepdims=False)
    channel_sums = lax.dynamic_index_in_dim(channel_sums, z_here, 1, keepdims=False)

    first_here = first_sums[:2]
    for axis in PLANE:
        first_here = first_here + lax.ppermute(first_here, axis, SWITCH)
    grouped = jnp.sum((first_here * gain_one).reshape(2, GROUPS, first_width), axis=2)
    grouped = jnp.repeat(grouped / (count * first_width), first_width, axis=1)
    row_valid = lax.dynamic_slice_in_dim(valid[:, :1], member * CHUNK, CHUNK, 0)
    rows_normed = (image_block.astype(jnp.float32) - first_stats[0]) * first_stats[1]
    image_grad = image_part - row_valid.astype(jnp.float32) * first_stats[1] * (
        grouped[1] + rows_normed * grouped[0]
    )
    image_grad = rounded(image_grad)
    qkv_weight_grad = qkv_finish(sources, qkv_sums, (image_grad,))
    image_grad = swapped(image_grad).astype(jnp.float32).reshape(1, -1, WIDTH, C_IN)
    first_grads = lax.dynamic_slice_in_dim(
        sum(turns_z(first_here)), device * first_width, first_width, 1
    )
    return (
        output.reshape(1, -1, WIDTH, C),
        image_grad,
        conv1_grad,
        conv2_grad,
        skip_grad,
        emb_weight_grad,
        qkv_weight_grad,
        out_weight_grad,
        text_weight_grad,
        first_grads[0],
        first_grads[1],
        emb_bias_grad,
        channel_sums[2],
        channel_sums[3],
        channel_sums[6],
        channel_sums[4],
        channel_sums[5],
        channel_sums[7],
    )


def solution(mesh):
    in_specs = (
        P("img", "ha", None, None),
        P("img", None, None),
        P("img"),
        P("img", None),
        P("img", None, None),
        P("img", None),
        P("img", "ha", None, None),
        P(("img", "ha"), None),
        P(("img", "ha"), None),
        P(("img", "ha"), None),
        P(("img", "ha"), None),
        P(("img", "ha"), None),
        P(("img", "ha"), None),
        P("img", "ha"),
        P(("img", "ha")),
        P(("img", "ha")),
        P(("img", "ha")),
        P(("img", "ha")),
        P(("img", "ha")),
        P(("img", "ha")),
        P(("img", "ha")),
        P(("img", "ha")),
        P(("img", "ha")),
    )
    out_specs = (
        P("img", "ha", None, None),
        P("img", "ha", None, None),
        P(("img", "ha"), None),
        P(("img", "ha"), None),
        P(("img", "ha"), None),
        P(("img", "ha"), None),
        P(("img", "ha"), None),
        P(("img", "ha"), None),
        P("img", "ha"),
        P(("img", "ha")),
        P(("img", "ha")),
        P(("img", "ha")),
        P(("img", "ha")),
        P(("img", "ha")),
        P(("img", "ha")),
        P(("img", "ha")),
        P(("img", "ha")),
        P(("img", "ha")),
    )
    split_mesh = plane_mesh(mesh)
    if split_mesh is None:
        return jax.shard_map(
            shards, mesh=mesh, in_specs=in_specs, out_specs=out_specs, check_vma=False
        )
    in_specs, out_specs = (tuple(split_spec(item) for item in specs) for specs in (in_specs, out_specs))
    return jax.shard_map(
        plane_shards, mesh=split_mesh, in_specs=in_specs, out_specs=out_specs, check_vma=False
    )
```

```python
import functools
import math

import jax
import jax.numpy as jnp
from jax import lax
from jax.experimental import pallas as pl
from jax.experimental.pallas import tpu as pltpu
from jax.sharding import Mesh
from jax.sharding import PartitionSpec as P

C_IN = 512
C = 1024
HEADS = 16
HEAD_DIM = 64
GROUPS = 32
EMB = 1024
HEIGHT = 64
WIDTH = 64


neg_big = -1e30
eps_norm = 1e-05


def extended(cells, sides, width):
    for axis, dim in sides:
        count = lax.axis_size(axis)
        ends = count - 1
        head = lax.slice_in_dim(cells, 0, width, axis=dim)
        tail = lax.slice_in_dim(cells, cells.shape[dim] - width, cells.shape[dim], axis=dim)
        cells = jnp.concatenate(
            [
                lax.ppermute(tail, axis, [(i, (i + 1) % count) for i in range(ends)]),
                cells,
                lax.ppermute(head, axis, [((i + 1) % count, i) for i in range(ends)]),
            ],
            axis=dim,
        )
    return cells


def rounded(values):
    return values.astype(jnp.bfloat16)


def silu_slope(inputs):
    sigmoid = jax.nn.sigmoid(inputs)
    return sigmoid * (1.0 + inputs * (1.0 - sigmoid))


def group_view(features):
    return features.reshape(
        features.shape[0], features.shape[1], GROUPS, features.shape[2] // GROUPS
    )


def group_totals(first_sum, second_sum):
    return lax.psum((first_sum, second_sum), "ha")


def norm_stats(features, validity, counts):
    shaped = group_view(features)
    masked = shaped * validity[:, :, None, None]
    first_sum, second_sum = group_totals(
        jnp.sum(masked, axis=(1, 3)), jnp.sum(masked * shaped, axis=(1, 3))
    )
    entries = counts[:, None] * shaped.shape[3]
    group_mean = first_sum / entries
    inv_std = lax.rsqrt(second_sum / entries - group_mean * group_mean + eps_norm)
    return (group_mean, inv_std)


def normalize(features, group_mean, inv_std):
    shaped = group_view(features)
    normed = (shaped - group_mean[:, None, :, None]) * inv_std[:, None, :, None]
    return normed.reshape(features.shape)


def norm_back(grad_normed, normed, validity, counts, inv_std):
    grad_shaped = group_view(grad_normed)
    norm_shaped = group_view(normed)
    first_sum, second_sum = group_totals(
        jnp.sum(grad_shaped, axis=(1, 3)), jnp.sum(grad_shaped * norm_shaped, axis=(1, 3))
    )
    entries = counts[:, None] * grad_shaped.shape[3]
    correction = (
        first_sum[:, None, :, None] + norm_shaped * second_sum[:, None, :, None]
    ) / entries[:, None, :, None]
    result = (grad_shaped - validity[:, :, None, None] * correction) * inv_std[:, None, :, None]
    return result.reshape(grad_normed.shape)


def conv_columns(features):
    padded = extended(features, (("ha", 1),), 1)
    padded = jnp.pad(padded, ((0, 0), (0, 0), (1, 1), (0, 0)))
    batch_size, row_count, col_count, channels = features.shape
    taps = [
        padded[:, row_off : row_off + row_count, col_off : col_off + col_count]
        for row_off in range(3)
        for col_off in range(3)
    ]
    return jnp.concatenate(taps, axis=-1).reshape(batch_size * row_count * col_count, 9 * channels)


def project(inputs, weight):
    return lax.dot_general(
        inputs, weight, (((1,), (1,)), ((), ())), preferred_element_type=jnp.float32
    )


def weight_grad(grads, inputs):
    return lax.dot_general(
        grads, inputs, (((0,), (0,)), ((), ())), preferred_element_type=jnp.float32
    )


def back_project(grads, weight):
    return jnp.dot(grads, weight, preferred_element_type=jnp.float32)


def flipped(weight, in_channels):
    out_channels = weight.shape[0]
    taps = weight.reshape(out_channels, 3, 3, in_channels)[:, ::-1, ::-1, :]
    return jnp.transpose(taps, (1, 2, 0, 3)).reshape(9 * out_channels, in_channels)


def split_heads(values):
    return values.reshape(values.shape[0], values.shape[1], HEADS, HEAD_DIM)


def score_block(head_queries, head_keys, valid_block):
    raw = jnp.einsum(
        "bqhd,bkhd->bhqk", head_queries, head_keys, preferred_element_type=jnp.float32
    ) * (1.0 / math.sqrt(HEAD_DIM))
    return jnp.where(valid_block[:, None, None, :] > 0, raw, neg_big)


def absorb(running, head_queries, pairs, valid_block):
    highest, totals, accumulated = running
    head_keys = split_heads(pairs[:, :, :C])
    head_values = split_heads(pairs[:, :, C:])
    scores = score_block(head_queries, head_keys, valid_block)
    new_high = jnp.maximum(highest, jnp.max(scores, axis=-1))
    weights = jnp.exp(scores - new_high[..., None])
    decay = jnp.exp(highest - new_high)
    totals = totals * decay + jnp.sum(weights, axis=-1)
    update = jnp.einsum(
        "bhqk,bkhd->bqhd", rounded(weights), head_values, preferred_element_type=jnp.float32
    )
    accumulated = accumulated * jnp.transpose(decay, (0, 2, 1))[..., None] + update
    return (new_high, totals, accumulated)


def back_block(grad_query, head_queries, grad_mixed, log_total, delta, pairs, valid_block):
    head_keys = split_heads(pairs[:, :, :C])
    head_values = split_heads(pairs[:, :, C:])
    scores = score_block(head_queries, head_keys, valid_block)
    probs = jnp.exp(scores - log_total[..., None])
    grad_values = jnp.einsum(
        "bhqk,bqhd->bkhd", rounded(probs), grad_mixed, preferred_element_type=jnp.float32
    )
    grad_probs = jnp.einsum(
        "bqhd,bkhd->bhqk", grad_mixed, head_values, preferred_element_type=jnp.float32
    )
    grad_scores = rounded(probs * (grad_probs - delta[..., None]))
    scale_factor = 1.0 / math.sqrt(HEAD_DIM)
    grad_query = (
        grad_query
        + jnp.einsum("bhqk,bkhd->bqhd", grad_scores, head_keys, preferred_element_type=jnp.float32)
        * scale_factor
    )
    grad_keys = (
        jnp.einsum("bhqk,bqhd->bkhd", grad_scores, head_queries, preferred_element_type=jnp.float32)
        * scale_factor
    )
    batch_size, key_count = (pairs.shape[0], pairs.shape[1])
    grad_pairs = jnp.concatenate(
        [
            grad_keys.reshape(batch_size, key_count, C),
            grad_values.reshape(batch_size, key_count, C),
        ],
        axis=2,
    )
    return (grad_query, grad_pairs)


def over_blocks(block_fn, running, pairs, validity):
    key_count = pairs.shape[1]
    block_len = 512

    def over_advance(block_index, carried):
        offset = block_index * block_len
        return block_fn(
            carried,
            lax.dynamic_slice_in_dim(pairs, offset, block_len, 1),
            lax.dynamic_slice_in_dim(validity, offset, block_len, 1),
        )

    return lax.fori_loop(0, key_count // block_len, over_advance, running)


def shards(
    image,
    mask,
    timestep,
    pooled,
    text,
    text_mask,
    cotangent,
    conv1_weight,
    conv2_weight,
    skip_weight,
    emb_weight,
    qkv_weight,
    out_weight,
    text_weight,
    gn1_gain,
    gn1_bias,
    emb_bias,
    gn2_gain,
    gn2_bias,
    skip_bias,
    gn3_gain,
    gn3_bias,
    out_bias,
):
    batch_size, row_count, col_count = (image.shape[0], image.shape[1], image.shape[2])
    pixel_count = row_count * col_count
    gathered = (
        lax.all_gather(conv1_weight, ("img", "ha"), axis=0, tiled=True),
        lax.all_gather(conv2_weight, ("img", "ha"), axis=0, tiled=True),
        lax.all_gather(skip_weight, ("img", "ha"), axis=0, tiled=True),
        lax.all_gather(emb_weight, ("img", "ha"), axis=0, tiled=True),
        lax.all_gather(qkv_weight, ("img", "ha"), axis=0, tiled=True),
        lax.all_gather(out_weight, ("img", "ha"), axis=0, tiled=True),
        lax.all_gather(gn1_gain, ("img", "ha"), axis=0, tiled=True),
        lax.all_gather(gn1_bias, ("img", "ha"), axis=0, tiled=True),
        lax.all_gather(emb_bias, ("img", "ha"), axis=0, tiled=True),
        lax.all_gather(gn2_gain, ("img", "ha"), axis=0, tiled=True),
        lax.all_gather(gn2_bias, ("img", "ha"), axis=0, tiled=True),
        lax.all_gather(skip_bias, ("img", "ha"), axis=0, tiled=True),
        lax.all_gather(gn3_gain, ("img", "ha"), axis=0, tiled=True),
        lax.all_gather(gn3_bias, ("img", "ha"), axis=0, tiled=True),
        lax.all_gather(out_bias, ("img", "ha"), axis=0, tiled=True),
    )
    conv1_full, conv2_full, skip_full, emb_full, qkv_full, out_full = gathered[:6]
    (
        gain_one,
        bias_one,
        emb_shift,
        gain_two,
        bias_two,
        skip_shift,
        gain_three,
        bias_three,
        out_shift,
    ) = (item.astype(jnp.float32) for item in gathered[6:])
    full_valid = mask.reshape(batch_size, HEIGHT * WIDTH).astype(jnp.float32)
    counts = jnp.sum(full_valid, axis=1)
    local_mask = lax.dynamic_slice_in_dim(mask, lax.axis_index("ha") * row_count, row_count, 1)
    validity = local_mask.reshape(batch_size, pixel_count).astype(jnp.float32)
    half_width = EMB // 2
    frequency = jnp.exp(-math.log(10000.0) * jnp.arange(half_width, dtype=jnp.float32) / half_width)
    angles = timestep.astype(jnp.float32)[:, None] * frequency[None, :]
    embedding = rounded(
        jax.nn.silu(jnp.concatenate([jnp.cos(angles), jnp.sin(angles)], axis=1) + pooled)
    )
    modulation = project(embedding, emb_full) + emb_shift
    scale_rows = 1.0 + modulation[:, None, :C]
    shift_rows = modulation[:, None, C:]
    image_flat = image.reshape(batch_size, pixel_count, C_IN)
    image_wide = image_flat.astype(jnp.float32)

    def front(known):
        fresh = known is None
        first_mean, first_std = norm_stats(image_wide, validity, counts) if fresh else known[0]
        first_normed = normalize(image_wide, first_mean, first_std)
        first_pre = first_normed * gain_one + bias_one
        first_act = rounded(jax.nn.silu(first_pre) * validity[:, :, None])
        first_columns = conv_columns(first_act.reshape(batch_size, row_count, col_count, C_IN))
        hidden_one = project(first_columns, conv1_full).reshape(batch_size, pixel_count, C)
        second_mean, second_std = norm_stats(hidden_one, validity, counts) if fresh else known[1]
        second_normed = normalize(hidden_one, second_mean, second_std)
        second_shifted = second_normed * gain_two + bias_two
        second_pre = second_shifted * scale_rows + shift_rows
        second_act = rounded(jax.nn.silu(second_pre) * validity[:, :, None])
        second_columns = conv_columns(second_act.reshape(batch_size, row_count, col_count, C))
        stats = ((first_mean, first_std), (second_mean, second_std))
        return (
            stats,
            (
                first_normed,
                first_pre,
                first_columns,
                second_normed,
                second_shifted,
                second_pre,
                second_columns,
            ),
        )

    stats, saved = front(None)
    residual = (
        project(saved[6], conv2_full) + project(image_flat.reshape(-1, C_IN), skip_full)
    ).reshape(batch_size, pixel_count, C) + skip_shift
    third_mean, third_std = norm_stats(residual, validity, counts)
    third_normed = normalize(residual, third_mean, third_std)
    attn_input = rounded(third_normed * gain_three + bias_three)
    triple = rounded(project(attn_input.reshape(-1, C), qkv_full)).reshape(
        batch_size, pixel_count, 3 * C
    )
    head_queries = split_heads(triple[:, :, :C])
    local_pairs = triple[:, :, C:]
    text_piece = lax.all_gather(text_weight, "img", axis=0, tiled=True)
    text_slice = rounded(
        jnp.einsum("blt,tc->blc", text, text_piece, preferred_element_type=jnp.float32)
    )
    text_pairs = lax.all_gather(text_slice, "ha", axis=2, tiled=True)
    text_valid = text_mask.astype(jnp.float32)

    def absorb_here(carried, pairs, valid_block):
        return absorb(carried, head_queries, pairs, valid_block)

    running = (
        jnp.full((batch_size, HEADS, pixel_count), neg_big, jnp.float32),
        jnp.zeros((batch_size, HEADS, pixel_count), jnp.float32),
        jnp.zeros((batch_size, pixel_count, HEADS, HEAD_DIM), jnp.float32),
    )
    running = absorb_here(running, text_pairs, text_valid)
    valid_block = full_valid
    running = over_blocks(
        absorb_here, running, lax.all_gather(local_pairs, "ha", axis=1, tiled=True), valid_block
    )
    highest, totals, accumulated = running
    attended = accumulated / jnp.transpose(totals, (0, 2, 1))[..., None]
    log_total = highest + jnp.log(totals)
    mixed_rows = rounded(attended.reshape(-1, C))
    output = residual.reshape(-1, C) + project(mixed_rows, out_full) + out_shift
    output = rounded(output).reshape(batch_size, row_count, col_count, C)
    cot_rows = cotangent.reshape(-1, C)
    out_weight_grad = weight_grad(cot_rows, mixed_rows)
    out_bias_grad = jnp.sum(cot_rows.astype(jnp.float32), axis=0)
    grad_mixed = split_heads(
        rounded(back_project(cot_rows, out_full)).reshape(batch_size, pixel_count, C)
    )
    delta = jnp.transpose(jnp.sum(grad_mixed.astype(jnp.float32) * attended, axis=-1), (0, 2, 1))

    def back_here(grad_query, pairs, valid_block):
        return back_block(
            grad_query, head_queries, grad_mixed, log_total, delta, pairs, valid_block
        )

    grad_query = jnp.zeros((batch_size, pixel_count, HEADS, HEAD_DIM), jnp.float32)
    grad_query, text_term = back_here(grad_query, text_pairs, text_valid)
    pixel_pairs = lax.all_gather(local_pairs, "ha", axis=1, tiled=True)
    key_count = pixel_pairs.shape[1]
    block_len = 512

    def body_advance(block_index, carried):
        query_grad, term_now = carried
        offset = block_index * block_len
        query_grad, grad_pairs = back_here(
            query_grad,
            lax.dynamic_slice_in_dim(pixel_pairs, offset, block_len, 1),
            lax.dynamic_slice_in_dim(full_valid, offset, block_len, 1),
        )
        return (query_grad, lax.dynamic_update_slice_in_dim(term_now, grad_pairs, offset, 1))

    key_term = jnp.zeros((batch_size, key_count, 2 * C), jnp.float32)
    grad_query, key_term = lax.fori_loop(
        0, key_count // block_len, body_advance, (grad_query, key_term)
    )
    pair_grads = rounded(
        lax.psum_scatter(
            key_term.astype(jnp.bfloat16), "ha", scatter_dimension=1, tiled=True
        ).astype(jnp.float32)
    )
    text_grads = rounded(
        lax.psum_scatter(
            text_term.astype(jnp.bfloat16), "ha", scatter_dimension=2, tiled=True
        ).astype(jnp.float32)
    )
    text_weight_grad = lax.psum_scatter(
        jnp.einsum("blt,blc->tc", text, text_grads, preferred_element_type=jnp.float32).astype(
            jnp.bfloat16
        ),
        "img",
        scatter_dimension=0,
        tiled=True,
    ).astype(jnp.float32)
    triple_grads = jnp.concatenate(
        [rounded(grad_query.reshape(batch_size, pixel_count, C)), pair_grads], axis=2
    ).reshape(-1, 3 * C)
    qkv_weight_grad = weight_grad(triple_grads, attn_input.reshape(-1, C))
    grad_third = back_project(triple_grads, qkv_full).reshape(batch_size, pixel_count, C)
    gain_three_grad = jnp.sum(grad_third * third_normed, axis=(0, 1))
    bias_three_grad = jnp.sum(grad_third, axis=(0, 1))
    attn_sums = (
        lax.psum_scatter(qkv_weight_grad, ("img", "ha"), scatter_dimension=0, tiled=True),
        lax.psum_scatter(out_weight_grad, ("img", "ha"), scatter_dimension=0, tiled=True),
        lax.psum_scatter(gain_three_grad, ("img", "ha"), scatter_dimension=0, tiled=True),
        lax.psum_scatter(bias_three_grad, ("img", "ha"), scatter_dimension=0, tiled=True),
        lax.psum_scatter(out_bias_grad, ("img", "ha"), scatter_dimension=0, tiled=True),
    )
    grad_residual = cot_rows.astype(jnp.float32).reshape(batch_size, pixel_count, C) + norm_back(
        grad_third * gain_three, third_normed, validity, counts, third_std
    )
    skip_bias_grad = jnp.sum(grad_residual, axis=(0, 1))
    residual_low = rounded(grad_residual)
    residual_rows = residual_low.reshape(-1, C)
    skip_weight_grad = weight_grad(residual_rows, image_flat.reshape(-1, C_IN))
    image_from_skip = back_project(residual_rows, skip_full)
    unused, kept = front(stats)
    (
        first_normed,
        first_pre,
        first_columns,
        second_normed,
        second_shifted,
        second_pre,
        second_columns,
    ) = kept
    conv2_weight_grad = weight_grad(residual_rows, second_columns)
    grad_second_act = jnp.dot(
        conv_columns(residual_low.reshape(batch_size, row_count, col_count, C)),
        flipped(conv2_full, C),
        preferred_element_type=jnp.float32,
    )
    grad_second_pre = (
        grad_second_act.reshape(batch_size, pixel_count, C)
        * validity[:, :, None]
        * silu_slope(second_pre)
    )
    grad_mods = jnp.concatenate(
        [jnp.sum(grad_second_pre * second_shifted, axis=1), jnp.sum(grad_second_pre, axis=1)],
        axis=1,
    )
    emb_weight_grad = jnp.dot(
        grad_mods.T, embedding.astype(jnp.float32), precision=lax.Precision.HIGHEST
    )
    emb_bias_grad = jnp.sum(grad_mods, axis=0)
    grad_second_shift = grad_second_pre * scale_rows
    gain_two_grad = jnp.sum(grad_second_shift * second_normed, axis=(0, 1))
    bias_two_grad = jnp.sum(grad_second_shift, axis=(0, 1))
    hidden_low = rounded(
        norm_back(grad_second_shift * gain_two, second_normed, validity, counts, stats[1][1])
    )
    conv1_weight_grad = weight_grad(hidden_low.reshape(-1, C), first_columns)
    grad_first_act = jnp.dot(
        conv_columns(hidden_low.reshape(batch_size, row_count, col_count, C)),
        flipped(conv1_full, C_IN),
        preferred_element_type=jnp.float32,
    )
    grad_first_pre = (
        grad_first_act.reshape(batch_size, pixel_count, C_IN)
        * validity[:, :, None]
        * silu_slope(first_pre)
    )
    gain_one_grad = jnp.sum(grad_first_pre * first_normed, axis=(0, 1))
    bias_one_grad = jnp.sum(grad_first_pre, axis=(0, 1))
    image_grad = norm_back(
        grad_first_pre * gain_one, first_normed, validity, counts, stats[0][1]
    ) + image_from_skip.reshape(batch_size, pixel_count, C_IN)
    block_sums = (
        lax.psum_scatter(conv1_weight_grad, ("img", "ha"), scatter_dimension=0, tiled=True),
        lax.psum_scatter(conv2_weight_grad, ("img", "ha"), scatter_dimension=0, tiled=True),
        lax.psum_scatter(skip_weight_grad, ("img", "ha"), scatter_dimension=0, tiled=True),
        lax.psum_scatter(emb_weight_grad, ("img", "ha"), scatter_dimension=0, tiled=True),
        lax.psum_scatter(gain_one_grad, ("img", "ha"), scatter_dimension=0, tiled=True),
        lax.psum_scatter(bias_one_grad, ("img", "ha"), scatter_dimension=0, tiled=True),
        lax.psum_scatter(emb_bias_grad, ("img", "ha"), scatter_dimension=0, tiled=True),
        lax.psum_scatter(gain_two_grad, ("img", "ha"), scatter_dimension=0, tiled=True),
        lax.psum_scatter(bias_two_grad, ("img", "ha"), scatter_dimension=0, tiled=True),
        lax.psum_scatter(skip_bias_grad, ("img", "ha"), scatter_dimension=0, tiled=True),
    )
    return (
        output,
        image_grad.reshape(batch_size, row_count, col_count, C_IN),
        block_sums[0],
        block_sums[1],
        block_sums[2],
        block_sums[3],
        attn_sums[0],
        attn_sums[1],
        text_weight_grad,
        block_sums[4],
        block_sums[5],
        block_sums[6],
        block_sums[7],
        block_sums[8],
        block_sums[9],
        attn_sums[2],
        attn_sums[3],
        attn_sums[4],
    )


EVERY = ("y", "core", "z", "x")
PLANE = ("core", "y", "x")
PLANE_SORTED = ("y", "core", "x")
PLANES = 4
ACROSS = 2
MEMBERS = 8
OWN = C // MEMBERS
LANES = 128
TEXT_PAD = 128
SLOTS = 4
ATTEND_ROWS = 1024
ATTEND_KEYS = 1024
BACK_ROWS = 512
BACK_KEYS = 1024
CHUNK = 512
STEPS = HEIGHT * WIDTH // CHUNK
PIXELS = HEIGHT * WIDTH
TAPS = 9 * OWN
VMEM_BYTES = 56 * 1024 * 1024
SWITCH = ((0, 1), (1, 0))
NT = (((1,), (1,)), ((), ()))
TN = (((0,), (0,)), ((), ()))


def plane_mesh(mesh):
    images, rows = mesh.shape["img"], mesh.shape["ha"]
    if images != PLANES or rows != PLANES * ACROSS:
        return None
    return Mesh(mesh.devices.reshape(PLANES // 2, 2, PLANES, ACROSS), EVERY)


def split_spec(spec):
    names = {"img": ("y", "core"), "ha": ("z", "x")}
    entries = []
    for entry in spec:
        parts = (entry,) if isinstance(entry, str) else (entry or ())
        axes = tuple(axis for part in parts for axis in names[part])
        entries.append(axes or None)
    return P(*entries)


def flat_device(y, core, z, x):
    return ((y * 2 + core) * PLANES + z) * ACROSS + x


def every_place():
    return [(y, c, z, x) for y in range(2) for c in range(2) for z in range(PLANES) for x in range(ACROSS)]


def swapped(values):
    pairs = [
        (flat_device(y, c, z, x), flat_device(z % 2, z // 2, 2 * c + y, x)) for y, c, z, x in every_place()
    ]
    return lax.ppermute(values, EVERY, pairs)


def crossing(first):
    pairs = []
    for place in range(MEMBERS):
        along_x = (place // 2 % 2 == 0) == (first == "x")
        pairs.append((place, place ^ (1 if along_x else 4)))
    return pairs


def by_core(first, second):
    return jnp.where(lax.axis_index("core") == 0, first, second)


def pick_kernel(core_ref, first_ref, second_ref, out_ref):
    out_ref[...] = jnp.where(core_ref[0] == 0, first_ref[...], second_ref[...])


def pick(first, second, after):
    rows, columns = first.shape
    steps = 4 if rows % 64 == 0 else 1
    block = (rows // steps, columns)
    return call(
        pick_kernel,
        "pick",
        (steps,),
        [(lax.axis_index("core").reshape(1), None, None)]
        + [(item, block, row_chunk) for item in (first, second)],
        [(first.shape, first.dtype, block, row_chunk)],
        read=3 * rows * columns * 2,
        after=after,
    )[0]


def plane_gather(piece, after=()):
    from_x = lax.ppermute(piece, "x", SWITCH)
    from_y = lax.ppermute(piece, "y", SWITCH)
    from_core = lax.ppermute(piece, "core", SWITCH)
    from_xy = lax.ppermute(pick(from_x, from_y, after), PLANE_SORTED, crossing("y"))
    near = [piece, from_x, from_y, from_xy]
    far = [from_core] + [lax.ppermute(item, "core", SWITCH) for item in near[1:]]
    return near + far


def added(first, second):
    return rounded(first.astype(jnp.float32) + second.astype(jnp.float32))


def plane_sum(terms, between=None):
    arrived = [lax.ppermute(terms[distance ^ 4], "core", SWITCH) for distance in (3, 1, 2, 0)]
    for_xy = added(terms[3], arrived[0])
    passing = lax.ppermute(for_xy, PLANE_SORTED, crossing("x"))
    for_x, for_y = added(terms[1], arrived[1]), added(terms[2], arrived[2])
    early = by_core(for_x, for_y)
    first = lax.ppermute(early, PLANE_SORTED, crossing("x"))
    second = added(by_core(for_y, for_x), passing)
    if between is not None:
        second = passed(second, between((early, for_xy)))
    mine = added(terms[0], arrived[3])
    return (mine, first, lax.ppermute(second, PLANE_SORTED, crossing("y"))), (early, second)


def small_gather(values):
    def both(item, axis):
        other = lax.ppermute(item, axis, SWITCH)
        low = lax.axis_index(axis) == 0
        return jnp.stack([jnp.where(low, item, other), jnp.where(low, other, item)])

    values = both(values, "x")
    z = lax.axis_index("z")
    turned = [values] + [
        lax.ppermute(values, "z", [(at, (at + turn) % PLANES) for at in range(PLANES)])
        for turn in range(1, PLANES)
    ]
    values = jnp.stack(
        [
            sum(jnp.where((z - at) % PLANES == turn, turned[turn], 0.0) for turn in range(PLANES))
            for at in range(PLANES)
        ]
    )
    values = both(both(values, "core"), "y")
    return values.reshape((PLANES,) + values.shape[2:])


def own_channels(by_device):
    a, x = lax.axis_index(("y", "core")), lax.axis_index("x")
    part = lax.dynamic_index_in_dim(by_device, a, 0, keepdims=False)
    return lax.dynamic_index_in_dim(part, x, 1, keepdims=False)


def to_own_order(values):
    lead = values.shape[:-1]
    shaped = values.reshape(lead + (2, 2, PLANES, ACROSS, -1))
    at = len(lead)
    order = tuple(range(at)) + (at + 1, at, at + 3, at + 2, at + 4)
    return jnp.transpose(shaped, order).reshape(lead + (MEMBERS, OWN))


def to_natural_order(values):
    lead = values.shape[:-2]
    shaped = values.reshape(lead + (2, 2, ACROSS, PLANES, -1))
    at = len(lead)
    order = tuple(range(at)) + (at + 1, at, at + 3, at + 2, at + 4)
    return jnp.transpose(shaped, order).reshape(lead + (C,))


def unit_tables():
    where, rows, back = {}, {}, {}
    for z in range(PLANES):
        for member in range(MEMBERS):
            home = flat_device(member // 2 % 2, member // 4, z, member % 2)
            for place in range(3):
                unit = 3 * home + place
                worker = unit % 32 // 4
                entry = where.setdefault((z, worker), [])
                back[home, place] = worker * SLOTS + len(entry)
                entry.append(3 * member + place)
                rows.setdefault((z, worker), []).append(unit // 32 * OWN + unit % 4 * 32)
    pad = {key: entry + entry[:1] * (SLOTS - len(entry)) for key, entry in where.items()}
    places = [[pad[z, t] for t in range(MEMBERS)] for z in range(PLANES)]
    pad = {key: entry + entry[:1] * (SLOTS - len(entry)) for key, entry in rows.items()}
    targets = [[pad[z, t] for t in range(MEMBERS)] for z in range(PLANES)]
    count = PLANES * MEMBERS
    return places, targets, [[back[home, place] for place in range(3)] for home in range(count)]


def call(kernel, name, grid, operands, outputs, scratch=(), flops=0, read=0, after=()):
    def body(*refs):
        kernel(*refs[len(after) :])

    def spec(shape, index):
        if shape is None:
            return pl.BlockSpec(memory_space=pltpu.SMEM)
        if index is None:
            return pl.BlockSpec(shape, lambda *_: (0,) * len(shape))
        return pl.BlockSpec(shape, index)

    return pl.pallas_call(
        body,
        grid=grid,
        in_specs=[pl.BlockSpec(memory_space=pl.ANY)] * len(after)
        + [spec(shape, index) for _, shape, index in operands],
        out_specs=[spec(shape, index) for _, _, shape, index in outputs],
        out_shape=[jax.ShapeDtypeStruct(full, dtype) for full, dtype, _, _ in outputs],
        scratch_shapes=list(scratch),
        compiler_params=pltpu.CompilerParams(vmem_limit_bytes=VMEM_BYTES),
        cost_estimate=pl.CostEstimate(flops=flops, bytes_accessed=read, transcendentals=0),
        name=name,
    )(*after, *[array for array, _, _ in operands])


def whole(array):
    return (array, array.shape, None)


def row_chunk(step):
    return (step, 0)


def group_matrix(channels, width):
    row = lax.broadcasted_iota(jnp.int32, (channels, channels), 0) // width
    column = lax.broadcasted_iota(jnp.int32, (channels, channels), 1) // width
    return (row == column).astype(jnp.float32)


def group_sums(first, second, width):
    channels = first.shape[1]
    rows = jnp.concatenate([first, second, jnp.zeros((6, channels), jnp.float32)], axis=0)
    sums = jnp.dot(
        rows,
        group_matrix(channels, width),
        precision=lax.Precision.HIGHEST,
        preferred_element_type=jnp.float32,
    )
    return sums[0:1], sums[1:2]


def column_sums(values):
    return jnp.sum(values, axis=0, keepdims=True)


def sigmoid(values):
    return 1.0 / (1.0 + jnp.exp(-values))


def chunk_rows(step):
    if isinstance(step, int):
        return slice(step * CHUNK, (step + 1) * CHUNK)
    return pl.ds(pl.multiple_of(step * CHUNK, CHUNK), CHUNK)


def padded_rows(step, row):
    start = step * CHUNK + (1 + row) * WIDTH
    if isinstance(step, int):
        return slice(start, start + CHUNK)
    return pl.ds(pl.multiple_of(start, WIDTH), CHUNK)


def sideways(values, by):
    place = lax.broadcasted_iota(jnp.int32, values.shape, 0) % WIDTH
    rolled = pltpu.roll(values, by % values.shape[0], 0)
    return jnp.where(place == (0 if by == 1 else WIDTH - 1), 0.0, rolled)


SUMS = (3, PIXELS + 2 * WIDTH + CHUNK, OWN)


def add_taps(sums_ref, products_ref, step):
    for tap in range(9):
        dy, dx = tap // 3, tap % 3
        rows = padded_rows(step + 1, 1 - dy)
        sums_ref[dx, rows, :] += products_ref[:, tap * OWN : (tap + 1) * OWN]


def tap_total(sums_ref, step):
    rows = padded_rows(step + 1, 0)
    return (
        sums_ref[1, rows, :]
        + sideways(sums_ref[0, rows, :], 1)
        + sideways(sums_ref[2, rows, :], -1)
    )


def write_sideways(taps_ref, values_fn):
    for dx in range(3):
        taps_ref[dx, 0:WIDTH, :] = jnp.zeros((WIDTH, OWN), jnp.bfloat16)
        taps_ref[dx, PIXELS + WIDTH :, :] = jnp.zeros((WIDTH, OWN), jnp.bfloat16)

    def advance(step, carried):
        values = values_fn(step)
        rows = padded_rows(step, 0)
        taps_ref[0, rows, :] = sideways(values, -1).astype(jnp.bfloat16)
        taps_ref[1, rows, :] = values.astype(jnp.bfloat16)
        taps_ref[2, rows, :] = sideways(values, 1).astype(jnp.bfloat16)
        return carried

    lax.fori_loop(0, STEPS, advance, 0)


def tap_chunk(taps_ref, step):
    return jnp.concatenate(
        [taps_ref[tap % 3, padded_rows(step, 1 - tap // 3), :] for tap in range(9)], axis=1
    )


def first_kernel(
    member_ref,
    *refs,
):
    blocks, refs = refs[:MEMBERS], refs[MEMBERS:]
    image_ref = refs[4]
    for distance in range(MEMBERS):
        image_ref[chunk_rows(member_ref[0] ^ distance), :] = blocks[distance][:CHUNK]
    first_rows(image_ref, *refs[:4], *refs[5:])


def first_rows(
    image_ref,
    valid_ref,
    raw_ref,
    full_ref,
    own_ref,
    act_ref,
    normed_ref,
    next_ref,
    weight_ref,
    first_ref,
    second_ref,
    sums_ref,
    *products_ref,
):
    for tap in range(9):
        weight_ref[tap * OWN : (tap + 1) * OWN, :] = raw_ref[:, tap * C_IN : (tap + 1) * C_IN]
    zero = jnp.zeros((1, C_IN), jnp.float32)

    def gather_sums(step, carried):
        values = image_ref[chunk_rows(step), :].astype(jnp.float32)
        valid = valid_ref[chunk_rows(step), :].astype(jnp.float32)
        masked = values * jnp.concatenate([valid] * (C_IN // LANES), axis=1)
        return (carried[0] + column_sums(masked), carried[1] + column_sums(masked * values))

    sums = lax.fori_loop(0, STEPS, gather_sums, (zero, zero))
    mean, square = (item * full_ref[2:3] for item in group_sums(*sums, C_IN // GROUPS))
    inv_std = lax.rsqrt(square - mean * mean + eps_norm)
    factor = inv_std * full_ref[0:1]
    offset = full_ref[1:2] - mean * factor
    first_ref[...] = jnp.concatenate(
        [mean, inv_std, factor, offset, jnp.zeros((4, C_IN), jnp.float32)], axis=0
    )
    sums_ref[...] = jnp.zeros_like(sums_ref)

    sums = [jnp.zeros((1, OWN), jnp.float32)] * 2
    for step in range(STEPS + 3):
        if 1 <= step <= STEPS:
            products_ref[step % 2][...] = lax.dot_general(
                act_ref[chunk_rows(step - 1), :],
                weight_ref[...],
                NT,
                preferred_element_type=jnp.float32,
            )
        if 2 <= step <= STEPS + 1:
            add_taps(sums_ref, products_ref[(step - 1) % 2], step - 2)
        if step < STEPS:
            rows = chunk_rows(step)
            values = image_ref[rows, :].astype(jnp.float32) * factor + offset
            valid = valid_ref[rows, :].astype(jnp.float32)
            valid = jnp.concatenate([valid] * (C_IN // LANES), axis=1)
            act_ref[rows, :] = (values * sigmoid(values) * valid).astype(jnp.bfloat16)
        if step >= 3:
            rows = chunk_rows(step - 3)
            values = tap_total(sums_ref, step - 3)
            masked = values * valid_ref[rows, :].astype(jnp.float32)
            normed_ref[rows, :] = values
            sums = [sums[0] + column_sums(masked), sums[1] + column_sums(masked * values)]

    mean, square = (item * own_ref[8:9] for item in group_sums(*sums, C // GROUPS))
    inv_std = lax.rsqrt(square - mean * mean + eps_norm)
    second_ref[...] = jnp.concatenate(
        [mean, inv_std, jnp.zeros((6, OWN), jnp.float32)], axis=0
    )

    def activate(step, carried):
        normed = (normed_ref[chunk_rows(step), :] - mean) * inv_std
        normed_ref[chunk_rows(step), :] = normed
        values = (normed * own_ref[0:1] + own_ref[1:2]) * own_ref[2:3] + own_ref[3:4]
        valid = valid_ref[chunk_rows(step), :].astype(jnp.float32)
        next_ref[chunk_rows(step), :] = (values * sigmoid(values) * valid).astype(jnp.bfloat16)
        return carried

    lax.fori_loop(0, STEPS, activate, 0)


def first_layer(member, blocks, valid, raw, full, own, after):
    return call(
        first_kernel,
        "first_layer",
        (),
        [(member, None, None)]
        + [whole(item) for item in blocks]
        + [whole(valid), whole(raw), whole(full), whole(own)],
        [
            ((PIXELS, C_IN), jnp.bfloat16, (PIXELS, C_IN), None),
            ((PIXELS, C_IN), jnp.bfloat16, (PIXELS, C_IN), None),
            ((PIXELS, OWN), jnp.float32, (PIXELS, OWN), None),
            ((PIXELS, OWN), jnp.bfloat16, (PIXELS, OWN), None),
            ((TAPS, C_IN), jnp.bfloat16, (TAPS, C_IN), None),
            ((8, C_IN), jnp.float32, (8, C_IN), None),
            ((8, OWN), jnp.float32, (8, OWN), None),
        ],
        [pltpu.VMEM(SUMS, jnp.float32)] + [pltpu.VMEM((CHUNK, TAPS), jnp.float32)] * 2,
        flops=2 * PIXELS * TAPS * C_IN,
        read=PIXELS * C_IN * 4,
        after=after,
    )


def near_weights(member_ref, weight_ref, near_ref):
    for distance in range(MEMBERS):
        near_ref[:, distance * OWN : (distance + 1) * OWN] = weight_ref[member_ref[0] ^ distance]


def second_kernel(
    member_ref,
    *refs,
):
    pieces_in, refs = refs[:MEMBERS], refs[MEMBERS:]
    image_ref, valid_ref, weight_ref, skip_ref, own_ref = refs[:5]
    normed_ref, next_ref, low_ref, third_ref, sums_ref, near_ref = refs[5:]
    step = pl.program_id(0)

    @pl.when(step == 0)
    def _():
        sums_ref[...] = jnp.zeros_like(sums_ref)
        near_weights(member_ref, weight_ref, near_ref)

    joined = jnp.concatenate([item[...] for item in pieces_in], axis=1)
    add_taps(
        sums_ref,
        lax.dot_general(joined, near_ref[...], NT, preferred_element_type=jnp.float32),
        step,
    )
    sums_ref[1, padded_rows(step + 1, 0), :] += lax.dot_general(
        image_ref[...], skip_ref[...], NT, preferred_element_type=jnp.float32
    )

    @pl.when(step == STEPS - 1)
    def _():
        zero = jnp.zeros((1, OWN), jnp.float32)

        def settle(at, carried):
            rows = chunk_rows(at)
            values = tap_total(sums_ref, at) + own_ref[6:7]
            masked = values * valid_ref[rows, :].astype(jnp.float32)
            normed_ref[rows, :] = values
            low_ref[rows, :] = values.astype(jnp.bfloat16)
            return (carried[0] + column_sums(masked), carried[1] + column_sums(masked * values))

        sums = lax.fori_loop(0, STEPS, settle, (zero, zero))
        mean, square = (item * own_ref[8:9] for item in group_sums(*sums, C // GROUPS))
        inv_std = lax.rsqrt(square - mean * mean + eps_norm)
        third_ref[...] = jnp.concatenate(
            [mean, inv_std, jnp.zeros((6, OWN), jnp.float32)], axis=0
        )

        def normalize_rows(step, carried):
            normed = (normed_ref[chunk_rows(step), :] - mean) * inv_std
            normed_ref[chunk_rows(step), :] = normed
            next_ref[chunk_rows(step), :] = (normed * own_ref[4:5] + own_ref[5:6]).astype(
                jnp.bfloat16
            )
            return carried

        lax.fori_loop(0, STEPS, normalize_rows, 0)


def skip_block(raw):
    return (raw, (OWN, C_IN), lambda step: (0, 9))


def second_layer(member, pieces_in, image_all, valid, weight, raw, own, after):
    return call(
        second_kernel,
        "second_layer",
        (STEPS,),
        [(member, None, None)]
        + [(item, (CHUNK, OWN), row_chunk) for item in pieces_in]
        + [(image_all, (CHUNK, C_IN), row_chunk)]
        + [whole(valid), whole(weight), skip_block(raw), whole(own)],
        [
            ((PIXELS, OWN), jnp.float32, (PIXELS, OWN), None),
            ((PIXELS, OWN), jnp.bfloat16, (PIXELS, OWN), None),
            ((PIXELS, OWN), jnp.bfloat16, (PIXELS, OWN), None),
            ((8, OWN), jnp.float32, (8, OWN), None),
        ],
        [
            pltpu.VMEM(SUMS, jnp.float32),
            pltpu.VMEM((TAPS, C), jnp.bfloat16),
        ],
        flops=2 * PIXELS * TAPS * C,
        read=PIXELS * C * 4,
        after=after,
    )


def head_columns(values, head):
    return values if head == 0 else pltpu.roll(values, HEAD_DIM, 1)


def beside(values, *columns):
    lane = lax.broadcasted_iota(jnp.int32, values.shape, 1)
    out = jnp.where(lane < HEAD_DIM, values, 0.0)
    for at, column in enumerate(columns):
        out = jnp.where(lane == HEAD_DIM + at, column, out)
    return out


def qkv_kernel(member_ref, *refs):
    pieces_in, refs = refs[:MEMBERS], refs[MEMBERS:]
    valid_ref, weight_ref, cot_ref, q_ref, k_ref, v_ref, rows_ref, near_ref = refs
    rows_ref[...] = cot_ref[...]

    @pl.when(pl.program_id(0) == 0)
    def _():
        near_weights(member_ref, weight_ref, near_ref)

    joined = jnp.concatenate([item[...] for item in pieces_in], axis=1)
    triple = lax.dot_general(joined, near_ref[...], NT, preferred_element_type=jnp.float32)
    queries, keys, values = (triple[:, at * OWN : (at + 1) * OWN] for at in range(3))
    bias = jnp.where(valid_ref[...].astype(jnp.float32) > 0, 0.0, neg_big)
    for head in range(2):
        q_ref[head] = beside(head_columns(queries, head) * (1.0 / math.sqrt(HEAD_DIM)), 1.0).astype(
            jnp.bfloat16
        )
        k_ref[head] = beside(head_columns(keys, head), bias, -1.0, -1.0, -1.0).astype(jnp.bfloat16)
        v_ref[head] = beside(head_columns(values, head), 1.0, -1.0, -1.0, -1.0).astype(jnp.bfloat16)


def project_qkv(member, pieces_in, valid, weight, cots):
    cot_spec = ((1, CHUNK, 2 * OWN), lambda step: (step, 0, 0))
    out = ((2, PIXELS, LANES), jnp.bfloat16, (2, CHUNK, LANES), lambda step: (0, step, 0))
    return call(
        qkv_kernel,
        "project_qkv",
        (STEPS,),
        [(member, None, None)]
        + [(item, (CHUNK, OWN), row_chunk) for item in pieces_in]
        + [(valid, (CHUNK, OWN), row_chunk), whole(weight)]
        + [(cots, *cot_spec)],
        [out] * 3 + [(cots.shape, jnp.bfloat16, *cot_spec)],
        [pltpu.VMEM((3 * OWN, C), jnp.bfloat16)],
        flops=2 * PIXELS * 3 * OWN * C,
        read=PIXELS * C * 4,
    )


def split_float(column):
    parts = []
    for _ in range(3):
        part = column.astype(jnp.bfloat16).astype(jnp.float32)
        parts.append(part)
        column = column - part
    return parts


def attend_kernel(
    q_ref, low_ref, k_ref, v_ref, tk_ref, tv_ref, attn_ref, mixed_ref, back_ref
):
    width = ATTEND_KEYS
    attended = []
    for head in range(2):
        queries = q_ref[head]
        parts = [(tk_ref[head], tv_ref[head])] + [
            (k_ref[head, at : at + width], v_ref[head, at : at + width])
            for at in range(0, PIXELS, width)
        ]
        highest, accumulated = None, None
        for keys, values in parts:
            scores = lax.dot_general(queries, keys, NT, preferred_element_type=jnp.float32)
            top = jnp.max(scores, axis=1, keepdims=True)
            if highest is not None:
                top = jnp.maximum(highest, top)
            weights = jnp.exp(scores - top).astype(jnp.bfloat16)
            update = jnp.dot(weights, values, preferred_element_type=jnp.float32)
            accumulated = (
                update if highest is None else accumulated * jnp.exp(highest - top) + update
            )
            highest = top
        total = accumulated[:, HEAD_DIM : HEAD_DIM + 1]
        attended.append(accumulated / total)
        logs = split_float(highest + jnp.log(total))
        back_ref[head] = beside(queries.astype(jnp.float32), 1.0, *logs).astype(jnp.bfloat16)
    lane = lax.broadcasted_iota(jnp.int32, attended[0].shape, 1)
    both = jnp.where(lane < HEAD_DIM, attended[0], pltpu.roll(attended[1], HEAD_DIM, 1))
    attn_ref[...] = both
    mixed_ref[:, :OWN] = both.astype(jnp.bfloat16)
    mixed_ref[:, OWN:] = low_ref[...]


def attend(queries, low, keys, values, text_keys, text_values):
    block = ATTEND_ROWS
    return call(
        attend_kernel,
        "attend",
        (PIXELS // block,),
        [(queries, (2, block, LANES), lambda step: (0, step, 0)), (low, (block, OWN), row_chunk)]
        + [whole(keys), whole(values), whole(text_keys), whole(text_values)],
        [
            ((PIXELS, OWN), jnp.float32, (block, OWN), row_chunk),
            ((PIXELS, 2 * OWN), jnp.bfloat16, (block, 2 * OWN), row_chunk),
            ((2, PIXELS, LANES), jnp.bfloat16, (2, block, LANES), lambda step: (0, step, 0)),
        ],
        flops=8 * PIXELS * (PIXELS + TEXT_PAD) * LANES,
        read=PIXELS * LANES * 12,
    )


def attend_back_kernel(
    q_ref,
    do_ref,
    attn_ref,
    k_ref,
    v_ref,
    tk_ref,
    tv_ref,
    dq_ref,
    dk_ref,
    dv_ref,
    dtk_ref,
    dtv_ref,
    grads_ref,
    dqt_ref,
):
    step = pl.program_id(0)
    block = BACK_ROWS

    @pl.when(step == 0)
    def _():
        dqt_ref[...] = jnp.zeros_like(dqt_ref)

        def prepare(at, carried):
            grads = do_ref[chunk_rows(at), :].astype(jnp.float32)
            terms = grads * attn_ref[chunk_rows(at), :]
            lane = lax.broadcasted_iota(jnp.int32, terms.shape, 1)
            for head in range(2):
                inside = (lane < HEAD_DIM) == (head == 0)
                delta = jnp.sum(jnp.where(inside, terms, 0.0), axis=1, keepdims=True)
                grads_ref[head, chunk_rows(at), :] = beside(
                    head_columns(grads, head), 0.0, *split_float(delta)
                ).astype(jnp.bfloat16)
            return carried

        lax.fori_loop(0, STEPS, prepare, 0)

    def absorb_keys(head, keys, values):
        keys_across = jnp.transpose(keys.astype(jnp.float32))[:HEAD_DIM].astype(jnp.bfloat16)
        grad_keys, grad_values = None, None
        for start in range(0, PIXELS, block):
            queries = q_ref[head, start : start + block]
            grads = grads_ref[head, start : start + block]
            scores = lax.dot_general(keys, queries, NT, preferred_element_type=jnp.float32)
            grad_probs = lax.dot_general(values, grads, NT, preferred_element_type=jnp.float32)
            probs = jnp.exp(scores)
            grad_scores = (probs * grad_probs).astype(jnp.bfloat16)
            value_term = jnp.dot(
                probs.astype(jnp.bfloat16), grads, preferred_element_type=jnp.float32
            )
            key_term = jnp.dot(grad_scores, queries, preferred_element_type=jnp.float32)
            grad_values = value_term if grad_values is None else grad_values + value_term
            grad_keys = key_term if grad_keys is None else grad_keys + key_term
            rows = slice(head * HEAD_DIM, (head + 1) * HEAD_DIM)
            dqt_ref[rows, start : start + block] += jnp.dot(
                keys_across, grad_scores, preferred_element_type=jnp.float32
            )
        return grad_keys, grad_values

    def both_heads(key_source, value_source):
        (dk0, dv0), (dk1, dv1) = (
            absorb_keys(head, key_source[head], value_source[head]) for head in range(2)
        )
        lane = lax.broadcasted_iota(jnp.int32, dk0.shape, 1)
        return (
            jnp.where(lane < HEAD_DIM, low, pltpu.roll(high, HEAD_DIM, 1)).astype(jnp.bfloat16)
            for low, high in ((dk0, dk1), (dv0, dv1))
        )

    dk_ref[...], dv_ref[...] = both_heads(k_ref, v_ref)

    @pl.when(step == pl.num_programs(0) - 1)
    def _():
        dtk_ref[...], dtv_ref[...] = both_heads(tk_ref, tv_ref)
        for start in range(0, PIXELS, block):
            dq_ref[start : start + block, :] = (
                jnp.transpose(dqt_ref[:, start : start + block]) * (1.0 / math.sqrt(HEAD_DIM))
            ).astype(jnp.bfloat16)


def attend_back(queries, grads, attended, keys, values, text_keys, text_values):
    block = BACK_KEYS
    rows = (PIXELS, OWN)
    text_rows = (TEXT_PAD, OWN)
    return call(
        attend_back_kernel,
        "attend_back",
        (PIXELS // block,),
        [whole(queries), whole(grads), whole(attended)]
        + [(item, (2, block, LANES), lambda step: (0, step, 0)) for item in (keys, values)]
        + [whole(text_keys), whole(text_values)],
        [
            (rows, jnp.bfloat16, rows, None),
            (rows, jnp.bfloat16, (block, OWN), row_chunk),
            (rows, jnp.bfloat16, (block, OWN), row_chunk),
            (text_rows, jnp.bfloat16, text_rows, None),
            (text_rows, jnp.bfloat16, text_rows, None),
        ],
        [
            pltpu.VMEM((2, PIXELS, LANES), jnp.bfloat16),
            pltpu.VMEM((OWN, PIXELS), jnp.float32),
        ],
        flops=20 * PIXELS * (PIXELS + TEXT_PAD) * LANES,
        read=PIXELS * LANES * 20,
    )


def triple_blocks(grads):
    return [(item, (CHUNK, OWN), row_chunk) for item in grads]


def join_triple(refs):
    return jnp.concatenate([item[...] for item in refs], axis=1)


def qkv_back_kernel(member_ref, *refs):
    triple, weight_ref, outs, near_ref = refs[:3], refs[3], refs[4 : 4 + MEMBERS], refs[4 + MEMBERS]

    @pl.when(pl.program_id(0) == 0)
    def _():
        near_weights(member_ref, weight_ref, near_ref)

    terms = jnp.dot(join_triple(triple), near_ref[...], preferred_element_type=jnp.float32)
    for distance in range(MEMBERS):
        outs[distance][...] = terms[:, distance * OWN : (distance + 1) * OWN].astype(jnp.bfloat16)


def qkv_back(member, grads, weight, after):
    return call(
        qkv_back_kernel,
        "qkv_back",
        (STEPS,),
        [(member, None, None)] + triple_blocks(grads) + [whole(weight)],
        [((PIXELS, OWN), jnp.bfloat16, (CHUNK, OWN), row_chunk)] * MEMBERS,
        [pltpu.VMEM((3 * OWN, C), jnp.bfloat16)],
        flops=2 * PIXELS * 3 * OWN * C,
        read=PIXELS * C * 4,
        after=after,
    )


def norm_back_terms(gain_sum, bias_sum, own_ref, gain):
    first, second = group_sums(gain * bias_sum, gain * gain_sum, C // GROUPS)
    return first * own_ref[8:9], second * own_ref[8:9]


def third_back_kernel(
    member_ref,
    mine_ref,
    first_ref,
    second_ref,
    normed_ref,
    cot_ref,
    valid_ref,
    third_ref,
    own_ref,
    weight_ref,
    *refs,
):
    outs, refs = refs[:MEMBERS], refs[MEMBERS:]
    low_ref, taps_ref, totals_ref, near_ref, grads_ref = refs
    step = pl.program_id(0)

    @pl.when(step == 0)
    def _():
        near_weights(member_ref, weight_ref, near_ref)
        zero = jnp.zeros((1, OWN), jnp.float32)

        def gather(at, carried):
            rows = chunk_rows(at)
            grads = (
                mine_ref[rows, :].astype(jnp.float32)
                + first_ref[rows, :].astype(jnp.float32)
                + second_ref[rows, :].astype(jnp.float32)
            )
            cots = cot_ref[at].astype(jnp.float32)
            grads_ref[rows, :] = grads * own_ref[4:5]
            return (
                carried[0] + column_sums(grads * normed_ref[rows, :]),
                carried[1] + column_sums(grads),
                carried[2] + column_sums(cots),
            )

        gain_sum, bias_sum, cot_sum = lax.fori_loop(0, STEPS, gather, (zero, zero, zero))

        first, second = norm_back_terms(gain_sum, bias_sum, own_ref, own_ref[4:5])
        totals_ref[...] = jnp.concatenate(
            [gain_sum, bias_sum, zero, cot_sum, jnp.zeros((4, OWN), jnp.float32)], axis=0
        )

        def finish(at):
            rows = chunk_rows(at)
            valid = valid_ref[rows, :].astype(jnp.float32)
            total = grads_ref[rows, :] - valid * (first + normed_ref[rows, :] * second)
            total = total * third_ref[1:2] + cot_ref[at].astype(jnp.float32)
            low_ref[rows, :] = total.astype(jnp.bfloat16)
            totals_ref[2:3] += column_sums(total)
            return total

        write_sideways(taps_ref, finish)

    terms = jnp.dot(tap_chunk(taps_ref, step), near_ref[...], preferred_element_type=jnp.float32)
    for distance in range(MEMBERS):
        outs[distance][...] = terms[:, distance * OWN : (distance + 1) * OWN].astype(jnp.bfloat16)


def third_back(member, sums, normed, cots, valid, third, own, weight, after):
    rows = (PIXELS, OWN)
    taps = (3, PIXELS + 2 * WIDTH, OWN)
    return call(
        third_back_kernel,
        "third_back",
        (STEPS,),
        [(member, None, None)]
        + [whole(item) for item in sums]
        + [whole(normed), whole(cots), whole(valid), whole(third), whole(own), whole(weight)],
        [(rows, jnp.bfloat16, (CHUNK, OWN), row_chunk)] * MEMBERS
        + [
            (rows, jnp.bfloat16, rows, None),
            (taps, jnp.bfloat16, taps, None),
            ((8, OWN), jnp.float32, (8, OWN), None),
        ],
        [
            pltpu.VMEM((TAPS, C), jnp.bfloat16),
            pltpu.VMEM(rows, jnp.float32),
        ],
        flops=2 * PIXELS * TAPS * C,
        read=PIXELS * C * 4,
        after=after,
    )


def second_back_kernel(
    member_ref,
    mine_ref,
    first_ref,
    second_ref,
    normed_ref,
    low_ref,
    valid_ref,
    stats_ref,
    own_ref,
    weight_ref,
    skip_ref,
    image_ref,
    full_ref,
    out_ref,
    taps_ref,
    totals_ref,
    firsts_ref,
    grads_ref,
):
    step = pl.program_id(0)

    @pl.when(step == 0)
    def _():
        zero = jnp.zeros((1, OWN), jnp.float32)

        def gather(at, carried):
            rows = chunk_rows(at)
            normed = normed_ref[rows, :]
            shifted_rows = normed * own_ref[0:1] + own_ref[1:2]
            values = shifted_rows * own_ref[2:3] + own_ref[3:4]
            gate = sigmoid(values)
            slope = gate * (1.0 + values * (1.0 - gate))
            grads = (
                mine_ref[rows, :].astype(jnp.float32)
                + first_ref[rows, :].astype(jnp.float32)
                + second_ref[rows, :].astype(jnp.float32)
            )
            grads = grads * valid_ref[rows, :].astype(jnp.float32) * slope
            inner = grads * own_ref[2:3]
            grads_ref[rows, :] = inner * own_ref[0:1]
            return (
                carried[0] + column_sums(grads * shifted_rows),
                carried[1] + column_sums(grads),
                carried[2] + column_sums(inner * normed),
                carried[3] + column_sums(inner),
            )

        totals = lax.fori_loop(0, STEPS, gather, (zero,) * 4)
        totals_ref[...] = jnp.concatenate(
            list(totals) + [jnp.zeros((4, OWN), jnp.float32)], axis=0
        )

        first, second = norm_back_terms(totals[2], totals[3], own_ref, own_ref[0:1])

        def finish(at):
            rows = chunk_rows(at)
            valid = valid_ref[rows, :].astype(jnp.float32)
            total = grads_ref[rows, :] - valid * (first + normed_ref[rows, :] * second)
            return total * stats_ref[1:2]

        write_sideways(taps_ref, finish)
        firsts_ref[...] = jnp.zeros_like(firsts_ref)

    at = member_ref[0] ^ step
    rows = chunk_rows(at)
    grads = jnp.dot(tap_chunk(taps_ref, at), weight_ref[...], preferred_element_type=jnp.float32)
    image = image_ref[rows, :].astype(jnp.float32)
    values = image * full_ref[2:3] + full_ref[3:4]
    gate = sigmoid(values)
    slope = gate * (1.0 + values * (1.0 - gate))
    valid = valid_ref[rows, :].astype(jnp.float32)
    grads = grads * jnp.concatenate([valid] * (C_IN // LANES), axis=1) * slope
    normed = (image - full_ref[0:1]) * full_ref[1:2]
    firsts_ref[0:1] += column_sums(grads * normed)
    firsts_ref[1:2] += column_sums(grads)
    skipped = jnp.dot(low_ref[rows, :], skip_ref[...], preferred_element_type=jnp.float32)
    out_ref[0] = (grads * full_ref[2:3] + skipped).astype(jnp.bfloat16)


def second_back(member, sums, normed, low, valid, stats, own, weight, raw, image_all, full, after):
    rows = (PIXELS, OWN)
    taps = (3, PIXELS + 2 * WIDTH, OWN)
    return call(
        second_back_kernel,
        "second_back",
        (STEPS,),
        [(member, None, None)]
        + [whole(item) for item in sums]
        + [whole(normed), whole(low), whole(valid), whole(stats), whole(own)]
        + [whole(weight), skip_block(raw), whole(image_all), whole(full)],
        [
            (
                (MEMBERS, CHUNK, C_IN),
                jnp.bfloat16,
                (1, CHUNK, C_IN),
                lambda step: (step, 0, 0),
            ),
            (taps, jnp.bfloat16, taps, None),
            ((8, OWN), jnp.float32, (8, OWN), None),
            ((8, C_IN), jnp.float32, (8, C_IN), None),
        ],
        [pltpu.VMEM(rows, jnp.float32)],
        flops=0,
        read=0,
        after=after,
    )


def tap_grad_kernel(count, member_ref, taps_ref, *refs):
    inputs, refs = refs[:count], refs[count:]
    if count == 1:
        low_ref, image_ref, out_ref, sums_ref, skip_ref = refs
    else:
        out_ref, sums_ref = refs
    step = pl.program_id(0)

    @pl.when(step == 0)
    def _():
        sums_ref[...] = jnp.zeros_like(sums_ref)
        if count == 1:
            skip_ref[...] = jnp.zeros_like(skip_ref)

    if count == 1:
        skip_ref[...] += lax.dot_general(
            low_ref[...], image_ref[...], TN, preferred_element_type=jnp.float32
        )

    joined = jnp.concatenate([item[...] for item in inputs], axis=1)
    sums_ref[...] += lax.dot_general(
        tap_chunk(taps_ref, step), joined, TN, preferred_element_type=jnp.float32
    )

    @pl.when(step == STEPS - 1)
    def _():
        share = OWN // PLANES
        if count == 1:
            for z in range(PLANES):
                out_ref[z, 0, 9] = skip_ref[z * share : (z + 1) * share, :].astype(jnp.bfloat16)
        for tap in range(9):
            for z in range(PLANES):
                rows = slice(tap * OWN + z * share, tap * OWN + (z + 1) * share)
                if count == 1:
                    out_ref[z, 0, tap] = sums_ref[rows, :].astype(jnp.bfloat16)
                else:
                    for distance in range(count):
                        columns = slice(distance * OWN, (distance + 1) * OWN)
                        out_ref[z, member_ref[0] ^ distance, tap] = sums_ref[rows, columns].astype(
                            jnp.bfloat16
                        )


def tap_grad(member, taps, inputs, skip=(), after=()):
    count, width = len(inputs), inputs[0].shape[1]
    shape = (PLANES, count, 10 if skip else 9, OWN // PLANES, width)
    return call(
        functools.partial(tap_grad_kernel, count),
        "tap_grad",
        (STEPS,),
        [(member, None, None), whole(taps)]
        + [(item, (CHUNK, item.shape[1]), row_chunk) for item in inputs + list(skip)],
        [(shape, jnp.bfloat16, shape, None)],
        [pltpu.VMEM((TAPS, count * width), jnp.float32)]
        + [pltpu.VMEM((OWN, C_IN), jnp.float32)] * (1 if skip else 0),
        flops=0,
        after=after,
    )[0]


def qkv_grad_kernel(member_ref, targets_ref, *refs):
    triple, inputs, (out_ref, sums_ref) = refs[:3], refs[3 : 3 + MEMBERS], refs[3 + MEMBERS :]
    step = pl.program_id(0)

    @pl.when(step == 0)
    def _():
        sums_ref[...] = jnp.zeros_like(sums_ref)

    joined = jnp.concatenate([item[...] for item in inputs], axis=1)
    sums_ref[...] += lax.dot_general(join_triple(triple), joined, TN, preferred_element_type=jnp.float32)

    @pl.when(step == STEPS - 1)
    def _():
        for z in range(PLANES):
            for slot in range(SLOTS):
                rows = pl.ds(pl.multiple_of(targets_ref[z * SLOTS + slot], 32), 32)
                for distance in range(MEMBERS):
                    columns = slice(distance * OWN, (distance + 1) * OWN)
                    out_ref[z, slot, member_ref[0] ^ distance] = sums_ref[rows, columns].astype(
                        jnp.bfloat16
                    )


def qkv_grad(member, targets, grads, inputs, after):
    shape = (PLANES, SLOTS, MEMBERS, OWN // PLANES, OWN)
    return call(
        qkv_grad_kernel,
        "qkv_grad",
        (STEPS,),
        [(member, None, None), (targets, None, None)]
        + triple_blocks(grads)
        + [(item, (CHUNK, OWN), row_chunk) for item in inputs],
        [(shape, jnp.bfloat16, shape, None)],
        [pltpu.VMEM((3 * OWN, C), jnp.float32)],
        flops=0,
        after=after,
    )[0]


def pass_kernel(value_ref, out_ref):
    out_ref[...] = value_ref[...]


def passed(values, after):
    spec = (values.shape, values.dtype, values.shape, None)
    return call(pass_kernel, "passed", (), [whole(values)], [spec], after=after)[0]


def widen_kernel(value_ref, out_ref):
    out_ref[...] = value_ref[...].astype(jnp.float32)


def widened(values, after):
    return call(
        widen_kernel,
        "widen",
        (),
        [whole(values)],
        [(values.shape, jnp.float32, values.shape, None)],
        after=after,
    )[0]


def along_z(blocks):
    z = lax.axis_index("z")

    def block(distance):
        return lax.dynamic_index_in_dim(blocks, z ^ distance, 0, keepdims=False)

    def moved(values, distance):
        return lax.ppermute(values, "z", [(at, at ^ distance) for at in range(PLANES)])

    near, far = moved(block(1), 1), moved(block(3), 1)
    far = rounded(block(2).astype(jnp.float32) + far.astype(jnp.float32))
    return (block(0), near, moved(far, 2)), far


def turns_z(piece):
    return [piece] + [
        lax.ppermute(piece, "z", [(at, (at + turn) % PLANES) for at in range(PLANES)])
        for turn in range(1, PLANES)
    ]


def gather_z(piece):
    z = lax.axis_index("z")
    turned = turns_z(piece)
    zero = jnp.zeros_like(piece)
    return jnp.stack(
        [
            sum(jnp.where((z - at) % PLANES == turn, turned[turn], zero) for turn in range(PLANES))
            for at in range(PLANES)
        ]
    )


def order_matrix(dtype):
    shape = (ACROSS * OWN, ACROSS * OWN)
    source = lax.broadcasted_iota(jnp.int32, shape, 0)
    target = lax.broadcasted_iota(jnp.int32, shape, 1)
    x, z, place = source // OWN, source % OWN // 32, source % 32
    return (target == (z * ACROSS + x) * 32 + place).astype(jnp.float32).astype(dtype)


def own_columns(values, order, y, core):
    start = (2 * y + core) * ACROSS * OWN
    block = values[:, start : start + ACROSS * OWN]
    return lax.dot_general(block, order, NT, preferred_element_type=jnp.float32).astype(jnp.bfloat16)


def square(count):
    return [(core, y) for core in range(2) for y in range(count)]


def conv2_kernel(raw_ref, out_ref):
    order = order_matrix(jnp.bfloat16)
    for tap in range(9):
        rows = slice(tap * OWN, (tap + 1) * OWN)
        values = raw_ref[:, tap * C : (tap + 1) * C]
        for core, y in square(2):
            columns = own_columns(values, order, y, core)
            for x in range(ACROSS):
                out_ref[4 * core + 2 * y + x, rows, :] = columns[:, x * OWN : (x + 1) * OWN]


def conv2_blocks(raw, after):
    shape = (MEMBERS, TAPS, OWN)
    return call(
        conv2_kernel,
        "conv2_blocks",
        (),
        [whole(raw)],
        [(shape, jnp.bfloat16, shape, None)],
        after=after,
    )[0]


def choose_kernel(places_ref, units_ref, out_ref):
    for slot in range(SLOTS):
        out_ref[slot] = units_ref[places_ref[slot]]


def choose_units(places, units):
    shape = (SLOTS,) + units.shape[1:]
    return call(
        choose_kernel,
        "choose_units",
        (),
        [(places, None, None), whole(units)],
        [(shape, units.dtype, shape, None)],
    )[0]


def qkv_blocks_kernel(targets_ref, units_ref, out_ref):
    order = order_matrix(jnp.bfloat16)
    for z in range(PLANES):
        for slot in range(SLOTS):
            rows = pl.ds(pl.multiple_of(targets_ref[z * SLOTS + slot], 32), 32)
            values = units_ref[z, slot]
            for core, y in square(2):
                columns = own_columns(values, order, y, core)
                for x in range(ACROSS):
                    out_ref[4 * core + 2 * y + x, rows, :] = columns[:, x * OWN : (x + 1) * OWN]


def qkv_blocks(targets, units, after):
    shape = (MEMBERS, 3 * OWN, OWN)
    return call(
        qkv_blocks_kernel,
        "qkv_blocks",
        (),
        [(targets, None, None), whole(units)],
        [(shape, jnp.bfloat16, shape, None)],
        after=after,
    )[0]


def qkv_finish_kernel(source_ref, units_ref, out_ref):
    order = order_matrix(jnp.bfloat16)
    for place in range(3):
        unit = units_ref[source_ref[place]]
        for core, y in square(2):
            member = 4 * core + 2 * y
            joined = jnp.concatenate([unit[member], unit[member + 1]], axis=1)
            start = (2 * y + core) * ACROSS * OWN
            out_ref[place * 32 : (place + 1) * 32, start : start + ACROSS * OWN] = jnp.dot(
                joined, order, preferred_element_type=jnp.float32
            )


def qkv_finish(source, units, after):
    shape = (3 * 32, C)
    return call(
        qkv_finish_kernel,
        "qkv_finish",
        (),
        [(source, None, None), whole(units)],
        [(shape, jnp.float32, shape, None)],
        after=after,
    )[0]


def cot_kernel(cot_ref, weight_ref, out_ref):
    cots = cot_ref[...]
    order = order_matrix(jnp.bfloat16)
    mixed = jnp.dot(cots, weight_ref[...], preferred_element_type=jnp.float32).astype(jnp.bfloat16)
    for core, y in square(2):
        columns = own_columns(cots, order, y, core)
        for x in range(ACROSS):
            out_ref[4 * core + 2 * y + x, :, :OWN] = columns[:, x * OWN : (x + 1) * OWN]
    for member in range(MEMBERS):
        out_ref[member, :, OWN:] = mixed[:, member * OWN : (member + 1) * OWN]


def cot_blocks(cots, weight):
    shape = (MEMBERS, CHUNK, 2 * OWN)
    return call(
        cot_kernel,
        "cot_blocks",
        (),
        [whole(cots), whole(weight)],
        [(shape, jnp.bfloat16, shape, None)],
        flops=2 * CHUNK * C * C,
    )[0]


def output_kernel(moved_ref, weight_ref, cot_ref, shift_ref, out_ref, grad_ref):
    mixed = jnp.concatenate([moved_ref[member, :, :OWN] for member in range(MEMBERS)], axis=1)
    product = lax.dot_general(mixed, weight_ref[...], NT, preferred_element_type=jnp.float32)
    order = order_matrix(jnp.bfloat16)
    for core, y in square(2):
        member = 4 * core + 2 * y
        residual = jnp.concatenate(
            [moved_ref[member, :, OWN:], moved_ref[member + 1, :, OWN:]], axis=1
        )
        residual = jnp.dot(residual, order, preferred_element_type=jnp.float32)
        start = (2 * y + core) * ACROSS * OWN
        columns = slice(start, start + ACROSS * OWN)
        out_ref[:, columns] = (residual + product[:, columns] + shift_ref[:, columns]).astype(
            jnp.bfloat16
        )
    grads = lax.dot_general(cot_ref[...], mixed, TN, preferred_element_type=jnp.float32)
    for core, y in square(2):
        for z in range(PLANES):
            for x in range(ACROSS):
                start = ((2 * y + core) * PLANES + z) * ACROSS * 32 + x * 32
                grad_ref[4 * core + 2 * y + x, z * 32 : (z + 1) * 32, :] = grads[
                    start : start + 32
                ].astype(jnp.bfloat16)


def output_rows(moved, weight, cots, shift, after):
    shapes = ((CHUNK, C), (MEMBERS, OWN, C))
    return call(
        output_kernel,
        "output_rows",
        (),
        [whole(moved), whole(weight), whole(cots), whole(shift)],
        [(shape, jnp.bfloat16, shape, None) for shape in shapes],
        flops=0,
        after=after,
    )


def natural_kernel(first_ref, second_ref, third_ref, out_ref):
    taps, rows = first_ref.shape[1], first_ref.shape[2]
    width = ACROSS * OWN
    order = order_matrix(jnp.float32)

    def total(at):
        parts = [item[at].astype(jnp.float32) for item in (first_ref, second_ref, third_ref)]
        return ((parts[0] + parts[1]) + parts[2]).reshape(taps * rows, OWN)

    for core in range(2):
        for y in range(2):
            at = 4 * core + 2 * y
            joined = jnp.concatenate([total(at), total(at + 1)], axis=1)
            ordered = jnp.dot(
                joined, order, precision=lax.Precision.HIGHEST, preferred_element_type=jnp.float32
            )
            for tap in range(taps):
                columns = slice(tap * C + (2 * y + core) * width, tap * C + (2 * y + core + 1) * width)
                out_ref[:, columns] = ordered[tap * rows : (tap + 1) * rows]


def natural_sum(parts, after):
    taps, rows = parts[0].shape[1:3]
    shape = (rows, taps * C)
    return call(
        natural_kernel,
        "natural_sum",
        (),
        [whole(item) for item in parts],
        [(shape, jnp.float32, shape, None)],
        after=after,
    )[0]


def plain_kernel(value_ref, out_ref, skip_ref):
    taps, width = value_ref.shape[0] - 1, value_ref.shape[2]
    for tap in range(taps):
        out_ref[:, tap * width : (tap + 1) * width] = value_ref[tap].astype(jnp.float32)
    skip_ref[...] = value_ref[taps].astype(jnp.float32)


def plain_sum(values, after):
    taps, rows, width = values.shape
    shapes = ((rows, (taps - 1) * width), (rows, width))
    return call(
        plain_kernel,
        "plain_sum",
        (),
        [whole(values)],
        [(shape, jnp.float32, shape, None) for shape in shapes],
        after=after,
    )


def text_pairs(back):
    rounds = ([], [])
    for y, c, z, x in every_place():
        piece, plane = 2 * z + x, 2 * c + y
        for half in range(2):
            member = 2 * (piece % 4) + half
            target = flat_device(member // 2 % 2, member // 4, plane, member % 2)
            pair = (flat_device(y, c, z, x), target)
            rounds[half ^ (piece // 4)].append(pair[::-1] if back else pair)
    return rounds


def text_to_heads(text_slice):
    late = (2 * lax.axis_index("z") + lax.axis_index("x")) // 4
    halves = (text_slice[:, :OWN], text_slice[:, OWN:])
    first, second = (
        lax.ppermute(jnp.where(late == at, halves[0], halves[1]), EVERY, text_pairs(False)[at])
        for at in range(2)
    )
    even = lax.axis_index("x") == 0
    return jnp.where(even, first, second), jnp.where(even, second, first)


def text_from_heads(text_keys, text_values):
    even = lax.axis_index("x") == 0
    first = jnp.where(even, text_keys, text_values)
    second = jnp.where(even, text_values, text_keys)
    first, second = (
        lax.ppermute(item, EVERY, text_pairs(True)[at]) for at, item in enumerate((first, second))
    )
    late = (2 * lax.axis_index("z") + lax.axis_index("x")) // 4 == 1
    return jnp.concatenate(
        [jnp.where(late, second, first), jnp.where(late, first, second)], axis=1
    )


def text_lanes(values, *columns):
    padded = jnp.pad(values, ((0, TEXT_PAD - values.shape[0]), (0, 0)))
    heads = jnp.transpose(padded.reshape(TEXT_PAD, 2, HEAD_DIM), (1, 0, 2))
    extra = [
        jnp.broadcast_to(jnp.asarray(column, jnp.bfloat16).reshape(1, -1, 1), (2, TEXT_PAD, 1))
        for column in columns
    ]
    joined = jnp.concatenate([heads] + extra, axis=2)
    return jnp.pad(joined, ((0, 0), (0, 0), (0, LANES - joined.shape[2])))


def plane_shards(
    image,
    mask,
    timestep,
    pooled,
    text,
    text_mask,
    cotangent,
    conv1_weight,
    conv2_weight,
    skip_weight,
    emb_weight,
    qkv_weight,
    out_weight,
    text_weight,
    gn1_gain,
    gn1_bias,
    emb_bias,
    gn2_gain,
    gn2_bias,
    skip_bias,
    gn3_gain,
    gn3_bias,
    out_bias,
):
    z_here, x_here = lax.axis_index("z"), lax.axis_index("x")
    a_here = lax.axis_index(("y", "core"))
    member = lax.axis_index(PLANE)
    member_word = member.reshape(1).astype(jnp.int32)
    device = lax.axis_index(EVERY)

    extents = jnp.stack([timestep[0], jnp.sum(mask[0, :, 0]), jnp.sum(mask[0, 0]), jnp.sum(text_mask)])
    exact = jnp.concatenate([pooled[0], extents.astype(jnp.float32)])

    def both(values, axis):
        other = lax.ppermute(values, axis, SWITCH)
        low = lax.axis_index(axis) == 0
        return jnp.stack([jnp.where(low, values, other), jnp.where(low, other, values)])

    image_halves = [
        swapped(half) for half in jnp.split(image[0].reshape(CHUNK, C_IN), 2, axis=0)
    ]
    exact = passed(both(exact, "y"), (image_halves[0],))
    exact = both(exact, "core").reshape(PLANES, -1)
    extents = exact[:, EMB:]
    valid_rows, valid_columns, text_count = extents[z_here, 1:]
    count = valid_rows * valid_columns
    pixel = lax.broadcasted_iota(jnp.int32, (PIXELS, OWN), 0).astype(jnp.float32)
    pixel_row = jnp.floor(pixel / WIDTH)
    valid = (pixel_row < valid_rows) & (pixel - pixel_row * WIDTH < valid_columns)
    valid = valid.astype(jnp.bfloat16)
    half_width = EMB // 2
    frequency = jnp.exp(-math.log(10000.0) * jnp.arange(half_width, dtype=jnp.float32) / half_width)
    angles = extents[:, :1] * frequency[None, :]
    embedding = rounded(
        jax.nn.silu(jnp.concatenate([jnp.cos(angles), jnp.sin(angles)], axis=1) + exact[:, :EMB])
    )
    rest = project(embedding, emb_weight) + emb_bias.astype(jnp.float32)

    rows_here = conv1_weight.shape[0]
    places, targets, sources = (jnp.array(table, jnp.int32) for table in unit_tables())
    places = lax.dynamic_slice(places, (z_here, member, 0), (1, 1, SLOTS)).reshape(-1)
    targets = lax.dynamic_slice_in_dim(targets, member, 1, 1).reshape(-1)
    sources = lax.dynamic_index_in_dim(sources, device, 0, keepdims=False)

    from_y = lax.ppermute(text_weight, "y", SWITCH)
    text_pieces = (text_weight, lax.ppermute(text_weight, "core", SWITCH), from_y)
    text_pieces += (lax.ppermute(from_y, "core", SWITCH),)
    text_len = text.shape[1]
    text_blocks = text[0].reshape(text_len, PLANES, -1)
    text_slice = rounded(
        sum(
            jnp.dot(
                lax.dynamic_index_in_dim(text_blocks, a_here ^ distance, 1, keepdims=False),
                piece,
                preferred_element_type=jnp.float32,
            )
            for distance, piece in enumerate(text_pieces)
        )
    )
    text_keys, text_values = text_to_heads(text_slice)
    text_bias = jnp.where(jnp.arange(TEXT_PAD) < text_count, 0.0, neg_big)
    minus = -jnp.ones((TEXT_PAD,), jnp.float32)
    text_keys = text_lanes(text_keys, text_bias, minus, minus, minus)
    text_values = text_lanes(text_values, -minus, minus, minus, minus)

    parts = []
    for _ in range(3):
        part = lax.reduce_precision(rest, 8, 7)
        parts.append(rounded(part).reshape(-1))
        rest = rest - part
    vectors = (
        gn1_gain,
        gn1_bias,
        gn2_gain,
        gn2_bias,
        skip_bias,
        gn3_gain,
        gn3_bias,
        out_bias,
    )
    packed = jnp.concatenate(list(vectors) + parts)
    image_block = jnp.concatenate(image_halves, axis=0)
    filled = -packed.shape[0] % (4 * C_IN) + packed.shape[0]
    packed = jnp.pad(packed, (0, filled - packed.shape[0])).reshape(-1, LANES)
    packed = gather_z(passed(packed, (image_halves[1],)))
    image_blocks = plane_gather(
        jnp.concatenate(image_halves + [packed.reshape(-1, C_IN)], axis=0),
        (text_keys, text_values),
    )
    small = jnp.stack([block[CHUNK:].reshape(PLANES, filled) for block in image_blocks])
    distances = jnp.arange(MEMBERS)[:, None] ^ member
    chosen = distances == jnp.arange(MEMBERS)[None, :]
    small = jnp.sum(
        jnp.where(chosen[:, :, None, None], small[None].astype(jnp.float32), 0.0), axis=1
    )
    small = jnp.transpose(small.reshape(2, 2, ACROSS, PLANES, filled), (1, 0, 3, 2, 4))
    small = small.reshape(PLANES, PLANES, ACROSS, filled)
    bounds = [0]
    for item in vectors:
        bounds.append(bounds[-1] + item.shape[0])
    small_parts = [small[..., bounds[at] : bounds[at + 1]] for at in range(len(vectors))]
    gain_one, bias_one = (part.reshape(-1) for part in small_parts[:2])
    out_shift = small_parts[7].reshape(1, C)
    own_parts = [own_channels(part).reshape(-1) for part in small_parts[2:7]]
    gain_two, bias_two, skip_shift, gain_three, bias_three = own_parts
    emb_rows = emb_weight.shape[0]
    mods = small[..., bounds[-1] : bounds[-1] + 3 * PLANES * emb_rows]
    mods = mods.reshape(PLANES * MEMBERS, 3, PLANES, emb_rows)
    mods = lax.dynamic_index_in_dim(mods, z_here, 2, keepdims=False)
    mods = ((mods[:, 0] + mods[:, 1]) + mods[:, 2]).reshape(2, PLANES, PLANES, ACROSS, -1)
    scale_own = 1.0 + own_channels(mods[0]).reshape(-1)
    shift_own = own_channels(mods[1]).reshape(-1)

    conv1_raw = jnp.concatenate([conv1_weight, skip_weight], axis=1)
    conv1_raw = lax.all_gather(passed(conv1_raw, (image_halves[1],)), "z", axis=0, tiled=True)
    cot_rows = swapped(cotangent[0].reshape(CHUNK, C))
    conv2_own = conv2_blocks(
        lax.all_gather(conv2_weight, "z", axis=0, tiled=True), (cot_rows,)
    )
    qkv_units = lax.all_gather(qkv_weight.reshape(3, rows_here, C), PLANE, axis=0, tiled=True)
    qkv_chosen = choose_units(places, qkv_units)
    qkv_units = lax.all_gather(qkv_chosen, "z", axis=0, tiled=False)
    qkv_own = qkv_blocks(targets, qkv_units, ())

    per_group, first_width = C // GROUPS, C_IN // GROUPS
    own = jnp.stack(
        [gain_two, bias_two, scale_own, shift_own, gain_three, bias_three, skip_shift, skip_shift]
        + [jnp.broadcast_to(1.0 / (count * per_group), (OWN,))]
        + [jnp.zeros((OWN,), jnp.float32)] * 7
    )
    full = jnp.stack(
        [gain_one, bias_one, jnp.broadcast_to(1.0 / (count * first_width), (C_IN,))]
        + [jnp.zeros((C_IN,), jnp.float32)] * 5
    )

    def exchange(blocks):
        return lax.all_to_all(blocks, PLANE, split_axis=0, concat_axis=0, tiled=True)

    out_all = lax.all_gather(out_weight, EVERY, axis=0, tiled=True)
    cot_ready = cot_blocks(cot_rows, out_all)

    image_all, first_act, second_normed, second_act, conv1_own, first_stats, second_stats = first_layer(
        member_word, image_blocks, valid, conv1_raw, full, own, ()
    )
    second_pieces = plane_gather(second_act, (conv2_own, qkv_chosen))
    third_normed, attn_input, residual_low, third_stats = second_layer(
        member_word, second_pieces, image_all, valid, conv2_own, conv1_raw, own, ()
    )

    attn_pieces = plane_gather(attn_input, (qkv_own,))

    queries, keys, values, cot_passed = project_qkv(
        member_word, attn_pieces, valid, qkv_own, cot_ready
    )
    cot_moved = exchange(cot_passed)
    cot_own, grad_mixed = cot_moved[:, :, :OWN], cot_moved[:, :, OWN:].reshape(PIXELS, OWN)

    attended, mixed, back_queries = attend(
        queries, residual_low, keys, values, text_keys, text_values
    )

    moved = exchange(mixed.reshape(MEMBERS, CHUNK, 2 * OWN))

    triple_grads = attend_back(
        back_queries, grad_mixed, attended, keys, values, text_keys, text_values
    )
    triple_grads, (text_dk, text_dv) = triple_grads[:3], triple_grads[3:]

    third_terms = qkv_back(member_word, triple_grads, qkv_own, (moved,))
    grad_third, third_tokens = plane_sum(third_terms)
    qkv_terms = qkv_grad(member_word, targets, triple_grads, attn_pieces, third_tokens[1:])
    qkv_sums = lax.psum_scatter(qkv_terms, "z", scatter_dimension=0, tiled=True)[0]

    output, out_grad = output_rows(moved, out_all, cot_rows, out_shift, third_tokens[1:])
    out_terms = out_grad
    out_grad = lax.psum_scatter(out_grad, PLANE, scatter_dimension=0, tiled=True)[0]

    text_grads = text_from_heads(text_dk[:text_len], text_dv[:text_len])
    text_terms = rounded(weight_grad(text[0], text_grads))
    text_weight_grad = lax.psum_scatter(
        text_terms, ("y", "core"), scatter_dimension=0, tiled=True
    )

    third = third_back(
        member_word,
        grad_third,
        third_normed,
        cot_own,
        valid,
        third_stats,
        own,
        conv2_own,
        (qkv_terms, out_terms, text_terms),
    )
    second_terms, (dres, residual_taps, third_sums) = third[:MEMBERS], third[MEMBERS:]
    conv2_terms = []

    def second_filler(early):
        conv2_terms.append(tap_grad(member_word, residual_taps, second_pieces, (), early))
        return conv2_terms

    grad_second, second_tokens = plane_sum(second_terms, second_filler)
    (conv2_terms,) = conv2_terms
    conv2_parts, conv2_sent = along_z(conv2_terms)

    qkv_sums = passed(qkv_sums, second_tokens[1:])
    out_grad = passed(out_grad, second_tokens[1:])
    out_grad = lax.psum_scatter(out_grad, "z", scatter_dimension=0, tiled=True)

    output = swapped(passed(output, second_tokens[1:]))

    image_terms, hidden_taps, second_sums, first_sums = second_back(
        member_word,
        grad_second,
        second_normed,
        dres,
        valid,
        second_stats,
        own,
        conv1_own,
        conv1_raw,
        image_all,
        first_stats,
        (conv2_sent,),
    )
    image_part, image_tokens = plane_sum([image_terms[distance] for distance in range(MEMBERS)])
    conv1_parts = tap_grad(
        member_word, hidden_taps, [first_act], (dres, image_all), (output, qkv_sums, conv2_parts[2])
    )
    image_part = sum(item.astype(jnp.float32) for item in image_part)
    qkv_sums = lax.all_gather(qkv_sums, PLANE, axis=0, tiled=True)
    conv1_sums = lax.psum_scatter(conv1_parts, "z", scatter_dimension=0, tiled=True)[0, 0]
    conv1_grad, skip_grad = plain_sum(conv1_sums, image_tokens[1:])
    conv2_grad = natural_sum(conv2_parts, image_tokens[1:])

    out_weight_grad = widened(out_grad, image_tokens[1:])
    text_weight_grad = widened(text_weight_grad, image_tokens[1:])

    own_all = small_gather(jnp.concatenate([second_sums[:4], third_sums[:4]], axis=0))
    own_all = own_all.reshape(PLANES, PLANES, ACROSS, 8, PLANES, OWN // PLANES)
    mods_grad = jnp.transpose(own_all[:, :, :, :2], (1, 3, 0, 4, 2, 5)).reshape(PLANES, 2 * C)
    mods_grad = lax.dynamic_slice_in_dim(mods_grad, device * emb_rows, emb_rows, 1)
    emb_weight_grad = jnp.dot(
        mods_grad.T, embedding.astype(jnp.float32), precision=lax.Precision.HIGHEST
    )
    emb_bias_grad = jnp.sum(mods_grad, axis=0)
    channel_sums = jnp.sum(own_all, axis=1)
    channel_sums = lax.dynamic_index_in_dim(channel_sums, a_here, 0, keepdims=False)
    channel_sums = lax.dynamic_index_in_dim(channel_sums, x_here, 0, keepdims=False)
    channel_sums = lax.dynamic_index_in_dim(channel_sums, z_here, 1, keepdims=False)

    first_here = first_sums[:2]
    for axis in PLANE:
        first_here = first_here + lax.ppermute(first_here, axis, SWITCH)
    grouped = jnp.sum((first_here * gain_one).reshape(2, GROUPS, first_width), axis=2)
    grouped = jnp.repeat(grouped / (count * first_width), first_width, axis=1)
    row_valid = lax.dynamic_slice_in_dim(valid[:, :1], member * CHUNK, CHUNK, 0)
    rows_normed = (image_block.astype(jnp.float32) - first_stats[0]) * first_stats[1]
    image_grad = image_part - row_valid.astype(jnp.float32) * first_stats[1] * (
        grouped[1] + rows_normed * grouped[0]
    )
    image_grad = rounded(image_grad)
    qkv_weight_grad = qkv_finish(sources, qkv_sums, (image_grad,))
    image_grad = swapped(image_grad).astype(jnp.float32).reshape(1, -1, WIDTH, C_IN)
    first_grads = lax.dynamic_slice_in_dim(
        sum(turns_z(first_here)), device * first_width, first_width, 1
    )
    return (
        output.reshape(1, -1, WIDTH, C),
        image_grad,
        conv1_grad,
        conv2_grad,
        skip_grad,
        emb_weight_grad,
        qkv_weight_grad,
        out_weight_grad,
        text_weight_grad,
        first_grads[0],
        first_grads[1],
        emb_bias_grad,
        channel_sums[2],
        channel_sums[3],
        channel_sums[6],
        channel_sums[4],
        channel_sums[5],
        channel_sums[7],
    )


def solution(mesh):
    in_specs = (
        P("img", "ha", None, None),
        P("img", None, None),
        P("img"),
        P("img", None),
        P("img", None, None),
        P("img", None),
        P("img", "ha", None, None),
        P(("img", "ha"), None),
        P(("img", "ha"), None),
        P(("img", "ha"), None),
        P(("img", "ha"), None),
        P(("img", "ha"), None),
        P(("img", "ha"), None),
        P("img", "ha"),
        P(("img", "ha")),
        P(("img", "ha")),
        P(("img", "ha")),
        P(("img", "ha")),
        P(("img", "ha")),
        P(("img", "ha")),
        P(("img", "ha")),
        P(("img", "ha")),
        P(("img", "ha")),
    )
    out_specs = (
        P("img", "ha", None, None),
        P("img", "ha", None, None),
        P(("img", "ha"), None),
        P(("img", "ha"), None),
        P(("img", "ha"), None),
        P(("img", "ha"), None),
        P(("img", "ha"), None),
        P(("img", "ha"), None),
        P("img", "ha"),
        P(("img", "ha")),
        P(("img", "ha")),
        P(("img", "ha")),
        P(("img", "ha")),
        P(("img", "ha")),
        P(("img", "ha")),
        P(("img", "ha")),
        P(("img", "ha")),
        P(("img", "ha")),
    )
    split_mesh = plane_mesh(mesh)
    if split_mesh is None:
        return jax.shard_map(
            shards, mesh=mesh, in_specs=in_specs, out_specs=out_specs, check_vma=False
        )
    in_specs, out_specs = (tuple(split_spec(item) for item in specs) for specs in (in_specs, out_specs))
    return jax.shard_map(
        plane_shards, mesh=split_mesh, in_specs=in_specs, out_specs=out_specs, check_vma=False
    )
```
